32 devices in a mesh: seq: 8 (over z, y), tp: 4 (over x, core).
Axes of the slice: x: 2, y: 2, z: 4, core: 2. Of those that a mesh axis runs over, the one named last changes fastest.
Arguments:
- tokens: bfloat16 [4096, 768], P('seq'), may hold values from -6 to 6
- cotangent: bfloat16 [4096, 768], P('seq'), may hold values from -6 to 6
- past_states: bfloat16 [4096, 768], P('seq'), may hold values from -6 to 6
- doc_ids: int32 [4096], P('seq'), may hold values from 0 to 4095, as said below
- cur_book: int32 [8], P('seq'), may hold values from 0 to 3
- past_book: int32 [8], P('seq'), may hold values from 0 to 3, as said below
- past_age: int32 [8], P('seq'), may hold values from 0 to 1, as said below
- ln1_gain: float32 [768], replicated, may hold values from 0.5 to 1.5
- ln1_bias: float32 [768], replicated, may hold values from -3 to 3
- qkv_weight: bfloat16 [768, 3, 768], P(None, None, 'tp'), may hold values from -0.21875 to 0.21875
- qv_bias: float32 [2, 768], P(None, 'tp'), may hold values from -3 to 3
- out_weight: bfloat16 [768, 768], P('tp'), may hold values from -0.75 to 0.75
- out_bias: float32 [768], replicated, may hold values from -3 to 3
- ln2_gain: float32 [768], replicated, may hold values from 0.5 to 1.5
- ln2_bias: float32 [768], replicated, may hold values from -3 to 3
- fc_weight: bfloat16 [768, 3072], P(None, 'tp'), may hold values from -0.21875 to 0.21875
- fc_bias: float32 [3072], P('tp'), may hold values from -3 to 3
- proj_weight: bfloat16 [3072, 768], P('tp'), may hold values from -0.109375 to 0.109375
- proj_bias: float32 [768], replicated, may hold values from -3 to 3
- mu_weight: float32 [12, 512], P('tp'), may hold values from -0.25 to 0.25
- sigma_weight: float32 [12, 512], P('tp'), may hold values from -0.25 to 0.25
Outputs:
- output: bfloat16 [4096, 768], P('seq')
- grad_tokens: bfloat16 [4096, 768], P('seq')
- grad_qkv_weight: float32 [768, 3, 768], P('seq', None, 'tp')
- grad_qv_bias: float32 [2, 768], P(None, 'tp')
- grad_out_weight: float32 [768, 768], P('tp', 'seq')
- grad_out_bias: float32 [768], replicated
- grad_fc_weight: float32 [768, 3072], P('seq', 'tp')
- grad_fc_bias: float32 [3072], P('tp')
- grad_proj_weight: float32 [3072, 768], P('tp', 'seq')
- grad_proj_bias: float32 [768], replicated
- grad_ln1_gain: float32 [768], replicated
- grad_ln1_bias: float32 [768], replicated
- grad_ln2_gain: float32 [768], replicated
- grad_ln2_bias: float32 [768], replicated
- grad_mu_weight: float32 [12, 512], P('tp')
- grad_sigma_weight: float32 [12, 512], P('tp')
The draws below stay inside these ranges and needn't reach their ends.
Inputs may be any that keep to these rules, and one draw needn't show every extreme that they name: `doc_ids`: each token's value is the position of the last token of its document, so values never fall along the tokens. One document starts inside the first 512 tokens and ends inside the last 512; the others are short. `past_book`: each of the 4 books has exactly 2 past segments. `past_age`: within each book the ages of its past segments are 0 to 1, each once.
All inputs are finite; a program needn't handle non-finite values.
Results may differ from the reference program's by a relative error of at most 0.019.
Values may be sent and summed in bfloat16 or wider, within the bound.
A program may use at most 128 MiB of HBM per device.

```python
import math
import jax
import jax.numpy as jnp
from jax import lax

D = 768
H = 12
DH = 64
FF = 3072
NB = 512
SEG = 512
BOOKS = 4
TOK_DEV = 512
SEGS = 8
TOKENS = 4096


def shared_order(key):
    return jax.random.permutation(key, SEGS).astype(jnp.int32)


def draw_past_book(key, part):
    order_perm = shared_order(key)
    return (order_perm % BOOKS).astype(jnp.int32)


def draw_past_age(key, part):
    order_perm = shared_order(key)
    return (order_perm // BOOKS).astype(jnp.int32)


def draw_doc_ids(key, part):
    key = jax.random.fold_in(key, 7)
    key_start, key_end, key_marks = jax.random.split(key, 3)
    long_start = jax.random.randint(key_start, (), 1, TOK_DEV)
    long_end = jax.random.randint(key_end, (), TOKENS - TOK_DEV + 1, TOKENS)
    index_all = jnp.arange(TOKENS, dtype=jnp.int32)
    marks = jax.random.randint(key_marks, (TOKENS,), 0, 100) == 0
    outside = (index_all < long_start) | (index_all > long_end)
    starts = marks & outside | (index_all == long_start) | (index_all == long_end)
    starts = starts & (index_all > 0)
    following_start = jnp.concatenate([starts[1:], jnp.ones((1,), dtype=bool)])
    last_marks = jnp.where(following_start, index_all, TOKENS).astype(jnp.int32)
    return lax.cummin(last_marks, reverse=True).astype(jnp.int32)


def place_ends(array, own_key, least, top_value):
    place = [jax.random.randint(jax.random.fold_in(own_key, axis), (), 0, length) for axis, length in enumerate(array.shape)]
    longest = array.shape.index(max(array.shape))
    next_to = place[:longest] + [(place[longest] + 1) % array.shape[longest]] + place[longest + 1:]
    return array.at[tuple(place)].set(least).at[tuple(next_to)].set(top_value)


def block_levels(own_key, shape, cuts, low, largest):
    loudness = 1.0
    for dim, shards_of in cuts:
        heights = jax.random.uniform(jax.random.fold_in(jax.random.fold_in(own_key, 6), dim), (shards_of,), jnp.float32, low / len(cuts), largest / len(cuts))
        loudness = loudness * jnp.repeat(jnp.exp(heights), shape[dim] // shards_of).reshape((-1,) + (1,) * (len(shape) - 1 - dim))
    return loudness


def normal_values(own_key, shape, width, reach, cuts=(), held_as=jnp.bfloat16):
    values = width * jax.random.normal(own_key, shape, jnp.float32)
    if cuts:
        values = values * block_levels(own_key, shape, cuts, -0.22, 0.18)
    return jnp.clip(values, -reach, reach).astype(held_as)


def setup_inputs(seed: int = 0) -> dict:
    streams_of = jax.random.split(jax.random.key(seed), 22)
    tokens = normal_values(streams_of[0], (TOKENS, D), 1.0, 6.0, ((0, 8),))
    cotangent = normal_values(streams_of[1], (TOKENS, D), 1.0, 6.0, ((0, 8),))
    past_states = normal_values(streams_of[2], (TOKENS, D), 1.0, 6.0, ((0, 8),))
    doc_ids = draw_doc_ids(jax.random.fold_in(streams_of[21], 71), 0)
    cur_book = place_ends(jax.random.randint(streams_of[4], (SEGS,), 0, BOOKS), jax.random.fold_in(streams_of[4], 1), 0, BOOKS - 1).astype(jnp.int32)
    past_book = draw_past_book(jax.random.fold_in(streams_of[21], 71), 0)
    past_age = draw_past_age(jax.random.fold_in(streams_of[21], 71), 0)
    ln1_gain = jnp.clip(1.0 + 0.1 * jax.random.normal(streams_of[7], (D,), jnp.float32), 0.5, 1.5)
    ln1_bias = normal_values(streams_of[8], (D,), 0.3, 3.0, (), jnp.float32)
    qkv_weight = normal_values(streams_of[9], (D, 3, D), D ** -0.5, 0.21875, ((2, 4),))
    qv_bias = normal_values(streams_of[10], (2, D), 0.5, 3.0, ((1, 4),), jnp.float32)
    out_weight = normal_values(streams_of[11], (D, D), DH ** -0.5, 0.75, ((0, 4),))
    out_bias = normal_values(streams_of[12], (D,), 0.3, 3.0, (), jnp.float32)
    ln2_gain = jnp.clip(1.0 + 0.1 * jax.random.normal(streams_of[13], (D,), jnp.float32), 0.5, 1.5)
    ln2_bias = normal_values(streams_of[14], (D,), 0.3, 3.0, (), jnp.float32)
    fc_weight = normal_values(streams_of[15], (D, FF), D ** -0.5, 0.21875, ((1, 4),))
    fc_bias = normal_values(streams_of[16], (FF,), 0.5, 3.0, ((0, 4),), jnp.float32)
    proj_weight = normal_values(streams_of[17], (FF, D), FF ** -0.5, 0.109375, ((0, 4),))
    proj_bias = normal_values(streams_of[18], (D,), 0.3, 3.0, (), jnp.float32)
    mu_weight = normal_values(streams_of[19], (H, NB), NB ** -0.5, 0.25, ((0, 4),), jnp.float32)
    sigma_weight = normal_values(streams_of[20], (H, NB), NB ** -0.5, 0.25, ((0, 4),), jnp.float32)
    return {"tokens": tokens, "cotangent": cotangent, "past_states": past_states, "doc_ids": doc_ids, "cur_book": cur_book, "past_book": past_book, "past_age": past_age, "ln1_gain": ln1_gain, "ln1_bias": ln1_bias, "qkv_weight": qkv_weight, "qv_bias": qv_bias, "out_weight": out_weight, "out_bias": out_bias, "ln2_gain": ln2_gain, "ln2_bias": ln2_bias, "fc_weight": fc_weight, "fc_bias": fc_bias, "proj_weight": proj_weight, "proj_bias": proj_bias, "mu_weight": mu_weight, "sigma_weight": sigma_weight}


EPS = 1e-05
TAU = 0.75
RIDGE = 1.0
SPREAD = 0.01
NEGATIVE = -1e+30
UPPER_LIMIT = lax.Precision.HIGHEST

@jax.custom_vjp
def low(v):
    return lax.optimization_barrier(v.astype(jnp.bfloat16)).astype(jnp.float32)

@jax.custom_vjp
def low_back(v):
    return v

def low_keep(v):
    return (low(v), None)

def low_pass(kept, grad):
    return (grad,)

def back_keep(v):
    return (v, None)

def back_low(kept, grad):
    return (low(grad),)
low.defvjp(low_keep, low_pass)
low_back.defvjp(back_keep, back_low)

def layer_norm(rows_in, gain_vec, bias_vec):
    average = lax.optimization_barrier(jnp.mean(rows_in, axis=-1, keepdims=True))
    centred = rows_in - average
    variance = lax.optimization_barrier(jnp.mean(centred * centred, axis=-1, keepdims=True))
    return centred * lax.rsqrt(variance + EPS) * gain_vec + bias_vec

def gelu_tanh(pre_act):
    return jax.nn.gelu(pre_act, approximate=True)

def radial_centres(basis_n):
    return (jnp.arange(basis_n, dtype=jnp.float32) + 0.5) / basis_n

def past_basis(seg_ages, basis_n, seg_len):
    shrink = jnp.power(jnp.float32(TAU), seg_ages.astype(jnp.float32))
    inside = (jnp.arange(seg_len, dtype=jnp.float32) + 0.5) / seg_len
    time_pts = shrink[:, None] * (TAU + (1.0 - TAU) * inside[None, :])
    offset = (time_pts[:, None, :] - radial_centres(basis_n)[None, :, None]) * basis_n
    return jnp.exp(-0.5 * offset * offset)

def memory_density(affinity, mu_weight, sigma_weight):
    basis_n = mu_weight.shape[1]
    rbf_width = 1.0 / basis_n
    centre = jax.nn.sigmoid(jnp.einsum('...hn,hn->...h', affinity, mu_weight, precision=UPPER_LIMIT))
    unconstrained_spread = jnp.einsum('...hn,hn->...h', affinity, sigma_weight, precision=UPPER_LIMIT)
    spread_sq = SPREAD * jax.nn.softplus(unconstrained_spread) + rbf_width * rbf_width
    centre_gap = centre[..., None] - radial_centres(basis_n)
    return rbf_width * lax.rsqrt(spread_sq)[..., None] * jnp.exp(-0.5 * centre_gap * centre_gap / spread_sq[..., None])

def solve_books(gram_sum, rhs_sum):
    basis_n = gram_sum.shape[1]
    factor = jnp.linalg.cholesky(gram_sum + RIDGE * jnp.eye(basis_n, dtype=jnp.float32))

    def solve_one(chol_fac, rhs_mat):
        return jax.scipy.linalg.cho_solve((chol_fac, True), rhs_mat)
    return jax.vmap(solve_one)(factor, rhs_sum)

def memory_coeffs(past_states, past_book, past_age):
    states = past_states.astype(jnp.float32).reshape(SEGS, SEG, D)
    basis_vals = past_basis(past_age, NB, SEG)
    member = (past_book[:, None] == jnp.arange(BOOKS, dtype=jnp.int32)[None, :]).astype(jnp.float32)

    def one_segment(running, seg_item):
        gram_sum, proj_sum = running
        seg_basis, seg_states, seg_member = seg_item
        gram_sum = gram_sum + seg_member[:, None, None] * jnp.dot(seg_basis, seg_basis.T, precision=UPPER_LIMIT)[None]
        proj_sum = proj_sum + seg_member[:, None, None] * jnp.dot(seg_basis, seg_states, precision=UPPER_LIMIT)[None]
        return ((gram_sum, proj_sum), None)
    start_sums = (jnp.zeros((BOOKS, NB, NB), jnp.float32), jnp.zeros((BOOKS, NB, D), jnp.float32))
    (gram_sum, proj_sum), unused = lax.scan(one_segment, start_sums, (basis_vals, states, member))
    return solve_books(gram_sum, proj_sum)

def local_attention(queries, key_rows, val_rows, doc_ids):
    blk_rows = math.gcd(TOKENS, 512)
    positions = jnp.arange(TOKENS, dtype=jnp.int32)
    scale_dh = DH ** (-0.5)

    def one_block(block_item):
        query_blk, query_pos, query_doc = block_item
        scores = low_back(jnp.einsum('qhd,khd->qhk', query_blk, key_rows, precision=UPPER_LIMIT) * scale_dh)
        allowed = (query_pos[:, None] >= positions[None, :]) & (query_doc[:, None] == doc_ids[None, :])
        scores = jnp.where(allowed[:, None, :], scores, NEGATIVE)
        row_top = lax.optimization_barrier(jnp.max(scores, axis=-1, keepdims=True))
        weights = jnp.exp(scores - row_top)
        prob_vals = low(weights / lax.optimization_barrier(jnp.sum(weights, axis=-1, keepdims=True)))
        return jnp.einsum('qhk,khd->qhd', prob_vals, val_rows, precision=UPPER_LIMIT)
    attended = lax.map(jax.checkpoint(one_block), (queries.reshape(TOKENS // blk_rows, blk_rows, H, DH), positions.reshape(-1, blk_rows), doc_ids.reshape(-1, blk_rows)))
    return attended.reshape(TOKENS, H, DH)

def memory_read(queries, mem_keys, mem_vals, cur_book, mu_weight, sigma_weight):
    scale_dh = DH ** (-0.5)

    def one_segment(seg_item):
        seg_queries, book_id = seg_item
        key_book = mem_keys[book_id]
        val_book = mem_vals[book_id]
        affinity = low_back(jnp.einsum('thd,nhd->thn', seg_queries, key_book, precision=UPPER_LIMIT) * scale_dh)
        density = low(memory_density(affinity, mu_weight, sigma_weight))
        return jnp.einsum('thn,nhd->thd', density, val_book, precision=UPPER_LIMIT)
    attended = lax.map(jax.checkpoint(one_segment), (queries.reshape(SEGS, SEG, H, DH), cur_book))
    return attended.reshape(TOKENS, H, DH)

def layer_forward(params, coeffs, doc_ids, cur_book):
    hidden_in, ln1_gain, ln1_bias, qkv_weight, qv_bias, out_weight, out_bias, ln2_gain, ln2_bias, fc_weight, fc_bias, proj_weight, proj_bias, mu_weight, sigma_weight = params
    head_shape = (TOKENS, H, DH)
    normed_one = low(layer_norm(hidden_in, ln1_gain, ln1_bias))
    mixed_qkv = jnp.einsum('td,dcm->tcm', normed_one, qkv_weight, precision=UPPER_LIMIT)
    queries = low(low_back(mixed_qkv[:, 0] + qv_bias[0])).reshape(head_shape)
    key_rows = low(low_back(mixed_qkv[:, 1])).reshape(head_shape)
    val_rows = low(low_back(mixed_qkv[:, 2] + qv_bias[1])).reshape(head_shape)
    local_out = local_attention(queries, key_rows, val_rows, doc_ids)
    mem_keys = low(jnp.einsum('bnd,dm->bnm', coeffs, qkv_weight[:, 1], precision=UPPER_LIMIT)).reshape(BOOKS, NB, H, DH)
    mem_vals = low(jnp.einsum('bnd,dm->bnm', coeffs, qkv_weight[:, 2], precision=UPPER_LIMIT)).reshape(BOOKS, NB, H, DH)
    mem_out = memory_read(queries, mem_keys, mem_vals, cur_book, mu_weight, sigma_weight)
    heads_out = low(low_back(local_out + mem_out)).reshape(TOKENS, H * DH)
    branch_one = low_back(jnp.dot(heads_out, out_weight, precision=UPPER_LIMIT) + out_bias)
    residual = hidden_in + branch_one
    normed_two = low(layer_norm(residual, ln2_gain, ln2_bias))
    pre_act = low_back(jnp.dot(normed_two, fc_weight, precision=UPPER_LIMIT) + fc_bias)
    activated = low(gelu_tanh(pre_act))
    branch_two = low_back(jnp.dot(activated, proj_weight, precision=UPPER_LIMIT) + proj_bias)
    return residual + branch_two

def reference(tokens, cotangent, past_states, doc_ids, cur_book, past_book, past_age, ln1_gain, ln1_bias, qkv_weight, qv_bias, out_weight, out_bias, ln2_gain, ln2_bias, fc_weight, fc_bias, proj_weight, proj_bias, mu_weight, sigma_weight):
    coeffs = memory_coeffs(past_states, past_book, past_age)
    params = (tokens.astype(jnp.float32), ln1_gain, ln1_bias, qkv_weight.astype(jnp.float32), qv_bias, out_weight.astype(jnp.float32), out_bias, ln2_gain, ln2_bias, fc_weight.astype(jnp.float32), fc_bias, proj_weight.astype(jnp.float32), proj_bias, mu_weight, sigma_weight)

    def forward(inputs):
        return layer_forward(inputs, coeffs, doc_ids, cur_book)
    output, pullback = jax.vjp(forward, params)
    all_grads, = pullback(cotangent.astype(jnp.float32))
    return (output.astype(jnp.bfloat16), all_grads[0].astype(jnp.bfloat16), all_grads[3], all_grads[4], all_grads[5], all_grads[6], all_grads[9], all_grads[10], all_grads[11], all_grads[12], all_grads[1], all_grads[2], all_grads[7], all_grads[8], all_grads[13], all_grads[14])
```

```python
import math

import ml_dtypes
import numpy as np

import jax
import jax.numpy as jnp
from jax import lax
from jax.sharding import PartitionSpec as P

D = 768
DH = 64
NB = 512
SEG = 512
BOOKS = 4


EPS = 1e-05
TAU = 0.75
RIDGE = 1.0
SPREAD = 0.01
NEGATIVE = -1e30
UPPER_LIMIT = lax.Precision.HIGHEST


def shifted(block, axis, distance):
    devices = range(lax.axis_size(axis))
    route = [(i - distance, i) for i in devices if i - distance in devices]
    return lax.ppermute(block, axis, route)


def passed_along(block, axis, distance):
    devices = range(lax.axis_size(axis))
    route = [((i - distance) % len(devices), i) for i in devices]
    return lax.ppermute(block, axis, route)


def layer_norm(rows_in, gain_vec, bias_vec):
    average = jnp.mean(rows_in, axis=-1, keepdims=True)
    centred = rows_in - average
    variance = jnp.mean(centred * centred, axis=-1, keepdims=True)
    return centred * lax.rsqrt(variance + EPS) * gain_vec + bias_vec


def gelu_tanh(pre_act):
    return jax.nn.gelu(pre_act, approximate=True)


def radial_centres(basis_n):
    return (jnp.arange(basis_n, dtype=jnp.float32) + 0.5) / basis_n


def past_basis(seg_ages, basis_n, seg_len):
    shrink = jnp.power(jnp.float32(TAU), seg_ages.astype(jnp.float32))
    inside = (jnp.arange(seg_len, dtype=jnp.float32) + 0.5) / seg_len
    time_pts = shrink[:, None] * (TAU + (1.0 - TAU) * inside[None, :])
    offset = (time_pts[:, None, :] - radial_centres(basis_n)[None, :, None]) * basis_n
    return jnp.exp(-0.5 * offset * offset)


def coefficient_tables(age_count, basis_n, seg_len):
    shrink = TAU ** np.arange(age_count, dtype=np.float64)
    inside = (np.arange(seg_len) + 0.5) / seg_len
    times = shrink[:, None] * (TAU + (1.0 - TAU) * inside[None, :])
    centres = (np.arange(basis_n) + 0.5) / basis_n
    offset = (times[:, None, :] - centres[None, :, None]) * basis_n
    basis = np.exp(-0.5 * offset * offset)
    gram = np.einsum("agx,ahx->gh", basis, basis) + RIDGE * np.eye(basis_n)
    table = np.linalg.solve(gram[None], basis)
    high = table.astype(ml_dtypes.bfloat16)
    lower = (table - high.astype(np.float64)).astype(ml_dtypes.bfloat16)
    return high, lower


def block_rows(row_count_total, tok_rows):
    return math.gcd(row_count_total, max(512, tok_rows))


def split_blocks(array_in, blk_rows):
    blk_count = array_in.shape[0] // blk_rows
    return array_in.reshape((blk_count, blk_rows) + array_in.shape[1:])


def keep_state(running):
    return running


def forward_folder(queries, own_pos, own_doc, scale_dh, fold_state, shard_piece):
    key_part, val_part, doc_part = shard_piece
    blk_rows = block_rows(key_part.shape[0], queries.shape[0])
    blk_count = key_part.shape[0] // blk_rows

    def one_block(running, block_item):
        key_blk, val_blk, doc_blk, blk_index = block_item
        key_pos = blk_index * blk_rows + jnp.arange(blk_rows, dtype=jnp.int32)

        def one_compute(current):
            row_max, row_sum, accumulated = current
            visible = (
                (own_pos[:, None] >= key_pos[None, :]) & (own_doc[:, None] == doc_blk[None, :])
            )[:, None, :]
            scores = (
                jnp.einsum("qhd,khd->qhk", queries, key_blk, preferred_element_type=jnp.float32)
                * scale_dh
            )
            scores = jnp.where(visible, scores, NEGATIVE)
            new_max = jnp.maximum(row_max, jnp.max(scores, axis=-1))
            exp_vals = jnp.where(visible, jnp.exp(scores - new_max[..., None]), 0.0)
            adjustment_term = jnp.exp(row_max - new_max)
            new_sum = row_sum * adjustment_term + jnp.sum(exp_vals, axis=-1)
            new_acc = accumulated * adjustment_term[..., None] + jnp.einsum(
                "qhk,khd->qhd",
                exp_vals.astype(jnp.bfloat16),
                val_blk,
                preferred_element_type=jnp.float32,
            )
            return (new_max, new_sum, new_acc)

        return (lax.cond(key_pos[0] <= own_pos[-1], one_compute, keep_state, running), None)

    blocks = (
        split_blocks(key_part, blk_rows),
        split_blocks(val_part, blk_rows),
        split_blocks(doc_part, blk_rows),
        jnp.arange(blk_count, dtype=jnp.int32),
    )
    result, unused = lax.scan(one_block, fold_state, blocks)
    return result


def local(
    tokens,
    cotangent,
    past_states,
    doc_ids,
    cur_book,
    past_book,
    past_age,
    ln1_gain,
    ln1_bias,
    qkv_weight,
    qv_bias,
    out_weight,
    out_bias,
    ln2_gain,
    ln2_bias,
    fc_weight,
    fc_bias,
    proj_weight,
    proj_bias,
    mu_weight,
    sigma_weight,
):
    tok_rows = tokens.shape[0]
    heads_here = mu_weight.shape[0]
    head_cols = qkv_weight.shape[2]
    seg_here = cur_book.shape[0]
    seq_count = lax.axis_size("seq")
    seq_index = lax.axis_index("seq")
    scale_dh = DH ** (-0.5)
    head_shape = (tok_rows, heads_here, DH)
    own_pos = seq_index * tok_rows + jnp.arange(tok_rows, dtype=jnp.int32)
    quarter = D // lax.axis_size("tp")
    my_quarter = lax.dynamic_slice_in_dim(
        past_states, lax.axis_index("tp") * quarter, quarter, axis=1
    )
    all_states = lax.all_gather(my_quarter, "seq", axis=0)
    books_ages = lax.all_gather(jnp.stack([past_book, past_age]), "seq", axis=1, tiled=True)
    age_count = seq_count * seg_here // BOOKS
    high, lower = coefficient_tables(age_count, NB, SEG)
    chosen = (books_ages[0] == cur_book[0])[None, :] & (
        books_ages[1][None, :] == jnp.arange(age_count, dtype=jnp.int32)[:, None]
    )
    by_age = jnp.einsum(
        "as,std->atd",
        chosen.astype(jnp.bfloat16),
        all_states,
        preferred_element_type=jnp.float32,
    ).astype(jnp.bfloat16)
    coeff_part = jnp.einsum(
        "ant,atd->nd", jnp.asarray(high), by_age, preferred_element_type=jnp.float32
    ) + jnp.einsum("ant,atd->nd", jnp.asarray(lower), by_age, preferred_element_type=jnp.float32)
    coeffs = lax.all_gather(coeff_part.astype(jnp.bfloat16), "tp", axis=1, tiled=True)
    mem_keys = (
        jnp.dot(coeffs, qkv_weight[:, 1], preferred_element_type=jnp.float32)
        .astype(jnp.bfloat16)
        .reshape(NB, heads_here, DH)
    )
    mem_vals = (
        jnp.dot(coeffs, qkv_weight[:, 2], preferred_element_type=jnp.float32)
        .astype(jnp.bfloat16)
        .reshape(NB, heads_here, DH)
    )
    key_mu = jnp.einsum("nhd,hn->hd", mem_keys.astype(jnp.float32), mu_weight, precision=UPPER_LIMIT) * scale_dh
    key_sigma = jnp.einsum("nhd,hn->hd", mem_keys.astype(jnp.float32), sigma_weight, precision=UPPER_LIMIT) * scale_dh
    hidden_in = tokens.astype(jnp.float32)
    normed_one_f, norm_one_back = jax.vjp(layer_norm, hidden_in, ln1_gain, ln1_bias)
    normed_one = normed_one_f.astype(jnp.bfloat16)
    mixed_qkv = jnp.einsum(
        "td,dcm->tcm", normed_one, qkv_weight, preferred_element_type=jnp.float32
    )
    queries = (mixed_qkv[:, 0] + qv_bias[0]).astype(jnp.bfloat16).reshape(head_shape)
    key_rows = mixed_qkv[:, 1].astype(jnp.bfloat16).reshape(head_shape)
    val_rows = (mixed_qkv[:, 2] + qv_bias[1]).astype(jnp.bfloat16).reshape(head_shape)
    zero_heads = jnp.zeros(head_shape, jnp.float32)
    fold_init = (
        jnp.full((tok_rows, heads_here), NEGATIVE, jnp.float32),
        jnp.zeros((tok_rows, heads_here), jnp.float32),
        zero_heads,
    )
    row_max, row_sum, accumulated = forward_folder(
        queries,
        own_pos,
        doc_ids,
        scale_dh,
        fold_init,
        (
            lax.all_gather(key_rows, "seq", axis=0, tiled=True),
            lax.all_gather(val_rows, "seq", axis=0, tiled=True),
            lax.all_gather(doc_ids, "seq", axis=0, tiled=True),
        ),
    )
    log_sum = row_max + jnp.log(row_sum)
    local_out = accumulated / row_sum[..., None]
    rbf_width = 1.0 / NB
    queries_f = queries.astype(jnp.float32)
    centre = jax.nn.sigmoid(jnp.sum(queries_f * key_mu, axis=-1))
    loose = jnp.sum(queries_f * key_sigma, axis=-1)
    spread_sq = SPREAD * jax.nn.softplus(loose) + rbf_width * rbf_width
    gap = centre[..., None] - radial_centres(NB)
    density_bf = (
        rbf_width
        * lax.rsqrt(spread_sq)[..., None]
        * jnp.exp(-0.5 * gap * gap / spread_sq[..., None])
    ).astype(jnp.bfloat16)
    mem_out = jnp.einsum(
        "thn,nhd->thd", density_bf, mem_vals, preferred_element_type=jnp.float32
    )
    heads_out = (local_out + mem_out).astype(jnp.bfloat16).reshape(tok_rows, head_cols)
    branch_one = (
        lax.psum(
            jnp.dot(heads_out, out_weight, preferred_element_type=jnp.float32).astype(jnp.bfloat16),
            "tp",
        ).astype(jnp.float32)
        + out_bias
    )
    residual = hidden_in + branch_one
    normed_two_f, norm_two_back = jax.vjp(layer_norm, residual, ln2_gain, ln2_bias)
    normed_two = normed_two_f.astype(jnp.bfloat16)
    pre_act = jnp.dot(normed_two, fc_weight, preferred_element_type=jnp.float32) + fc_bias
    activated, gelu_back = jax.vjp(gelu_tanh, pre_act)
    act_bf = activated.astype(jnp.bfloat16)
    branch_two = (
        lax.psum(
            jnp.dot(act_bf, proj_weight, preferred_element_type=jnp.float32).astype(jnp.bfloat16),
            "tp",
        ).astype(jnp.float32)
        + proj_bias
    )
    output = (residual + branch_two).astype(jnp.bfloat16)
    grad_out = cotangent.astype(jnp.float32)
    grad_proj_w = jnp.einsum("tf,td->fd", act_bf, cotangent, preferred_element_type=jnp.float32)
    grad_proj_b = jnp.sum(grad_out, axis=0)
    (grad_pre,) = gelu_back(
        jnp.einsum("td,fd->tf", cotangent, proj_weight, preferred_element_type=jnp.float32)
    )
    pre_bf = grad_pre.astype(jnp.bfloat16)
    grad_fc_w = jnp.einsum("td,tf->df", normed_two, pre_bf, preferred_element_type=jnp.float32)
    grad_fc_b = jnp.sum(pre_bf.astype(jnp.float32), axis=0)
    grad_normed_two = lax.psum(
        jnp.einsum("tf,df->td", pre_bf, fc_weight, preferred_element_type=jnp.float32).astype(
            jnp.bfloat16
        ),
        "tp",
    ).astype(jnp.float32)
    grad_resid_part, grad_ln2_g, grad_ln2_b = norm_two_back(grad_normed_two)
    grad_resid = grad_out + grad_resid_part
    resid_bf = grad_resid.astype(jnp.bfloat16)
    grad_out_w = jnp.einsum("tm,td->md", heads_out, resid_bf, preferred_element_type=jnp.float32)
    grad_out_b = jnp.sum(resid_bf.astype(jnp.float32), axis=0)
    grad_heads = (
        jnp.einsum("td,md->tm", resid_bf, out_weight, preferred_element_type=jnp.float32)
        .astype(jnp.bfloat16)
        .reshape(head_shape)
    )
    grad_density = jnp.einsum(
        "thd,nhd->thn", grad_heads, mem_vals, preferred_element_type=jnp.float32
    )
    grad_mem_vals = jnp.einsum(
        "thn,thd->nhd", density_bf, grad_heads, preferred_element_type=jnp.float32
    )
    weighed = grad_density * density_bf.astype(jnp.float32)
    sum_gap = jnp.sum(weighed * gap, axis=-1)
    sum_gap_sq = jnp.sum(weighed * gap * gap, axis=-1)
    sum_zero = jnp.sum(weighed, axis=-1)
    grad_centre = -sum_gap / spread_sq
    grad_spread = 0.5 * (sum_gap_sq / spread_sq - sum_zero) / spread_sq
    pull_mu = grad_centre * centre * (1.0 - centre)
    pull_sigma = grad_spread * SPREAD * jax.nn.sigmoid(loose)
    grad_q_mem = pull_mu[..., None] * key_mu + pull_sigma[..., None] * key_sigma
    query_mu = jnp.sum(pull_mu[..., None] * queries_f, axis=0) * scale_dh
    query_sigma = jnp.sum(pull_sigma[..., None] * queries_f, axis=0) * scale_dh
    mem_keys_f = mem_keys.astype(jnp.float32)
    grad_mu_w = jnp.einsum("nhd,hd->hn", mem_keys_f, query_mu, precision=UPPER_LIMIT)
    grad_sigma_w = jnp.einsum("nhd,hd->hn", mem_keys_f, query_sigma, precision=UPPER_LIMIT)
    grad_mem_keys = (
        mu_weight.T[:, :, None] * query_mu[None] + sigma_weight.T[:, :, None] * query_sigma[None]
    )
    grad_mem_seg = jnp.concatenate(
        [grad_mem_keys.reshape(NB, head_cols), grad_mem_vals.reshape(NB, head_cols)], axis=-1
    ).astype(jnp.bfloat16)
    row_delta = jnp.sum(grad_heads.astype(jnp.float32) * local_out, axis=-1)

    def cycle_step(step, carry):
        key_blk, val_blk, doc_blk, grad_k, grad_v, grad_q = carry
        anchor = (seq_index - step) % seq_count
        key_pos = anchor * tok_rows + jnp.arange(tok_rows, dtype=jnp.int32)

        def cycle_compute(current):
            acc_k, acc_v, acc_q = current
            visible = (
                (own_pos[:, None] >= key_pos[None, :]) & (doc_ids[:, None] == doc_blk[None, :])
            )[:, None, :]
            scores = (
                jnp.einsum("qhd,khd->qhk", queries, key_blk, preferred_element_type=jnp.float32)
                * scale_dh
            )
            prob_vals = jnp.where(
                visible, jnp.exp(jnp.where(visible, scores, NEGATIVE) - log_sum[..., None]), 0.0
            )
            acc_v = acc_v + jnp.einsum(
                "qhk,qhd->khd",
                prob_vals.astype(jnp.bfloat16),
                grad_heads,
                preferred_element_type=jnp.float32,
            )
            grad_prob = jnp.einsum(
                "qhd,khd->qhk", grad_heads, val_blk, preferred_element_type=jnp.float32
            )
            grad_score = (prob_vals * (grad_prob - row_delta[..., None])).astype(jnp.bfloat16)
            acc_q = (
                acc_q
                + jnp.einsum(
                    "qhk,khd->qhd", grad_score, key_blk, preferred_element_type=jnp.float32
                )
                * scale_dh
            )
            acc_k = (
                acc_k
                + jnp.einsum(
                    "qhk,qhd->khd", grad_score, queries, preferred_element_type=jnp.float32
                )
                * scale_dh
            )
            return (acc_k, acc_v, acc_q)

        grad_k, grad_v, grad_q = lax.cond(
            anchor <= seq_index, cycle_compute, keep_state, (grad_k, grad_v, grad_q)
        )
        key_blk, val_blk, doc_blk = shifted((key_blk, val_blk, doc_blk), "seq", 1)
        grad_k, grad_v = (
            passed_along(grad_k.astype(jnp.bfloat16), "seq", 1).astype(grad_k.dtype),
            passed_along(grad_v.astype(jnp.bfloat16), "seq", 1).astype(grad_v.dtype),
        )
        return (key_blk, val_blk, doc_blk, grad_k, grad_v, grad_q)

    cycle_init = (key_rows, val_rows, doc_ids, zero_heads, zero_heads, zero_heads)
    cycle_final = lax.fori_loop(0, seq_count, cycle_step, cycle_init)
    grad_keys, grad_vals, grad_q_local = (cycle_final[3], cycle_final[4], cycle_final[5])
    grad_q_bf = (grad_q_local + grad_q_mem).astype(jnp.bfloat16).reshape(tok_rows, head_cols)
    grad_k_bf = grad_keys.astype(jnp.bfloat16).reshape(tok_rows, head_cols)
    grad_v_bf = grad_vals.astype(jnp.bfloat16).reshape(tok_rows, head_cols)
    grad_qkv = jnp.stack([grad_q_bf, grad_k_bf, grad_v_bf], axis=1)
    grad_qkv_w = jnp.einsum("td,tcm->dcm", normed_one, grad_qkv, preferred_element_type=jnp.float32)
    grad_kv_w = jnp.einsum("nd,nm->dm", coeffs, grad_mem_seg, preferred_element_type=jnp.float32)
    grad_qkv_w = grad_qkv_w.at[:, 1:].add(grad_kv_w.reshape(D, 2, head_cols))
    grad_qv_b = jnp.stack(
        [
            jnp.sum(grad_q_bf.astype(jnp.float32), axis=0),
            jnp.sum(grad_v_bf.astype(jnp.float32), axis=0),
        ]
    )
    grad_normed_one = lax.psum(
        jnp.einsum("tcm,dcm->td", grad_qkv, qkv_weight, preferred_element_type=jnp.float32).astype(
            jnp.bfloat16
        ),
        "tp",
    ).astype(jnp.float32)
    grad_in_part, grad_ln1_g, grad_ln1_b = norm_one_back(grad_normed_one)
    grad_tokens = (grad_resid + grad_in_part).astype(jnp.bfloat16)
    qkv_share, out_share, fc_share, proj_share = (
        lax.psum_scatter(grad_qkv_w.reshape(D, -1).astype(jnp.bfloat16), "seq", scatter_dimension=0, tiled=True),
        lax.psum_scatter(grad_out_w.astype(jnp.bfloat16), "seq", scatter_dimension=1, tiled=True),
        lax.psum_scatter(grad_fc_w.astype(jnp.bfloat16), "seq", scatter_dimension=0, tiled=True),
        lax.psum_scatter(grad_proj_w.astype(jnp.bfloat16), "seq", scatter_dimension=1, tiled=True),
    )
    qkv_share = qkv_share.astype(jnp.float32).reshape(-1, 3, head_cols)
    out_share, fc_share, proj_share = (
        out_share.astype(jnp.float32),
        fc_share.astype(jnp.float32),
        proj_share.astype(jnp.float32),
    )
    small_sums = lax.psum(
        (
            grad_ln1_g,
            grad_ln1_b,
            grad_qv_b,
            grad_out_b,
            grad_ln2_g,
            grad_ln2_b,
            grad_fc_b,
            grad_proj_b,
            grad_mu_w,
            grad_sigma_w,
        ),
        "seq",
    )
    return (
        output,
        grad_tokens,
        qkv_share,
        small_sums[2],
        out_share,
        small_sums[3],
        fc_share,
        small_sums[6],
        proj_share,
        small_sums[7],
        small_sums[0],
        small_sums[1],
        small_sums[4],
        small_sums[5],
        small_sums[8],
        small_sums[9],
    )


def solution(mesh):
    in_specs = (
        P("seq", None),
        P("seq", None),
        P("seq", None),
        P("seq"),
        P("seq"),
        P("seq"),
        P("seq"),
        P(),
        P(),
        P(None, None, "tp"),
        P(None, "tp"),
        P("tp", None),
        P(),
        P(),
        P(),
        P(None, "tp"),
        P("tp"),
        P("tp", None),
        P(),
        P("tp", None),
        P("tp", None),
    )
    out_specs = (
        P("seq", None),
        P("seq", None),
        P("seq", None, "tp"),
        P(None, "tp"),
        P("tp", "seq"),
        P(),
        P("seq", "tp"),
        P("tp"),
        P("tp", "seq"),
        P(),
        P(),
        P(),
        P(),
        P(),
        P("tp", None),
        P("tp", None),
    )
    return jax.shard_map(local, mesh=mesh, in_specs=in_specs, out_specs=out_specs, check_vma=False)
```

```python
import functools

import ml_dtypes
import numpy as np

import jax
import jax.numpy as jnp
from jax import lax
from jax.experimental import pallas as pl
from jax.experimental.pallas import tpu as pltpu
from jax.sharding import PartitionSpec as P

D = 768
DH = 64
NB = 512
SEG = 512
BOOKS = 4


EPS = 1e-05
TAU = 0.75
RIDGE = 1.0
SPREAD = 0.01
NEGATIVE = -1e30
UPPER_LIMIT = lax.Precision.HIGHEST
MESH_ID = pl.DeviceIdType.MESH
VMEM_LIMIT = 60 * 2**20


def layer_norm(rows_in, gain_vec, bias_vec):
    average = jnp.mean(rows_in, axis=-1, keepdims=True)
    centred = rows_in - average
    variance = jnp.mean(centred * centred, axis=-1, keepdims=True)
    return centred * lax.rsqrt(variance + EPS) * gain_vec + bias_vec


def gelu_tanh(pre_act):
    return jax.nn.gelu(pre_act, approximate=True)


def radial_centres(basis_n):
    return (jnp.arange(basis_n, dtype=jnp.float32) + 0.5) / basis_n


def past_basis(seg_ages, basis_n, seg_len):
    shrink = jnp.power(jnp.float32(TAU), seg_ages.astype(jnp.float32))
    inside = (jnp.arange(seg_len, dtype=jnp.float32) + 0.5) / seg_len
    time_pts = shrink[:, None] * (TAU + (1.0 - TAU) * inside[None, :])
    offset = (time_pts[:, None, :] - radial_centres(basis_n)[None, :, None]) * basis_n
    return jnp.exp(-0.5 * offset * offset)


def coefficient_tables(age_count, basis_n, seg_len):
    shrink = TAU ** np.arange(age_count, dtype=np.float64)
    inside = (np.arange(seg_len) + 0.5) / seg_len
    times = shrink[:, None] * (TAU + (1.0 - TAU) * inside[None, :])
    centres = (np.arange(basis_n) + 0.5) / basis_n
    offset = (times[:, None, :] - centres[None, :, None]) * basis_n
    basis = np.exp(-0.5 * offset * offset)
    gram = np.einsum("agx,ahx->gh", basis, basis) + RIDGE * np.eye(basis_n)
    table = np.linalg.solve(gram[None], basis)
    high = table.astype(ml_dtypes.bfloat16)
    lower = (table - high.astype(np.float64)).astype(ml_dtypes.bfloat16)
    return high, lower


LANES_OUT = 256


def head_of_lane(width):
    return lax.broadcasted_iota(jnp.int32, (1, width), 1) // DH


def head_masks(width):
    lane_head = head_of_lane(width)
    return [(lane_head == head).astype(jnp.float32).astype(jnp.bfloat16) for head in range(width // DH)]


def pick_heads(per_head, lane_head):
    chosen = per_head[0]
    for head in range(1, len(per_head)):
        chosen = jnp.where(lane_head == head, per_head[head], chosen)
    return chosen


def dot_rows(left, right):
    return lax.dot_general(left, right, (((1,), (1,)), ((), ())), preferred_element_type=jnp.float32)


def dot_plain(left, right):
    return lax.dot_general(left, right, (((1,), (0,)), ((), ())), preferred_element_type=jnp.float32)


def thirds(value):
    first = value.astype(jnp.bfloat16)
    rest = value - first.astype(jnp.float32)
    second = rest.astype(jnp.bfloat16)
    third = (rest - second.astype(jnp.float32)).astype(jnp.bfloat16)
    return first, second, third


def with_stats(block, stats):
    rows, width = block.shape
    spare = LANES_OUT - width
    lane = lax.broadcasted_iota(jnp.int32, (1, spare), 1)
    tail = jnp.zeros((rows, spare), jnp.float32)
    for index, column in enumerate(stats):
        for part, value in enumerate(thirds(column)):
            tail = jnp.where(lane == 3 * index + part, value.astype(jnp.float32), tail)
    return jnp.concatenate([block, tail.astype(jnp.bfloat16)], axis=1)


def stat_column(extended, width, index):
    lane = lax.broadcasted_iota(jnp.int32, (1, LANES_OUT), 1)
    start = width + 3 * index
    mine = (lane >= start) & (lane < start + 3)
    return jnp.sum(jnp.where(mine, extended.astype(jnp.float32), 0.0), axis=1, keepdims=True)


def stat_rows(extended, width, count):
    row = lax.broadcasted_iota(jnp.int32, (count, LANES_OUT), 0)
    lane = lax.broadcasted_iota(jnp.int32, (count, LANES_OUT), 1)
    start = width + 3 * row
    chooser = ((lane >= start) & (lane < start + 3)).astype(jnp.float32).astype(jnp.bfloat16)
    return dot_rows(chooser, extended)


def greet(levels):
    seq, tp = lax.axis_index("seq"), lax.axis_index("tp")
    level, side = seq // 2, seq % 2
    barrier = pltpu.get_barrier_semaphore()
    pl.semaphore_signal(barrier, inc=1, device_id=(2 * level + 1 - side, tp), device_id_type=MESH_ID)

    def one(step, unused):
        other = lax.rem(level + step, levels)
        pl.semaphore_signal(barrier, inc=1, device_id=(2 * other + side, tp), device_id_type=MESH_ID)
        return unused

    lax.fori_loop(1, levels, one, 0)
    return barrier, levels


def forward_kernel(
    levels,
    tok_ref,
    norm_ref,
    weight_ref,
    bias_ref,
    doc_col_ref,
    doc_row_ref,
    key_mask_ref,
    normed_ref,
    query_out_ref,
    kv_out_ref,
    out_ref,
    lse_ref,
    pair_ref,
    top_ref,
    total_ref,
    acc_ref,
    part_ref,
    part_in_ref,
    kv_send,
    kv_recv,
    q_send,
    q_recv,
    pair_sem,
    part_sem,
):
    seq, tp = lax.axis_index("seq"), lax.axis_index("tp")
    level, side = seq // 2, seq % 2
    rows = tok_ref.shape[0]
    width = pair_ref.shape[2]
    heads = width // DH
    partner = (2 * level + 1 - side, tp)
    lane_head = head_of_lane(width)
    head_mask = head_masks(width)
    barrier, greetings = greet(levels)

    chunk = rows // 2

    def project(index, unused):
        here = pl.ds(pl.multiple_of(index * chunk, chunk), chunk)
        x = tok_ref[here, :].astype(jnp.float32)
        centred = x - jnp.mean(x, axis=1, keepdims=True)
        variance = jnp.mean(centred * centred, axis=1, keepdims=True)
        a = centred * lax.rsqrt(variance + EPS) * norm_ref[0:1, :] + norm_ref[1:2, :]
        a = a.astype(jnp.bfloat16)
        normed_ref[here, :] = a
        mixed = (dot_plain(a, weight_ref[...]) + bias_ref[0:1, :]).astype(jnp.bfloat16)
        query = mixed[:, :width] * jnp.bfloat16(DH**-0.5)
        pair_ref[0, here, :] = query
        query_out_ref[level, here, :] = query
        kv_out_ref[level, here, :] = mixed[:, width:]
        return unused

    lax.fori_loop(0, rows // chunk, project, 0)
    kv_out_ref[level, rows:, :] = key_mask_ref[...]

    pl.semaphore_wait(barrier, greetings)
    pair_copy = pltpu.make_async_remote_copy(
        pair_ref.at[0], pair_ref.at[1], pair_sem.at[0], pair_sem.at[1], device_id=partner, device_id_type=MESH_ID
    )
    pair_copy.start()

    def kv_copy(from_level):
        return pltpu.make_async_remote_copy(
            kv_out_ref.at[from_level],
            kv_out_ref.at[from_level],
            kv_send.at[from_level],
            kv_recv.at[from_level],
            device_id=(lax.rem(2 * level + 2, 2 * levels) + side, tp),
            device_id_type=MESH_ID,
        )

    def query_copy(from_level, to_level):
        return pltpu.make_async_remote_copy(
            query_out_ref.at[from_level],
            query_out_ref.at[from_level],
            q_send.at[to_level],
            q_recv.at[from_level],
            device_id=(2 * to_level + side, tp),
            device_id_type=MESH_ID,
        )

    @pl.when(level < levels - 1)
    def _():
        kv_copy(level).start()

    def send_down(step, unused):
        query_copy(level, level - step).start()
        return unused

    lax.fori_loop(1, level + 1, send_down, 0)

    top_ref[...] = jnp.full(top_ref.shape, NEGATIVE, jnp.float32)
    total_ref[...] = jnp.zeros(total_ref.shape, jnp.float32)
    acc_ref[...] = jnp.zeros(acc_ref.shape, jnp.float32)

    doc_first = doc_row_ref[0:1, 0:1]
    def reach_of(here):
        docs = doc_col_ref[here, :]
        last = (level == levels - 1) & (side == 1)
        return jnp.where(last & (docs != doc_first), NEGATIVE, 0.0)

    def fold(slot, from_level, mask_kind):
        mask_rows = kv_out_ref[from_level, rows:, :].astype(jnp.float32)
        key_mask = jnp.concatenate([mask_rows[0:1, : rows // 2], mask_rows[1:2, : rows // 2]], axis=1)

        def part(index, unused):
            here = pl.ds(pl.multiple_of(index * chunk, chunk), chunk)
            query = pair_ref[slot, here, :]
            keys = kv_out_ref[from_level, :rows, :width]
            vals = kv_out_ref[from_level, :rows, width:]
            if mask_kind == "own":
                q_pos = index * chunk + lax.broadcasted_iota(jnp.int32, (chunk, rows), 0)
                k_pos = lax.broadcasted_iota(jnp.int32, (chunk, rows), 1)
                visible = (q_pos >= k_pos) & (doc_col_ref[here, :] == doc_row_ref[0:1, :])
            products, scales = [], []
            for head in range(heads):
                scores = dot_rows(query * head_mask[head], keys)
                old_top = top_ref[slot, head, here, :]
                if mask_kind == "own":
                    scores = jnp.where(visible, scores, NEGATIVE)
                    reach = 0.0
                else:
                    scores = scores + key_mask
                    reach = jnp.where(slot == 0, reach_of(here), 0.0)
                new_top = jnp.maximum(old_top, jnp.max(scores, axis=1, keepdims=True) + reach)
                weights = jnp.exp(scores - (new_top - reach))
                scale = jnp.exp(old_top - new_top)
                top_ref[slot, head, here, :] = new_top
                total_ref[slot, head, here, :] = total_ref[slot, head, here, :] * scale + jnp.sum(
                    weights, axis=1, keepdims=True
                )
                products.append(dot_plain(weights.astype(jnp.bfloat16), vals))
                scales.append(scale)
            acc_ref[slot, here, :] = acc_ref[slot, here, :] * pick_heads(scales, lane_head) + pick_heads(
                products, lane_head
            )
            return unused

        lax.fori_loop(0, rows // chunk, part, 0)

    fold(0, level, "own")
    pair_copy.wait()

    @pl.when(side == 0)
    def _():
        fold(1, level, "off")

    def arrived(step, unused):
        from_level = level - step
        kv_copy(from_level).wait_recv()

        @pl.when(level < levels - 1)
        def _():
            kv_copy(from_level).start()

        def both(slot, inner):
            fold(slot, from_level, "off")
            return inner

        lax.fori_loop(0, 2, both, 0)
        return unused

    lax.fori_loop(1, level + 1, arrived, 0)

    def finish(index, unused):
        here = pl.ds(pl.multiple_of(index * chunk, chunk), chunk)
        totals = [total_ref[1, head, here, :] for head in range(heads)]
        tops = [top_ref[1, head, here, :] for head in range(heads)]
        some = [value > 0.0 for value in totals]
        inverse = [jnp.where(ok, 1.0 / jnp.where(ok, value, 1.0), 0.0) for ok, value in zip(some, totals)]
        logs = [
            jnp.where(ok, top + jnp.log(jnp.where(ok, value, 1.0)), NEGATIVE)
            for ok, top, value in zip(some, tops, totals)
        ]
        share = (acc_ref[1, here, :] * pick_heads(inverse, lane_head)).astype(jnp.bfloat16)
        part_ref[here, :] = with_stats(share, logs)
        return unused

    lax.fori_loop(0, rows // chunk, finish, 0)
    part_copy = pltpu.make_async_remote_copy(
        part_ref, part_in_ref, part_sem.at[0], part_sem.at[1], device_id=partner, device_id_type=MESH_ID
    )
    part_copy.start()
    part_copy.wait()

    def merge(index, unused):
        here = pl.ds(pl.multiple_of(index * chunk, chunk), chunk)
        reach = reach_of(here)
        received = part_in_ref[here, :]
        mine, theirs, columns = [], [], []
        for head in range(heads):
            total = total_ref[0, head, here, :]
            own_log = top_ref[0, head, here, :] + jnp.log(total)
            other_log = stat_column(received, width, head) + reach
            high = jnp.maximum(own_log, other_log)
            both_log = high + jnp.log(jnp.exp(own_log - high) + jnp.exp(other_log - high))
            mine.append(jnp.exp(own_log - both_log) / total)
            theirs.append(jnp.exp(other_log - both_log))
            columns.append(both_log)
        out_ref[here, :] = acc_ref[0, here, :] * pick_heads(mine, lane_head) + received[
            :, :width
        ].astype(jnp.float32) * pick_heads(theirs, lane_head)
        lane = lax.broadcasted_iota(jnp.int32, (1, 8), 1)
        packed = jnp.zeros((chunk, 8), jnp.float32)
        for head in range(heads):
            packed = jnp.where(lane == head, columns[head], packed)
        lse_ref[here, :] = packed
        return unused

    lax.fori_loop(0, rows // chunk, merge, 0)

    def sent_down(step, unused):
        query_copy(level, level - step).wait_send()
        return unused

    lax.fori_loop(1, level + 1, sent_down, 0)

    def from_above(step, unused):
        query_copy(level + step, level).wait_recv()
        return unused

    lax.fori_loop(1, levels - level, from_above, 0)

    @pl.when(level < levels - 1)
    def _():
        def sent_up(from_level, unused):
            kv_copy(from_level).wait_send()
            return unused

        lax.fori_loop(0, level + 1, sent_up, 0)


def attention_forward(levels, tokens, norm, weight, bias, doc_ids, key_mask):
    rows = tokens.shape[0]
    width = weight.shape[1] // 3
    heads = width // DH
    vmem = pl.BlockSpec(memory_space=pltpu.VMEM)
    dma = pltpu.SemaphoreType.DMA
    return pl.pallas_call(
        functools.partial(forward_kernel, levels),
        out_shape=(
            jax.ShapeDtypeStruct((rows, D), jnp.bfloat16),
            jax.ShapeDtypeStruct((levels, rows, width), jnp.bfloat16),
            jax.ShapeDtypeStruct((levels, rows + 16, 2 * width), jnp.bfloat16),
            jax.ShapeDtypeStruct((rows, width), jnp.float32),
            jax.ShapeDtypeStruct((rows, 8), jnp.float32),
        ),
        in_specs=[vmem] * 7,
        out_specs=(vmem,) * 5,
        scratch_shapes=[
            pltpu.VMEM((2, rows, width), jnp.bfloat16),
            pltpu.VMEM((2, heads, rows, 1), jnp.float32),
            pltpu.VMEM((2, heads, rows, 1), jnp.float32),
            pltpu.VMEM((2, rows, width), jnp.float32),
            pltpu.VMEM((rows, LANES_OUT), jnp.bfloat16),
            pltpu.VMEM((rows, LANES_OUT), jnp.bfloat16),
            dma((levels,)),
            dma((levels,)),
            dma((levels,)),
            dma((levels,)),
            dma((2,)),
            dma((2,)),
        ],
        name="attention_forward",
        compiler_params=pltpu.CompilerParams(
            collective_id=1, has_side_effects=True, vmem_limit_bytes=VMEM_LIMIT
        ),
    )(tokens, norm, weight, bias, doc_ids[:, None], doc_ids[None, :], key_mask)


def backward_kernel(
    levels,
    grad_ref,
    attended_ref,
    lse_ref,
    query_col_ref,
    query_oth_ref,
    kv_col_ref,
    kv_oth_ref,
    doc_col_ref,
    doc_row_ref,
    dq_ref,
    dk_ref,
    dv_ref,
    own_ref,
    grad_col_ref,
    grad_oth_ref,
    stat_ref,
    col_send,
    col_recv,
    oth_send,
    oth_recv,
    *staging,
):
    seq, tp = lax.axis_index("seq"), lax.axis_index("tp")
    level, side = seq // 2, seq % 2
    rows, width = grad_ref.shape
    heads = width // DH
    partner = (2 * level + 1 - side, tp)
    lane_head = head_of_lane(width)
    head_mask = head_masks(width)
    chunk = rows // 2
    barrier, greetings = greet(levels)
    doc_first = doc_row_ref[0:1, 0:1]
    last = (level == levels - 1) & (side == 1)

    def prepare(index, unused):
        here = pl.ds(pl.multiple_of(index * chunk, chunk), chunk)
        grad = grad_ref[here, :]
        product = grad.astype(jnp.float32) * attended_ref[here, :]
        far = jnp.where(last & (doc_col_ref[here, :] != doc_first), -NEGATIVE, 0.0)
        lses = [lse_ref[here, head : head + 1] for head in range(heads)]
        deltas = [
            jnp.sum(jnp.where(lane_head == head, product, 0.0), axis=1, keepdims=True)
            for head in range(heads)
        ]
        own_ref[here, :] = with_stats(grad, lses + deltas)
        grad_col_ref[level, here, :] = with_stats(grad, [lse + far for lse in lses] + deltas)
        for head in range(heads):
            stat_ref[head, here, :] = lses[head]
            stat_ref[heads + head, here, :] = lses[head] + far
            stat_ref[2 * heads + head, here, :] = deltas[head]
        return unused

    lax.fori_loop(0, rows // chunk, prepare, 0)
    pl.semaphore_wait(barrier, greetings)

    def col_copy(from_level, to_level):
        return pltpu.make_async_remote_copy(
            grad_col_ref.at[from_level],
            grad_col_ref.at[from_level],
            col_send.at[to_level],
            col_recv.at[from_level],
            device_id=(2 * to_level + side, tp),
            device_id_type=MESH_ID,
        )

    def oth_copy(from_level):
        return pltpu.make_async_remote_copy(
            grad_col_ref.at[from_level],
            grad_oth_ref.at[from_level],
            oth_send.at[from_level],
            oth_recv.at[from_level],
            device_id=partner,
            device_id_type=MESH_ID,
        )

    @pl.when(side == 1)
    def _():
        oth_copy(level).start()

    def send_down(step, unused):
        col_copy(level, level - step).start()
        return unused

    lax.fori_loop(1, level + 1, send_down, 0)

    dq_ref[...] = jnp.zeros(dq_ref.shape, jnp.float32)
    dk_ref[...] = jnp.zeros(dk_ref.shape, jnp.float32)
    dv_ref[...] = jnp.zeros(dv_ref.shape, jnp.float32)

    def block_of(kv_ref, from_level):
        if not staging:
            return kv_ref.at[from_level]
        block_ref, block_sem = staging
        copy = pltpu.make_async_copy(kv_ref.at[from_level], block_ref, block_sem)
        copy.start()
        copy.wait()
        return block_ref

    def query_fold(kv_ref, from_level, own):
        block_ref = block_of(kv_ref, from_level)
        if own:
            key_mask = None
        else:
            mask_rows = block_ref[rows:, :].astype(jnp.float32)
            key_mask = jnp.concatenate(
                [mask_rows[0:1, : rows // 2], mask_rows[1:2, : rows // 2]], axis=1
            )

        def part(index, unused):
            here = pl.ds(pl.multiple_of(index * chunk, chunk), chunk)
            query = query_col_ref[level, here, :]
            grad = grad_ref[here, :]
            keys = block_ref[:rows, :width]
            vals = block_ref[:rows, width:]
            if own:
                q_pos = index * chunk + lax.broadcasted_iota(jnp.int32, (chunk, rows), 0)
                k_pos = lax.broadcasted_iota(jnp.int32, (chunk, rows), 1)
                visible = (q_pos >= k_pos) & (doc_col_ref[here, :] == doc_row_ref[0:1, :])
            products = []
            for head in range(heads):
                scores = dot_rows(query * head_mask[head], keys)
                if own:
                    scores = jnp.where(visible, scores, NEGATIVE)
                    lse = stat_ref[head, here, :]
                else:
                    scores = scores + key_mask
                    lse = stat_ref[heads + head, here, :]
                probs = jnp.exp(scores - lse)
                pull = dot_rows(grad * head_mask[head], vals) - stat_ref[2 * heads + head, here, :]
                products.append(dot_plain((probs * pull).astype(jnp.bfloat16), keys))
            dq_ref[here, :] = dq_ref[here, :] + pick_heads(products, lane_head)
            return unused

        lax.fori_loop(0, rows // chunk, part, 0)

    query_fold(kv_col_ref, level, True)

    @pl.when(side == 1)
    def _():
        query_fold(kv_oth_ref, level, False)

    def earlier(from_level, unused):
        query_fold(kv_col_ref, from_level, False)
        query_fold(kv_oth_ref, from_level, False)
        return unused

    lax.fori_loop(0, level, earlier, 0)
    dq_ref[...] = dq_ref[...] * (DH**-0.5)

    own_block_ref = block_of(kv_col_ref, level)

    def key_fold(query_ref, grads_ref, from_level, own):
        def part(index, unused):
            here = pl.ds(pl.multiple_of(index * chunk, chunk), chunk)
            keys = own_block_ref[here, :width]
            vals = own_block_ref[here, width:]
            if own:
                query = query_col_ref[level]
                extended = own_ref[...]
                k_pos = index * chunk + lax.broadcasted_iota(jnp.int32, (chunk, rows), 0)
                q_pos = lax.broadcasted_iota(jnp.int32, (chunk, rows), 1)
                visible = (q_pos >= k_pos) & (doc_col_ref[here, :] == doc_row_ref[0:1, :])
            else:
                query = query_ref[from_level]
                extended = grads_ref[from_level]
            grad = extended[:, :width]
            stats = stat_rows(extended, width, 8)
            key_parts, val_parts = [], []
            for head in range(heads):
                scores = dot_rows(keys * head_mask[head], query)
                if own:
                    scores = jnp.where(visible, scores, NEGATIVE)
                probs = jnp.exp(scores - stats[head : head + 1, :])
                val_parts.append(dot_plain(probs.astype(jnp.bfloat16), grad))
                pull = dot_rows(vals * head_mask[head], grad) - stats[heads + head : heads + head + 1, :]
                key_parts.append(dot_plain((probs * pull).astype(jnp.bfloat16), query))
            dk_ref[here, :] = dk_ref[here, :] + pick_heads(key_parts, lane_head)
            dv_ref[here, :] = dv_ref[here, :] + pick_heads(val_parts, lane_head)
            return unused

        lax.fori_loop(0, rows // chunk, part, 0)

    @pl.when(side == 0)
    def _():
        oth_copy(level).wait_recv()
        key_fold(query_oth_ref, grad_oth_ref, level, False)

    def later(step, unused):
        from_level = level + step
        col_copy(from_level, level).wait_recv()
        oth_copy(from_level).start()
        key_fold(query_col_ref, grad_col_ref, from_level, False)
        oth_copy(from_level).wait_recv()
        key_fold(query_oth_ref, grad_oth_ref, from_level, False)
        return unused

    lax.fori_loop(1, levels - level, later, 0)
    reaches = doc_col_ref[...] >= (seq + 1) * rows
    dk_ref[...] = jnp.where(reaches, dk_ref[...], 0.0)
    dv_ref[...] = jnp.where(reaches, dv_ref[...], 0.0)
    key_fold(None, None, level, True)

    @pl.when(side == 1)
    def _():
        oth_copy(level).wait_send()

    def sent_down(step, unused):
        col_copy(level, level - step).wait_send()
        return unused

    lax.fori_loop(1, level + 1, sent_down, 0)

    def sent_on(step, unused):
        oth_copy(level + step).wait_send()
        return unused

    lax.fori_loop(1, levels - level, sent_on, 0)


def attention_backward(levels, grad, attended, lse, query_col, query_oth, kv_col, kv_oth, doc_ids):
    rows, width = grad.shape
    heads = width // DH
    vmem = pl.BlockSpec(memory_space=pltpu.VMEM)
    dma = pltpu.SemaphoreType.DMA
    full = jax.ShapeDtypeStruct((rows, width), jnp.float32)
    staged = levels > 8
    far = pl.BlockSpec(memory_space=pl.ANY) if staged else vmem
    staging = [pltpu.VMEM(kv_col.shape[1:], kv_col.dtype), dma(())] if staged else []
    return pl.pallas_call(
        functools.partial(backward_kernel, levels),
        out_shape=(full, full, full),
        in_specs=[vmem] * 5 + [far] * 2 + [vmem] * 2,
        out_specs=(vmem,) * 3,
        scratch_shapes=[
            pltpu.VMEM((rows, LANES_OUT), jnp.bfloat16),
            pltpu.VMEM((levels, rows, LANES_OUT), jnp.bfloat16),
            pltpu.VMEM((levels, rows, LANES_OUT), jnp.bfloat16),
            pltpu.VMEM((3 * heads, rows, 1), jnp.float32),
            dma((levels,)),
            dma((levels,)),
            dma((levels,)),
            dma((levels,)),
            *staging,
        ],
        name="attention_backward",
        compiler_params=pltpu.CompilerParams(
            collective_id=2, has_side_effects=True, vmem_limit_bytes=VMEM_LIMIT
        ),
    )(grad, attended, lse, query_col, query_oth, kv_col, kv_oth, doc_ids[:, None], doc_ids[None, :])


def local(
    tokens,
    cotangent,
    past_states,
    doc_ids,
    cur_book,
    past_book,
    past_age,
    ln1_gain,
    ln1_bias,
    qkv_weight,
    qv_bias,
    out_weight,
    out_bias,
    ln2_gain,
    ln2_bias,
    fc_weight,
    fc_bias,
    proj_weight,
    proj_bias,
    mu_weight,
    sigma_weight,
):
    tok_rows = tokens.shape[0]
    heads_here = mu_weight.shape[0]
    head_cols = qkv_weight.shape[2]
    seg_here = cur_book.shape[0]
    seq_count = lax.axis_size("seq")
    seq_index = lax.axis_index("seq")
    scale_dh = DH ** (-0.5)
    head_shape = (tok_rows, heads_here, DH)
    own_pos = seq_index * tok_rows + jnp.arange(tok_rows, dtype=jnp.int32)
    quarter = D // lax.axis_size("tp")
    my_quarter = lax.dynamic_slice_in_dim(
        past_states, lax.axis_index("tp") * quarter, quarter, axis=1
    )
    all_states = lax.all_gather(my_quarter, "seq", axis=0)
    books_ages = lax.all_gather(jnp.stack([past_book, past_age]), "seq", axis=1, tiled=True)
    age_count = seq_count * seg_here // BOOKS
    high, lower = coefficient_tables(age_count, NB, SEG)
    chosen = (books_ages[0] == cur_book[0])[None, :] & (
        books_ages[1][None, :] == jnp.arange(age_count, dtype=jnp.int32)[:, None]
    )
    by_age = jnp.einsum(
        "as,std->atd",
        chosen.astype(jnp.bfloat16),
        all_states,
        preferred_element_type=jnp.float32,
    ).astype(jnp.bfloat16)
    coeff_part = jnp.einsum(
        "ant,atd->nd", jnp.asarray(high), by_age, preferred_element_type=jnp.float32
    ) + jnp.einsum("ant,atd->nd", jnp.asarray(lower), by_age, preferred_element_type=jnp.float32)
    coeffs = lax.all_gather(coeff_part.astype(jnp.bfloat16), "tp", axis=1, tiled=True)
    mem_keys = (
        jnp.dot(coeffs, qkv_weight[:, 1], preferred_element_type=jnp.float32)
        .astype(jnp.bfloat16)
        .reshape(NB, heads_here, DH)
    )
    mem_vals = (
        jnp.dot(coeffs, qkv_weight[:, 2], preferred_element_type=jnp.float32)
        .astype(jnp.bfloat16)
        .reshape(NB, heads_here, DH)
    )
    key_mu = jnp.einsum("nhd,hn->hd", mem_keys.astype(jnp.float32), mu_weight, precision=UPPER_LIMIT) * scale_dh
    key_sigma = jnp.einsum("nhd,hn->hd", mem_keys.astype(jnp.float32), sigma_weight, precision=UPPER_LIMIT) * scale_dh
    hidden_in = tokens.astype(jnp.float32)
    unused, norm_one_back = jax.vjp(layer_norm, hidden_in, ln1_gain, ln1_bias)
    levels = seq_count // 2
    row_pad = ((0, 6), (0, 0))
    norm_rows = jnp.pad(jnp.stack([ln1_gain, ln1_bias]), row_pad)
    qkv_flat = qkv_weight.reshape(D, 3 * head_cols)
    bias_row = jnp.concatenate([qv_bias[0], jnp.zeros(head_cols, jnp.float32), qv_bias[1]])
    bias_rows = jnp.broadcast_to(bias_row[None], (8, 3 * head_cols))
    reaches = doc_ids >= (seq_index + 1) * tok_rows
    key_mask = jnp.where(reaches, 0.0, NEGATIVE).astype(jnp.bfloat16).reshape(2, tok_rows // 2)
    key_mask = jnp.pad(key_mask, ((0, 14), (0, 2 * head_cols - tok_rows // 2)))
    normed_one, query_col, kv_col, local_flat, log_sum = attention_forward(
        levels, tokens, norm_rows, qkv_flat, bias_rows, doc_ids, key_mask
    )
    swap = [(index, index ^ 1) for index in range(seq_count)]
    query_oth = lax.ppermute(query_col, "seq", swap)
    kv_oth = lax.ppermute(kv_col, "seq", swap)
    queries = lax.dynamic_index_in_dim(query_col, seq_index // 2, 0, False)
    queries = (queries.astype(jnp.float32) / scale_dh).reshape(head_shape)
    local_out = local_flat.reshape(head_shape)
    rbf_width = 1.0 / NB
    queries_f = queries
    centre = jax.nn.sigmoid(jnp.sum(queries_f * key_mu, axis=-1))
    loose = jnp.sum(queries_f * key_sigma, axis=-1)
    spread_sq = SPREAD * jax.nn.softplus(loose) + rbf_width * rbf_width
    gap = centre[..., None] - radial_centres(NB)
    density_bf = (
        rbf_width
        * lax.rsqrt(spread_sq)[..., None]
        * jnp.exp(-0.5 * gap * gap / spread_sq[..., None])
    ).astype(jnp.bfloat16)
    mem_out = jnp.einsum(
        "thn,nhd->thd", density_bf, mem_vals, preferred_element_type=jnp.float32
    )
    heads_out = (local_out + mem_out).astype(jnp.bfloat16).reshape(tok_rows, head_cols)
    branch_one = (
        lax.psum(
            jnp.dot(heads_out, out_weight, preferred_element_type=jnp.float32).astype(jnp.bfloat16),
            "tp",
        ).astype(jnp.float32)
        + out_bias
    )
    residual = hidden_in + branch_one
    normed_two_f, norm_two_back = jax.vjp(layer_norm, residual, ln2_gain, ln2_bias)
    normed_two = normed_two_f.astype(jnp.bfloat16)
    pre_act = jnp.dot(normed_two, fc_weight, preferred_element_type=jnp.float32) + fc_bias
    activated, gelu_back = jax.vjp(gelu_tanh, pre_act)
    act_bf = activated.astype(jnp.bfloat16)
    branch_two = (
        lax.psum(
            jnp.dot(act_bf, proj_weight, preferred_element_type=jnp.float32).astype(jnp.bfloat16),
            "tp",
        ).astype(jnp.float32)
        + proj_bias
    )
    output = (residual + branch_two).astype(jnp.bfloat16)
    grad_out = cotangent.astype(jnp.float32)
    grad_proj_w = jnp.einsum("tf,td->fd", act_bf, cotangent, preferred_element_type=jnp.float32)
    grad_proj_b = jnp.sum(grad_out, axis=0)
    (grad_pre,) = gelu_back(
        jnp.einsum("td,fd->tf", cotangent, proj_weight, preferred_element_type=jnp.float32)
    )
    pre_bf = grad_pre.astype(jnp.bfloat16)
    grad_fc_w = jnp.einsum("td,tf->df", normed_two, pre_bf, preferred_element_type=jnp.float32)
    grad_fc_b = jnp.sum(pre_bf.astype(jnp.float32), axis=0)
    grad_normed_two = lax.psum(
        jnp.einsum("tf,df->td", pre_bf, fc_weight, preferred_element_type=jnp.float32).astype(
            jnp.bfloat16
        ),
        "tp",
    ).astype(jnp.float32)
    grad_resid_part, grad_ln2_g, grad_ln2_b = norm_two_back(grad_normed_two)
    grad_resid = grad_out + grad_resid_part
    resid_bf = grad_resid.astype(jnp.bfloat16)
    grad_out_w = jnp.einsum("tm,td->md", heads_out, resid_bf, preferred_element_type=jnp.float32)
    grad_out_b = jnp.sum(resid_bf.astype(jnp.float32), axis=0)
    grad_heads = (
        jnp.einsum("td,md->tm", resid_bf, out_weight, preferred_element_type=jnp.float32)
        .astype(jnp.bfloat16)
        .reshape(head_shape)
    )
    grad_density = jnp.einsum(
        "thd,nhd->thn", grad_heads, mem_vals, preferred_element_type=jnp.float32
    )
    grad_mem_vals = jnp.einsum(
        "thn,thd->nhd", density_bf, grad_heads, preferred_element_type=jnp.float32
    )
    weighed = grad_density * density_bf.astype(jnp.float32)
    sum_gap = jnp.sum(weighed * gap, axis=-1)
    sum_gap_sq = jnp.sum(weighed * gap * gap, axis=-1)
    sum_zero = jnp.sum(weighed, axis=-1)
    grad_centre = -sum_gap / spread_sq
    grad_spread = 0.5 * (sum_gap_sq / spread_sq - sum_zero) / spread_sq
    pull_mu = grad_centre * centre * (1.0 - centre)
    pull_sigma = grad_spread * SPREAD * jax.nn.sigmoid(loose)
    grad_q_mem = pull_mu[..., None] * key_mu + pull_sigma[..., None] * key_sigma
    query_mu = jnp.sum(pull_mu[..., None] * queries_f, axis=0) * scale_dh
    query_sigma = jnp.sum(pull_sigma[..., None] * queries_f, axis=0) * scale_dh
    mem_keys_f = mem_keys.astype(jnp.float32)
    grad_mu_w = jnp.einsum("nhd,hd->hn", mem_keys_f, query_mu, precision=UPPER_LIMIT)
    grad_sigma_w = jnp.einsum("nhd,hd->hn", mem_keys_f, query_sigma, precision=UPPER_LIMIT)
    grad_mem_keys = (
        mu_weight.T[:, :, None] * query_mu[None] + sigma_weight.T[:, :, None] * query_sigma[None]
    )
    grad_mem_seg = jnp.concatenate(
        [grad_mem_keys.reshape(NB, head_cols), grad_mem_vals.reshape(NB, head_cols)], axis=-1
    ).astype(jnp.bfloat16)
    grad_q_local, grad_keys, grad_vals = attention_backward(
        levels,
        grad_heads.reshape(tok_rows, head_cols),
        local_flat,
        log_sum,
        query_col,
        query_oth,
        kv_col,
        kv_oth,
        doc_ids,
    )
    grad_q_bf = (grad_q_local + grad_q_mem.reshape(tok_rows, head_cols)).astype(jnp.bfloat16)
    grad_k_bf = grad_keys.astype(jnp.bfloat16)
    grad_v_bf = grad_vals.astype(jnp.bfloat16)
    grad_qkv = jnp.stack([grad_q_bf, grad_k_bf, grad_v_bf], axis=1)
    grad_qkv_w = jnp.einsum("td,tcm->dcm", normed_one, grad_qkv, preferred_element_type=jnp.float32)
    grad_kv_w = jnp.einsum("nd,nm->dm", coeffs, grad_mem_seg, preferred_element_type=jnp.float32)
    grad_qkv_w = grad_qkv_w.at[:, 1:].add(grad_kv_w.reshape(D, 2, head_cols))
    grad_qv_b = jnp.stack(
        [
            jnp.sum(grad_q_bf.astype(jnp.float32), axis=0),
            jnp.sum(grad_v_bf.astype(jnp.float32), axis=0),
        ]
    )
    grad_normed_one = lax.psum(
        jnp.einsum("tcm,dcm->td", grad_qkv, qkv_weight, preferred_element_type=jnp.float32).astype(
            jnp.bfloat16
        ),
        "tp",
    ).astype(jnp.float32)
    grad_in_part, grad_ln1_g, grad_ln1_b = norm_one_back(grad_normed_one)
    grad_tokens = (grad_resid + grad_in_part).astype(jnp.bfloat16)
    qkv_share, out_share, fc_share, proj_share = (
        lax.psum_scatter(grad_qkv_w.reshape(D, -1).astype(jnp.bfloat16), "seq", scatter_dimension=0, tiled=True),
        lax.psum_scatter(grad_out_w.astype(jnp.bfloat16), "seq", scatter_dimension=1, tiled=True),
        lax.psum_scatter(grad_fc_w.astype(jnp.bfloat16), "seq", scatter_dimension=0, tiled=True),
        lax.psum_scatter(grad_proj_w.astype(jnp.bfloat16), "seq", scatter_dimension=1, tiled=True),
    )
    qkv_share = qkv_share.astype(jnp.float32).reshape(-1, 3, head_cols)
    out_share, fc_share, proj_share = (
        out_share.astype(jnp.float32),
        fc_share.astype(jnp.float32),
        proj_share.astype(jnp.float32),
    )
    small_sums = lax.psum(
        (
            grad_ln1_g,
            grad_ln1_b,
            grad_qv_b,
            grad_out_b,
            grad_ln2_g,
            grad_ln2_b,
            grad_fc_b,
            grad_proj_b,
            grad_mu_w,
            grad_sigma_w,
        ),
        "seq",
    )
    return (
        output,
        grad_tokens,
        qkv_share,
        small_sums[2],
        out_share,
        small_sums[3],
        fc_share,
        small_sums[6],
        proj_share,
        small_sums[7],
        small_sums[0],
        small_sums[1],
        small_sums[4],
        small_sums[5],
        small_sums[8],
        small_sums[9],
    )


def solution(mesh):
    in_specs = (
        P("seq", None),
        P("seq", None),
        P("seq", None),
        P("seq"),
        P("seq"),
        P("seq"),
        P("seq"),
        P(),
        P(),
        P(None, None, "tp"),
        P(None, "tp"),
        P("tp", None),
        P(),
        P(),
        P(),
        P(None, "tp"),
        P("tp"),
        P("tp", None),
        P(),
        P("tp", None),
        P("tp", None),
    )
    out_specs = (
        P("seq", None),
        P("seq", None),
        P("seq", None, "tp"),
        P(None, "tp"),
        P("tp", "seq"),
        P(),
        P("seq", "tp"),
        P("tp"),
        P("tp", "seq"),
        P(),
        P(),
        P(),
        P(),
        P(),
        P("tp", None),
        P("tp", None),
    )
    return jax.shard_map(local, mesh=mesh, in_specs=in_specs, out_specs=out_specs, check_vma=False)
```

```python
import functools

import ml_dtypes
import numpy as np

import jax
import jax.numpy as jnp
from jax import lax
from jax.experimental import pallas as pl
from jax.experimental.pallas import tpu as pltpu
from jax.sharding import PartitionSpec as P

D = 768
DH = 64
NB = 512
SEG = 512
BOOKS = 4


EPS = 1e-05
TAU = 0.75
RIDGE = 1.0
SPREAD = 0.01
NEGATIVE = -1e30
UPPER_LIMIT = lax.Precision.HIGHEST
MESH_ID = pl.DeviceIdType.MESH
VMEM_LIMIT = 60 * 2**20


def layer_norm(rows_in, gain_vec, bias_vec):
    average = jnp.mean(rows_in, axis=-1, keepdims=True)
    centred = rows_in - average
    variance = jnp.mean(centred * centred, axis=-1, keepdims=True)
    return centred * lax.rsqrt(variance + EPS) * gain_vec + bias_vec


def gelu_tanh(pre_act):
    return jax.nn.gelu(pre_act, approximate=True)


def radial_centres(basis_n):
    return (jnp.arange(basis_n, dtype=jnp.float32) + 0.5) / basis_n


def past_basis(seg_ages, basis_n, seg_len):
    shrink = jnp.power(jnp.float32(TAU), seg_ages.astype(jnp.float32))
    inside = (jnp.arange(seg_len, dtype=jnp.float32) + 0.5) / seg_len
    time_pts = shrink[:, None] * (TAU + (1.0 - TAU) * inside[None, :])
    offset = (time_pts[:, None, :] - radial_centres(basis_n)[None, :, None]) * basis_n
    return jnp.exp(-0.5 * offset * offset)


def coefficient_tables(age_count, basis_n, seg_len):
    shrink = TAU ** np.arange(age_count, dtype=np.float64)
    inside = (np.arange(seg_len) + 0.5) / seg_len
    times = shrink[:, None] * (TAU + (1.0 - TAU) * inside[None, :])
    centres = (np.arange(basis_n) + 0.5) / basis_n
    offset = (times[:, None, :] - centres[None, :, None]) * basis_n
    basis = np.exp(-0.5 * offset * offset)
    gram = np.einsum("agx,ahx->gh", basis, basis) + RIDGE * np.eye(basis_n)
    table = np.linalg.solve(gram[None], basis)
    high = table.astype(ml_dtypes.bfloat16)
    lower = (table - high.astype(np.float64)).astype(ml_dtypes.bfloat16)
    return high, lower


LANES_OUT = 256


def head_of_lane(width):
    return lax.broadcasted_iota(jnp.int32, (1, width), 1) // DH


def head_masks(width):
    lane_head = head_of_lane(width)
    return [(lane_head == head).astype(jnp.float32).astype(jnp.bfloat16) for head in range(width // DH)]


def pick_heads(per_head, lane_head):
    chosen = per_head[0]
    for head in range(1, len(per_head)):
        chosen = jnp.where(lane_head == head, per_head[head], chosen)
    return chosen


def dot_rows(left, right):
    return lax.dot_general(left, right, (((1,), (1,)), ((), ())), preferred_element_type=jnp.float32)


def dot_plain(left, right):
    return lax.dot_general(left, right, (((1,), (0,)), ((), ())), preferred_element_type=jnp.float32)


def thirds(value):
    first = value.astype(jnp.bfloat16)
    rest = value - first.astype(jnp.float32)
    second = rest.astype(jnp.bfloat16)
    third = (rest - second.astype(jnp.float32)).astype(jnp.bfloat16)
    return first, second, third


def with_stats(block, stats):
    rows, width = block.shape
    spare = LANES_OUT - width
    lane = lax.broadcasted_iota(jnp.int32, (1, spare), 1)
    tail = jnp.zeros((rows, spare), jnp.float32)
    for index, column in enumerate(stats):
        for part, value in enumerate(thirds(column)):
            tail = jnp.where(lane == 3 * index + part, value.astype(jnp.float32), tail)
    return jnp.concatenate([block, tail.astype(jnp.bfloat16)], axis=1)


def stat_column(extended, width, index):
    lane = lax.broadcasted_iota(jnp.int32, (1, LANES_OUT), 1)
    start = width + 3 * index
    mine = (lane >= start) & (lane < start + 3)
    return jnp.sum(jnp.where(mine, extended.astype(jnp.float32), 0.0), axis=1, keepdims=True)


def stat_rows(extended, width, count):
    row = lax.broadcasted_iota(jnp.int32, (count, LANES_OUT), 0)
    lane = lax.broadcasted_iota(jnp.int32, (count, LANES_OUT), 1)
    start = width + 3 * row
    chooser = ((lane >= start) & (lane < start + 3)).astype(jnp.float32).astype(jnp.bfloat16)
    return dot_rows(chooser, extended)


def greet(levels):
    seq, tp = lax.axis_index("seq"), lax.axis_index("tp")
    level, side = seq // 2, seq % 2
    barrier = pltpu.get_barrier_semaphore()
    pl.semaphore_signal(barrier, inc=1, device_id=(2 * level + 1 - side, tp), device_id_type=MESH_ID)

    def one(step, unused):
        other = lax.rem(level + step, levels)
        pl.semaphore_signal(barrier, inc=1, device_id=(2 * other + side, tp), device_id_type=MESH_ID)
        return unused

    lax.fori_loop(1, levels, one, 0)
    return barrier, levels


def forward_kernel(
    levels,
    tok_ref,
    norm_ref,
    weight_ref,
    bias_ref,
    doc_col_ref,
    doc_row_ref,
    key_mask_ref,
    normed_ref,
    query_out_ref,
    kv_out_ref,
    out_ref,
    lse_ref,
    pair_ref,
    top_ref,
    total_ref,
    acc_ref,
    part_ref,
    part_in_ref,
    kv_send,
    kv_recv,
    q_send,
    q_recv,
    pair_sem,
    part_sem,
):
    seq, tp = lax.axis_index("seq"), lax.axis_index("tp")
    level, side = seq // 2, seq % 2
    rows = tok_ref.shape[0]
    width = pair_ref.shape[2]
    heads = width // DH
    partner = (2 * level + 1 - side, tp)
    lane_head = head_of_lane(width)
    head_mask = head_masks(width)
    barrier, greetings = greet(levels)

    chunk = rows // 2

    def project(index, unused):
        here = pl.ds(pl.multiple_of(index * chunk, chunk), chunk)
        x = tok_ref[here, :].astype(jnp.float32)
        centred = x - jnp.mean(x, axis=1, keepdims=True)
        variance = jnp.mean(centred * centred, axis=1, keepdims=True)
        a = centred * lax.rsqrt(variance + EPS) * norm_ref[0:1, :] + norm_ref[1:2, :]
        a = a.astype(jnp.bfloat16)
        normed_ref[here, :] = a
        mixed = (dot_plain(a, weight_ref[...]) + bias_ref[0:1, :]).astype(jnp.bfloat16)
        query = mixed[:, :width] * jnp.bfloat16(DH**-0.5)
        pair_ref[0, here, :] = query
        query_out_ref[level, here, :] = query
        kv_out_ref[level, here, :] = mixed[:, width:]
        return unused

    lax.fori_loop(0, rows // chunk, project, 0)
    kv_out_ref[level, rows:, :] = key_mask_ref[...]

    pl.semaphore_wait(barrier, greetings)
    pair_copy = pltpu.make_async_remote_copy(
        pair_ref.at[0], pair_ref.at[1], pair_sem.at[0], pair_sem.at[1], device_id=partner, device_id_type=MESH_ID
    )
    pair_copy.start()

    def kv_copy(from_level):
        return pltpu.make_async_remote_copy(
            kv_out_ref.at[from_level],
            kv_out_ref.at[from_level],
            kv_send.at[from_level],
            kv_recv.at[from_level],
            device_id=(lax.rem(2 * level + 2, 2 * levels) + side, tp),
            device_id_type=MESH_ID,
        )

    def query_copy(from_level, to_level):
        return pltpu.make_async_remote_copy(
            query_out_ref.at[from_level],
            query_out_ref.at[from_level],
            q_send.at[to_level],
            q_recv.at[from_level],
            device_id=(2 * to_level + side, tp),
            device_id_type=MESH_ID,
        )

    @pl.when(level < levels - 1)
    def _():
        kv_copy(level).start()

    def send_down(step, unused):
        query_copy(level, level - step).start()
        return unused

    lax.fori_loop(1, level + 1, send_down, 0)

    top_ref[...] = jnp.full(top_ref.shape, NEGATIVE, jnp.float32)
    total_ref[...] = jnp.zeros(total_ref.shape, jnp.float32)
    acc_ref[...] = jnp.zeros(acc_ref.shape, jnp.float32)

    doc_first = doc_row_ref[0:1, 0:1]
    def reach_of(here):
        docs = doc_col_ref[here, :]
        last = (level == levels - 1) & (side == 1)
        return jnp.where(last & (docs != doc_first), NEGATIVE, 0.0)

    def fold(slot, from_level, mask_kind):
        mask_rows = kv_out_ref[from_level, rows:, :].astype(jnp.float32)
        key_mask = jnp.concatenate([mask_rows[0:1, : rows // 2], mask_rows[1:2, : rows // 2]], axis=1)

        def part(index, unused):
            here = pl.ds(pl.multiple_of(index * chunk, chunk), chunk)
            query = pair_ref[slot, here, :]
            keys = kv_out_ref[from_level, :rows, :width]
            vals = kv_out_ref[from_level, :rows, width:]
            if mask_kind == "own":
                q_pos = index * chunk + lax.broadcasted_iota(jnp.int32, (chunk, rows), 0)
                k_pos = lax.broadcasted_iota(jnp.int32, (chunk, rows), 1)
                visible = (q_pos >= k_pos) & (doc_col_ref[here, :] == doc_row_ref[0:1, :])
            products, scales = [], []
            for head in range(heads):
                scores = dot_rows(query * head_mask[head], keys)
                old_top = top_ref[slot, head, here, :]
                if mask_kind == "own":
                    scores = jnp.where(visible, scores, NEGATIVE)
                    reach = 0.0
                else:
                    scores = scores + key_mask
                    reach = jnp.where(slot == 0, reach_of(here), 0.0)
                new_top = jnp.maximum(old_top, jnp.max(scores, axis=1, keepdims=True) + reach)
                weights = jnp.exp(scores - (new_top - reach))
                scale = jnp.exp(old_top - new_top)
                top_ref[slot, head, here, :] = new_top
                total_ref[slot, head, here, :] = total_ref[slot, head, here, :] * scale + jnp.sum(
                    weights, axis=1, keepdims=True
                )
                products.append(dot_plain(weights.astype(jnp.bfloat16), vals))
                scales.append(scale)
            acc_ref[slot, here, :] = acc_ref[slot, here, :] * pick_heads(scales, lane_head) + pick_heads(
                products, lane_head
            )
            return unused

        lax.fori_loop(0, rows // chunk, part, 0)

    fold(0, level, "own")
    pair_copy.wait()

    @pl.when(side == 0)
    def _():
        fold(1, level, "off")

    def arrived(step, unused):
        from_level = level - step
        kv_copy(from_level).wait_recv()

        @pl.when(level < levels - 1)
        def _():
            kv_copy(from_level).start()

        def both(slot, inner):
            fold(slot, from_level, "off")
            return inner

        lax.fori_loop(0, 2, both, 0)
        return unused

    lax.fori_loop(1, level + 1, arrived, 0)

    def finish(index, unused):
        here = pl.ds(pl.multiple_of(index * chunk, chunk), chunk)
        totals = [total_ref[1, head, here, :] for head in range(heads)]
        tops = [top_ref[1, head, here, :] for head in range(heads)]
        some = [value > 0.0 for value in totals]
        inverse = [jnp.where(ok, 1.0 / jnp.where(ok, value, 1.0), 0.0) for ok, value in zip(some, totals)]
        logs = [
            jnp.where(ok, top + jnp.log(jnp.where(ok, value, 1.0)), NEGATIVE)
            for ok, top, value in zip(some, tops, totals)
        ]
        share = (acc_ref[1, here, :] * pick_heads(inverse, lane_head)).astype(jnp.bfloat16)
        part_ref[here, :] = with_stats(share, logs)
        return unused

    lax.fori_loop(0, rows // chunk, finish, 0)
    part_copy = pltpu.make_async_remote_copy(
        part_ref, part_in_ref, part_sem.at[0], part_sem.at[1], device_id=partner, device_id_type=MESH_ID
    )
    part_copy.start()
    part_copy.wait()

    def merge(index, unused):
        here = pl.ds(pl.multiple_of(index * chunk, chunk), chunk)
        reach = reach_of(here)
        received = part_in_ref[here, :]
        mine, theirs, columns = [], [], []
        for head in range(heads):
            total = total_ref[0, head, here, :]
            own_log = top_ref[0, head, here, :] + jnp.log(total)
            other_log = stat_column(received, width, head) + reach
            high = jnp.maximum(own_log, other_log)
            both_log = high + jnp.log(jnp.exp(own_log - high) + jnp.exp(other_log - high))
            mine.append(jnp.exp(own_log - both_log) / total)
            theirs.append(jnp.exp(other_log - both_log))
            columns.append(both_log)
        out_ref[here, :] = acc_ref[0, here, :] * pick_heads(mine, lane_head) + received[
            :, :width
        ].astype(jnp.float32) * pick_heads(theirs, lane_head)
        lane = lax.broadcasted_iota(jnp.int32, (1, 8), 1)
        packed = jnp.zeros((chunk, 8), jnp.float32)
        for head in range(heads):
            packed = jnp.where(lane == head, columns[head], packed)
        lse_ref[here, :] = packed
        return unused

    lax.fori_loop(0, rows // chunk, merge, 0)

    def sent_down(step, unused):
        query_copy(level, level - step).wait_send()
        return unused

    lax.fori_loop(1, level + 1, sent_down, 0)

    def from_above(step, unused):
        query_copy(level + step, level).wait_recv()
        return unused

    lax.fori_loop(1, levels - level, from_above, 0)

    @pl.when(level < levels - 1)
    def _():
        def sent_up(from_level, unused):
            kv_copy(from_level).wait_send()
            return unused

        lax.fori_loop(0, level + 1, sent_up, 0)


def attention_forward(levels, tokens, norm, weight, bias, doc_ids, key_mask):
    rows = tokens.shape[0]
    width = weight.shape[1] // 3
    heads = width // DH
    vmem = pl.BlockSpec(memory_space=pltpu.VMEM)
    dma = pltpu.SemaphoreType.DMA
    return pl.pallas_call(
        functools.partial(forward_kernel, levels),
        out_shape=(
            jax.ShapeDtypeStruct((rows, D), jnp.bfloat16),
            jax.ShapeDtypeStruct((levels, rows, width), jnp.bfloat16),
            jax.ShapeDtypeStruct((levels, rows + 16, 2 * width), jnp.bfloat16),
            jax.ShapeDtypeStruct((rows, width), jnp.float32),
            jax.ShapeDtypeStruct((rows, 8), jnp.float32),
        ),
        in_specs=[vmem] * 7,
        out_specs=(vmem,) * 5,
        scratch_shapes=[
            pltpu.VMEM((2, rows, width), jnp.bfloat16),
            pltpu.VMEM((2, heads, rows, 1), jnp.float32),
            pltpu.VMEM((2, heads, rows, 1), jnp.float32),
            pltpu.VMEM((2, rows, width), jnp.float32),
            pltpu.VMEM((rows, LANES_OUT), jnp.bfloat16),
            pltpu.VMEM((rows, LANES_OUT), jnp.bfloat16),
            dma((levels,)),
            dma((levels,)),
            dma((levels,)),
            dma((levels,)),
            dma((2,)),
            dma((2,)),
        ],
        name="attention_forward",
        compiler_params=pltpu.CompilerParams(
            collective_id=1, has_side_effects=True, vmem_limit_bytes=VMEM_LIMIT
        ),
    )(tokens, norm, weight, bias, doc_ids[:, None], doc_ids[None, :], key_mask)


def backward_kernel(
    levels,
    grad_ref,
    attended_ref,
    lse_ref,
    query_col_ref,
    query_oth_ref,
    kv_col_ref,
    kv_oth_ref,
    doc_col_ref,
    doc_row_ref,
    dq_ref,
    dk_ref,
    dv_ref,
    own_ref,
    grad_col_ref,
    grad_oth_ref,
    stat_ref,
    col_send,
    col_recv,
    oth_send,
    oth_recv,
    *staging,
):
    seq, tp = lax.axis_index("seq"), lax.axis_index("tp")
    level, side = seq // 2, seq % 2
    rows, width = grad_ref.shape
    heads = width // DH
    partner = (2 * level + 1 - side, tp)
    lane_head = head_of_lane(width)
    head_mask = head_masks(width)
    chunk = rows // 2
    barrier, greetings = greet(levels)
    doc_first = doc_row_ref[0:1, 0:1]
    last = (level == levels - 1) & (side == 1)

    def prepare(index, unused):
        here = pl.ds(pl.multiple_of(index * chunk, chunk), chunk)
        grad = grad_ref[here, :]
        product = grad.astype(jnp.float32) * attended_ref[here, :]
        far = jnp.where(last & (doc_col_ref[here, :] != doc_first), -NEGATIVE, 0.0)
        lses = [lse_ref[here, head : head + 1] for head in range(heads)]
        deltas = [
            jnp.sum(jnp.where(lane_head == head, product, 0.0), axis=1, keepdims=True)
            for head in range(heads)
        ]
        own_ref[here, :] = with_stats(grad, lses + deltas)
        grad_col_ref[level, here, :] = with_stats(grad, [lse + far for lse in lses] + deltas)
        for head in range(heads):
            stat_ref[head, here, :] = lses[head]
            stat_ref[heads + head, here, :] = lses[head] + far
            stat_ref[2 * heads + head, here, :] = deltas[head]
        return unused

    lax.fori_loop(0, rows // chunk, prepare, 0)
    pl.semaphore_wait(barrier, greetings)

    def col_copy(from_level, to_level):
        return pltpu.make_async_remote_copy(
            grad_col_ref.at[from_level],
            grad_col_ref.at[from_level],
            col_send.at[to_level],
            col_recv.at[from_level],
            device_id=(2 * to_level + side, tp),
            device_id_type=MESH_ID,
        )

    def oth_copy(from_level):
        return pltpu.make_async_remote_copy(
            grad_col_ref.at[from_level],
            grad_oth_ref.at[from_level],
            oth_send.at[from_level],
            oth_recv.at[from_level],
            device_id=partner,
            device_id_type=MESH_ID,
        )

    @pl.when(side == 1)
    def _():
        oth_copy(level).start()

    def send_down(step, unused):
        col_copy(level, level - step).start()
        return unused

    lax.fori_loop(1, level + 1, send_down, 0)

    dq_ref[...] = jnp.zeros(dq_ref.shape, jnp.float32)
    dk_ref[...] = jnp.zeros(dk_ref.shape, jnp.float32)
    dv_ref[...] = jnp.zeros(dv_ref.shape, jnp.float32)

    def block_of(kv_ref, from_level):
        if not staging:
            return kv_ref.at[from_level]
        block_ref, block_sem = staging
        copy = pltpu.make_async_copy(kv_ref.at[from_level], block_ref, block_sem)
        copy.start()
        copy.wait()
        return block_ref

    def query_fold(kv_ref, from_level, own):
        block_ref = block_of(kv_ref, from_level)
        if own:
            key_mask = None
        else:
            mask_rows = block_ref[rows:, :].astype(jnp.float32)
            key_mask = jnp.concatenate(
                [mask_rows[0:1, : rows // 2], mask_rows[1:2, : rows // 2]], axis=1
            )

        def part(index, unused):
            here = pl.ds(pl.multiple_of(index * chunk, chunk), chunk)
            query = query_col_ref[level, here, :]
            grad = grad_ref[here, :]
            keys = block_ref[:rows, :width]
            vals = block_ref[:rows, width:]
            if own:
                q_pos = index * chunk + lax.broadcasted_iota(jnp.int32, (chunk, rows), 0)
                k_pos = lax.broadcasted_iota(jnp.int32, (chunk, rows), 1)
                visible = (q_pos >= k_pos) & (doc_col_ref[here, :] == doc_row_ref[0:1, :])
            products = []
            for head in range(heads):
                scores = dot_rows(query * head_mask[head], keys)
                if own:
                    scores = jnp.where(visible, scores, NEGATIVE)
                    lse = stat_ref[head, here, :]
                else:
                    scores = scores + key_mask
                    lse = stat_ref[heads + head, here, :]
                probs = jnp.exp(scores - lse)
                pull = dot_rows(grad * head_mask[head], vals) - stat_ref[2 * heads + head, here, :]
                products.append(dot_plain((probs * pull).astype(jnp.bfloat16), keys))
            dq_ref[here, :] = dq_ref[here, :] + pick_heads(products, lane_head)
            return unused

        lax.fori_loop(0, rows // chunk, part, 0)

    query_fold(kv_col_ref, level, True)

    @pl.when(side == 1)
    def _():
        query_fold(kv_oth_ref, level, False)

    def earlier(from_level, unused):
        query_fold(kv_col_ref, from_level, False)
        query_fold(kv_oth_ref, from_level, False)
        return unused

    lax.fori_loop(0, level, earlier, 0)
    dq_ref[...] = dq_ref[...] * (DH**-0.5)

    own_block_ref = block_of(kv_col_ref, level)

    def key_fold(query_ref, grads_ref, from_level, own):
        def part(index, unused):
            here = pl.ds(pl.multiple_of(index * chunk, chunk), chunk)
            keys = own_block_ref[here, :width]
            vals = own_block_ref[here, width:]
            if own:
                query = query_col_ref[level]
                extended = own_ref[...]
                k_pos = index * chunk + lax.broadcasted_iota(jnp.int32, (chunk, rows), 0)
                q_pos = lax.broadcasted_iota(jnp.int32, (chunk, rows), 1)
                visible = (q_pos >= k_pos) & (doc_col_ref[here, :] == doc_row_ref[0:1, :])
            else:
                query = query_ref[from_level]
                extended = grads_ref[from_level]
            grad = extended[:, :width]
            stats = stat_rows(extended, width, 8)
            key_parts, val_parts = [], []
            for head in range(heads):
                scores = dot_rows(keys * head_mask[head], query)
                if own:
                    scores = jnp.where(visible, scores, NEGATIVE)
                probs = jnp.exp(scores - stats[head : head + 1, :])
                val_parts.append(dot_plain(probs.astype(jnp.bfloat16), grad))
                pull = dot_rows(vals * head_mask[head], grad) - stats[heads + head : heads + head + 1, :]
                key_parts.append(dot_plain((probs * pull).astype(jnp.bfloat16), query))
            dk_ref[here, :] = dk_ref[here, :] + pick_heads(key_parts, lane_head)
            dv_ref[here, :] = dv_ref[here, :] + pick_heads(val_parts, lane_head)
            return unused

        lax.fori_loop(0, rows // chunk, part, 0)

    @pl.when(side == 0)
    def _():
        oth_copy(level).wait_recv()
        key_fold(query_oth_ref, grad_oth_ref, level, False)

    def later(step, unused):
        from_level = level + step
        col_copy(from_level, level).wait_recv()
        oth_copy(from_level).start()
        key_fold(query_col_ref, grad_col_ref, from_level, False)
        oth_copy(from_level).wait_recv()
        key_fold(query_oth_ref, grad_oth_ref, from_level, False)
        return unused

    lax.fori_loop(1, levels - level, later, 0)
    reaches = doc_col_ref[...] >= (seq + 1) * rows
    dk_ref[...] = jnp.where(reaches, dk_ref[...], 0.0)
    dv_ref[...] = jnp.where(reaches, dv_ref[...], 0.0)
    key_fold(None, None, level, True)

    @pl.when(side == 1)
    def _():
        oth_copy(level).wait_send()

    def sent_down(step, unused):
        col_copy(level, level - step).wait_send()
        return unused

    lax.fori_loop(1, level + 1, sent_down, 0)

    def sent_on(step, unused):
        oth_copy(level + step).wait_send()
        return unused

    lax.fori_loop(1, levels - level, sent_on, 0)


def attention_backward(levels, grad, attended, lse, query_col, query_oth, kv_col, kv_oth, doc_ids):
    rows, width = grad.shape
    heads = width // DH
    vmem = pl.BlockSpec(memory_space=pltpu.VMEM)
    dma = pltpu.SemaphoreType.DMA
    full = jax.ShapeDtypeStruct((rows, width), jnp.float32)
    staged = levels > 8
    far = pl.BlockSpec(memory_space=pl.ANY) if staged else vmem
    staging = [pltpu.VMEM(kv_col.shape[1:], kv_col.dtype), dma(())] if staged else []
    return pl.pallas_call(
        functools.partial(backward_kernel, levels),
        out_shape=(full, full, full),
        in_specs=[vmem] * 5 + [far] * 2 + [vmem] * 2,
        out_specs=(vmem,) * 3,
        scratch_shapes=[
            pltpu.VMEM((rows, LANES_OUT), jnp.bfloat16),
            pltpu.VMEM((levels, rows, LANES_OUT), jnp.bfloat16),
            pltpu.VMEM((levels, rows, LANES_OUT), jnp.bfloat16),
            pltpu.VMEM((3 * heads, rows, 1), jnp.float32),
            dma((levels,)),
            dma((levels,)),
            dma((levels,)),
            dma((levels,)),
            *staging,
        ],
        name="attention_backward",
        compiler_params=pltpu.CompilerParams(
            collective_id=2, has_side_effects=True, vmem_limit_bytes=VMEM_LIMIT
        ),
    )(grad, attended, lse, query_col, query_oth, kv_col, kv_oth, doc_ids[:, None], doc_ids[None, :])


def column_copy(block_ref, from_level, landing_ref, send_sem, recv_sem, to_level):
    seq, tp = lax.axis_index("seq"), lax.axis_index("tp")
    return pltpu.make_async_remote_copy(
        block_ref,
        landing_ref.at[from_level],
        send_sem.at[to_level],
        recv_sem.at[from_level],
        device_id=(2 * to_level + seq % 2, tp),
        device_id_type=MESH_ID,
    )


class Scatter:
    def __init__(self, levels, blocks, plane_in, plane_sum, column_in, sems):
        self.levels, self.blocks = levels, blocks
        self.plane_in, self.plane_sum, self.column_in = plane_in, plane_sum, column_in
        self.plane_send, self.plane_recv, self.column_send, self.column_recv = sems
        seq, tp = lax.axis_index("seq"), lax.axis_index("tp")
        self.level, self.side, self.tp = seq // 2, seq % 2, tp

    def plane_copy(self, to_level):
        return pltpu.make_async_remote_copy(
            self.blocks.at[2 * to_level + 1 - self.side],
            self.plane_in.at[to_level],
            self.plane_send.at[to_level],
            self.plane_recv.at[to_level],
            device_id=(2 * self.level + 1 - self.side, self.tp),
            device_id_type=MESH_ID,
        )

    def swap_copy(self, from_level, to_level):
        return column_copy(
            self.plane_sum.at[to_level], from_level, self.column_in, self.column_send, self.column_recv, to_level
        )

    def loop(self, first, body):
        def one(step, unused):
            body(lax.rem(self.level + step, self.levels))
            return unused

        lax.fori_loop(first, self.levels, one, 0)

    def start(self):
        self.loop(0, lambda other: self.plane_copy(other).start())

    def middle(self):
        def one(other):
            self.plane_copy(other).wait_recv()
            total = self.blocks[2 * other + self.side].astype(jnp.float32) + self.plane_in[other].astype(
                jnp.float32
            )
            self.plane_sum[other] = total.astype(jnp.bfloat16)
            self.swap_copy(self.level, other).start()

        self.loop(1, one)

    def finish(self, out_ref):
        self.plane_copy(self.level).wait_recv()
        out_ref[...] = self.blocks[2 * self.level + self.side].astype(jnp.float32) + self.plane_in[
            self.level
        ].astype(jnp.float32)

        def one(other):
            self.swap_copy(other, self.level).wait_recv()
            out_ref[...] += self.column_in[other].astype(jnp.float32)

        self.loop(1, one)
        self.loop(0, lambda other: self.plane_copy(other).wait_send())
        self.loop(1, lambda other: self.swap_copy(self.level, other).wait_send())

    @staticmethod
    def scratch(levels, rows, width):
        buffer = pltpu.VMEM((levels, rows, width), jnp.bfloat16)
        return [buffer] * 3 + [pltpu.SemaphoreType.DMA((levels,))] * 4


class SmallSum:
    def __init__(self, levels, small, plane_in, column_in, sems):
        self.levels, self.small, self.plane_in, self.column_in = levels, small, plane_in, column_in
        self.plane_sem, self.column_send, self.column_recv = sems
        seq, tp = lax.axis_index("seq"), lax.axis_index("tp")
        self.level, self.side, self.tp = seq // 2, seq % 2, tp

    def plane_copy(self):
        return pltpu.make_async_remote_copy(
            self.small,
            self.plane_in,
            self.plane_sem.at[0],
            self.plane_sem.at[1],
            device_id=(2 * self.level + 1 - self.side, self.tp),
            device_id_type=MESH_ID,
        )

    def swap_copy(self, from_level, to_level):
        return column_copy(
            self.column_in.at[from_level], from_level, self.column_in, self.column_send, self.column_recv, to_level
        )

    def loop(self, body):
        def one(step, unused):
            body(lax.rem(self.level + step, self.levels))
            return unused

        lax.fori_loop(1, self.levels, one, 0)

    def start(self):
        self.plane_copy().start()

    def middle(self):
        self.plane_copy().wait()
        self.column_in[self.level] = self.small[...] + self.plane_in[...]
        self.loop(lambda other: self.swap_copy(self.level, other).start())

    def finish(self, out_ref):
        self.loop(lambda other: self.swap_copy(other, self.level).wait_recv())
        self.loop(lambda other: self.swap_copy(self.level, other).wait_send())
        out_ref[...] = self.column_in[0]

        def one(other, unused):
            out_ref[...] += self.column_in[other]
            return unused

        lax.fori_loop(1, self.levels, one, 0)

    @staticmethod
    def scratch(levels, shape):
        dma = pltpu.SemaphoreType.DMA
        return [
            pltpu.VMEM(shape, jnp.float32),
            pltpu.VMEM((levels,) + shape, jnp.float32),
            dma((2,)),
            dma((levels,)),
            dma((levels,)),
        ]


def gradient_kernel(levels, count, *refs):
    blocks, refs = refs[:count], refs[count:]
    small_ref, refs = refs[0], refs[1:]
    outs, refs = refs[:count], refs[count:]
    small_out, refs = refs[0], refs[1:]
    sums = []
    for index in range(count):
        own, refs = refs[:7], refs[7:]
        sums.append(Scatter(levels, blocks[index], own[0], own[1], own[2], own[3:]))
    small = SmallSum(levels, small_ref, refs[0], refs[1], refs[2:])
    barrier, greetings = greet(levels)
    pl.semaphore_wait(barrier, greetings)
    small.start()
    for one in sums:
        one.start()
    small.middle()
    for one in sums:
        one.middle()
    small.finish(small_out)
    for one, out_ref in zip(sums, outs):
        one.finish(out_ref)


def sum_gradients(levels, blocks, small):
    vmem = pl.BlockSpec(memory_space=pltpu.VMEM)
    scratch = []
    for block in blocks:
        scratch += Scatter.scratch(levels, *block.shape[1:])
    scratch += SmallSum.scratch(levels, small.shape)
    return pl.pallas_call(
        functools.partial(gradient_kernel, levels, len(blocks)),
        out_shape=tuple(jax.ShapeDtypeStruct(block.shape[1:], jnp.float32) for block in blocks)
        + (jax.ShapeDtypeStruct(small.shape, jnp.float32),),
        in_specs=[vmem] * (len(blocks) + 1),
        out_specs=(vmem,) * (len(blocks) + 1),
        scratch_shapes=scratch,
        name="sum_gradients",
        compiler_params=pltpu.CompilerParams(
            collective_id=3, has_side_effects=True, vmem_limit_bytes=VMEM_LIMIT
        ),
    )(*blocks, small)


def local(
    tokens,
    cotangent,
    past_states,
    doc_ids,
    cur_book,
    past_book,
    past_age,
    ln1_gain,
    ln1_bias,
    qkv_weight,
    qv_bias,
    out_weight,
    out_bias,
    ln2_gain,
    ln2_bias,
    fc_weight,
    fc_bias,
    proj_weight,
    proj_bias,
    mu_weight,
    sigma_weight,
):
    tok_rows = tokens.shape[0]
    heads_here = mu_weight.shape[0]
    head_cols = qkv_weight.shape[2]
    seg_here = cur_book.shape[0]
    seq_count = lax.axis_size("seq")
    seq_index = lax.axis_index("seq")
    scale_dh = DH ** (-0.5)
    head_shape = (tok_rows, heads_here, DH)
    own_pos = seq_index * tok_rows + jnp.arange(tok_rows, dtype=jnp.int32)
    quarter = D // lax.axis_size("tp")
    my_quarter = lax.dynamic_slice_in_dim(
        past_states, lax.axis_index("tp") * quarter, quarter, axis=1
    )
    all_states = lax.all_gather(my_quarter, "seq", axis=0)
    books_ages = lax.all_gather(jnp.stack([past_book, past_age]), "seq", axis=1, tiled=True)
    age_count = seq_count * seg_here // BOOKS
    high, lower = coefficient_tables(age_count, NB, SEG)
    chosen = (books_ages[0] == cur_book[0])[None, :] & (
        books_ages[1][None, :] == jnp.arange(age_count, dtype=jnp.int32)[:, None]
    )
    by_age = jnp.einsum(
        "as,std->atd",
        chosen.astype(jnp.bfloat16),
        all_states,
        preferred_element_type=jnp.float32,
    ).astype(jnp.bfloat16)
    coeff_part = jnp.einsum(
        "ant,atd->nd", jnp.asarray(high), by_age, preferred_element_type=jnp.float32
    ) + jnp.einsum("ant,atd->nd", jnp.asarray(lower), by_age, preferred_element_type=jnp.float32)
    coeffs = lax.all_gather(coeff_part.astype(jnp.bfloat16), "tp", axis=1, tiled=True)
    mem_keys = (
        jnp.dot(coeffs, qkv_weight[:, 1], preferred_element_type=jnp.float32)
        .astype(jnp.bfloat16)
        .reshape(NB, heads_here, DH)
    )
    mem_vals = (
        jnp.dot(coeffs, qkv_weight[:, 2], preferred_element_type=jnp.float32)
        .astype(jnp.bfloat16)
        .reshape(NB, heads_here, DH)
    )
    key_mu = jnp.einsum("nhd,hn->hd", mem_keys.astype(jnp.float32), mu_weight, precision=UPPER_LIMIT) * scale_dh
    key_sigma = jnp.einsum("nhd,hn->hd", mem_keys.astype(jnp.float32), sigma_weight, precision=UPPER_LIMIT) * scale_dh
    hidden_in = tokens.astype(jnp.float32)
    unused, norm_one_back = jax.vjp(layer_norm, hidden_in, ln1_gain, ln1_bias)
    levels = seq_count // 2
    row_pad = ((0, 6), (0, 0))
    norm_rows = jnp.pad(jnp.stack([ln1_gain, ln1_bias]), row_pad)
    qkv_flat = qkv_weight.reshape(D, 3 * head_cols)
    bias_row = jnp.concatenate([qv_bias[0], jnp.zeros(head_cols, jnp.float32), qv_bias[1]])
    bias_rows = jnp.broadcast_to(bias_row[None], (8, 3 * head_cols))
    reaches = doc_ids >= (seq_index + 1) * tok_rows
    key_mask = jnp.where(reaches, 0.0, NEGATIVE).astype(jnp.bfloat16).reshape(2, tok_rows // 2)
    key_mask = jnp.pad(key_mask, ((0, 14), (0, 2 * head_cols - tok_rows // 2)))
    normed_one, query_col, kv_col, local_flat, log_sum = attention_forward(
        levels, tokens, norm_rows, qkv_flat, bias_rows, doc_ids, key_mask
    )
    swap = [(index, index ^ 1) for index in range(seq_count)]
    query_oth = lax.ppermute(query_col, "seq", swap)
    kv_oth = lax.ppermute(kv_col, "seq", swap)
    queries = lax.dynamic_index_in_dim(query_col, seq_index // 2, 0, False)
    queries = (queries.astype(jnp.float32) / scale_dh).reshape(head_shape)
    local_out = local_flat.reshape(head_shape)
    rbf_width = 1.0 / NB
    queries_f = queries
    centre = jax.nn.sigmoid(jnp.sum(queries_f * key_mu, axis=-1))
    loose = jnp.sum(queries_f * key_sigma, axis=-1)
    spread_sq = SPREAD * jax.nn.softplus(loose) + rbf_width * rbf_width
    gap = centre[..., None] - radial_centres(NB)
    density_bf = (
        rbf_width
        * lax.rsqrt(spread_sq)[..., None]
        * jnp.exp(-0.5 * gap * gap / spread_sq[..., None])
    ).astype(jnp.bfloat16)
    mem_out = jnp.einsum(
        "thn,nhd->thd", density_bf, mem_vals, preferred_element_type=jnp.float32
    )
    heads_out = (local_out + mem_out).astype(jnp.bfloat16).reshape(tok_rows, head_cols)
    branch_one = (
        lax.psum(
            jnp.dot(heads_out, out_weight, preferred_element_type=jnp.float32).astype(jnp.bfloat16),
            "tp",
        ).astype(jnp.float32)
        + out_bias
    )
    residual = hidden_in + branch_one
    normed_two_f, norm_two_back = jax.vjp(layer_norm, residual, ln2_gain, ln2_bias)
    normed_two = normed_two_f.astype(jnp.bfloat16)
    pre_act = jnp.dot(normed_two, fc_weight, preferred_element_type=jnp.float32) + fc_bias
    activated, gelu_back = jax.vjp(gelu_tanh, pre_act)
    act_bf = activated.astype(jnp.bfloat16)
    branch_two = (
        lax.psum(
            jnp.dot(act_bf, proj_weight, preferred_element_type=jnp.float32).astype(jnp.bfloat16),
            "tp",
        ).astype(jnp.float32)
        + proj_bias
    )
    output = (residual + branch_two).astype(jnp.bfloat16)
    grad_out = cotangent.astype(jnp.float32)
    grad_proj_w = jnp.einsum("td,tf->df", cotangent, act_bf, preferred_element_type=jnp.float32)
    grad_proj_b = jnp.sum(grad_out, axis=0)
    (grad_pre,) = gelu_back(
        jnp.einsum("td,fd->tf", cotangent, proj_weight, preferred_element_type=jnp.float32)
    )
    pre_bf = grad_pre.astype(jnp.bfloat16)
    grad_fc_w = jnp.einsum("td,tf->df", normed_two, pre_bf, preferred_element_type=jnp.float32)
    grad_fc_b = jnp.sum(pre_bf.astype(jnp.float32), axis=0)
    grad_normed_two = lax.psum(
        jnp.einsum("tf,df->td", pre_bf, fc_weight, preferred_element_type=jnp.float32).astype(
            jnp.bfloat16
        ),
        "tp",
    ).astype(jnp.float32)
    grad_resid_part, grad_ln2_g, grad_ln2_b = norm_two_back(grad_normed_two)
    grad_resid = grad_out + grad_resid_part
    resid_bf = grad_resid.astype(jnp.bfloat16)
    grad_out_w = jnp.einsum("td,tm->dm", resid_bf, heads_out, preferred_element_type=jnp.float32)
    grad_out_b = jnp.sum(resid_bf.astype(jnp.float32), axis=0)
    grad_heads = (
        jnp.einsum("td,md->tm", resid_bf, out_weight, preferred_element_type=jnp.float32)
        .astype(jnp.bfloat16)
        .reshape(head_shape)
    )
    grad_density = jnp.einsum(
        "thd,nhd->thn", grad_heads, mem_vals, preferred_element_type=jnp.float32
    )
    grad_mem_vals = jnp.einsum(
        "thn,thd->nhd", density_bf, grad_heads, preferred_element_type=jnp.float32
    )
    weighed = grad_density * density_bf.astype(jnp.float32)
    sum_gap = jnp.sum(weighed * gap, axis=-1)
    sum_gap_sq = jnp.sum(weighed * gap * gap, axis=-1)
    sum_zero = jnp.sum(weighed, axis=-1)
    grad_centre = -sum_gap / spread_sq
    grad_spread = 0.5 * (sum_gap_sq / spread_sq - sum_zero) / spread_sq
    pull_mu = grad_centre * centre * (1.0 - centre)
    pull_sigma = grad_spread * SPREAD * jax.nn.sigmoid(loose)
    grad_q_mem = pull_mu[..., None] * key_mu + pull_sigma[..., None] * key_sigma
    query_mu = jnp.sum(pull_mu[..., None] * queries_f, axis=0) * scale_dh
    query_sigma = jnp.sum(pull_sigma[..., None] * queries_f, axis=0) * scale_dh
    mem_keys_f = mem_keys.astype(jnp.float32)
    grad_mu_w = jnp.einsum("nhd,hd->hn", mem_keys_f, query_mu, precision=UPPER_LIMIT)
    grad_sigma_w = jnp.einsum("nhd,hd->hn", mem_keys_f, query_sigma, precision=UPPER_LIMIT)
    grad_mem_keys = (
        mu_weight.T[:, :, None] * query_mu[None] + sigma_weight.T[:, :, None] * query_sigma[None]
    )
    grad_mem_seg = jnp.concatenate(
        [grad_mem_keys.reshape(NB, head_cols), grad_mem_vals.reshape(NB, head_cols)], axis=-1
    ).astype(jnp.bfloat16)
    grad_q_local, grad_keys, grad_vals = attention_backward(
        levels,
        grad_heads.reshape(tok_rows, head_cols),
        local_flat,
        log_sum,
        query_col,
        query_oth,
        kv_col,
        kv_oth,
        doc_ids,
    )
    grad_q_bf = (grad_q_local + grad_q_mem.reshape(tok_rows, head_cols)).astype(jnp.bfloat16)
    grad_k_bf = grad_keys.astype(jnp.bfloat16)
    grad_v_bf = grad_vals.astype(jnp.bfloat16)
    grad_qkv = jnp.stack([grad_q_bf, grad_k_bf, grad_v_bf], axis=1)
    grad_qkv_w = jnp.einsum("td,tcm->dcm", normed_one, grad_qkv, preferred_element_type=jnp.float32)
    grad_kv_w = jnp.einsum("nd,nm->dm", coeffs, grad_mem_seg, preferred_element_type=jnp.float32)
    grad_qkv_w = grad_qkv_w.at[:, 1:].add(grad_kv_w.reshape(D, 2, head_cols))
    grad_qv_b = jnp.stack(
        [
            jnp.sum(grad_q_bf.astype(jnp.float32), axis=0),
            jnp.sum(grad_v_bf.astype(jnp.float32), axis=0),
        ]
    )
    grad_normed_one = lax.psum(
        jnp.einsum("tcm,dcm->td", grad_qkv, qkv_weight, preferred_element_type=jnp.float32).astype(
            jnp.bfloat16
        ),
        "tp",
    ).astype(jnp.float32)
    grad_in_part, grad_ln1_g, grad_ln1_b = norm_one_back(grad_normed_one)
    grad_tokens = (grad_resid + grad_in_part).astype(jnp.bfloat16)
    def shards(grad):
        return grad.astype(jnp.bfloat16).reshape(seq_count, D // seq_count, -1)

    small = jnp.concatenate(
        [
            grad_ln1_g[None],
            grad_ln1_b[None],
            grad_out_b[None],
            grad_ln2_g[None],
            grad_ln2_b[None],
            grad_proj_b[None],
            grad_fc_b[None],
            jnp.pad(grad_qv_b.reshape(1, -1), ((0, 0), (0, D - 2 * head_cols))),
            grad_mu_w.reshape(2, D),
            grad_sigma_w.reshape(2, D),
            jnp.zeros((4, D), jnp.float32),
        ]
    )
    proj_share, fc_share, rest_share, small = sum_gradients(
        levels,
        [
            shards(grad_proj_w),
            shards(grad_fc_w),
            shards(jnp.concatenate([grad_qkv_w.reshape(D, -1), grad_out_w], axis=1)),
        ],
        small,
    )
    qkv_share = rest_share[:, : 3 * head_cols].reshape(-1, 3, head_cols)
    out_share = rest_share[:, 3 * head_cols :].T
    return (
        output,
        grad_tokens,
        qkv_share,
        small[7, : 2 * head_cols].reshape(2, head_cols),
        out_share,
        small[2],
        fc_share,
        small[6],
        proj_share.T,
        small[5],
        small[0],
        small[1],
        small[3],
        small[4],
        small[8:10].reshape(heads_here, NB),
        small[10:12].reshape(heads_here, NB),
    )


def solution(mesh):
    in_specs = (
        P("seq", None),
        P("seq", None),
        P("seq", None),
        P("seq"),
        P("seq"),
        P("seq"),
        P("seq"),
        P(),
        P(),
        P(None, None, "tp"),
        P(None, "tp"),
        P("tp", None),
        P(),
        P(),
        P(),
        P(None, "tp"),
        P("tp"),
        P("tp", None),
        P(),
        P("tp", None),
        P("tp", None),
    )
    out_specs = (
        P("seq", None),
        P("seq", None),
        P("seq", None, "tp"),
        P(None, "tp"),
        P("tp", "seq"),
        P(),
        P("seq", "tp"),
        P("tp"),
        P("tp", "seq"),
        P(),
        P(),
        P(),
        P(),
        P(),
        P("tp", None),
        P("tp", None),
    )
    return jax.shard_map(local, mesh=mesh, in_specs=in_specs, out_specs=out_specs, check_vma=False)
```

```python
import functools

import ml_dtypes
import numpy as np

import jax
import jax.numpy as jnp
from jax import lax
from jax.experimental import pallas as pl
from jax.experimental.pallas import tpu as pltpu
from jax.sharding import PartitionSpec as P

D = 768
DH = 64
NB = 512
SEG = 512
BOOKS = 4


EPS = 1e-05
TAU = 0.75
RIDGE = 1.0
SPREAD = 0.01
NEGATIVE = -1e30
UPPER_LIMIT = lax.Precision.HIGHEST
MESH_ID = pl.DeviceIdType.MESH
VMEM_LIMIT = 60 * 2**20


def radial_centres(basis_n):
    return (jnp.arange(basis_n, dtype=jnp.float32) + 0.5) / basis_n


def past_basis(seg_ages, basis_n, seg_len):
    shrink = jnp.power(jnp.float32(TAU), seg_ages.astype(jnp.float32))
    inside = (jnp.arange(seg_len, dtype=jnp.float32) + 0.5) / seg_len
    time_pts = shrink[:, None] * (TAU + (1.0 - TAU) * inside[None, :])
    offset = (time_pts[:, None, :] - radial_centres(basis_n)[None, :, None]) * basis_n
    return jnp.exp(-0.5 * offset * offset)


def coefficient_tables(age_count, basis_n, seg_len):
    shrink = TAU ** np.arange(age_count, dtype=np.float64)
    inside = (np.arange(seg_len) + 0.5) / seg_len
    times = shrink[:, None] * (TAU + (1.0 - TAU) * inside[None, :])
    centres = (np.arange(basis_n) + 0.5) / basis_n
    offset = (times[:, None, :] - centres[None, :, None]) * basis_n
    basis = np.exp(-0.5 * offset * offset)
    gram = np.einsum("agx,ahx->gh", basis, basis) + RIDGE * np.eye(basis_n)
    table = np.linalg.solve(gram[None], basis)
    high = table.astype(ml_dtypes.bfloat16)
    lower = (table - high.astype(np.float64)).astype(ml_dtypes.bfloat16)
    return high, lower


LANES_OUT = 256


def head_of_lane(width):
    return lax.broadcasted_iota(jnp.int32, (1, width), 1) // DH


def head_masks(width):
    lane_head = head_of_lane(width)
    return [(lane_head == head).astype(jnp.float32).astype(jnp.bfloat16) for head in range(width // DH)]


def pick_heads(per_head, lane_head):
    chosen = per_head[0]
    for head in range(1, len(per_head)):
        chosen = jnp.where(lane_head == head, per_head[head], chosen)
    return chosen


def dot_rows(left, right):
    return lax.dot_general(left, right, (((1,), (1,)), ((), ())), preferred_element_type=jnp.float32)


def dot_plain(left, right):
    return lax.dot_general(left, right, (((1,), (0,)), ((), ())), preferred_element_type=jnp.float32)


def thirds(value):
    first = value.astype(jnp.bfloat16)
    rest = value - first.astype(jnp.float32)
    second = rest.astype(jnp.bfloat16)
    third = (rest - second.astype(jnp.float32)).astype(jnp.bfloat16)
    return first, second, third


def with_stats(block, stats):
    rows, width = block.shape
    spare = LANES_OUT - width
    lane = lax.broadcasted_iota(jnp.int32, (1, spare), 1)
    tail = jnp.zeros((rows, spare), jnp.float32)
    for index, column in enumerate(stats):
        for part, value in enumerate(thirds(column)):
            tail = jnp.where(lane == 3 * index + part, value.astype(jnp.float32), tail)
    return jnp.concatenate([block, tail.astype(jnp.bfloat16)], axis=1)


def stat_column(extended, width, index):
    lane = lax.broadcasted_iota(jnp.int32, (1, LANES_OUT), 1)
    start = width + 3 * index
    mine = (lane >= start) & (lane < start + 3)
    return jnp.sum(jnp.where(mine, extended.astype(jnp.float32), 0.0), axis=1, keepdims=True)


def stat_rows(extended, width, count):
    row = lax.broadcasted_iota(jnp.int32, (count, LANES_OUT), 0)
    lane = lax.broadcasted_iota(jnp.int32, (count, LANES_OUT), 1)
    start = width + 3 * row
    chooser = ((lane >= start) & (lane < start + 3)).astype(jnp.float32).astype(jnp.bfloat16)
    return dot_rows(chooser, extended)


def greet(levels, whole_tp=False):
    seq, tp = lax.axis_index("seq"), lax.axis_index("tp")
    level, side = seq // 2, seq % 2
    barrier = pltpu.get_barrier_semaphore()
    pl.semaphore_signal(barrier, inc=1, device_id=(2 * level + 1 - side, tp), device_id_type=MESH_ID)

    def one(step, unused):
        other = lax.rem(level + step, levels)
        pl.semaphore_signal(barrier, inc=1, device_id=(2 * other + side, tp), device_id_type=MESH_ID)
        return unused

    lax.fori_loop(1, levels, one, 0)
    if not whole_tp:
        return barrier, levels
    greet_tp()
    return barrier, levels + 2


def forward_kernel(
    levels,
    tok_ref,
    norm_ref,
    weight_ref,
    bias_ref,
    doc_col_ref,
    doc_row_ref,
    key_mask_ref,
    normed_ref,
    query_out_ref,
    kv_out_ref,
    out_ref,
    lse_ref,
    pair_ref,
    top_ref,
    total_ref,
    acc_ref,
    part_ref,
    part_in_ref,
    kv_send,
    kv_recv,
    q_send,
    q_recv,
    pair_sem,
    part_sem,
):
    seq, tp = lax.axis_index("seq"), lax.axis_index("tp")
    level, side = seq // 2, seq % 2
    rows = tok_ref.shape[0]
    width = pair_ref.shape[2]
    heads = width // DH
    partner = (2 * level + 1 - side, tp)
    lane_head = head_of_lane(width)
    head_mask = head_masks(width)
    barrier, greetings = greet(levels)

    chunk = rows // 2

    def project(index, unused):
        here = pl.ds(pl.multiple_of(index * chunk, chunk), chunk)
        x = tok_ref[here, :].astype(jnp.float32)
        centred = x - jnp.mean(x, axis=1, keepdims=True)
        variance = jnp.mean(centred * centred, axis=1, keepdims=True)
        a = centred * lax.rsqrt(variance + EPS) * norm_ref[0:1, :] + norm_ref[1:2, :]
        a = a.astype(jnp.bfloat16)
        normed_ref[here, :] = a
        mixed = (dot_plain(a, weight_ref[...]) + bias_ref[0:1, :]).astype(jnp.bfloat16)
        query = mixed[:, :width] * jnp.bfloat16(DH**-0.5)
        pair_ref[0, here, :] = query
        query_out_ref[level, here, :] = query
        kv_out_ref[level, here, :] = mixed[:, width:]
        return unused

    lax.fori_loop(0, rows // chunk, project, 0)
    kv_out_ref[level, rows:, :] = key_mask_ref[...]

    pl.semaphore_wait(barrier, greetings)
    pair_copy = pltpu.make_async_remote_copy(
        pair_ref.at[0], pair_ref.at[1], pair_sem.at[0], pair_sem.at[1], device_id=partner, device_id_type=MESH_ID
    )
    pair_copy.start()

    def kv_copy(from_level):
        return pltpu.make_async_remote_copy(
            kv_out_ref.at[from_level],
            kv_out_ref.at[from_level],
            kv_send.at[from_level],
            kv_recv.at[from_level],
            device_id=(lax.rem(2 * level + 2, 2 * levels) + side, tp),
            device_id_type=MESH_ID,
        )

    def query_copy(from_level, to_level):
        return pltpu.make_async_remote_copy(
            query_out_ref.at[from_level],
            query_out_ref.at[from_level],
            q_send.at[to_level],
            q_recv.at[from_level],
            device_id=(2 * to_level + side, tp),
            device_id_type=MESH_ID,
        )

    @pl.when(level < levels - 1)
    def _():
        kv_copy(level).start()

    def send_down(step, unused):
        query_copy(level, level - step).start()
        return unused

    lax.fori_loop(1, level + 1, send_down, 0)

    top_ref[...] = jnp.full(top_ref.shape, NEGATIVE, jnp.float32)
    total_ref[...] = jnp.zeros(total_ref.shape, jnp.float32)
    acc_ref[...] = jnp.zeros(acc_ref.shape, jnp.float32)

    doc_first = doc_row_ref[0:1, 0:1]
    def reach_of(here):
        docs = doc_col_ref[here, :]
        last = (level == levels - 1) & (side == 1)
        return jnp.where(last & (docs != doc_first), NEGATIVE, 0.0)

    def fold(slot, from_level, mask_kind):
        mask_rows = kv_out_ref[from_level, rows:, :].astype(jnp.float32)
        key_mask = jnp.concatenate([mask_rows[0:1, : rows // 2], mask_rows[1:2, : rows // 2]], axis=1)

        def part(index, unused):
            here = pl.ds(pl.multiple_of(index * chunk, chunk), chunk)
            query = pair_ref[slot, here, :]
            keys = kv_out_ref[from_level, :rows, :width]
            vals = kv_out_ref[from_level, :rows, width:]
            if mask_kind == "own":
                q_pos = index * chunk + lax.broadcasted_iota(jnp.int32, (chunk, rows), 0)
                k_pos = lax.broadcasted_iota(jnp.int32, (chunk, rows), 1)
                visible = (q_pos >= k_pos) & (doc_col_ref[here, :] == doc_row_ref[0:1, :])
            products, scales = [], []
            for head in range(heads):
                scores = dot_rows(query * head_mask[head], keys)
                old_top = top_ref[slot, head, here, :]
                if mask_kind == "own":
                    scores = jnp.where(visible, scores, NEGATIVE)
                    reach = 0.0
                else:
                    scores = scores + key_mask
                    reach = jnp.where(slot == 0, reach_of(here), 0.0)
                new_top = jnp.maximum(old_top, jnp.max(scores, axis=1, keepdims=True) + reach)
                weights = jnp.exp(scores - (new_top - reach))
                scale = jnp.exp(old_top - new_top)
                top_ref[slot, head, here, :] = new_top
                total_ref[slot, head, here, :] = total_ref[slot, head, here, :] * scale + jnp.sum(
                    weights, axis=1, keepdims=True
                )
                products.append(dot_plain(weights.astype(jnp.bfloat16), vals))
                scales.append(scale)
            acc_ref[slot, here, :] = acc_ref[slot, here, :] * pick_heads(scales, lane_head) + pick_heads(
                products, lane_head
            )
            return unused

        lax.fori_loop(0, rows // chunk, part, 0)

    fold(0, level, "own")
    pair_copy.wait()

    @pl.when(side == 0)
    def _():
        fold(1, level, "off")

    def arrived(step, unused):
        from_level = level - step
        kv_copy(from_level).wait_recv()

        @pl.when(level < levels - 1)
        def _():
            kv_copy(from_level).start()

        def both(slot, inner):
            fold(slot, from_level, "off")
            return inner

        lax.fori_loop(0, 2, both, 0)
        return unused

    lax.fori_loop(1, level + 1, arrived, 0)

    def finish(index, unused):
        here = pl.ds(pl.multiple_of(index * chunk, chunk), chunk)
        totals = [total_ref[1, head, here, :] for head in range(heads)]
        tops = [top_ref[1, head, here, :] for head in range(heads)]
        some = [value > 0.0 for value in totals]
        inverse = [jnp.where(ok, 1.0 / jnp.where(ok, value, 1.0), 0.0) for ok, value in zip(some, totals)]
        logs = [
            jnp.where(ok, top + jnp.log(jnp.where(ok, value, 1.0)), NEGATIVE)
            for ok, top, value in zip(some, tops, totals)
        ]
        share = (acc_ref[1, here, :] * pick_heads(inverse, lane_head)).astype(jnp.bfloat16)
        part_ref[here, :] = with_stats(share, logs)
        return unused

    lax.fori_loop(0, rows // chunk, finish, 0)
    part_copy = pltpu.make_async_remote_copy(
        part_ref, part_in_ref, part_sem.at[0], part_sem.at[1], device_id=partner, device_id_type=MESH_ID
    )
    part_copy.start()
    part_copy.wait()

    def merge(index, unused):
        here = pl.ds(pl.multiple_of(index * chunk, chunk), chunk)
        reach = reach_of(here)
        received = part_in_ref[here, :]
        mine, theirs, columns = [], [], []
        for head in range(heads):
            total = total_ref[0, head, here, :]
            own_log = top_ref[0, head, here, :] + jnp.log(total)
            other_log = stat_column(received, width, head) + reach
            high = jnp.maximum(own_log, other_log)
            both_log = high + jnp.log(jnp.exp(own_log - high) + jnp.exp(other_log - high))
            mine.append(jnp.exp(own_log - both_log) / total)
            theirs.append(jnp.exp(other_log - both_log))
            columns.append(both_log)
        out_ref[here, :] = acc_ref[0, here, :] * pick_heads(mine, lane_head) + received[
            :, :width
        ].astype(jnp.float32) * pick_heads(theirs, lane_head)
        lane = lax.broadcasted_iota(jnp.int32, (1, 8), 1)
        packed = jnp.zeros((chunk, 8), jnp.float32)
        for head in range(heads):
            packed = jnp.where(lane == head, columns[head], packed)
        lse_ref[here, :] = packed
        return unused

    lax.fori_loop(0, rows // chunk, merge, 0)

    def sent_down(step, unused):
        query_copy(level, level - step).wait_send()
        return unused

    lax.fori_loop(1, level + 1, sent_down, 0)

    def from_above(step, unused):
        query_copy(level + step, level).wait_recv()
        return unused

    lax.fori_loop(1, levels - level, from_above, 0)

    @pl.when(level < levels - 1)
    def _():
        def sent_up(from_level, unused):
            kv_copy(from_level).wait_send()
            return unused

        lax.fori_loop(0, level + 1, sent_up, 0)


def attention_forward(levels, tokens, norm, weight, bias, doc_ids, key_mask):
    rows = tokens.shape[0]
    width = weight.shape[1] // 3
    heads = width // DH
    vmem = pl.BlockSpec(memory_space=pltpu.VMEM)
    dma = pltpu.SemaphoreType.DMA
    return pl.pallas_call(
        functools.partial(forward_kernel, levels),
        out_shape=(
            jax.ShapeDtypeStruct((rows, D), jnp.bfloat16),
            jax.ShapeDtypeStruct((levels, rows, width), jnp.bfloat16),
            jax.ShapeDtypeStruct((levels, rows + 16, 2 * width), jnp.bfloat16),
            jax.ShapeDtypeStruct((rows, width), jnp.float32),
            jax.ShapeDtypeStruct((rows, 8), jnp.float32),
        ),
        in_specs=[vmem] * 7,
        out_specs=(vmem,) * 5,
        scratch_shapes=[
            pltpu.VMEM((2, rows, width), jnp.bfloat16),
            pltpu.VMEM((2, heads, rows, 1), jnp.float32),
            pltpu.VMEM((2, heads, rows, 1), jnp.float32),
            pltpu.VMEM((2, rows, width), jnp.float32),
            pltpu.VMEM((rows, LANES_OUT), jnp.bfloat16),
            pltpu.VMEM((rows, LANES_OUT), jnp.bfloat16),
            dma((levels,)),
            dma((levels,)),
            dma((levels,)),
            dma((levels,)),
            dma((2,)),
            dma((2,)),
        ],
        name="attention_forward",
        compiler_params=pltpu.CompilerParams(
            collective_id=1, has_side_effects=True, vmem_limit_bytes=VMEM_LIMIT
        ),
    )(tokens, norm, weight, bias, doc_ids[:, None], doc_ids[None, :], key_mask)


def backward_kernel(
    levels,
    grad_ref,
    attended_ref,
    lse_ref,
    query_col_ref,
    query_oth_ref,
    kv_col_ref,
    kv_oth_ref,
    doc_col_ref,
    doc_row_ref,
    proj_blocks_ref,
    fc_blocks_ref,
    out_blocks_ref,
    base_ref,
    own_two_ref,
    other_two_ref,
    dq_ref,
    dk_ref,
    dv_ref,
    proj_share_ref,
    fc_share_ref,
    out_share_ref,
    output_ref,
    own_ref,
    grad_col_ref,
    grad_oth_ref,
    stat_ref,
    col_send,
    col_recv,
    oth_send,
    oth_recv,
    *rest,
):
    scatters = []
    for blocks_ref in (proj_blocks_ref, fc_blocks_ref, out_blocks_ref):
        scatters.append(Scatter(levels, blocks_ref, *rest[:3], rest[3:7]))
        rest = rest[7:]
    late = LateOutput(base_ref, own_two_ref, other_two_ref, output_ref, rest[: LateOutput.COUNT])
    staging = rest[LateOutput.COUNT :]
    seq, tp = lax.axis_index("seq"), lax.axis_index("tp")
    level, side = seq // 2, seq % 2
    rows, width = grad_ref.shape
    heads = width // DH
    partner = (2 * level + 1 - side, tp)
    lane_head = head_of_lane(width)
    head_mask = head_masks(width)
    chunk = rows // 2
    barrier, greetings = greet(levels, True)
    doc_first = doc_row_ref[0:1, 0:1]
    last = (level == levels - 1) & (side == 1)

    def prepare(index, unused):
        here = pl.ds(pl.multiple_of(index * chunk, chunk), chunk)
        grad = grad_ref[here, :]
        product = grad.astype(jnp.float32) * attended_ref[here, :]
        far = jnp.where(last & (doc_col_ref[here, :] != doc_first), -NEGATIVE, 0.0)
        lses = [lse_ref[here, head : head + 1] for head in range(heads)]
        deltas = [
            jnp.sum(jnp.where(lane_head == head, product, 0.0), axis=1, keepdims=True)
            for head in range(heads)
        ]
        own_ref[here, :] = with_stats(grad, lses + deltas)
        grad_col_ref[level, here, :] = with_stats(grad, [lse + far for lse in lses] + deltas)
        for head in range(heads):
            stat_ref[head, here, :] = lses[head]
            stat_ref[heads + head, here, :] = lses[head] + far
            stat_ref[2 * heads + head, here, :] = deltas[head]
        return unused

    lax.fori_loop(0, rows // chunk, prepare, 0)
    pl.semaphore_wait(barrier, greetings)

    def col_copy(from_level, to_level):
        return pltpu.make_async_remote_copy(
            grad_col_ref.at[from_level],
            grad_col_ref.at[from_level],
            col_send.at[to_level],
            col_recv.at[from_level],
            device_id=(2 * to_level + side, tp),
            device_id_type=MESH_ID,
        )

    def oth_copy(from_level):
        return pltpu.make_async_remote_copy(
            grad_col_ref.at[from_level],
            grad_oth_ref.at[from_level],
            oth_send.at[from_level],
            oth_recv.at[from_level],
            device_id=partner,
            device_id_type=MESH_ID,
        )

    @pl.when(side == 1)
    def _():
        oth_copy(level).start()

    def send_down(step, unused):
        col_copy(level, level - step).start()
        return unused

    lax.fori_loop(1, level + 1, send_down, 0)
    late.start()
    for scatter in scatters:
        scatter.start()

    dq_ref[...] = jnp.zeros(dq_ref.shape, jnp.float32)
    dk_ref[...] = jnp.zeros(dk_ref.shape, jnp.float32)
    dv_ref[...] = jnp.zeros(dv_ref.shape, jnp.float32)

    def block_of(kv_ref, from_level):
        if not staging:
            return kv_ref.at[from_level]
        block_ref, block_sem = staging
        copy = pltpu.make_async_copy(kv_ref.at[from_level], block_ref, block_sem)
        copy.start()
        copy.wait()
        return block_ref

    def query_fold(kv_ref, from_level, own):
        block_ref = block_of(kv_ref, from_level)
        if own:
            key_mask = None
        else:
            mask_rows = block_ref[rows:, :].astype(jnp.float32)
            key_mask = jnp.concatenate(
                [mask_rows[0:1, : rows // 2], mask_rows[1:2, : rows // 2]], axis=1
            )

        def part(index, unused):
            here = pl.ds(pl.multiple_of(index * chunk, chunk), chunk)
            query = query_col_ref[level, here, :]
            grad = grad_ref[here, :]
            keys = block_ref[:rows, :width]
            vals = block_ref[:rows, width:]
            if own:
                q_pos = index * chunk + lax.broadcasted_iota(jnp.int32, (chunk, rows), 0)
                k_pos = lax.broadcasted_iota(jnp.int32, (chunk, rows), 1)
                visible = (q_pos >= k_pos) & (doc_col_ref[here, :] == doc_row_ref[0:1, :])
            products = []
            for head in range(heads):
                scores = dot_rows(query * head_mask[head], keys)
                if own:
                    scores = jnp.where(visible, scores, NEGATIVE)
                    lse = stat_ref[head, here, :]
                else:
                    scores = scores + key_mask
                    lse = stat_ref[heads + head, here, :]
                probs = jnp.exp(scores - lse)
                pull = dot_rows(grad * head_mask[head], vals) - stat_ref[2 * heads + head, here, :]
                products.append(dot_plain((probs * pull).astype(jnp.bfloat16), keys))
            dq_ref[here, :] = dq_ref[here, :] + pick_heads(products, lane_head)
            return unused

        lax.fori_loop(0, rows // chunk, part, 0)

    query_fold(kv_col_ref, level, True)

    @pl.when(side == 1)
    def _():
        query_fold(kv_oth_ref, level, False)

    def earlier(from_level, unused):
        query_fold(kv_col_ref, from_level, False)
        query_fold(kv_oth_ref, from_level, False)
        return unused

    lax.fori_loop(0, level, earlier, 0)
    late.middle()
    dq_ref[...] = dq_ref[...] * (DH**-0.5)

    own_block_ref = block_of(kv_col_ref, level)

    def key_fold(query_ref, grads_ref, from_level, own):
        def part(index, unused):
            here = pl.ds(pl.multiple_of(index * chunk, chunk), chunk)
            keys = own_block_ref[here, :width]
            vals = own_block_ref[here, width:]
            if own:
                query = query_col_ref[level]
                extended = own_ref[...]
                k_pos = index * chunk + lax.broadcasted_iota(jnp.int32, (chunk, rows), 0)
                q_pos = lax.broadcasted_iota(jnp.int32, (chunk, rows), 1)
                visible = (q_pos >= k_pos) & (doc_col_ref[here, :] == doc_row_ref[0:1, :])
            else:
                query = query_ref[from_level]
                extended = grads_ref[from_level]
            grad = extended[:, :width]
            stats = stat_rows(extended, width, 8)
            key_parts, val_parts = [], []
            for head in range(heads):
                scores = dot_rows(keys * head_mask[head], query)
                if own:
                    scores = jnp.where(visible, scores, NEGATIVE)
                probs = jnp.exp(scores - stats[head : head + 1, :])
                val_parts.append(dot_plain(probs.astype(jnp.bfloat16), grad))
                pull = dot_rows(vals * head_mask[head], grad) - stats[heads + head : heads + head + 1, :]
                key_parts.append(dot_plain((probs * pull).astype(jnp.bfloat16), query))
            dk_ref[here, :] = dk_ref[here, :] + pick_heads(key_parts, lane_head)
            dv_ref[here, :] = dv_ref[here, :] + pick_heads(val_parts, lane_head)
            return unused

        lax.fori_loop(0, rows // chunk, part, 0)

    @pl.when(side == 0)
    def _():
        oth_copy(level).wait_recv()
        key_fold(query_oth_ref, grad_oth_ref, level, False)

    def later(step, unused):
        from_level = level + step
        col_copy(from_level, level).wait_recv()
        oth_copy(from_level).start()
        key_fold(query_col_ref, grad_col_ref, from_level, False)
        oth_copy(from_level).wait_recv()
        key_fold(query_oth_ref, grad_oth_ref, from_level, False)
        return unused

    lax.fori_loop(1, levels - level, later, 0)
    for scatter in scatters:
        scatter.middle()
    late.late()
    reaches = doc_col_ref[...] >= (seq + 1) * rows
    dk_ref[...] = jnp.where(reaches, dk_ref[...], 0.0)
    dv_ref[...] = jnp.where(reaches, dv_ref[...], 0.0)
    key_fold(None, None, level, True)
    late.finish()
    for scatter, share_ref in zip(scatters, (proj_share_ref, fc_share_ref, out_share_ref)):
        scatter.finish(share_ref)

    @pl.when(side == 1)
    def _():
        oth_copy(level).wait_send()

    def sent_down(step, unused):
        col_copy(level, level - step).wait_send()
        return unused

    lax.fori_loop(1, level + 1, sent_down, 0)

    def sent_on(step, unused):
        oth_copy(level + step).wait_send()
        return unused

    lax.fori_loop(1, levels - level, sent_on, 0)


def attention_backward(
    levels,
    grad,
    attended,
    lse,
    query_col,
    query_oth,
    kv_col,
    kv_oth,
    doc_ids,
    blocks,
    base,
    own_two,
    other_two,
):
    rows, width = grad.shape
    heads = width // DH
    vmem = pl.BlockSpec(memory_space=pltpu.VMEM)
    dma = pltpu.SemaphoreType.DMA
    full = jax.ShapeDtypeStruct((rows, width), jnp.float32)
    staged = levels > 8
    far = pl.BlockSpec(memory_space=pl.ANY) if staged else vmem
    staging = [pltpu.VMEM(kv_col.shape[1:], kv_col.dtype), dma(())] if staged else []
    return pl.pallas_call(
        functools.partial(backward_kernel, levels),
        out_shape=(
            full,
            full,
            full,
            *(jax.ShapeDtypeStruct(block.shape[1:], jnp.float32) for block in blocks),
            jax.ShapeDtypeStruct((rows, D), jnp.bfloat16),
        ),
        in_specs=[vmem] * 5 + [far] * 2 + [vmem] * 8,
        out_specs=(vmem,) * 7,
        scratch_shapes=[
            pltpu.VMEM((rows, LANES_OUT), jnp.bfloat16),
            pltpu.VMEM((levels, rows, LANES_OUT), jnp.bfloat16),
            pltpu.VMEM((levels, rows, LANES_OUT), jnp.bfloat16),
            pltpu.VMEM((3 * heads, rows, 1), jnp.float32),
            dma((levels,)),
            dma((levels,)),
            dma((levels,)),
            dma((levels,)),
            *(item for block in blocks for item in Scatter.scratch(levels, *block.shape[1:])),
            *LateOutput.scratch(rows // 2, D),
            *staging,
        ],
        name="attention_backward",
        compiler_params=pltpu.CompilerParams(
            collective_id=2, has_side_effects=True, vmem_limit_bytes=VMEM_LIMIT
        ),
    )(
        grad,
        attended,
        lse,
        query_col,
        query_oth,
        kv_col,
        kv_oth,
        doc_ids[:, None],
        doc_ids[None, :],
        *blocks,
        base,
        own_two,
        other_two,
    )


def column_copy(block_ref, from_level, landing_ref, send_sem, recv_sem, to_level):
    seq, tp = lax.axis_index("seq"), lax.axis_index("tp")
    return pltpu.make_async_remote_copy(
        block_ref,
        landing_ref.at[from_level],
        send_sem.at[to_level],
        recv_sem.at[from_level],
        device_id=(2 * to_level + seq % 2, tp),
        device_id_type=MESH_ID,
    )


class Scatter:
    def __init__(self, levels, blocks, plane_in, plane_sum, column_in, sems):
        self.levels, self.blocks = levels, blocks
        self.plane_in, self.plane_sum, self.column_in = plane_in, plane_sum, column_in
        self.plane_send, self.plane_recv, self.column_send, self.column_recv = sems
        seq, tp = lax.axis_index("seq"), lax.axis_index("tp")
        self.level, self.side, self.tp = seq // 2, seq % 2, tp

    def plane_copy(self, to_level):
        return pltpu.make_async_remote_copy(
            self.blocks.at[2 * to_level + 1 - self.side],
            self.plane_in.at[to_level],
            self.plane_send.at[to_level],
            self.plane_recv.at[to_level],
            device_id=(2 * self.level + 1 - self.side, self.tp),
            device_id_type=MESH_ID,
        )

    def swap_copy(self, from_level, to_level):
        return column_copy(
            self.plane_sum.at[to_level], from_level, self.column_in, self.column_send, self.column_recv, to_level
        )

    def loop(self, first, body):
        def one(step, unused):
            body(lax.rem(self.level + step, self.levels))
            return unused

        lax.fori_loop(first, self.levels, one, 0)

    def start(self):
        self.loop(0, lambda other: self.plane_copy(other).start())

    def middle(self):
        def one(other):
            self.plane_copy(other).wait_recv()
            total = self.blocks[2 * other + self.side].astype(jnp.float32) + self.plane_in[other].astype(
                jnp.float32
            )
            self.plane_sum[other] = total.astype(jnp.bfloat16)
            self.swap_copy(self.level, other).start()

        self.loop(1, one)

    def finish(self, out_ref):
        self.plane_copy(self.level).wait_recv()
        out_ref[...] = self.blocks[2 * self.level + self.side].astype(jnp.float32) + self.plane_in[
            self.level
        ].astype(jnp.float32)

        def one(other):
            self.swap_copy(other, self.level).wait_recv()
            out_ref[...] += self.column_in[other].astype(jnp.float32)

        self.loop(1, one)
        self.loop(0, lambda other: self.plane_copy(other).wait_send())
        self.loop(1, lambda other: self.swap_copy(self.level, other).wait_send())

    @staticmethod
    def scratch(levels, rows, width):
        buffer = pltpu.VMEM((levels, rows, width), jnp.bfloat16)
        return [buffer] * 3 + [pltpu.SemaphoreType.DMA((levels,))] * 4


class SmallSum:
    def __init__(self, levels, small, plane_in, column_in, sems):
        self.levels, self.small, self.plane_in, self.column_in = levels, small, plane_in, column_in
        self.plane_sem, self.column_send, self.column_recv = sems
        seq, tp = lax.axis_index("seq"), lax.axis_index("tp")
        self.level, self.side, self.tp = seq // 2, seq % 2, tp

    def plane_copy(self):
        return pltpu.make_async_remote_copy(
            self.small,
            self.plane_in,
            self.plane_sem.at[0],
            self.plane_sem.at[1],
            device_id=(2 * self.level + 1 - self.side, self.tp),
            device_id_type=MESH_ID,
        )

    def swap_copy(self, from_level, to_level):
        return column_copy(
            self.column_in.at[from_level], from_level, self.column_in, self.column_send, self.column_recv, to_level
        )

    def loop(self, body):
        def one(step, unused):
            body(lax.rem(self.level + step, self.levels))
            return unused

        lax.fori_loop(1, self.levels, one, 0)

    def start(self):
        self.plane_copy().start()

    def middle(self):
        self.plane_copy().wait()
        self.column_in[self.level] = self.small[...] + self.plane_in[...]
        self.loop(lambda other: self.swap_copy(self.level, other).start())

    def finish(self, out_ref):
        self.loop(lambda other: self.swap_copy(other, self.level).wait_recv())
        self.loop(lambda other: self.swap_copy(self.level, other).wait_send())
        out_ref[...] = self.column_in[0]

        def one(other, unused):
            out_ref[...] += self.column_in[other]
            return unused

        lax.fori_loop(1, self.levels, one, 0)

    @staticmethod
    def scratch(levels, shape):
        dma = pltpu.SemaphoreType.DMA
        return [
            pltpu.VMEM(shape, jnp.float32),
            pltpu.VMEM((levels,) + shape, jnp.float32),
            dma((2,)),
            dma((levels,)),
            dma((levels,)),
        ]


def tp_partner(kind):
    seq, tp = lax.axis_index("seq"), lax.axis_index("tp")
    if kind == "core":
        return (seq, tp + 1 - 2 * (tp % 2))
    return (seq, lax.rem(tp + 2, 4))


def greet_tp():
    barrier = pltpu.get_barrier_semaphore()
    for kind in ("core", "chip"):
        pl.semaphore_signal(barrier, inc=1, device_id=tp_partner(kind), device_id_type=MESH_ID)
    return barrier, 2


def swap_with(kind, source, target, sems, index):
    send, recv = sems
    return pltpu.make_async_remote_copy(
        source, target, send.at[index], recv.at[index], device_id=tp_partner(kind), device_id_type=MESH_ID
    )


class TpSum:
    def __init__(self, core_out, core_in, chip_out, chip_in, sems):
        self.core_out, self.core_in, self.chip_out, self.chip_in = core_out, core_in, chip_out, chip_in
        self.core_sems, self.chip_sems = sems[:2], sems[2:]

    def core_copy(self, part):
        return swap_with("core", self.core_out.at[part], self.core_in.at[part], self.core_sems, part)

    def chip_copy(self, part):
        return swap_with("chip", self.chip_out.at[part], self.chip_in.at[part], self.chip_sems, part)

    def start(self, part, for_other_core):
        self.core_out[part] = for_other_core.astype(jnp.bfloat16)
        self.core_copy(part).start()

    def middle(self, part, own):
        self.core_copy(part).wait()
        self.chip_out[part] = (own + self.core_in[part].astype(jnp.float32)).astype(jnp.bfloat16)
        self.chip_copy(part).start()

    def result(self, part):
        self.chip_copy(part).wait()
        return self.chip_out[part].astype(jnp.float32) + self.chip_in[part].astype(jnp.float32)

    @staticmethod
    def scratch(parts, rows, width):
        buffer = pltpu.VMEM((parts, rows, width), jnp.bfloat16)
        return [buffer] * 4 + [pltpu.SemaphoreType.DMA((parts,))] * 4

    COUNT = 8


class RowShare:
    def __init__(self, whole, rows, sems):
        self.whole, self.rows, self.sems = whole, rows, sems

    def copy(self, part, start):
        here = self.whole.at[pl.ds(pl.multiple_of(start, self.rows), self.rows), :]
        return swap_with("core", here, here, self.sems, part)


def normalize(v):
    centred = v - jnp.mean(v, axis=1, keepdims=True)
    scale = lax.rsqrt(jnp.mean(centred * centred, axis=1, keepdims=True) + EPS)
    return centred * scale, scale


def norm_back(grad, nhat, scale, gain):
    inner = grad * gain
    return (
        inner
        - jnp.mean(inner, axis=1, keepdims=True)
        - nhat * jnp.mean(inner * nhat, axis=1, keepdims=True)
    ) * scale


def gelu_and_slope(f):
    root = (2.0 / np.pi) ** 0.5
    square = f * f
    bend = jnp.tanh(root * f * (1.0 + 0.044715 * square))
    half = 0.5 * (1.0 + bend)
    slope = half + 0.5 * f * (1.0 - bend * bend) * (root * (1.0 + 3.0 * 0.044715 * square))
    return f * half, slope


def dot_columns(left, right):
    return lax.dot_general(left, right, (((0,), (0,)), ((), ())), preferred_element_type=jnp.float32)


def column_sum(v):
    return jnp.sum(v, axis=0, keepdims=True)


FEED_PARTS = 2


def feed_kernel(
    heads_ref,
    tok_ref,
    cot_ref,
    out_w_ref,
    fc_w_ref,
    proj_w_ref,
    vec_ref,
    proj_grad_ref,
    fc_grad_ref,
    out_grad_ref,
    head_grad_ref,
    mid_grad_ref,
    base_ref,
    own_two_ref,
    other_two_ref,
    sums_ref,
    c_ref,
    e1_ref,
    u_ref,
    ef_ref,
    pull_ref,
    h1_ref,
    own_ref,
    fold_in_ref,
    *sems,
):
    parts = FEED_PARTS
    rows = tok_ref.shape[0]
    half = rows // 2
    size = half // parts
    tp = lax.axis_index("tp")
    core = tp % 2
    first = TpSum(*sems[:4], sems[4 : TpSum.COUNT])
    second = TpSum(*sems[TpSum.COUNT : TpSum.COUNT + 4], sems[TpSum.COUNT + 4 : 2 * TpSum.COUNT])
    sems = sems[2 * TpSum.COUNT :]
    c_share = RowShare(c_ref, size, sems[0:2])
    e_share = RowShare(e1_ref, size, sems[2:4])
    fold_sems = sems[4:6]
    barrier, greetings = greet_tp()
    gain, offset, out_b, fc_b, proj_b = (vec_ref[i : i + 1, :] for i in range(5))

    def span(start, count=size):
        return pl.ds(pl.multiple_of(start, size), count)

    def mine(part):
        return core * half + part * size

    def theirs(part):
        return (1 - core) * half + part * size

    pl.semaphore_wait(barrier, greetings)
    for part in range(parts):
        first.start(part, dot_plain(heads_ref[span(theirs(part)), :], out_w_ref[...]))
        own_ref[span(part * size), :] = dot_plain(heads_ref[span(mine(part)), :], out_w_ref[...])
    for part in range(parts):
        first.middle(part, own_ref[span(part * size), :])

    def early(index, unused):
        here = span(index * size)
        pull_ref[here, :] = dot_rows(cot_ref[here, :], proj_w_ref[...])
        return unused

    lax.fori_loop(0, rows // size, early, 0)

    def feed(start):
        here = span(start)
        f = dot_plain(c_ref[here, :], fc_w_ref[...]) + fc_b
        u, slope = gelu_and_slope(f)
        u_ref[here, :] = u.astype(jnp.bfloat16)
        ef = (pull_ref[here, :] * slope).astype(jnp.bfloat16)
        ef_ref[here, :] = ef
        return dot_rows(ef, fc_w_ref[...])

    for part in range(parts):
        total = first.result(part) + out_b
        h1 = tok_ref[span(mine(part)), :].astype(jnp.float32) + total
        h1_ref[span(part * size), :] = h1
        nhat, scale = normalize(h1)
        c_ref[span(mine(part)), :] = (nhat * gain + offset).astype(jnp.bfloat16)
        c_share.copy(part, mine(part)).start()
        own_ref[span(part * size), :] = feed(mine(part))
        c_share.copy(part, theirs(part)).wait_recv()
        second.start(part, feed(theirs(part)))
        other_two_ref[span(part * size), :] = dot_plain(u_ref[span(theirs(part)), :], proj_w_ref[...]).astype(
            jnp.bfloat16
        )
        own_two_ref[span(part * size), :] = dot_plain(u_ref[span(mine(part)), :], proj_w_ref[...])
        second.middle(part, own_ref[span(part * size), :])

    base_ref[...] = h1_ref[...] + proj_b
    block = 256

    def weights(index, unused):
        here = pl.ds(pl.multiple_of(index * block, block), block)
        proj_grad_ref[here, :] = dot_columns(cot_ref[:, here], u_ref[...]).astype(jnp.bfloat16)
        fc_grad_ref[here, :] = dot_columns(c_ref[:, here], ef_ref[...]).astype(jnp.bfloat16)
        return unused

    lax.fori_loop(0, D // block, weights, 0)
    fc_sum = column_sum(ef_ref[...].astype(jnp.float32))

    gain_sum = jnp.zeros((1, D), jnp.float32)
    offset_sum = jnp.zeros((1, D), jnp.float32)
    out_sum = jnp.zeros((1, D), jnp.float32)
    for part in range(parts):
        grad = second.result(part)
        nhat, scale = normalize(h1_ref[span(part * size), :])
        gain_sum = gain_sum + column_sum(grad * nhat)
        offset_sum = offset_sum + column_sum(grad)
        mid = cot_ref[span(mine(part)), :].astype(jnp.float32) + norm_back(grad, nhat, scale, gain)
        mid_grad_ref[span(part * size), :] = mid
        e1 = mid.astype(jnp.bfloat16)
        out_sum = out_sum + column_sum(e1.astype(jnp.float32))
        e1_ref[span(mine(part)), :] = e1
        e_share.copy(part, mine(part)).start()
        head_grad_ref[span(mine(part)), :] = dot_rows(e1, out_w_ref[...]).astype(jnp.bfloat16)
    row = lax.broadcasted_iota(jnp.int32, (8, 1), 0)
    sums_ref[...] = jnp.where(row == 0, gain_sum, jnp.where(row == 1, offset_sum, out_sum))
    fold_copy = swap_with("core", sums_ref, fold_in_ref, fold_sems, 0)
    fold_copy.start()
    for part in range(parts):
        e_share.copy(part, theirs(part)).wait_recv()
        head_grad_ref[span(theirs(part)), :] = dot_rows(e1_ref[span(theirs(part)), :], out_w_ref[...]).astype(
            jnp.bfloat16
        )

    def out_weights(index, unused):
        here = pl.ds(pl.multiple_of(index * block, block), block)
        out_grad_ref[here, :] = dot_columns(e1_ref[:, here], heads_ref[...]).astype(jnp.bfloat16)
        return unused

    lax.fori_loop(0, D // block, out_weights, 0)
    fold_copy.wait()
    sums_ref[...] = jnp.where(row == 3, fc_sum, sums_ref[...] + fold_in_ref[...])
    for part in range(parts):
        c_share.copy(part, mine(part)).wait_send()
        e_share.copy(part, mine(part)).wait_send()


def feed_forward(heads, tokens, cotangent, out_w, fc_w, proj_w, vectors):
    rows, width = heads.shape
    half = rows // 2
    hidden = fc_w.shape[1]
    parts, size = FEED_PARTS, half // FEED_PARTS
    vmem = pl.BlockSpec(memory_space=pltpu.VMEM)
    dma = pltpu.SemaphoreType.DMA
    bf, fl = jnp.bfloat16, jnp.float32
    shape = jax.ShapeDtypeStruct
    return pl.pallas_call(
        feed_kernel,
        out_shape=(
            shape((D, hidden), bf),
            shape((D, hidden), bf),
            shape((D, width), bf),
            shape((rows, width), bf),
            shape((half, D), fl),
            shape((half, D), fl),
            shape((half, D), fl),
            shape((half, D), bf),
            shape((8, D), fl),
        ),
        in_specs=[vmem] * 7,
        out_specs=(vmem,) * 9,
        scratch_shapes=[
            pltpu.VMEM((rows, D), bf),
            pltpu.VMEM((rows, D), bf),
            pltpu.VMEM((rows, hidden), bf),
            pltpu.VMEM((rows, hidden), bf),
            pltpu.VMEM((rows, hidden), fl),
            pltpu.VMEM((half, D), fl),
            pltpu.VMEM((half, D), fl),
            pltpu.VMEM((8, D), fl),
            *TpSum.scratch(parts, size, D),
            *TpSum.scratch(parts, size, D),
            dma((parts,)),
            dma((parts,)),
            dma((parts,)),
            dma((parts,)),
            dma((1,)),
            dma((1,)),
        ],
        name="feed_forward",
        compiler_params=pltpu.CompilerParams(
            collective_id=4, has_side_effects=True, vmem_limit_bytes=VMEM_LIMIT
        ),
    )(heads, tokens, cotangent, out_w, fc_w, proj_w, vectors)


class LateOutput:
    def __init__(self, base, own, other, whole, sems):
        self.base, self.own, self.other, self.whole = base, own, other, whole
        self.half = own.shape[0]
        self.core_in, self.chip_out, self.chip_in = sems[:3]
        self.core_sems, self.chip_sems, self.share_sems = sems[3:5], sems[5:7], sems[7:9]
        self.share = RowShare(whole, self.half, self.share_sems)
        self.core = lax.axis_index("tp") % 2

    COUNT = 9

    def core_copy(self):
        return swap_with("core", self.other, self.core_in, self.core_sems, 0)

    def chip_copy(self):
        return swap_with("chip", self.chip_out, self.chip_in, self.chip_sems, 0)

    def start(self):
        self.core_copy().start()

    def middle(self):
        self.core_copy().wait()
        self.chip_out[...] = (self.own[...] + self.core_in[...].astype(jnp.float32)).astype(jnp.bfloat16)
        self.chip_copy().start()

    def late(self):
        self.chip_copy().wait()
        total = self.chip_out[...].astype(jnp.float32) + self.chip_in[...].astype(jnp.float32)
        here = pl.ds(pl.multiple_of(self.core * self.half, self.half), self.half)
        self.whole[here, :] = (self.base[...] + total).astype(jnp.bfloat16)
        self.share.copy(0, self.core * self.half).start()

    def finish(self):
        self.share.copy(0, (1 - self.core) * self.half).wait_recv()
        self.share.copy(0, self.core * self.half).wait_send()

    @staticmethod
    def scratch(half, width):
        buffer = pltpu.VMEM((half, width), jnp.bfloat16)
        return [buffer] * 3 + [pltpu.SemaphoreType.DMA((1,))] * 6


def finish_kernel(
    levels,
    grads_ref,
    weight_ref,
    tok_ref,
    mid_grad_ref,
    norm_ref,
    blocks_ref,
    small_in_ref,
    tokens_out_ref,
    share_ref,
    small_out_ref,
    own_ref,
    small_ref,
    fold_ref,
    fold_in_ref,
    *rest,
):
    parts = FEED_PARTS
    rows = tok_ref.shape[0]
    half = rows // 2
    size = half // parts
    core = lax.axis_index("tp") % 2
    total = TpSum(*rest[:4], rest[4 : TpSum.COUNT])
    rest = rest[TpSum.COUNT :]
    scatter = Scatter(levels, blocks_ref, *rest[:3], rest[3:7])
    rest = rest[7:]
    small = SmallSum(levels, small_ref, rest[0], rest[1], rest[2:5])
    rest = rest[5:]
    share = RowShare(tokens_out_ref, size, rest[0:2])
    fold_sems = rest[2:4]
    barrier, greetings = greet(levels, True)
    gain = norm_ref[0:1, :]

    def span(start, count=size):
        return pl.ds(pl.multiple_of(start, size), count)

    def mine(part):
        return core * half + part * size

    def theirs(part):
        return (1 - core) * half + part * size

    pl.semaphore_wait(barrier, greetings)
    scatter.start()
    for part in range(parts):
        total.start(part, dot_rows(grads_ref[span(theirs(part)), :], weight_ref[...]))
        own_ref[span(part * size), :] = dot_rows(grads_ref[span(mine(part)), :], weight_ref[...])
    for part in range(parts):
        total.middle(part, own_ref[span(part * size), :])
    scatter.middle()
    gain_sum = jnp.zeros((1, D), jnp.float32)
    offset_sum = jnp.zeros((1, D), jnp.float32)
    for part in range(parts):
        grad = total.result(part)
        nhat, scale = normalize(tok_ref[span(mine(part)), :].astype(jnp.float32))
        gain_sum = gain_sum + column_sum(grad * nhat)
        offset_sum = offset_sum + column_sum(grad)
        out = mid_grad_ref[span(part * size), :] + norm_back(grad, nhat, scale, gain)
        tokens_out_ref[span(mine(part)), :] = out.astype(jnp.bfloat16)
        share.copy(part, mine(part)).start()
    row = lax.broadcasted_iota(jnp.int32, (8, 1), 0)
    fold_ref[...] = jnp.where(row == 0, gain_sum, jnp.where(row == 1, offset_sum, 0.0))
    fold_copy = swap_with("core", fold_ref, fold_in_ref, fold_sems, 0)
    fold_copy.start()
    fold_copy.wait()
    small_ref[8:, :] = small_in_ref[8:, :]
    small_ref[:8, :] = small_in_ref[:8, :] + (fold_ref[...] + fold_in_ref[...])
    small.start()
    small.middle()
    scatter.finish(share_ref)
    small.finish(small_out_ref)
    for part in range(parts):
        share.copy(part, theirs(part)).wait_recv()
        share.copy(part, mine(part)).wait_send()


def finish_layer(levels, grads, weight, tokens, mid_grad, norm, blocks, small):
    rows = tokens.shape[0]
    half = rows // 2
    parts, size = FEED_PARTS, half // FEED_PARTS
    vmem = pl.BlockSpec(memory_space=pltpu.VMEM)
    dma = pltpu.SemaphoreType.DMA
    shape = jax.ShapeDtypeStruct
    return pl.pallas_call(
        functools.partial(finish_kernel, levels),
        out_shape=(
            shape((rows, D), jnp.bfloat16),
            shape(blocks.shape[1:], jnp.float32),
            shape(small.shape, jnp.float32),
        ),
        in_specs=[vmem] * 7,
        out_specs=(vmem,) * 3,
        scratch_shapes=[
            pltpu.VMEM((half, D), jnp.float32),
            pltpu.VMEM(small.shape, jnp.float32),
            pltpu.VMEM((8, D), jnp.float32),
            pltpu.VMEM((8, D), jnp.float32),
            *TpSum.scratch(parts, size, D),
            *Scatter.scratch(levels, *blocks.shape[1:]),
            *SmallSum.scratch(levels, small.shape),
            dma((parts,)),
            dma((parts,)),
            dma((1,)),
            dma((1,)),
        ],
        name="finish_layer",
        compiler_params=pltpu.CompilerParams(
            collective_id=3, has_side_effects=True, vmem_limit_bytes=VMEM_LIMIT
        ),
    )(grads, weight, tokens, mid_grad, norm, blocks, small)


def local(
    tokens,
    cotangent,
    past_states,
    doc_ids,
    cur_book,
    past_book,
    past_age,
    ln1_gain,
    ln1_bias,
    qkv_weight,
    qv_bias,
    out_weight,
    out_bias,
    ln2_gain,
    ln2_bias,
    fc_weight,
    fc_bias,
    proj_weight,
    proj_bias,
    mu_weight,
    sigma_weight,
):
    tok_rows = tokens.shape[0]
    heads_here = mu_weight.shape[0]
    head_cols = qkv_weight.shape[2]
    seg_here = cur_book.shape[0]
    seq_count = lax.axis_size("seq")
    seq_index = lax.axis_index("seq")
    scale_dh = DH ** (-0.5)
    head_shape = (tok_rows, heads_here, DH)
    quarter = D // lax.axis_size("tp")
    my_quarter = lax.dynamic_slice_in_dim(
        past_states, lax.axis_index("tp") * quarter, quarter, axis=1
    )
    all_states = lax.all_gather(my_quarter, "seq", axis=0)
    books_ages = lax.all_gather(jnp.stack([past_book, past_age]), "seq", axis=1, tiled=True)
    age_count = seq_count * seg_here // BOOKS
    high, lower = coefficient_tables(age_count, NB, SEG)
    chosen = (books_ages[0] == cur_book[0])[None, :] & (
        books_ages[1][None, :] == jnp.arange(age_count, dtype=jnp.int32)[:, None]
    )
    by_age = jnp.einsum(
        "as,std->atd",
        chosen.astype(jnp.bfloat16),
        all_states,
        preferred_element_type=jnp.float32,
    ).astype(jnp.bfloat16)
    coeff_part = jnp.einsum(
        "ant,atd->nd", jnp.asarray(high), by_age, preferred_element_type=jnp.float32
    ) + jnp.einsum("ant,atd->nd", jnp.asarray(lower), by_age, preferred_element_type=jnp.float32)
    coeffs = lax.all_gather(coeff_part.astype(jnp.bfloat16), "tp", axis=1, tiled=True)
    mem_keys = (
        jnp.dot(coeffs, qkv_weight[:, 1], preferred_element_type=jnp.float32)
        .astype(jnp.bfloat16)
        .reshape(NB, heads_here, DH)
    )
    mem_vals = (
        jnp.dot(coeffs, qkv_weight[:, 2], preferred_element_type=jnp.float32)
        .astype(jnp.bfloat16)
        .reshape(NB, heads_here, DH)
    )
    key_mu = jnp.einsum("nhd,hn->hd", mem_keys.astype(jnp.float32), mu_weight, precision=UPPER_LIMIT) * scale_dh
    key_sigma = jnp.einsum("nhd,hn->hd", mem_keys.astype(jnp.float32), sigma_weight, precision=UPPER_LIMIT) * scale_dh
    levels = seq_count // 2
    row_pad = ((0, 6), (0, 0))
    norm_rows = jnp.pad(jnp.stack([ln1_gain, ln1_bias]), row_pad)
    qkv_flat = qkv_weight.reshape(D, 3 * head_cols)
    bias_row = jnp.concatenate([qv_bias[0], jnp.zeros(head_cols, jnp.float32), qv_bias[1]])
    bias_rows = jnp.broadcast_to(bias_row[None], (8, 3 * head_cols))
    reaches = doc_ids >= (seq_index + 1) * tok_rows
    key_mask = jnp.where(reaches, 0.0, NEGATIVE).astype(jnp.bfloat16).reshape(2, tok_rows // 2)
    key_mask = jnp.pad(key_mask, ((0, 14), (0, 2 * head_cols - tok_rows // 2)))
    normed_one, query_col, kv_col, local_flat, log_sum = attention_forward(
        levels, tokens, norm_rows, qkv_flat, bias_rows, doc_ids, key_mask
    )
    swap = [(index, index ^ 1) for index in range(seq_count)]
    query_oth = lax.ppermute(query_col, "seq", swap)
    kv_oth = lax.ppermute(kv_col, "seq", swap)
    queries = lax.dynamic_index_in_dim(query_col, seq_index // 2, 0, False)
    queries = (queries.astype(jnp.float32) / scale_dh).reshape(head_shape)
    local_out = local_flat.reshape(head_shape)
    rbf_width = 1.0 / NB
    queries_f = queries
    centre = jax.nn.sigmoid(jnp.sum(queries_f * key_mu, axis=-1))
    loose = jnp.sum(queries_f * key_sigma, axis=-1)
    spread_sq = SPREAD * jax.nn.softplus(loose) + rbf_width * rbf_width
    gap = centre[..., None] - radial_centres(NB)
    density_bf = (
        rbf_width
        * lax.rsqrt(spread_sq)[..., None]
        * jnp.exp(-0.5 * gap * gap / spread_sq[..., None])
    ).astype(jnp.bfloat16)
    mem_out = jnp.einsum(
        "thn,nhd->thd", density_bf, mem_vals, preferred_element_type=jnp.float32
    )
    heads_out = (local_out + mem_out).astype(jnp.bfloat16).reshape(tok_rows, head_cols)
    vectors = jnp.pad(
        jnp.stack([ln2_gain, ln2_bias, out_bias, fc_bias, proj_bias]), ((0, 3), (0, 0))
    )
    proj_grad, fc_grad, out_grad, grad_heads_flat, mid_grad, base, own_two, other_two, mid_sums = (
        feed_forward(heads_out, tokens, cotangent, out_weight, fc_weight, proj_weight, vectors)
    )
    grad_heads = grad_heads_flat.reshape(head_shape)
    grad_proj_b = jnp.sum(cotangent.astype(jnp.float32), axis=0)
    grad_density = jnp.einsum(
        "thd,nhd->thn", grad_heads, mem_vals, preferred_element_type=jnp.float32
    )
    grad_mem_vals = jnp.einsum(
        "thn,thd->nhd", density_bf, grad_heads, preferred_element_type=jnp.float32
    )
    weighed = grad_density * density_bf.astype(jnp.float32)
    sum_gap = jnp.sum(weighed * gap, axis=-1)
    sum_gap_sq = jnp.sum(weighed * gap * gap, axis=-1)
    sum_zero = jnp.sum(weighed, axis=-1)
    grad_centre = -sum_gap / spread_sq
    grad_spread = 0.5 * (sum_gap_sq / spread_sq - sum_zero) / spread_sq
    pull_mu = grad_centre * centre * (1.0 - centre)
    pull_sigma = grad_spread * SPREAD * jax.nn.sigmoid(loose)
    grad_q_mem = pull_mu[..., None] * key_mu + pull_sigma[..., None] * key_sigma
    query_mu = jnp.sum(pull_mu[..., None] * queries_f, axis=0) * scale_dh
    query_sigma = jnp.sum(pull_sigma[..., None] * queries_f, axis=0) * scale_dh
    mem_keys_f = mem_keys.astype(jnp.float32)
    grad_mu_w = jnp.einsum("nhd,hd->hn", mem_keys_f, query_mu, precision=UPPER_LIMIT)
    grad_sigma_w = jnp.einsum("nhd,hd->hn", mem_keys_f, query_sigma, precision=UPPER_LIMIT)
    grad_mem_keys = (
        mu_weight.T[:, :, None] * query_mu[None] + sigma_weight.T[:, :, None] * query_sigma[None]
    )
    grad_mem_seg = jnp.concatenate(
        [grad_mem_keys.reshape(NB, head_cols), grad_mem_vals.reshape(NB, head_cols)], axis=-1
    ).astype(jnp.bfloat16)

    def shards(grad):
        return grad.astype(jnp.bfloat16).reshape(seq_count, D // seq_count, -1)

    grad_q_local, grad_keys, grad_vals, proj_share, fc_share, out_share, output = attention_backward(
        levels,
        grad_heads_flat,
        local_flat,
        log_sum,
        query_col,
        query_oth,
        kv_col,
        kv_oth,
        doc_ids,
        [shards(proj_grad), shards(fc_grad), shards(out_grad)],
        base,
        own_two,
        other_two,
    )
    grad_q_bf = (grad_q_local + grad_q_mem.reshape(tok_rows, head_cols)).astype(jnp.bfloat16)
    grad_k_bf = grad_keys.astype(jnp.bfloat16)
    grad_v_bf = grad_vals.astype(jnp.bfloat16)
    grad_qkv = jnp.concatenate([grad_q_bf, grad_k_bf, grad_v_bf], axis=1)
    grad_kv_w = jnp.einsum("nd,nm->dm", coeffs, grad_mem_seg, preferred_element_type=jnp.float32)
    grad_qkv_w = jnp.einsum("td,tm->dm", normed_one, grad_qkv, preferred_element_type=jnp.float32)
    grad_qkv_w = grad_qkv_w + jnp.pad(grad_kv_w, ((0, 0), (head_cols, 0)))
    grad_qv_b = jnp.concatenate(
        [
            jnp.sum(grad_q_bf.astype(jnp.float32), axis=0),
            jnp.sum(grad_v_bf.astype(jnp.float32), axis=0),
        ]
    )
    nothing = jnp.zeros((2, D), jnp.float32)
    small = jnp.concatenate(
        [
            nothing,
            mid_sums[:4],
            grad_proj_b[None],
            jnp.pad(grad_qv_b[None], ((0, 0), (0, D - 2 * head_cols))),
            grad_mu_w.reshape(2, D),
            grad_sigma_w.reshape(2, D),
            nothing,
            nothing,
        ]
    )
    grad_tokens, qkv_share, small = finish_layer(
        levels, grad_qkv, qkv_flat, tokens, mid_grad, norm_rows, shards(grad_qkv_w), small
    )
    return (
        output,
        grad_tokens,
        qkv_share.reshape(-1, 3, head_cols),
        small[7, : 2 * head_cols].reshape(2, head_cols),
        out_share.T,
        small[4],
        fc_share,
        small[5],
        proj_share.T,
        small[6],
        small[0],
        small[1],
        small[2],
        small[3],
        small[8:10].reshape(heads_here, NB),
        small[10:12].reshape(heads_here, NB),
    )


def solution(mesh):
    in_specs = (
        P("seq", None),
        P("seq", None),
        P("seq", None),
        P("seq"),
        P("seq"),
        P("seq"),
        P("seq"),
        P(),
        P(),
        P(None, None, "tp"),
        P(None, "tp"),
        P("tp", None),
        P(),
        P(),
        P(),
        P(None, "tp"),
        P("tp"),
        P("tp", None),
        P(),
        P("tp", None),
        P("tp", None),
    )
    out_specs = (
        P("seq", None),
        P("seq", None),
        P("seq", None, "tp"),
        P(None, "tp"),
        P("tp", "seq"),
        P(),
        P("seq", "tp"),
        P("tp"),
        P("tp", "seq"),
        P(),
        P(),
        P(),
        P(),
        P(),
        P("tp", None),
        P("tp", None),
    )
    return jax.shard_map(local, mesh=mesh, in_specs=in_specs, out_specs=out_specs, check_vma=False)
```

```python
import functools
from typing import NamedTuple

import ml_dtypes
import numpy as np

import jax
import jax.numpy as jnp
from jax import lax
from jax.experimental import pallas as pl
from jax.experimental.pallas import tpu as pltpu
from jax.sharding import PartitionSpec as P

D = 768
DH = 64
NB = 512
SEG = 512
BOOKS = 4


EPS = 1e-05
TAU = 0.75
RIDGE = 1.0
SPREAD = 0.01
NEGATIVE = -1e30
MESH_ID = pl.DeviceIdType.MESH
VMEM_LIMIT = 60 * 2**20


def coefficient_tables(age_count, basis_n, seg_len):
    shrink = TAU ** np.arange(age_count, dtype=np.float64)
    inside = (np.arange(seg_len) + 0.5) / seg_len
    times = shrink[:, None] * (TAU + (1.0 - TAU) * inside[None, :])
    centres = (np.arange(basis_n) + 0.5) / basis_n
    offset = (times[:, None, :] - centres[None, :, None]) * basis_n
    basis = np.exp(-0.5 * offset * offset)
    gram = np.einsum("agx,ahx->gh", basis, basis) + RIDGE * np.eye(basis_n)
    table = np.linalg.solve(gram[None], basis)
    high = table.astype(ml_dtypes.bfloat16)
    lower = (table - high.astype(np.float64)).astype(ml_dtypes.bfloat16)
    return high, lower


LANES_OUT = 256


def head_of_lane(width):
    return lax.broadcasted_iota(jnp.int32, (1, width), 1) // DH


def head_masks(width):
    lane_head = head_of_lane(width)
    return [(lane_head == head).astype(jnp.float32).astype(jnp.bfloat16) for head in range(width // DH)]


def pick_heads(per_head, lane_head):
    chosen = per_head[0]
    for head in range(1, len(per_head)):
        chosen = jnp.where(lane_head == head, per_head[head], chosen)
    return chosen


def dot_rows(left, right):
    return lax.dot_general(left, right, (((1,), (1,)), ((), ())), preferred_element_type=jnp.float32)


def dot_plain(left, right):
    return lax.dot_general(left, right, (((1,), (0,)), ((), ())), preferred_element_type=jnp.float32)


def thirds(value):
    first = value.astype(jnp.bfloat16)
    rest = value - first.astype(jnp.float32)
    second = rest.astype(jnp.bfloat16)
    third = (rest - second.astype(jnp.float32)).astype(jnp.bfloat16)
    return first, second, third


def with_stats(block, stats):
    rows, width = block.shape
    spare = LANES_OUT - width
    lane = lax.broadcasted_iota(jnp.int32, (1, spare), 1)
    tail = jnp.zeros((rows, spare), jnp.float32)
    for index, column in enumerate(stats):
        for part, value in enumerate(thirds(column)):
            tail = jnp.where(lane == 3 * index + part, value.astype(jnp.float32), tail)
    return jnp.concatenate([block, tail.astype(jnp.bfloat16)], axis=1)


def stat_column(extended, width, index):
    lane = lax.broadcasted_iota(jnp.int32, (1, LANES_OUT), 1)
    start = width + 3 * index
    mine = (lane >= start) & (lane < start + 3)
    return jnp.sum(jnp.where(mine, extended.astype(jnp.float32), 0.0), axis=1, keepdims=True)


def stat_rows(extended, width, count):
    row = lax.broadcasted_iota(jnp.int32, (count, LANES_OUT), 0)
    lane = lax.broadcasted_iota(jnp.int32, (count, LANES_OUT), 1)
    start = width + 3 * row
    chooser = ((lane >= start) & (lane < start + 3)).astype(jnp.float32).astype(jnp.bfloat16)
    return dot_rows(chooser, extended)


def greet(levels, whole_tp=False):
    seq, tp = lax.axis_index("seq"), lax.axis_index("tp")
    level, side = seq // 2, seq % 2
    barrier = pltpu.get_barrier_semaphore()
    pl.semaphore_signal(barrier, inc=1, device_id=(2 * level + 1 - side, tp), device_id_type=MESH_ID)

    def one(step, unused):
        other = lax.rem(level + step, levels)
        pl.semaphore_signal(barrier, inc=1, device_id=(2 * other + side, tp), device_id_type=MESH_ID)
        return unused

    lax.fori_loop(1, levels, one, 0)
    if not whole_tp:
        return barrier, levels
    greet_tp()
    return barrier, levels + 2


class MemoryPlace(NamedTuple):
    loose: jax.Array
    centre: jax.Array
    spread: jax.Array
    height: jax.Array
    gap: jax.Array


def memory_place(query, spot_rows, in_head):
    width_sq = 1.0 / (NB * NB)
    centre = 1.0 / (
        1.0 + jnp.exp(-jnp.sum(jnp.where(in_head, query * spot_rows[0:1, :], 0.0), axis=1, keepdims=True))
    )
    loose = jnp.sum(jnp.where(in_head, query * spot_rows[1:2, :], 0.0), axis=1, keepdims=True)
    soft = jnp.maximum(loose, 0.0) + jnp.log(1.0 + jnp.exp(-jnp.abs(loose)))
    spread = SPREAD * soft + width_sq
    height = (1.0 / NB) * lax.rsqrt(spread)
    centres = (lax.broadcasted_iota(jnp.int32, (1, NB), 1).astype(jnp.float32) + 0.5) / NB
    return MemoryPlace(loose, centre, spread, height, centre - centres)


def forward_kernel(
    levels,
    tok_ref,
    norm_ref,
    weight_ref,
    bias_ref,
    doc_col_ref,
    doc_row_ref,
    key_mask_ref,
    past_ref,
    book_ref,
    spot_ref,
    table_ref,
    normed_ref,
    query_out_ref,
    kv_out_ref,
    out_ref,
    lse_ref,
    heads_ref,
    coeff_ref,
    mem_ref,
    spot_row_ref,
    pair_ref,
    top_ref,
    total_ref,
    acc_ref,
    part_ref,
    part_in_ref,
    kv_send,
    kv_recv,
    q_send,
    q_recv,
    pair_sem,
    part_sem,
    past_col_ref,
    past_oth_ref,
    table_in_ref,
    past_up,
    past_down,
    past_side,
    coeff_sems,
    table_sem,
):
    seq, tp = lax.axis_index("seq"), lax.axis_index("tp")
    level, side = seq // 2, seq % 2
    rows = tok_ref.shape[0]
    width = pair_ref.shape[2]
    heads = width // DH
    partner = (2 * level + 1 - side, tp)
    lane_head = head_of_lane(width)
    head_mask = head_masks(width)
    barrier, greetings = greet(levels, True)

    chunk = rows // 2
    past_col_ref[level] = past_ref[...]

    def past_copy(direction, from_level):
        block = past_col_ref.at[from_level]
        if direction == "side":
            sems, target, place = past_side, partner, past_oth_ref.at[from_level]
        elif direction == "up":
            sems, target, place = past_up, (lax.rem(2 * level + 2, 2 * levels) + side, tp), block
        else:
            sems, target, place = past_down, (lax.rem(2 * (level + levels - 1), 2 * levels) + side, tp), block
        return pltpu.make_async_remote_copy(
            block,
            place,
            sems.at[0, from_level],
            sems.at[1, from_level],
            device_id=target,
            device_id_type=MESH_ID,
        )

    pl.semaphore_wait(barrier, greetings)

    def pass_past(from_level, up, down):
        past_copy("side", from_level).start()
        if up:

            @pl.when(level < levels - 1)
            def _():
                past_copy("up", from_level).start()

        if down:

            @pl.when(level > 0)
            def _():
                past_copy("down", from_level).start()

    pass_past(level, True, True)

    def project(index, unused):
        here = pl.ds(pl.multiple_of(index * chunk, chunk), chunk)
        x = tok_ref[here, :].astype(jnp.float32)
        centred = x - jnp.mean(x, axis=1, keepdims=True)
        variance = jnp.mean(centred * centred, axis=1, keepdims=True)
        a = centred * lax.rsqrt(variance + EPS) * norm_ref[0:1, :] + norm_ref[1:2, :]
        a = a.astype(jnp.bfloat16)
        normed_ref[here, :] = a
        mixed = (dot_plain(a, weight_ref[...]) + bias_ref[0:1, :]).astype(jnp.bfloat16)
        query = mixed[:, :width] * jnp.bfloat16(DH**-0.5)
        pair_ref[0, here, :] = query
        query_out_ref[level, here, :] = query
        kv_out_ref[level, here, :] = mixed[:, width:]
        return unused

    lax.fori_loop(0, rows // chunk, project, 0)
    kv_out_ref[level, rows:, :] = key_mask_ref[...]

    pair_copy = pltpu.make_async_remote_copy(
        pair_ref.at[0], pair_ref.at[1], pair_sem.at[0], pair_sem.at[1], device_id=partner, device_id_type=MESH_ID
    )
    pair_copy.start()

    def kv_copy(from_level):
        return pltpu.make_async_remote_copy(
            kv_out_ref.at[from_level],
            kv_out_ref.at[from_level],
            kv_send.at[from_level],
            kv_recv.at[from_level],
            device_id=(lax.rem(2 * level + 2, 2 * levels) + side, tp),
            device_id_type=MESH_ID,
        )

    def query_copy(from_level, to_level):
        return pltpu.make_async_remote_copy(
            query_out_ref.at[from_level],
            query_out_ref.at[from_level],
            q_send.at[to_level],
            q_recv.at[from_level],
            device_id=(2 * to_level + side, tp),
            device_id_type=MESH_ID,
        )

    @pl.when(level < levels - 1)
    def _():
        kv_copy(level).start()

    def send_down(step, unused):
        query_copy(level, level - step).start()
        return unused

    lax.fori_loop(1, level + 1, send_down, 0)

    top_ref[...] = jnp.full(top_ref.shape, NEGATIVE, jnp.float32)
    total_ref[...] = jnp.zeros(total_ref.shape, jnp.float32)
    acc_ref[...] = jnp.zeros(acc_ref.shape, jnp.float32)

    doc_first = doc_row_ref[0:1, 0:1]
    def reach_of(here):
        docs = doc_col_ref[here, :]
        last = (level == levels - 1) & (side == 1)
        return jnp.where(last & (docs != doc_first), NEGATIVE, 0.0)

    def fold(slot, from_level, mask_kind):
        mask_rows = kv_out_ref[from_level, rows:, :].astype(jnp.float32)
        key_mask = jnp.concatenate([mask_rows[0:1, : rows // 2], mask_rows[1:2, : rows // 2]], axis=1)

        def part(index, unused):
            here = pl.ds(pl.multiple_of(index * chunk, chunk), chunk)
            query = pair_ref[slot, here, :]
            keys = kv_out_ref[from_level, :rows, :width]
            vals = kv_out_ref[from_level, :rows, width:]
            if mask_kind == "own":
                q_pos = index * chunk + lax.broadcasted_iota(jnp.int32, (chunk, rows), 0)
                k_pos = lax.broadcasted_iota(jnp.int32, (chunk, rows), 1)
                visible = (q_pos >= k_pos) & (doc_col_ref[here, :] == doc_row_ref[0:1, :])
            products, scales = [], []
            for head in range(heads):
                scores = dot_rows(query * head_mask[head], keys)
                old_top = top_ref[slot, head, here, :]
                if mask_kind == "own":
                    scores = jnp.where(visible, scores, NEGATIVE)
                    reach = 0.0
                else:
                    scores = scores + key_mask
                    reach = jnp.where(slot == 0, reach_of(here), 0.0)
                new_top = jnp.maximum(old_top, jnp.max(scores, axis=1, keepdims=True) + reach)
                weights = jnp.exp(scores - (new_top - reach))
                scale = jnp.exp(old_top - new_top)
                top_ref[slot, head, here, :] = new_top
                total_ref[slot, head, here, :] = total_ref[slot, head, here, :] * scale + jnp.sum(
                    weights, axis=1, keepdims=True
                )
                products.append(dot_plain(weights.astype(jnp.bfloat16), vals))
                scales.append(scale)
            acc_ref[slot, here, :] = acc_ref[slot, here, :] * pick_heads(scales, lane_head) + pick_heads(
                products, lane_head
            )
            return unused

        lax.fori_loop(0, rows // chunk, part, 0)

    fold(0, level, "own")
    pair_copy.wait()

    @pl.when(side == 0)
    def _():
        fold(1, level, "off")

    def keys_arrived(step):
        from_level = level - step
        kv_copy(from_level).wait_recv()

        @pl.when(level < levels - 1)
        def _():
            kv_copy(from_level).start()

        def both(slot, inner):
            fold(slot, from_level, "off")
            return inner

        lax.fori_loop(0, 2, both, 0)

    def arrived(step, unused):
        @pl.when(level >= step)
        def _():
            past_copy("up", level - step).wait_recv()
            pass_past(level - step, True, False)

        @pl.when(level + step < levels)
        def _():
            past_copy("down", level + step).wait_recv()
            pass_past(level + step, False, True)

        @pl.when((level >= step) & (step < levels - 1))
        def _():
            keys_arrived(step)

        return unused

    lax.fori_loop(1, levels, arrived, 0)

    def from_side(other, unused):
        past_copy("side", other).wait_recv()
        return unused

    lax.fori_loop(0, levels, from_side, 0)
    own_book = book_ref[0:1, :]
    time_half = rows // 2
    ages = table_ref.shape[0]

    def one_age(age, total):
        table_copy = pltpu.make_async_copy(table_ref.at[age], table_in_ref, table_sem)
        table_copy.start()

        def one_level(other, found):
            for blocks_ref in (past_col_ref, past_oth_ref):
                mark = blocks_ref[other, time_half:, :].astype(jnp.float32)
                chosen = (mark[0:1, :] == own_book) & (mark[1:2, :] == age.astype(jnp.float32))
                found = jnp.where(chosen, blocks_ref[other, :time_half, :].astype(jnp.float32), found)
            return found

        found = lax.fori_loop(
            0, levels, one_level, jnp.zeros((time_half, 2 * width), jnp.float32)
        ).astype(jnp.bfloat16)
        table_copy.wait()
        for index in range(2):
            table = table_in_ref[index]
            total = total + (
                dot_plain(table[:, :time_half], found)[:, :width]
                + dot_plain(table[:, time_half:], found)[:, width:]
            )
        return total

    coeff = lax.fori_loop(0, ages, one_age, jnp.zeros((NB, width), jnp.float32))
    coeff_ref[tp] = coeff.astype(jnp.bfloat16)

    def coeff_copy(kind, slot, index):
        return swap_with(kind, coeff_ref.at[slot], coeff_ref.at[slot], (coeff_sems.at[0], coeff_sems.at[1]), index)

    core_mate, chip_mate = tp + 1 - 2 * (tp % 2), lax.rem(tp + 2, 4)
    coeff_copy("chip", tp, 0).start()
    coeff_copy("core", tp, 1).start()

    @pl.when(level == levels - 1)
    def _():
        keys_arrived(levels - 1)

    def finish(index, unused):
        here = pl.ds(pl.multiple_of(index * chunk, chunk), chunk)
        totals = [total_ref[1, head, here, :] for head in range(heads)]
        tops = [top_ref[1, head, here, :] for head in range(heads)]
        some = [value > 0.0 for value in totals]
        inverse = [jnp.where(ok, 1.0 / jnp.where(ok, value, 1.0), 0.0) for ok, value in zip(some, totals)]
        logs = [
            jnp.where(ok, top + jnp.log(jnp.where(ok, value, 1.0)), NEGATIVE)
            for ok, top, value in zip(some, tops, totals)
        ]
        share = (acc_ref[1, here, :] * pick_heads(inverse, lane_head)).astype(jnp.bfloat16)
        part_ref[here, :] = with_stats(share, logs)
        return unused

    lax.fori_loop(0, rows // chunk, finish, 0)
    part_copy = pltpu.make_async_remote_copy(
        part_ref, part_in_ref, part_sem.at[0], part_sem.at[1], device_id=partner, device_id_type=MESH_ID
    )
    part_copy.start()

    coeff_copy("chip", chip_mate, 0).wait_recv()
    coeff_copy("core", chip_mate, 2).start()
    coeff_copy("core", core_mate, 1).wait_recv()
    coeff_copy("core", lax.rem(core_mate + 2, 4), 2).wait_recv()
    memory = jnp.zeros((NB, 2 * width), jnp.float32)
    for slot in range(4):
        memory = memory + dot_plain(
            coeff_ref[slot], weight_ref[slot * width : (slot + 1) * width, width:]
        )
    mem_ref[...] = memory.astype(jnp.bfloat16)
    for index in range(2):
        spots = spot_ref[8 * index : 8 * index + 8, :]
        row = sum(dot_plain(third, mem_ref[:, :width]) for third in thirds(spots))
        spot_row_ref[index : index + 1, :] = pick_heads(
            [row[head : head + 1, :] for head in range(heads)], lane_head
        )
    part_copy.wait()

    def merge(index, unused):
        here = pl.ds(pl.multiple_of(index * chunk, chunk), chunk)
        reach = reach_of(here)
        received = part_in_ref[here, :]
        mine, theirs, columns = [], [], []
        for head in range(heads):
            total = total_ref[0, head, here, :]
            own_log = top_ref[0, head, here, :] + jnp.log(total)
            other_log = stat_column(received, width, head) + reach
            high = jnp.maximum(own_log, other_log)
            both_log = high + jnp.log(jnp.exp(own_log - high) + jnp.exp(other_log - high))
            mine.append(jnp.exp(own_log - both_log) / total)
            theirs.append(jnp.exp(other_log - both_log))
            columns.append(both_log)
        attended = acc_ref[0, here, :] * pick_heads(mine, lane_head) + received[:, :width].astype(
            jnp.float32
        ) * pick_heads(theirs, lane_head)
        out_ref[here, :] = attended
        query = pair_ref[0, here, :].astype(jnp.float32)
        reads = []
        for head in range(heads):
            place = memory_place(query, spot_row_ref[0:2, :], lane_head == head)
            density = place.height * jnp.exp(place.gap * place.gap * (-0.5 / place.spread))
            reads.append(dot_plain(density.astype(jnp.bfloat16), mem_ref[:, width:]))
        heads_ref[here, :] = (attended + pick_heads(reads, lane_head)).astype(jnp.bfloat16)
        lane = lax.broadcasted_iota(jnp.int32, (1, 8), 1)
        packed = jnp.zeros((chunk, 8), jnp.float32)
        for head in range(heads):
            packed = jnp.where(lane == head, columns[head], packed)
        lse_ref[here, :] = packed
        return unused

    lax.fori_loop(0, rows // chunk, merge, 0)

    coeff_copy("chip", tp, 0).wait_send()
    coeff_copy("core", tp, 1).wait_send()
    coeff_copy("core", chip_mate, 2).wait_send()

    def past_sent(other, unused):
        past_copy("side", other).wait_send()

        @pl.when((level < levels - 1) & (other <= level))
        def _():
            past_copy("up", other).wait_send()

        @pl.when((level > 0) & (other >= level))
        def _():
            past_copy("down", other).wait_send()

        return unused

    lax.fori_loop(0, levels, past_sent, 0)

    def sent_down(step, unused):
        query_copy(level, level - step).wait_send()
        return unused

    lax.fori_loop(1, level + 1, sent_down, 0)

    def from_above(step, unused):
        query_copy(level + step, level).wait_recv()
        return unused

    lax.fori_loop(1, levels - level, from_above, 0)

    @pl.when(level < levels - 1)
    def _():
        def sent_up(from_level, unused):
            kv_copy(from_level).wait_send()
            return unused

        lax.fori_loop(0, level + 1, sent_up, 0)


def attention_forward(levels, tokens, norm, weight, bias, doc_ids, key_mask, past, book, spots, table):
    rows = tokens.shape[0]
    width = weight.shape[1] // 3
    heads = width // DH
    vmem = pl.BlockSpec(memory_space=pltpu.VMEM)
    dma = pltpu.SemaphoreType.DMA
    return pl.pallas_call(
        functools.partial(forward_kernel, levels),
        out_shape=(
            jax.ShapeDtypeStruct((rows, D), jnp.bfloat16),
            jax.ShapeDtypeStruct((levels, rows, width), jnp.bfloat16),
            jax.ShapeDtypeStruct((levels, rows + 16, 2 * width), jnp.bfloat16),
            jax.ShapeDtypeStruct((rows, width), jnp.float32),
            jax.ShapeDtypeStruct((rows, 8), jnp.float32),
            jax.ShapeDtypeStruct((rows, width), jnp.bfloat16),
            jax.ShapeDtypeStruct((4, NB, width), jnp.bfloat16),
            jax.ShapeDtypeStruct((NB, 2 * width), jnp.bfloat16),
            jax.ShapeDtypeStruct((8, width), jnp.float32),
        ),
        in_specs=[vmem] * 10 + [pl.BlockSpec(memory_space=pl.ANY)],
        out_specs=(vmem,) * 9,
        scratch_shapes=[
            pltpu.VMEM((2, rows, width), jnp.bfloat16),
            pltpu.VMEM((2, heads, rows, 1), jnp.float32),
            pltpu.VMEM((2, heads, rows, 1), jnp.float32),
            pltpu.VMEM((2, rows, width), jnp.float32),
            pltpu.VMEM((rows, LANES_OUT), jnp.bfloat16),
            pltpu.VMEM((rows, LANES_OUT), jnp.bfloat16),
            dma((levels,)),
            dma((levels,)),
            dma((levels,)),
            dma((levels,)),
            dma((2,)),
            dma((2,)),
            pltpu.VMEM((levels,) + past.shape, jnp.bfloat16),
            pltpu.VMEM((levels,) + past.shape, jnp.bfloat16),
            pltpu.VMEM(table.shape[1:], jnp.bfloat16),
            dma((2, levels)),
            dma((2, levels)),
            dma((2, levels)),
            dma((2, 3)),
            dma(()),
        ],
        name="attention_forward",
        compiler_params=pltpu.CompilerParams(
            collective_id=1, has_side_effects=True, vmem_limit_bytes=VMEM_LIMIT
        ),
    )(
        tokens,
        norm,
        weight,
        bias,
        doc_ids[:, None],
        doc_ids[None, :],
        key_mask,
        past,
        book,
        spots,
        table,
    )


def backward_kernel(
    levels,
    grad_ref,
    attended_ref,
    lse_ref,
    query_col_ref,
    query_oth_ref,
    kv_col_ref,
    kv_oth_ref,
    doc_col_ref,
    doc_row_ref,
    proj_blocks_ref,
    fc_blocks_ref,
    out_blocks_ref,
    base_ref,
    own_two_ref,
    other_two_ref,
    normed_ref,
    coeff_ref,
    mem_ref,
    spot_row_ref,
    spot_ref,
    grads_ref,
    weight_grad_ref,
    bias_grad_ref,
    spot_grad_ref,
    proj_share_ref,
    fc_share_ref,
    out_share_ref,
    output_ref,
    dq_ref,
    dk_ref,
    dv_ref,
    mem_acc_ref,
    pull_ref,
    own_ref,
    grad_col_ref,
    grad_oth_ref,
    stat_ref,
    col_send,
    col_recv,
    oth_send,
    oth_recv,
    *rest,
):
    scatters = []
    for blocks_ref in (proj_blocks_ref, fc_blocks_ref, out_blocks_ref):
        scatters.append(Scatter(levels, blocks_ref, *rest[:3], rest[3:7]))
        rest = rest[7:]
    late = LateOutput(base_ref, own_two_ref, other_two_ref, output_ref, rest[: LateOutput.COUNT])
    staging = rest[LateOutput.COUNT :]
    seq, tp = lax.axis_index("seq"), lax.axis_index("tp")
    level, side = seq // 2, seq % 2
    rows, width = grad_ref.shape
    heads = width // DH
    partner = (2 * level + 1 - side, tp)
    lane_head = head_of_lane(width)
    head_mask = head_masks(width)
    chunk = rows // 2
    barrier, greetings = greet(levels, True)

    def block_of(blocks_ref, from_level, place):
        if not staging:
            return blocks_ref.at[from_level]
        copy = pltpu.make_async_copy(blocks_ref.at[from_level], staging[place], staging[3])
        copy.start()
        copy.wait()
        return staging[place]

    own_query_ref = block_of(query_col_ref, level, 0)
    doc_first = doc_row_ref[0:1, 0:1]
    last = (level == levels - 1) & (side == 1)

    def prepare(index, unused):
        here = pl.ds(pl.multiple_of(index * chunk, chunk), chunk)
        grad = grad_ref[here, :]
        product = grad.astype(jnp.float32) * attended_ref[here, :]
        far = jnp.where(last & (doc_col_ref[here, :] != doc_first), -NEGATIVE, 0.0)
        lses = [lse_ref[here, head : head + 1] for head in range(heads)]
        deltas = [
            jnp.sum(jnp.where(lane_head == head, product, 0.0), axis=1, keepdims=True)
            for head in range(heads)
        ]
        own_ref[here, :] = with_stats(grad, lses + deltas)
        grad_col_ref[level, here, :] = with_stats(grad, [lse + far for lse in lses] + deltas)
        for head in range(heads):
            stat_ref[head, here, :] = lses[head]
            stat_ref[heads + head, here, :] = lses[head] + far
            stat_ref[2 * heads + head, here, :] = deltas[head]
        return unused

    lax.fori_loop(0, rows // chunk, prepare, 0)
    pl.semaphore_wait(barrier, greetings)

    def col_copy(from_level, to_level):
        return pltpu.make_async_remote_copy(
            grad_col_ref.at[from_level],
            grad_col_ref.at[from_level],
            col_send.at[to_level],
            col_recv.at[from_level],
            device_id=(2 * to_level + side, tp),
            device_id_type=MESH_ID,
        )

    def oth_copy(from_level):
        return pltpu.make_async_remote_copy(
            grad_col_ref.at[from_level],
            grad_oth_ref.at[from_level],
            oth_send.at[from_level],
            oth_recv.at[from_level],
            device_id=partner,
            device_id_type=MESH_ID,
        )

    @pl.when(side == 1)
    def _():
        oth_copy(level).start()

    def send_down(step, unused):
        col_copy(level, level - step).start()
        return unused

    lax.fori_loop(1, level + 1, send_down, 0)
    late.start()
    for scatter in scatters:
        scatter.start()

    mem_acc_ref[...] = jnp.zeros(mem_acc_ref.shape, jnp.float32)
    pull_ref[...] = jnp.zeros(pull_ref.shape, jnp.float32)

    def memory_back(index, unused):
        here = pl.ds(pl.multiple_of(index * chunk, chunk), chunk)
        query = own_query_ref[here, :].astype(jnp.float32)
        grad = grad_ref[here, :]
        val_parts, mu_pulls, sigma_pulls = [], [], []
        for head in range(heads):
            place = memory_place(query, spot_row_ref[0:2, :], lane_head == head)
            slope = place.gap / place.spread
            square = place.gap * slope
            density = place.height * jnp.exp(-0.5 * square)
            val_parts.append(dot_columns(density.astype(jnp.bfloat16), grad))
            weighed = dot_rows(grad * head_mask[head], mem_ref[:, width:]) * density
            to_centre = -jnp.sum(weighed * slope, axis=1, keepdims=True)
            to_spread = 0.5 * jnp.sum(weighed * (square - 1.0), axis=1, keepdims=True) / place.spread
            mu_pulls.append(to_centre * place.centre * (1.0 - place.centre))
            sigma_pulls.append(to_spread * SPREAD / (1.0 + jnp.exp(-place.loose)))
        mu_pull, sigma_pull = pick_heads(mu_pulls, lane_head), pick_heads(sigma_pulls, lane_head)
        dq_ref[here, :] = mu_pull * spot_row_ref[0:1, :] + sigma_pull * spot_row_ref[1:2, :]
        mem_acc_ref[...] += pick_heads(val_parts, lane_head)
        pull_ref[0:1, :] += column_sum(mu_pull * query)
        pull_ref[1:2, :] += column_sum(sigma_pull * query)
        return unused

    lax.fori_loop(0, rows // chunk, memory_back, 0)
    by_head = lax.broadcasted_iota(jnp.int32, (8, 1), 0) == lane_head
    pulls = [jnp.where(by_head, pull_ref[i : i + 1, :], 0.0) for i in range(2)]
    for index in range(2):
        spot_grad_ref[8 * index : 8 * index + 8, :] = sum(
            dot_rows(third, mem_ref[:, :width]) for third in thirds(pulls[index])
        )
    key_grad = dot_columns(
        spot_ref[...].astype(jnp.bfloat16), jnp.concatenate(pulls, axis=0).astype(jnp.bfloat16)
    )
    memory_grad = jnp.concatenate([key_grad, mem_acc_ref[...]], axis=1).astype(jnp.bfloat16)
    for slot in range(4):
        weight_grad_ref[slot * width : (slot + 1) * width, :] = jnp.concatenate(
            [jnp.zeros((width, width), jnp.float32), dot_columns(coeff_ref[slot], memory_grad)], axis=1
        ).astype(weight_grad_ref.dtype)

    dk_ref[...] = jnp.zeros(dk_ref.shape, jnp.float32)
    dv_ref[...] = jnp.zeros(dv_ref.shape, jnp.float32)

    def query_fold(kv_ref, from_level, own):
        block_ref = block_of(kv_ref, from_level, 2)
        if own:
            key_mask = None
        else:
            mask_rows = block_ref[rows:, :].astype(jnp.float32)
            key_mask = jnp.concatenate(
                [mask_rows[0:1, : rows // 2], mask_rows[1:2, : rows // 2]], axis=1
            )

        def part(index, unused):
            here = pl.ds(pl.multiple_of(index * chunk, chunk), chunk)
            query = own_query_ref[here, :]
            grad = grad_ref[here, :]
            keys = block_ref[:rows, :width]
            vals = block_ref[:rows, width:]
            if own:
                q_pos = index * chunk + lax.broadcasted_iota(jnp.int32, (chunk, rows), 0)
                k_pos = lax.broadcasted_iota(jnp.int32, (chunk, rows), 1)
                visible = (q_pos >= k_pos) & (doc_col_ref[here, :] == doc_row_ref[0:1, :])
            products = []
            for head in range(heads):
                scores = dot_rows(query * head_mask[head], keys)
                if own:
                    scores = jnp.where(visible, scores, NEGATIVE)
                    lse = stat_ref[head, here, :]
                else:
                    scores = scores + key_mask
                    lse = stat_ref[heads + head, here, :]
                probs = jnp.exp(scores - lse)
                pull = dot_rows(grad * head_mask[head], vals) - stat_ref[2 * heads + head, here, :]
                products.append(dot_plain((probs * pull).astype(jnp.bfloat16), keys))
            dq_ref[here, :] = dq_ref[here, :] + pick_heads(products, lane_head)
            return unused

        lax.fori_loop(0, rows // chunk, part, 0)

    query_fold(kv_col_ref, level, True)

    @pl.when(side == 1)
    def _():
        query_fold(kv_oth_ref, level, False)

    def earlier(from_level, unused):
        query_fold(kv_col_ref, from_level, False)
        query_fold(kv_oth_ref, from_level, False)
        return unused

    lax.fori_loop(0, level, earlier, 0)
    late.middle()
    for scatter in scatters:
        scatter.middle()

    own_block_ref = block_of(kv_col_ref, level, 2)

    def key_fold(query_ref, grads_ref, from_level, own):
        query_block_ref = own_query_ref if own else block_of(query_ref, from_level, 1)

        def part(index, unused):
            here = pl.ds(pl.multiple_of(index * chunk, chunk), chunk)
            keys = own_block_ref[here, :width]
            vals = own_block_ref[here, width:]
            if own:
                query = query_block_ref[...]
                extended = own_ref[...]
                k_pos = index * chunk + lax.broadcasted_iota(jnp.int32, (chunk, rows), 0)
                q_pos = lax.broadcasted_iota(jnp.int32, (chunk, rows), 1)
                visible = (q_pos >= k_pos) & (doc_col_ref[here, :] == doc_row_ref[0:1, :])
            else:
                query = query_block_ref[...]
                extended = grads_ref[from_level]
            grad = extended[:, :width]
            stats = stat_rows(extended, width, 8)
            key_parts, val_parts = [], []
            for head in range(heads):
                scores = dot_rows(keys * head_mask[head], query)
                if own:
                    scores = jnp.where(visible, scores, NEGATIVE)
                probs = jnp.exp(scores - stats[head : head + 1, :])
                val_parts.append(dot_plain(probs.astype(jnp.bfloat16), grad))
                pull = dot_rows(vals * head_mask[head], grad) - stats[heads + head : heads + head + 1, :]
                key_parts.append(dot_plain((probs * pull).astype(jnp.bfloat16), query))
            dk_ref[here, :] = dk_ref[here, :] + pick_heads(key_parts, lane_head)
            dv_ref[here, :] = dv_ref[here, :] + pick_heads(val_parts, lane_head)
            return unused

        lax.fori_loop(0, rows // chunk, part, 0)

    @pl.when(side == 0)
    def _():
        oth_copy(level).wait_recv()
        key_fold(query_oth_ref, grad_oth_ref, level, False)

    def later(step, unused):
        from_level = level + step
        col_copy(from_level, level).wait_recv()
        oth_copy(from_level).start()
        key_fold(query_col_ref, grad_col_ref, from_level, False)
        oth_copy(from_level).wait_recv()
        key_fold(query_oth_ref, grad_oth_ref, from_level, False)
        return unused

    lax.fori_loop(1, levels - level, later, 0)
    late.late()
    reaches = doc_col_ref[...] >= (seq + 1) * rows
    dk_ref[...] = jnp.where(reaches, dk_ref[...], 0.0)
    dv_ref[...] = jnp.where(reaches, dv_ref[...], 0.0)
    key_fold(None, None, level, True)
    grads_ref[...] = jnp.concatenate(
        [dq_ref[...] * (DH**-0.5), dk_ref[...], dv_ref[...]], axis=1
    ).astype(jnp.bfloat16)
    bias_grad_ref[...] = jnp.broadcast_to(
        column_sum(grads_ref[...].astype(jnp.float32)), bias_grad_ref.shape
    )

    def weights(index, unused):
        here = pl.ds(pl.multiple_of(index * 256, 256), 256)
        weight_grad_ref[here, :] = (
            weight_grad_ref[here, :].astype(jnp.float32) + dot_columns(normed_ref[:, here], grads_ref[...])
        ).astype(weight_grad_ref.dtype)
        return unused

    lax.fori_loop(0, D // 256, weights, 0)
    late.finish()
    for scatter, share_ref in zip(scatters, (proj_share_ref, fc_share_ref, out_share_ref)):
        scatter.finish(share_ref)

    @pl.when(side == 1)
    def _():
        oth_copy(level).wait_send()

    def sent_down(step, unused):
        col_copy(level, level - step).wait_send()
        return unused

    lax.fori_loop(1, level + 1, sent_down, 0)

    def sent_on(step, unused):
        oth_copy(level + step).wait_send()
        return unused

    lax.fori_loop(1, levels - level, sent_on, 0)


def attention_backward(
    levels,
    grad,
    attended,
    lse,
    query_col,
    query_oth,
    kv_col,
    kv_oth,
    doc_ids,
    blocks,
    base,
    own_two,
    other_two,
    normed,
    coeff,
    memory,
    spot_rows,
    spots,
):
    rows, width = grad.shape
    heads = width // DH
    vmem = pl.BlockSpec(memory_space=pltpu.VMEM)
    dma = pltpu.SemaphoreType.DMA
    staged = levels > 8
    far = pl.BlockSpec(memory_space=pl.ANY) if staged else vmem
    staging = []
    if staged:
        staging = [pltpu.VMEM(a.shape[1:], a.dtype) for a in (query_col, query_col, kv_col)] + [dma(())]
    return pl.pallas_call(
        functools.partial(backward_kernel, levels),
        out_shape=(
            jax.ShapeDtypeStruct((rows, 3 * width), jnp.bfloat16),
            jax.ShapeDtypeStruct((D, 3 * width), jnp.float32),
            jax.ShapeDtypeStruct((8, 3 * width), jnp.float32),
            jax.ShapeDtypeStruct((16, NB), jnp.float32),
            *(jax.ShapeDtypeStruct(block.shape[1:], jnp.float32) for block in blocks),
            jax.ShapeDtypeStruct((rows, D), jnp.bfloat16),
        ),
        in_specs=[vmem] * 3 + [far] * 4 + [vmem] * 13,
        out_specs=(vmem,) * 8,
        scratch_shapes=[
            pltpu.VMEM((rows, width), jnp.float32),
            pltpu.VMEM((rows, width), jnp.float32),
            pltpu.VMEM((rows, width), jnp.float32),
            pltpu.VMEM((NB, width), jnp.float32),
            pltpu.VMEM((8, width), jnp.float32),
            pltpu.VMEM((rows, LANES_OUT), jnp.bfloat16),
            pltpu.VMEM((levels, rows, LANES_OUT), jnp.bfloat16),
            pltpu.VMEM((levels, rows, LANES_OUT), jnp.bfloat16),
            pltpu.VMEM((3 * heads, rows, 1), jnp.float32),
            dma((levels,)),
            dma((levels,)),
            dma((levels,)),
            dma((levels,)),
            *(item for block in blocks for item in Scatter.scratch(levels, *block.shape[1:])),
            *LateOutput.scratch(rows // 2, D),
            *staging,
        ],
        name="attention_backward",
        compiler_params=pltpu.CompilerParams(
            collective_id=2, has_side_effects=True, vmem_limit_bytes=VMEM_LIMIT
        ),
    )(
        grad,
        attended,
        lse,
        query_col,
        query_oth,
        kv_col,
        kv_oth,
        doc_ids[:, None],
        doc_ids[None, :],
        *blocks,
        base,
        own_two,
        other_two,
        normed,
        coeff,
        memory,
        spot_rows,
        spots,
    )


def column_copy(block_ref, from_level, landing_ref, send_sem, recv_sem, to_level):
    seq, tp = lax.axis_index("seq"), lax.axis_index("tp")
    return pltpu.make_async_remote_copy(
        block_ref,
        landing_ref.at[from_level],
        send_sem.at[to_level],
        recv_sem.at[from_level],
        device_id=(2 * to_level + seq % 2, tp),
        device_id_type=MESH_ID,
    )


class Scatter:
    def __init__(self, levels, blocks, plane_in, plane_sum, column_in, sems):
        self.levels, self.blocks = levels, blocks
        self.plane_in, self.plane_sum, self.column_in = plane_in, plane_sum, column_in
        self.plane_send, self.plane_recv, self.column_send, self.column_recv = sems
        seq, tp = lax.axis_index("seq"), lax.axis_index("tp")
        self.level, self.side, self.tp = seq // 2, seq % 2, tp

    def plane_copy(self, to_level):
        return pltpu.make_async_remote_copy(
            self.blocks.at[2 * to_level + 1 - self.side],
            self.plane_in.at[to_level],
            self.plane_send.at[to_level],
            self.plane_recv.at[to_level],
            device_id=(2 * self.level + 1 - self.side, self.tp),
            device_id_type=MESH_ID,
        )

    def swap_copy(self, from_level, to_level):
        return column_copy(
            self.plane_sum.at[to_level], from_level, self.column_in, self.column_send, self.column_recv, to_level
        )

    def loop(self, first, body):
        def one(step, unused):
            body(lax.rem(self.level + step, self.levels))
            return unused

        lax.fori_loop(first, self.levels, one, 0)

    def start(self):
        self.loop(0, lambda other: self.plane_copy(other).start())

    def middle(self):
        def one(other):
            self.plane_copy(other).wait_recv()
            total = self.blocks[2 * other + self.side].astype(jnp.float32) + self.plane_in[other].astype(
                jnp.float32
            )
            self.plane_sum[other] = total.astype(jnp.bfloat16)
            self.swap_copy(self.level, other).start()

        self.loop(1, one)

    def finish(self, out_ref):
        self.plane_copy(self.level).wait_recv()
        out_ref[...] = self.blocks[2 * self.level + self.side].astype(jnp.float32) + self.plane_in[
            self.level
        ].astype(jnp.float32)

        def one(other):
            self.swap_copy(other, self.level).wait_recv()
            out_ref[...] += self.column_in[other].astype(jnp.float32)

        self.loop(1, one)
        self.loop(0, lambda other: self.plane_copy(other).wait_send())
        self.loop(1, lambda other: self.swap_copy(self.level, other).wait_send())

    @staticmethod
    def scratch(levels, rows, width):
        buffer = pltpu.VMEM((levels, rows, width), jnp.bfloat16)
        return [buffer] * 3 + [pltpu.SemaphoreType.DMA((levels,))] * 4


class SmallSum:
    def __init__(self, levels, small, plane_in, column_in, sems):
        self.levels, self.small, self.plane_in, self.column_in = levels, small, plane_in, column_in
        self.plane_sem, self.column_send, self.column_recv = sems
        seq, tp = lax.axis_index("seq"), lax.axis_index("tp")
        self.level, self.side, self.tp = seq // 2, seq % 2, tp

    def plane_copy(self):
        return pltpu.make_async_remote_copy(
            self.small,
            self.plane_in,
            self.plane_sem.at[0],
            self.plane_sem.at[1],
            device_id=(2 * self.level + 1 - self.side, self.tp),
            device_id_type=MESH_ID,
        )

    def swap_copy(self, from_level, to_level):
        return column_copy(
            self.column_in.at[from_level], from_level, self.column_in, self.column_send, self.column_recv, to_level
        )

    def loop(self, body):
        def one(step, unused):
            body(lax.rem(self.level + step, self.levels))
            return unused

        lax.fori_loop(1, self.levels, one, 0)

    def start(self):
        self.plane_copy().start()

    def middle(self):
        self.plane_copy().wait()
        self.column_in[self.level] = self.small[...] + self.plane_in[...]
        self.loop(lambda other: self.swap_copy(self.level, other).start())

    def finish(self, out_ref):
        self.loop(lambda other: self.swap_copy(other, self.level).wait_recv())
        self.loop(lambda other: self.swap_copy(self.level, other).wait_send())
        out_ref[...] = self.column_in[0]

        def one(other, unused):
            out_ref[...] += self.column_in[other]
            return unused

        lax.fori_loop(1, self.levels, one, 0)

    @staticmethod
    def scratch(levels, shape):
        dma = pltpu.SemaphoreType.DMA
        return [
            pltpu.VMEM(shape, jnp.float32),
            pltpu.VMEM((levels,) + shape, jnp.float32),
            dma((2,)),
            dma((levels,)),
            dma((levels,)),
        ]


def tp_partner(kind):
    seq, tp = lax.axis_index("seq"), lax.axis_index("tp")
    if kind == "core":
        return (seq, tp + 1 - 2 * (tp % 2))
    return (seq, lax.rem(tp + 2, 4))


def greet_tp():
    barrier = pltpu.get_barrier_semaphore()
    for kind in ("core", "chip"):
        pl.semaphore_signal(barrier, inc=1, device_id=tp_partner(kind), device_id_type=MESH_ID)
    return barrier, 2


def swap_with(kind, source, target, sems, index):
    send, recv = sems
    return pltpu.make_async_remote_copy(
        source, target, send.at[index], recv.at[index], device_id=tp_partner(kind), device_id_type=MESH_ID
    )


class TpSum:
    def __init__(self, core_out, core_in, chip_out, chip_in, sems):
        self.core_out, self.core_in, self.chip_out, self.chip_in = core_out, core_in, chip_out, chip_in
        self.core_sems, self.chip_sems = sems[:2], sems[2:]

    def core_copy(self, part):
        return swap_with("core", self.core_out.at[part], self.core_in.at[part], self.core_sems, part)

    def chip_copy(self, part):
        return swap_with("chip", self.chip_out.at[part], self.chip_in.at[part], self.chip_sems, part)

    def start(self, part, for_other_core):
        self.core_out[part] = for_other_core.astype(jnp.bfloat16)
        self.core_copy(part).start()

    def middle(self, part, own):
        self.core_copy(part).wait()
        self.chip_out[part] = (own + self.core_in[part].astype(jnp.float32)).astype(jnp.bfloat16)
        self.chip_copy(part).start()

    def result(self, part):
        self.chip_copy(part).wait()
        return self.chip_out[part].astype(jnp.float32) + self.chip_in[part].astype(jnp.float32)

    @staticmethod
    def scratch(parts, rows, width):
        buffer = pltpu.VMEM((parts, rows, width), jnp.bfloat16)
        return [buffer] * 4 + [pltpu.SemaphoreType.DMA((parts,))] * 4

    COUNT = 8


class RowShare:
    def __init__(self, whole, rows, sems):
        self.whole, self.rows, self.sems = whole, rows, sems

    def copy(self, part, start):
        here = self.whole.at[pl.ds(pl.multiple_of(start, self.rows), self.rows), :]
        return swap_with("core", here, here, self.sems, part)


def normalize(v):
    centred = v - jnp.mean(v, axis=1, keepdims=True)
    scale = lax.rsqrt(jnp.mean(centred * centred, axis=1, keepdims=True) + EPS)
    return centred * scale, scale


def norm_back(grad, nhat, scale, gain):
    inner = grad * gain
    return (
        inner
        - jnp.mean(inner, axis=1, keepdims=True)
        - nhat * jnp.mean(inner * nhat, axis=1, keepdims=True)
    ) * scale


def gelu_and_slope(f):
    root = (2.0 / np.pi) ** 0.5
    square = f * f
    bend = jnp.tanh(root * f * (1.0 + 0.044715 * square))
    half = 0.5 * (1.0 + bend)
    slope = half + 0.5 * f * (1.0 - bend * bend) * (root * (1.0 + 3.0 * 0.044715 * square))
    return f * half, slope


def dot_columns(left, right):
    return lax.dot_general(left, right, (((0,), (0,)), ((), ())), preferred_element_type=jnp.float32)


def column_sum(v):
    return jnp.sum(v, axis=0, keepdims=True)


FEED_PARTS = 2


def feed_kernel(
    heads_ref,
    tok_ref,
    cot_ref,
    out_w_ref,
    fc_w_ref,
    proj_w_ref,
    vec_ref,
    proj_grad_ref,
    fc_grad_ref,
    out_grad_ref,
    head_grad_ref,
    mid_grad_ref,
    base_ref,
    own_two_ref,
    other_two_ref,
    sums_ref,
    c_ref,
    e1_ref,
    u_ref,
    ef_ref,
    pull_ref,
    h1_ref,
    own_ref,
    fold_in_ref,
    *sems,
):
    parts = FEED_PARTS
    rows = tok_ref.shape[0]
    half = rows // 2
    size = half // parts
    tp = lax.axis_index("tp")
    core = tp % 2
    first = TpSum(*sems[:4], sems[4 : TpSum.COUNT])
    second = TpSum(*sems[TpSum.COUNT : TpSum.COUNT + 4], sems[TpSum.COUNT + 4 : 2 * TpSum.COUNT])
    sems = sems[2 * TpSum.COUNT :]
    c_share = RowShare(c_ref, size, sems[0:2])
    e_share = RowShare(e1_ref, size, sems[2:4])
    fold_sems = sems[4:6]
    barrier, greetings = greet_tp()
    gain, offset, out_b, fc_b, proj_b = (vec_ref[i : i + 1, :] for i in range(5))

    def span(start, count=size):
        return pl.ds(pl.multiple_of(start, size), count)

    def mine(part):
        return core * half + part * size

    def theirs(part):
        return (1 - core) * half + part * size

    pl.semaphore_wait(barrier, greetings)
    for part in range(parts):
        first.start(part, dot_plain(heads_ref[span(theirs(part)), :], out_w_ref[...]))
        own_ref[span(part * size), :] = dot_plain(heads_ref[span(mine(part)), :], out_w_ref[...])
    for part in range(parts):
        first.middle(part, own_ref[span(part * size), :])

    def early(index, unused):
        here = span(index * size)
        pull_ref[here, :] = dot_rows(cot_ref[here, :], proj_w_ref[...])
        return unused

    lax.fori_loop(0, rows // size, early, 0)

    def feed(start):
        here = span(start)
        f = dot_plain(c_ref[here, :], fc_w_ref[...]) + fc_b
        u, slope = gelu_and_slope(f)
        u_ref[here, :] = u.astype(jnp.bfloat16)
        ef = (pull_ref[here, :] * slope).astype(jnp.bfloat16)
        ef_ref[here, :] = ef
        return dot_rows(ef, fc_w_ref[...])

    for part in range(parts):
        total = first.result(part) + out_b
        h1 = tok_ref[span(mine(part)), :].astype(jnp.float32) + total
        h1_ref[span(part * size), :] = h1
        nhat, scale = normalize(h1)
        c_ref[span(mine(part)), :] = (nhat * gain + offset).astype(jnp.bfloat16)
        c_share.copy(part, mine(part)).start()
        own_ref[span(part * size), :] = feed(mine(part))
        c_share.copy(part, theirs(part)).wait_recv()
        second.start(part, feed(theirs(part)))
        other_two_ref[span(part * size), :] = dot_plain(u_ref[span(theirs(part)), :], proj_w_ref[...]).astype(
            jnp.bfloat16
        )
        own_two_ref[span(part * size), :] = dot_plain(u_ref[span(mine(part)), :], proj_w_ref[...])
        second.middle(part, own_ref[span(part * size), :])

    base_ref[...] = h1_ref[...] + proj_b
    block = 256

    def weights(index, unused):
        here = pl.ds(pl.multiple_of(index * block, block), block)
        proj_grad_ref[here, :] = dot_columns(cot_ref[:, here], u_ref[...]).astype(jnp.bfloat16)
        fc_grad_ref[here, :] = dot_columns(c_ref[:, here], ef_ref[...]).astype(jnp.bfloat16)
        return unused

    lax.fori_loop(0, D // block, weights, 0)
    fc_sum = column_sum(ef_ref[...].astype(jnp.float32))

    gain_sum = jnp.zeros((1, D), jnp.float32)
    offset_sum = jnp.zeros((1, D), jnp.float32)
    out_sum = jnp.zeros((1, D), jnp.float32)
    for part in range(parts):
        grad = second.result(part)
        nhat, scale = normalize(h1_ref[span(part * size), :])
        gain_sum = gain_sum + column_sum(grad * nhat)
        offset_sum = offset_sum + column_sum(grad)
        mid = cot_ref[span(mine(part)), :].astype(jnp.float32) + norm_back(grad, nhat, scale, gain)
        mid_grad_ref[span(part * size), :] = mid
        e1 = mid.astype(jnp.bfloat16)
        out_sum = out_sum + column_sum(e1.astype(jnp.float32))
        e1_ref[span(mine(part)), :] = e1
        e_share.copy(part, mine(part)).start()
        head_grad_ref[span(mine(part)), :] = dot_rows(e1, out_w_ref[...]).astype(jnp.bfloat16)
    row = lax.broadcasted_iota(jnp.int32, (8, 1), 0)
    sums_ref[...] = jnp.where(row == 0, gain_sum, jnp.where(row == 1, offset_sum, out_sum))
    fold_copy = swap_with("core", sums_ref, fold_in_ref, fold_sems, 0)
    fold_copy.start()
    for part in range(parts):
        e_share.copy(part, theirs(part)).wait_recv()
        head_grad_ref[span(theirs(part)), :] = dot_rows(e1_ref[span(theirs(part)), :], out_w_ref[...]).astype(
            jnp.bfloat16
        )

    def out_weights(index, unused):
        here = pl.ds(pl.multiple_of(index * block, block), block)
        out_grad_ref[here, :] = dot_columns(e1_ref[:, here], heads_ref[...]).astype(jnp.bfloat16)
        return unused

    lax.fori_loop(0, D // block, out_weights, 0)
    fold_copy.wait()
    sums_ref[...] = jnp.where(row == 3, fc_sum, sums_ref[...] + fold_in_ref[...])
    for part in range(parts):
        c_share.copy(part, mine(part)).wait_send()
        e_share.copy(part, mine(part)).wait_send()


def feed_forward(heads, tokens, cotangent, out_w, fc_w, proj_w, vectors):
    rows, width = heads.shape
    half = rows // 2
    hidden = fc_w.shape[1]
    parts, size = FEED_PARTS, half // FEED_PARTS
    vmem = pl.BlockSpec(memory_space=pltpu.VMEM)
    dma = pltpu.SemaphoreType.DMA
    bf, fl = jnp.bfloat16, jnp.float32
    shape = jax.ShapeDtypeStruct
    return pl.pallas_call(
        feed_kernel,
        out_shape=(
            shape((D, hidden), bf),
            shape((D, hidden), bf),
            shape((D, width), bf),
            shape((rows, width), bf),
            shape((half, D), fl),
            shape((half, D), fl),
            shape((half, D), fl),
            shape((half, D), bf),
            shape((8, D), fl),
        ),
        in_specs=[vmem] * 7,
        out_specs=(vmem,) * 9,
        scratch_shapes=[
            pltpu.VMEM((rows, D), bf),
            pltpu.VMEM((rows, D), bf),
            pltpu.VMEM((rows, hidden), bf),
            pltpu.VMEM((rows, hidden), bf),
            pltpu.VMEM((rows, hidden), fl),
            pltpu.VMEM((half, D), fl),
            pltpu.VMEM((half, D), fl),
            pltpu.VMEM((8, D), fl),
            *TpSum.scratch(parts, size, D),
            *TpSum.scratch(parts, size, D),
            dma((parts,)),
            dma((parts,)),
            dma((parts,)),
            dma((parts,)),
            dma((1,)),
            dma((1,)),
        ],
        name="feed_forward",
        compiler_params=pltpu.CompilerParams(
            collective_id=4, has_side_effects=True, vmem_limit_bytes=VMEM_LIMIT
        ),
    )(heads, tokens, cotangent, out_w, fc_w, proj_w, vectors)


class LateOutput:
    def __init__(self, base, own, other, whole, sems):
        self.base, self.own, self.other, self.whole = base, own, other, whole
        self.half = own.shape[0]
        self.core_in, self.chip_out, self.chip_in = sems[:3]
        self.core_sems, self.chip_sems, self.share_sems = sems[3:5], sems[5:7], sems[7:9]
        self.share = RowShare(whole, self.half, self.share_sems)
        self.core = lax.axis_index("tp") % 2

    COUNT = 9

    def core_copy(self):
        return swap_with("core", self.other, self.core_in, self.core_sems, 0)

    def chip_copy(self):
        return swap_with("chip", self.chip_out, self.chip_in, self.chip_sems, 0)

    def start(self):
        self.core_copy().start()

    def middle(self):
        self.core_copy().wait()
        self.chip_out[...] = (self.own[...] + self.core_in[...].astype(jnp.float32)).astype(jnp.bfloat16)
        self.chip_copy().start()

    def late(self):
        self.chip_copy().wait()
        total = self.chip_out[...].astype(jnp.float32) + self.chip_in[...].astype(jnp.float32)
        here = pl.ds(pl.multiple_of(self.core * self.half, self.half), self.half)
        self.whole[here, :] = (self.base[...] + total).astype(jnp.bfloat16)
        self.share.copy(0, self.core * self.half).start()

    def finish(self):
        self.share.copy(0, (1 - self.core) * self.half).wait_recv()
        self.share.copy(0, self.core * self.half).wait_send()

    @staticmethod
    def scratch(half, width):
        buffer = pltpu.VMEM((half, width), jnp.bfloat16)
        return [buffer] * 3 + [pltpu.SemaphoreType.DMA((1,))] * 6


def finish_kernel(
    levels,
    grads_ref,
    weight_ref,
    tok_ref,
    mid_grad_ref,
    norm_ref,
    blocks_ref,
    small_in_ref,
    tokens_out_ref,
    share_ref,
    small_out_ref,
    own_ref,
    small_ref,
    fold_ref,
    fold_in_ref,
    *rest,
):
    parts = FEED_PARTS
    rows = tok_ref.shape[0]
    half = rows // 2
    size = half // parts
    core = lax.axis_index("tp") % 2
    total = TpSum(*rest[:4], rest[4 : TpSum.COUNT])
    rest = rest[TpSum.COUNT :]
    scatter = Scatter(levels, blocks_ref, *rest[:3], rest[3:7])
    rest = rest[7:]
    small = SmallSum(levels, small_ref, rest[0], rest[1], rest[2:5])
    rest = rest[5:]
    share = RowShare(tokens_out_ref, size, rest[0:2])
    fold_sems = rest[2:4]
    barrier, greetings = greet(levels, True)
    gain = norm_ref[0:1, :]

    def span(start, count=size):
        return pl.ds(pl.multiple_of(start, size), count)

    def mine(part):
        return core * half + part * size

    def theirs(part):
        return (1 - core) * half + part * size

    pl.semaphore_wait(barrier, greetings)
    scatter.start()
    for part in range(parts):
        total.start(part, dot_rows(grads_ref[span(theirs(part)), :], weight_ref[...]))
        own_ref[span(part * size), :] = dot_rows(grads_ref[span(mine(part)), :], weight_ref[...])
    for part in range(parts):
        total.middle(part, own_ref[span(part * size), :])
    scatter.middle()
    gain_sum = jnp.zeros((1, D), jnp.float32)
    offset_sum = jnp.zeros((1, D), jnp.float32)
    for part in range(parts):
        grad = total.result(part)
        nhat, scale = normalize(tok_ref[span(mine(part)), :].astype(jnp.float32))
        gain_sum = gain_sum + column_sum(grad * nhat)
        offset_sum = offset_sum + column_sum(grad)
        out = mid_grad_ref[span(part * size), :] + norm_back(grad, nhat, scale, gain)
        tokens_out_ref[span(mine(part)), :] = out.astype(jnp.bfloat16)
        share.copy(part, mine(part)).start()
    row = lax.broadcasted_iota(jnp.int32, (8, 1), 0)
    fold_ref[...] = jnp.where(row == 0, gain_sum, jnp.where(row == 1, offset_sum, 0.0))
    fold_copy = swap_with("core", fold_ref, fold_in_ref, fold_sems, 0)
    fold_copy.start()
    fold_copy.wait()
    small_ref[8:, :] = small_in_ref[8:, :]
    small_ref[:8, :] = small_in_ref[:8, :] + (fold_ref[...] + fold_in_ref[...])
    small.start()
    small.middle()
    scatter.finish(share_ref)
    small.finish(small_out_ref)
    for part in range(parts):
        share.copy(part, theirs(part)).wait_recv()
        share.copy(part, mine(part)).wait_send()


def finish_layer(levels, grads, weight, tokens, mid_grad, norm, blocks, small):
    rows = tokens.shape[0]
    half = rows // 2
    parts, size = FEED_PARTS, half // FEED_PARTS
    vmem = pl.BlockSpec(memory_space=pltpu.VMEM)
    dma = pltpu.SemaphoreType.DMA
    shape = jax.ShapeDtypeStruct
    return pl.pallas_call(
        functools.partial(finish_kernel, levels),
        out_shape=(
            shape((rows, D), jnp.bfloat16),
            shape(blocks.shape[1:], jnp.float32),
            shape(small.shape, jnp.float32),
        ),
        in_specs=[vmem] * 7,
        out_specs=(vmem,) * 3,
        scratch_shapes=[
            pltpu.VMEM((half, D), jnp.float32),
            pltpu.VMEM(small.shape, jnp.float32),
            pltpu.VMEM((8, D), jnp.float32),
            pltpu.VMEM((8, D), jnp.float32),
            *TpSum.scratch(parts, size, D),
            *Scatter.scratch(levels, *blocks.shape[1:]),
            *SmallSum.scratch(levels, small.shape),
            dma((parts,)),
            dma((parts,)),
            dma((1,)),
            dma((1,)),
        ],
        name="finish_layer",
        compiler_params=pltpu.CompilerParams(
            collective_id=3, has_side_effects=True, vmem_limit_bytes=VMEM_LIMIT
        ),
    )(grads, weight, tokens, mid_grad, norm, blocks, small)


def local(
    tokens,
    cotangent,
    past_states,
    doc_ids,
    cur_book,
    past_book,
    past_age,
    ln1_gain,
    ln1_bias,
    qkv_weight,
    qv_bias,
    out_weight,
    out_bias,
    ln2_gain,
    ln2_bias,
    fc_weight,
    fc_bias,
    proj_weight,
    proj_bias,
    mu_weight,
    sigma_weight,
):
    tok_rows = tokens.shape[0]
    heads_here = mu_weight.shape[0]
    head_cols = qkv_weight.shape[2]
    seq_count = lax.axis_size("seq")
    seq_index = lax.axis_index("seq")
    levels = seq_count // 2
    row_pad = ((0, 6), (0, 0))
    norm_rows = jnp.pad(jnp.stack([ln1_gain, ln1_bias]), row_pad)
    qkv_flat = qkv_weight.reshape(D, 3 * head_cols)
    bias_row = jnp.concatenate([qv_bias[0], jnp.zeros(head_cols, jnp.float32), qv_bias[1]])
    bias_rows = jnp.broadcast_to(bias_row[None], (8, 3 * head_cols))
    reaches = doc_ids >= (seq_index + 1) * tok_rows
    key_mask = jnp.where(reaches, 0.0, NEGATIVE).astype(jnp.bfloat16).reshape(2, tok_rows // 2)
    key_mask = jnp.pad(key_mask, ((0, 14), (0, 2 * head_cols - tok_rows // 2)))

    quarter = D // lax.axis_size("tp")
    columns = lax.dynamic_slice_in_dim(
        past_states, lax.axis_index("tp") * quarter, quarter, axis=1
    )
    half = SEG // 2
    marks = jnp.concatenate([past_book, past_age, jnp.zeros(14, jnp.int32)]).astype(jnp.bfloat16)
    past = jnp.concatenate(
        [
            jnp.concatenate([columns[:half], columns[half:]], axis=1),
            jnp.broadcast_to(marks[:, None], (16, 2 * quarter)),
        ]
    )
    book = jnp.broadcast_to(cur_book.astype(jnp.float32)[:, None], (8, 2 * quarter))
    spots = jnp.pad(jnp.stack([mu_weight, sigma_weight]), ((0, 0), (0, 8 - heads_here), (0, 0)))
    spots = spots.reshape(16, NB)
    table = jnp.asarray(np.stack(coefficient_tables(seq_count // BOOKS, NB, SEG), axis=1))

    normed_one, query_col, kv_col, attended, log_sum, heads_out, coeff, memory, spot_rows = (
        attention_forward(
            levels,
            tokens,
            norm_rows,
            qkv_flat,
            bias_rows,
            doc_ids,
            key_mask,
            past,
            book,
            spots,
            table,
        )
    )
    swap = [(index, index ^ 1) for index in range(seq_count)]
    query_oth = lax.ppermute(query_col, "seq", swap)
    kv_oth = lax.ppermute(kv_col, "seq", swap)

    vectors = jnp.pad(
        jnp.stack([ln2_gain, ln2_bias, out_bias, fc_bias, proj_bias]), ((0, 3), (0, 0))
    )
    proj_grad, fc_grad, out_grad, grad_heads, mid_grad, base, own_two, other_two, mid_sums = (
        feed_forward(heads_out, tokens, cotangent, out_weight, fc_weight, proj_weight, vectors)
    )
    grad_proj_b = jnp.sum(cotangent.astype(jnp.float32), axis=0)

    def shards(grad):
        return grad.astype(jnp.bfloat16).reshape(seq_count, D // seq_count, -1)

    grad_qkv, qkv_grad, bias_grad, spot_grad, proj_share, fc_share, out_share, output = (
        attention_backward(
            levels,
            grad_heads,
            attended,
            log_sum,
            query_col,
            query_oth,
            kv_col,
            kv_oth,
            doc_ids,
            [shards(proj_grad), shards(fc_grad), shards(out_grad)],
            base,
            own_two,
            other_two,
            normed_one,
            coeff,
            memory,
            spot_rows,
            spots,
        )
    )
    bias_sums = jnp.concatenate([bias_grad[0, :head_cols], bias_grad[0, 2 * head_cols :]])
    nothing = jnp.zeros((2, D), jnp.float32)
    small = jnp.concatenate(
        [
            nothing,
            mid_sums[:4],
            grad_proj_b[None],
            jnp.pad(bias_sums[None], ((0, 0), (0, D - 2 * head_cols))),
            spot_grad[:heads_here].reshape(2, D),
            spot_grad[8 : 8 + heads_here].reshape(2, D),
            nothing,
            nothing,
        ]
    )
    grad_tokens, qkv_share, small = finish_layer(
        levels, grad_qkv, qkv_flat, tokens, mid_grad, norm_rows, shards(qkv_grad), small
    )
    return (
        output,
        grad_tokens,
        qkv_share.reshape(-1, 3, head_cols),
        small[7, : 2 * head_cols].reshape(2, head_cols),
        out_share.T,
        small[4],
        fc_share,
        small[5],
        proj_share.T,
        small[6],
        small[0],
        small[1],
        small[2],
        small[3],
        small[8:10].reshape(heads_here, NB),
        small[10:12].reshape(heads_here, NB),
    )


def solution(mesh):
    in_specs = (
        P("seq", None),
        P("seq", None),
        P("seq", None),
        P("seq"),
        P("seq"),
        P("seq"),
        P("seq"),
        P(),
        P(),
        P(None, None, "tp"),
        P(None, "tp"),
        P("tp", None),
        P(),
        P(),
        P(),
        P(None, "tp"),
        P("tp"),
        P("tp", None),
        P(),
        P("tp", None),
        P("tp", None),
    )
    out_specs = (
        P("seq", None),
        P("seq", None),
        P("seq", None, "tp"),
        P(None, "tp"),
        P("tp", "seq"),
        P(),
        P("seq", "tp"),
        P("tp"),
        P("tp", "seq"),
        P(),
        P(),
        P(),
        P(),
        P(),
        P("tp", None),
        P("tp", None),
    )
    return jax.shard_map(local, mesh=mesh, in_specs=in_specs, out_specs=out_specs, check_vma=False)
```

```python
import functools
from types import SimpleNamespace
from typing import NamedTuple

import ml_dtypes
import numpy as np

import jax
import jax.numpy as jnp
from jax import lax
from jax.experimental import pallas as pl
from jax.experimental.pallas import tpu as pltpu
from jax.sharding import PartitionSpec as P

D = 768
DH = 64
NB = 512
SEG = 512
BOOKS = 4


EPS = 1e-05
TAU = 0.75
RIDGE = 1.0
SPREAD = 0.01
NEGATIVE = -1e30
MESH_ID = pl.DeviceIdType.MESH
VMEM_LIMIT = 60 * 2**20


def coefficient_tables(age_count, basis_n, seg_len):
    shrink = TAU ** np.arange(age_count, dtype=np.float64)
    inside = (np.arange(seg_len) + 0.5) / seg_len
    times = shrink[:, None] * (TAU + (1.0 - TAU) * inside[None, :])
    centres = (np.arange(basis_n) + 0.5) / basis_n
    offset = (times[:, None, :] - centres[None, :, None]) * basis_n
    basis = np.exp(-0.5 * offset * offset)
    gram = np.einsum("agx,ahx->gh", basis, basis) + RIDGE * np.eye(basis_n)
    table = np.linalg.solve(gram[None], basis)
    high = table.astype(ml_dtypes.bfloat16)
    lower = (table - high.astype(np.float64)).astype(ml_dtypes.bfloat16)
    return high, lower


LANES_OUT = 256


def head_of_lane(width):
    return lax.broadcasted_iota(jnp.int32, (1, width), 1) // DH


def head_masks(width):
    lane_head = head_of_lane(width)
    return [(lane_head == head).astype(jnp.float32).astype(jnp.bfloat16) for head in range(width // DH)]


def pick_heads(per_head, lane_head):
    chosen = per_head[0]
    for head in range(1, len(per_head)):
        chosen = jnp.where(lane_head == head, per_head[head], chosen)
    return chosen


def dot_rows(left, right):
    return lax.dot_general(left, right, (((1,), (1,)), ((), ())), preferred_element_type=jnp.float32)


def dot_plain(left, right):
    return lax.dot_general(left, right, (((1,), (0,)), ((), ())), preferred_element_type=jnp.float32)


def thirds(value):
    first = value.astype(jnp.bfloat16)
    rest = value - first.astype(jnp.float32)
    second = rest.astype(jnp.bfloat16)
    third = (rest - second.astype(jnp.float32)).astype(jnp.bfloat16)
    return first, second, third


def with_stats(block, stats):
    rows, width = block.shape
    spare = LANES_OUT - width
    lane = lax.broadcasted_iota(jnp.int32, (1, spare), 1)
    tail = jnp.zeros((rows, spare), jnp.float32)
    for index, column in enumerate(stats):
        for part, value in enumerate(thirds(column)):
            tail = jnp.where(lane == 3 * index + part, value.astype(jnp.float32), tail)
    return jnp.concatenate([block, tail.astype(jnp.bfloat16)], axis=1)


def stat_column(extended, width, index):
    lane = lax.broadcasted_iota(jnp.int32, (1, LANES_OUT), 1)
    start = width + 3 * index
    mine = (lane >= start) & (lane < start + 3)
    return jnp.sum(jnp.where(mine, extended.astype(jnp.float32), 0.0), axis=1, keepdims=True)


def stat_rows(extended, width, count):
    row = lax.broadcasted_iota(jnp.int32, (count, LANES_OUT), 0)
    lane = lax.broadcasted_iota(jnp.int32, (count, LANES_OUT), 1)
    start = width + 3 * row
    chooser = ((lane >= start) & (lane < start + 3)).astype(jnp.float32).astype(jnp.bfloat16)
    return dot_rows(chooser, extended)


def greet(levels, whole_tp=False):
    seq, tp = lax.axis_index("seq"), lax.axis_index("tp")
    level, side = seq // 2, seq % 2
    barrier = pltpu.get_barrier_semaphore()
    pl.semaphore_signal(barrier, inc=1, device_id=(2 * level + 1 - side, tp), device_id_type=MESH_ID)

    def one(step, unused):
        other = lax.rem(level + step, levels)
        pl.semaphore_signal(barrier, inc=1, device_id=(2 * other + side, tp), device_id_type=MESH_ID)
        return unused

    lax.fori_loop(1, levels, one, 0)
    if not whole_tp:
        return barrier, levels
    greet_tp()
    return barrier, levels + 2


class MemoryPlace(NamedTuple):
    loose: jax.Array
    centre: jax.Array
    spread: jax.Array
    height: jax.Array
    gap: jax.Array


def memory_place(query, spot_rows, in_head):
    width_sq = 1.0 / (NB * NB)
    centre = 1.0 / (
        1.0 + jnp.exp(-jnp.sum(jnp.where(in_head, query * spot_rows[0:1, :], 0.0), axis=1, keepdims=True))
    )
    loose = jnp.sum(jnp.where(in_head, query * spot_rows[1:2, :], 0.0), axis=1, keepdims=True)
    soft = jnp.maximum(loose, 0.0) + jnp.log(1.0 + jnp.exp(-jnp.abs(loose)))
    spread = SPREAD * soft + width_sq
    height = (1.0 / NB) * lax.rsqrt(spread)
    centres = (lax.broadcasted_iota(jnp.int32, (1, NB), 1).astype(jnp.float32) + 0.5) / NB
    return MemoryPlace(loose, centre, spread, height, centre - centres)


def forward_kernel(
    levels,
    tok_ref,
    norm_ref,
    weight_ref,
    bias_ref,
    doc_col_ref,
    doc_row_ref,
    key_mask_ref,
    past_ref,
    book_ref,
    spot_ref,
    table_ref,
    normed_ref,
    pair_ref,
    kv_out_ref,
    out_ref,
    lse_ref,
    heads_ref,
    coeff_ref,
    mem_ref,
    spot_row_ref,
    top_ref,
    total_ref,
    acc_ref,
    part_ref,
    part_in_ref,
    kv_send,
    kv_recv,
    pair_sem,
    part_sem,
    past_col_ref,
    past_oth_ref,
    table_in_ref,
    past_up,
    past_down,
    past_side,
    coeff_sems,
    table_sem,
):
    seq, tp = lax.axis_index("seq"), lax.axis_index("tp")
    level, side = seq // 2, seq % 2
    rows = tok_ref.shape[0]
    width = pair_ref.shape[2]
    heads = width // DH
    partner = (2 * level + 1 - side, tp)
    lane_head = head_of_lane(width)
    head_mask = head_masks(width)
    barrier, greetings = greet(levels, True)

    chunk = rows // 2
    past_col_ref[level] = past_ref[...]

    def past_copy(direction, from_level):
        block = past_col_ref.at[from_level]
        if direction == "side":
            sems, target, place = past_side, partner, past_oth_ref.at[from_level]
        elif direction == "up":
            sems, target, place = past_up, (lax.rem(2 * level + 2, 2 * levels) + side, tp), block
        else:
            sems, target, place = past_down, (lax.rem(2 * (level + levels - 1), 2 * levels) + side, tp), block
        return pltpu.make_async_remote_copy(
            block,
            place,
            sems.at[0, from_level],
            sems.at[1, from_level],
            device_id=target,
            device_id_type=MESH_ID,
        )

    pl.semaphore_wait(barrier, greetings)

    def pass_past(from_level, up, down):
        past_copy("side", from_level).start()
        if up:

            @pl.when(level < levels - 1)
            def _():
                past_copy("up", from_level).start()

        if down:

            @pl.when(level > 0)
            def _():
                past_copy("down", from_level).start()

    pass_past(level, True, True)

    def project(index, unused):
        here = pl.ds(pl.multiple_of(index * chunk, chunk), chunk)
        x = tok_ref[here, :].astype(jnp.float32)
        centred = x - jnp.mean(x, axis=1, keepdims=True)
        variance = jnp.mean(centred * centred, axis=1, keepdims=True)
        a = centred * lax.rsqrt(variance + EPS) * norm_ref[0:1, :] + norm_ref[1:2, :]
        a = a.astype(jnp.bfloat16)
        normed_ref[here, :] = a
        mixed = (dot_plain(a, weight_ref[...]) + bias_ref[0:1, :]).astype(jnp.bfloat16)
        query = mixed[:, :width] * jnp.bfloat16(DH**-0.5)
        pair_ref[0, here, :] = query
        kv_out_ref[level, here, :] = mixed[:, width:]
        return unused

    lax.fori_loop(0, rows // chunk, project, 0)
    kv_out_ref[level, rows:, :] = key_mask_ref[...]

    pair_copy = pltpu.make_async_remote_copy(
        pair_ref.at[0], pair_ref.at[1], pair_sem.at[0], pair_sem.at[1], device_id=partner, device_id_type=MESH_ID
    )
    pair_copy.start()

    def kv_copy(from_level):
        return pltpu.make_async_remote_copy(
            kv_out_ref.at[from_level],
            kv_out_ref.at[from_level],
            kv_send.at[from_level],
            kv_recv.at[from_level],
            device_id=(lax.rem(2 * level + 2, 2 * levels) + side, tp),
            device_id_type=MESH_ID,
        )

    @pl.when(level < levels - 1)
    def _():
        kv_copy(level).start()

    top_ref[...] = jnp.full(top_ref.shape, NEGATIVE, jnp.float32)
    total_ref[...] = jnp.zeros(total_ref.shape, jnp.float32)
    acc_ref[...] = jnp.zeros(acc_ref.shape, jnp.float32)

    doc_first = doc_row_ref[0:1, 0:1]
    def reach_of(here):
        docs = doc_col_ref[here, :]
        last = (level == levels - 1) & (side == 1)
        return jnp.where(last & (docs != doc_first), NEGATIVE, 0.0)

    def fold(slot, from_level, mask_kind):
        mask_rows = kv_out_ref[from_level, rows:, :].astype(jnp.float32)
        key_mask = jnp.concatenate([mask_rows[0:1, : rows // 2], mask_rows[1:2, : rows // 2]], axis=1)

        def part(index, unused):
            here = pl.ds(pl.multiple_of(index * chunk, chunk), chunk)
            query = pair_ref[slot, here, :]
            keys = kv_out_ref[from_level, :rows, :width]
            vals = kv_out_ref[from_level, :rows, width:]
            if mask_kind == "own":
                q_pos = index * chunk + lax.broadcasted_iota(jnp.int32, (chunk, rows), 0)
                k_pos = lax.broadcasted_iota(jnp.int32, (chunk, rows), 1)
                visible = (q_pos >= k_pos) & (doc_col_ref[here, :] == doc_row_ref[0:1, :])
            products, scales = [], []
            for head in range(heads):
                scores = dot_rows(query * head_mask[head], keys)
                old_top = top_ref[slot, head, here, :]
                if mask_kind == "own":
                    scores = jnp.where(visible, scores, NEGATIVE)
                    reach = 0.0
                else:
                    scores = scores + key_mask
                    reach = jnp.where(slot == 0, reach_of(here), 0.0)
                new_top = jnp.maximum(old_top, jnp.max(scores, axis=1, keepdims=True) + reach)
                weights = jnp.exp(scores - (new_top - reach))
                scale = jnp.exp(old_top - new_top)
                top_ref[slot, head, here, :] = new_top
                total_ref[slot, head, here, :] = total_ref[slot, head, here, :] * scale + jnp.sum(
                    weights, axis=1, keepdims=True
                )
                products.append(dot_plain(weights.astype(jnp.bfloat16), vals))
                scales.append(scale)
            acc_ref[slot, here, :] = acc_ref[slot, here, :] * pick_heads(scales, lane_head) + pick_heads(
                products, lane_head
            )
            return unused

        lax.fori_loop(0, rows // chunk, part, 0)

    fold(0, level, "own")
    pair_copy.wait()

    @pl.when(side == 0)
    def _():
        fold(1, level, "off")

    def keys_arrived(step):
        from_level = level - step
        kv_copy(from_level).wait_recv()

        @pl.when(level < levels - 1)
        def _():
            kv_copy(from_level).start()

        def both(slot, inner):
            fold(slot, from_level, "off")
            return inner

        lax.fori_loop(0, 2, both, 0)

    def arrived(step, unused):
        @pl.when(level >= step)
        def _():
            past_copy("up", level - step).wait_recv()
            pass_past(level - step, True, False)

        @pl.when(level + step < levels)
        def _():
            past_copy("down", level + step).wait_recv()
            pass_past(level + step, False, True)

        @pl.when((level >= step) & (step < levels - 1))
        def _():
            keys_arrived(step)

        return unused

    lax.fori_loop(1, levels, arrived, 0)

    def from_side(other, unused):
        past_copy("side", other).wait_recv()
        return unused

    lax.fori_loop(0, levels, from_side, 0)
    own_book = book_ref[0:1, :]
    time_half = rows // 2
    ages = table_ref.shape[0]

    def one_age(age, total):
        table_copy = pltpu.make_async_copy(table_ref.at[age], table_in_ref, table_sem)
        table_copy.start()

        def one_level(other, found):
            for blocks_ref in (past_col_ref, past_oth_ref):
                mark = blocks_ref[other, time_half:, :].astype(jnp.float32)
                chosen = (mark[0:1, :] == own_book) & (mark[1:2, :] == age.astype(jnp.float32))
                found = jnp.where(chosen, blocks_ref[other, :time_half, :].astype(jnp.float32), found)
            return found

        found = lax.fori_loop(
            0, levels, one_level, jnp.zeros((time_half, 2 * width), jnp.float32)
        ).astype(jnp.bfloat16)
        table_copy.wait()
        for index in range(2):
            table = table_in_ref[index]
            total = total + (
                dot_plain(table[:, :time_half], found)[:, :width]
                + dot_plain(table[:, time_half:], found)[:, width:]
            )
        return total

    coeff = lax.fori_loop(0, ages, one_age, jnp.zeros((NB, width), jnp.float32))
    coeff_ref[tp] = coeff.astype(jnp.bfloat16)

    def coeff_copy(kind, slot, index):
        return swap_with(kind, coeff_ref.at[slot], coeff_ref.at[slot], (coeff_sems.at[0], coeff_sems.at[1]), index)

    core_mate, chip_mate = tp + 1 - 2 * (tp % 2), lax.rem(tp + 2, 4)
    coeff_copy("chip", tp, 0).start()
    coeff_copy("core", tp, 1).start()

    @pl.when(level == levels - 1)
    def _():
        keys_arrived(levels - 1)

    def finish(index, unused):
        here = pl.ds(pl.multiple_of(index * chunk, chunk), chunk)
        totals = [total_ref[1, head, here, :] for head in range(heads)]
        tops = [top_ref[1, head, here, :] for head in range(heads)]
        some = [value > 0.0 for value in totals]
        inverse = [jnp.where(ok, 1.0 / jnp.where(ok, value, 1.0), 0.0) for ok, value in zip(some, totals)]
        logs = [
            jnp.where(ok, top + jnp.log(jnp.where(ok, value, 1.0)), NEGATIVE)
            for ok, top, value in zip(some, tops, totals)
        ]
        share = (acc_ref[1, here, :] * pick_heads(inverse, lane_head)).astype(jnp.bfloat16)
        part_ref[here, :] = with_stats(share, logs)
        return unused

    lax.fori_loop(0, rows // chunk, finish, 0)
    part_copy = pltpu.make_async_remote_copy(
        part_ref, part_in_ref, part_sem.at[0], part_sem.at[1], device_id=partner, device_id_type=MESH_ID
    )
    part_copy.start()

    coeff_copy("chip", chip_mate, 0).wait_recv()
    coeff_copy("core", chip_mate, 2).start()
    coeff_copy("core", core_mate, 1).wait_recv()
    coeff_copy("core", lax.rem(core_mate + 2, 4), 2).wait_recv()
    memory = jnp.zeros((NB, 2 * width), jnp.float32)
    for slot in range(4):
        memory = memory + dot_plain(
            coeff_ref[slot], weight_ref[slot * width : (slot + 1) * width, width:]
        )
    mem_ref[...] = memory.astype(jnp.bfloat16)
    for index in range(2):
        spots = spot_ref[8 * index : 8 * index + 8, :]
        row = sum(dot_plain(third, mem_ref[:, :width]) for third in thirds(spots))
        spot_row_ref[index : index + 1, :] = pick_heads(
            [row[head : head + 1, :] for head in range(heads)], lane_head
        )
    part_copy.wait()

    def merge(index, unused):
        here = pl.ds(pl.multiple_of(index * chunk, chunk), chunk)
        reach = reach_of(here)
        received = part_in_ref[here, :]
        mine, theirs, columns = [], [], []
        for head in range(heads):
            total = total_ref[0, head, here, :]
            own_log = top_ref[0, head, here, :] + jnp.log(total)
            other_log = stat_column(received, width, head) + reach
            high = jnp.maximum(own_log, other_log)
            both_log = high + jnp.log(jnp.exp(own_log - high) + jnp.exp(other_log - high))
            mine.append(jnp.exp(own_log - both_log) / total)
            theirs.append(jnp.exp(other_log - both_log))
            columns.append(both_log)
        attended = acc_ref[0, here, :] * pick_heads(mine, lane_head) + received[:, :width].astype(
            jnp.float32
        ) * pick_heads(theirs, lane_head)
        out_ref[here, :] = attended
        query = pair_ref[0, here, :].astype(jnp.float32)
        reads = []
        for head in range(heads):
            place = memory_place(query, spot_row_ref[0:2, :], lane_head == head)
            density = place.height * jnp.exp(place.gap * place.gap * (-0.5 / place.spread))
            reads.append(dot_plain(density.astype(jnp.bfloat16), mem_ref[:, width:]))
        heads_ref[here, :] = (attended + pick_heads(reads, lane_head)).astype(jnp.bfloat16)
        lane = lax.broadcasted_iota(jnp.int32, (1, 8), 1)
        packed = jnp.zeros((chunk, 8), jnp.float32)
        for head in range(heads):
            packed = jnp.where(lane == head, columns[head], packed)
        lse_ref[here, :] = packed
        return unused

    lax.fori_loop(0, rows // chunk, merge, 0)

    coeff_copy("chip", tp, 0).wait_send()
    coeff_copy("core", tp, 1).wait_send()
    coeff_copy("core", chip_mate, 2).wait_send()

    def past_sent(other, unused):
        past_copy("side", other).wait_send()

        @pl.when((level < levels - 1) & (other <= level))
        def _():
            past_copy("up", other).wait_send()

        @pl.when((level > 0) & (other >= level))
        def _():
            past_copy("down", other).wait_send()

        return unused

    lax.fori_loop(0, levels, past_sent, 0)

    @pl.when(level < levels - 1)
    def _():
        def sent_up(from_level, unused):
            kv_copy(from_level).wait_send()
            return unused

        lax.fori_loop(0, level + 1, sent_up, 0)


def attention_forward(levels, tokens, norm, weight, bias, doc_ids, key_mask, past, book, spots, table):
    rows = tokens.shape[0]
    width = weight.shape[1] // 3
    heads = width // DH
    vmem = pl.BlockSpec(memory_space=pltpu.VMEM)
    dma = pltpu.SemaphoreType.DMA
    return pl.pallas_call(
        functools.partial(forward_kernel, levels),
        out_shape=(
            jax.ShapeDtypeStruct((rows, D), jnp.bfloat16),
            jax.ShapeDtypeStruct((2, rows, width), jnp.bfloat16),
            jax.ShapeDtypeStruct((levels, rows + 16, 2 * width), jnp.bfloat16),
            jax.ShapeDtypeStruct((rows, width), jnp.float32),
            jax.ShapeDtypeStruct((rows, 8), jnp.float32),
            jax.ShapeDtypeStruct((rows, width), jnp.bfloat16),
            jax.ShapeDtypeStruct((4, NB, width), jnp.bfloat16),
            jax.ShapeDtypeStruct((NB, 2 * width), jnp.bfloat16),
            jax.ShapeDtypeStruct((8, width), jnp.float32),
        ),
        in_specs=[vmem] * 10 + [pl.BlockSpec(memory_space=pl.ANY)],
        out_specs=(vmem,) * 9,
        scratch_shapes=[
            pltpu.VMEM((2, heads, rows, 1), jnp.float32),
            pltpu.VMEM((2, heads, rows, 1), jnp.float32),
            pltpu.VMEM((2, rows, width), jnp.float32),
            pltpu.VMEM((rows, LANES_OUT), jnp.bfloat16),
            pltpu.VMEM((rows, LANES_OUT), jnp.bfloat16),
            dma((levels,)),
            dma((levels,)),
            dma((2,)),
            dma((2,)),
            pltpu.VMEM((levels,) + past.shape, jnp.bfloat16),
            pltpu.VMEM((levels,) + past.shape, jnp.bfloat16),
            pltpu.VMEM(table.shape[1:], jnp.bfloat16),
            dma((2, levels)),
            dma((2, levels)),
            dma((2, levels)),
            dma((2, 3)),
            dma(()),
        ],
        name="attention_forward",
        compiler_params=pltpu.CompilerParams(
            collective_id=1, has_side_effects=True, vmem_limit_bytes=VMEM_LIMIT
        ),
    )(
        tokens,
        norm,
        weight,
        bias,
        doc_ids[:, None],
        doc_ids[None, :],
        key_mask,
        past,
        book,
        spots,
        table,
    )


def column_copy(block_ref, from_level, landing_ref, send_sem, recv_sem, to_level):
    seq, tp = lax.axis_index("seq"), lax.axis_index("tp")
    return pltpu.make_async_remote_copy(
        block_ref,
        landing_ref.at[from_level],
        send_sem.at[to_level],
        recv_sem.at[from_level],
        device_id=(2 * to_level + seq % 2, tp),
        device_id_type=MESH_ID,
    )


class Scatter:
    def __init__(self, levels, blocks, plane_in, plane_sum, column_in, sems):
        self.levels, self.blocks = levels, blocks
        self.plane_in, self.plane_sum, self.column_in = plane_in, plane_sum, column_in
        self.plane_send, self.plane_recv, self.column_send, self.column_recv = sems
        seq, tp = lax.axis_index("seq"), lax.axis_index("tp")
        self.level, self.side, self.tp = seq // 2, seq % 2, tp

    def plane_copy(self, to_level):
        return pltpu.make_async_remote_copy(
            self.blocks.at[2 * to_level + 1 - self.side],
            self.plane_in.at[to_level],
            self.plane_send.at[to_level],
            self.plane_recv.at[to_level],
            device_id=(2 * self.level + 1 - self.side, self.tp),
            device_id_type=MESH_ID,
        )

    def swap_copy(self, from_level, to_level):
        return column_copy(
            self.plane_sum.at[to_level], from_level, self.column_in, self.column_send, self.column_recv, to_level
        )

    def loop(self, first, body):
        def one(step, unused):
            body(lax.rem(self.level + step, self.levels))
            return unused

        lax.fori_loop(first, self.levels, one, 0)

    def start(self):
        self.loop(0, lambda other: self.plane_copy(other).start())

    def middle(self):
        def one(other):
            self.plane_copy(other).wait_recv()
            total = self.blocks[2 * other + self.side].astype(jnp.float32) + self.plane_in[other].astype(
                jnp.float32
            )
            self.plane_sum[other] = total.astype(jnp.bfloat16)
            self.swap_copy(self.level, other).start()

        self.loop(1, one)

    def finish(self, out_ref):
        self.plane_copy(self.level).wait_recv()
        out_ref[...] = self.blocks[2 * self.level + self.side].astype(jnp.float32) + self.plane_in[
            self.level
        ].astype(jnp.float32)

        def one(other):
            self.swap_copy(other, self.level).wait_recv()
            out_ref[...] += self.column_in[other].astype(jnp.float32)

        self.loop(1, one)
        self.loop(0, lambda other: self.plane_copy(other).wait_send())
        self.loop(1, lambda other: self.swap_copy(self.level, other).wait_send())

    @staticmethod
    def scratch(levels, rows, width):
        buffer = pltpu.VMEM((levels, rows, width), jnp.bfloat16)
        return [buffer] * 3 + [pltpu.SemaphoreType.DMA((levels,))] * 4


class SmallSum:
    def __init__(self, levels, small, plane_in, column_in, sems):
        self.levels, self.small, self.plane_in, self.column_in = levels, small, plane_in, column_in
        self.plane_sem, self.column_send, self.column_recv = sems
        seq, tp = lax.axis_index("seq"), lax.axis_index("tp")
        self.level, self.side, self.tp = seq // 2, seq % 2, tp

    def plane_copy(self):
        return pltpu.make_async_remote_copy(
            self.small,
            self.plane_in,
            self.plane_sem.at[0],
            self.plane_sem.at[1],
            device_id=(2 * self.level + 1 - self.side, self.tp),
            device_id_type=MESH_ID,
        )

    def swap_copy(self, from_level, to_level):
        return column_copy(
            self.column_in.at[from_level], from_level, self.column_in, self.column_send, self.column_recv, to_level
        )

    def loop(self, body):
        def one(step, unused):
            body(lax.rem(self.level + step, self.levels))
            return unused

        lax.fori_loop(1, self.levels, one, 0)

    def start(self):
        self.plane_copy().start()

    def middle(self):
        self.plane_copy().wait()
        self.column_in[self.level] = self.small[...] + self.plane_in[...]
        self.loop(lambda other: self.swap_copy(self.level, other).start())

    def finish(self, out_ref):
        self.loop(lambda other: self.swap_copy(other, self.level).wait_recv())
        self.loop(lambda other: self.swap_copy(self.level, other).wait_send())
        out_ref[...] = self.column_in[0]

        def one(other, unused):
            out_ref[...] += self.column_in[other]
            return unused

        lax.fori_loop(1, self.levels, one, 0)

    @staticmethod
    def scratch(levels, shape):
        dma = pltpu.SemaphoreType.DMA
        return [
            pltpu.VMEM(shape, jnp.float32),
            pltpu.VMEM((levels,) + shape, jnp.float32),
            dma((2,)),
            dma((levels,)),
            dma((levels,)),
        ]


def tp_partner(kind):
    seq, tp = lax.axis_index("seq"), lax.axis_index("tp")
    if kind == "core":
        return (seq, tp + 1 - 2 * (tp % 2))
    return (seq, lax.rem(tp + 2, 4))


def greet_tp():
    barrier = pltpu.get_barrier_semaphore()
    for kind in ("core", "chip"):
        pl.semaphore_signal(barrier, inc=1, device_id=tp_partner(kind), device_id_type=MESH_ID)
    return barrier, 2


def swap_with(kind, source, target, sems, index):
    send, recv = sems
    return pltpu.make_async_remote_copy(
        source, target, send.at[index], recv.at[index], device_id=tp_partner(kind), device_id_type=MESH_ID
    )


class TpSum:
    def __init__(self, core_out, core_in, chip_out, chip_in, sems):
        self.core_out, self.core_in, self.chip_out, self.chip_in = core_out, core_in, chip_out, chip_in
        self.core_sems, self.chip_sems = sems[:2], sems[2:]

    def core_copy(self, part):
        return swap_with("core", self.core_out.at[part], self.core_in.at[part], self.core_sems, part)

    def chip_copy(self, part):
        return swap_with("chip", self.chip_out.at[part], self.chip_in.at[part], self.chip_sems, part)

    def start(self, part, for_other_core):
        self.core_out[part] = for_other_core.astype(jnp.bfloat16)
        self.core_copy(part).start()

    def middle(self, part, own):
        self.core_copy(part).wait()
        self.chip_out[part] = (own + self.core_in[part].astype(jnp.float32)).astype(jnp.bfloat16)
        self.chip_copy(part).start()

    def result(self, part):
        self.chip_copy(part).wait()
        return self.chip_out[part].astype(jnp.float32) + self.chip_in[part].astype(jnp.float32)

    @staticmethod
    def scratch(parts, rows, width):
        buffer = pltpu.VMEM((parts, rows, width), jnp.bfloat16)
        return [buffer] * 4 + [pltpu.SemaphoreType.DMA((parts,))] * 4

    COUNT = 8


class RowShare:
    def __init__(self, whole, rows, sems):
        self.whole, self.rows, self.sems = whole, rows, sems

    def copy(self, part, start):
        here = self.whole.at[pl.ds(pl.multiple_of(start, self.rows), self.rows), :]
        return swap_with("core", here, here, self.sems, part)


def normalize(v):
    centred = v - jnp.mean(v, axis=1, keepdims=True)
    scale = lax.rsqrt(jnp.mean(centred * centred, axis=1, keepdims=True) + EPS)
    return centred * scale, scale


def norm_back(grad, nhat, scale, gain):
    inner = grad * gain
    return (
        inner
        - jnp.mean(inner, axis=1, keepdims=True)
        - nhat * jnp.mean(inner * nhat, axis=1, keepdims=True)
    ) * scale


def gelu_and_slope(f):
    root = (2.0 / np.pi) ** 0.5
    square = f * f
    bend = jnp.tanh(root * f * (1.0 + 0.044715 * square))
    half = 0.5 * (1.0 + bend)
    slope = half + 0.5 * f * (1.0 - bend * bend) * (root * (1.0 + 3.0 * 0.044715 * square))
    return f * half, slope


def dot_columns(left, right):
    return lax.dot_general(left, right, (((0,), (0,)), ((), ())), preferred_element_type=jnp.float32)


def column_sum(v):
    return jnp.sum(v, axis=0, keepdims=True)


class LateOutput:
    def __init__(self, base, own, other, whole, sems):
        self.base, self.own, self.other, self.whole = base, own, other, whole
        self.half = own.shape[0]
        self.core_in, self.chip_out, self.chip_in = sems[:3]
        self.core_sems, self.chip_sems, self.share_sems = sems[3:5], sems[5:7], sems[7:9]
        self.share = RowShare(whole, self.half, self.share_sems)
        self.core = lax.axis_index("tp") % 2

    COUNT = 9

    def core_copy(self):
        return swap_with("core", self.other, self.core_in, self.core_sems, 0)

    def chip_copy(self):
        return swap_with("chip", self.chip_out, self.chip_in, self.chip_sems, 0)

    def start(self):
        self.core_copy().start()

    def middle(self):
        self.core_copy().wait()
        self.chip_out[...] = (self.own[...] + self.core_in[...].astype(jnp.float32)).astype(jnp.bfloat16)
        self.chip_copy().start()

    def late(self):
        self.chip_copy().wait()
        total = self.chip_out[...].astype(jnp.float32) + self.chip_in[...].astype(jnp.float32)
        here = pl.ds(pl.multiple_of(self.core * self.half, self.half), self.half)
        self.whole[here, :] = (self.base[...] + total).astype(jnp.bfloat16)
        self.share.copy(0, self.core * self.half).start()

    def finish(self):
        self.share.copy(0, (1 - self.core) * self.half).wait_recv()
        self.share.copy(0, self.core * self.half).wait_send()

    @staticmethod
    def scratch(half, width):
        buffer = pltpu.VMEM((half, width), jnp.bfloat16)
        return [buffer] * 3 + [pltpu.SemaphoreType.DMA((1,))] * 6


PARTS = 2


def back_kernel(levels, names, *refs):
    r = SimpleNamespace(**dict(zip(names, refs)))
    seq, tp = lax.axis_index("seq"), lax.axis_index("tp")
    level, side, core = seq // 2, seq % 2, tp % 2
    rows, width = r.heads.shape
    heads = width // DH
    half = rows // 2
    size = half // PARTS
    partner = (2 * level + 1 - side, tp)
    lane_head = head_of_lane(width)
    head_mask = head_masks(width)
    chunk = rows // 2
    staged = hasattr(r, "stage_query")

    first, second, third = (
        TpSum(*(getattr(r, f"{name}_{i}") for i in range(4)), [getattr(r, f"{name}_{i}") for i in range(4, 8)])
        for name in ("first", "second", "third")
    )
    scatters = [
        Scatter(
            levels,
            getattr(r, f"{name}_blocks"),
            *(getattr(r, f"{name}_{i}") for i in range(3)),
            [getattr(r, f"{name}_{i}") for i in range(3, 7)],
        )
        for name in ("proj", "fc", "out", "qkv")
    ]
    small = SmallSum(levels, r.small, r.small_0, r.small_1, (r.small_2, r.small_3, r.small_4))
    late = LateOutput(
        r.base, r.own_two, r.other_two, r.output, [getattr(r, f"late_{i}") for i in range(LateOutput.COUNT)]
    )
    c_share = RowShare(r.c, size, (r.share_0, r.share_1))
    e_share = RowShare(r.e1, size, (r.share_2, r.share_3))
    token_share = RowShare(r.tokens_out, size, (r.share_4, r.share_5))
    gain, offset, out_b, fc_b, proj_b, first_gain = (r.vec[i : i + 1, :] for i in range(6))
    barrier, greetings = greet(levels, True)

    def span(start, count=size):
        return pl.ds(pl.multiple_of(start, size), count)

    def mine(part):
        return core * half + part * size

    def theirs(part):
        return (1 - core) * half + part * size

    def block_of(blocks_ref, from_level, place):
        if not staged:
            return blocks_ref.at[from_level]
        target = getattr(r, "stage_" + place)
        copy = pltpu.make_async_copy(blocks_ref.at[from_level], target, r.stage_sem)
        copy.start()
        copy.wait()
        return target

    def down_copy(source_ref, landing_ref, sems, from_level, to_level):
        send, recv = sems
        return pltpu.make_async_remote_copy(
            source_ref,
            landing_ref.at[from_level],
            send.at[to_level],
            recv.at[from_level],
            device_id=(2 * to_level + side, tp),
            device_id_type=MESH_ID,
        )

    def side_copy(source_ref, landing_ref, sems, from_level):
        send, recv = sems
        return pltpu.make_async_remote_copy(
            source_ref,
            landing_ref.at[from_level],
            send.at[from_level],
            recv.at[from_level],
            device_id=partner,
            device_id_type=MESH_ID,
        )

    def query_down(from_level, to_level):
        return down_copy(r.pair.at[0], r.query_col, (r.qd_send, r.qd_recv), from_level, to_level)

    def query_side(from_level):
        return side_copy(r.query_col.at[from_level], r.query_oth, (r.qs_send, r.qs_recv), from_level)

    def grad_down(from_level, to_level):
        return down_copy(r.far, r.grad_col, (r.gd_send, r.gd_recv), from_level, to_level)

    def grad_side(from_level):
        return side_copy(r.grad_col.at[from_level], r.grad_oth, (r.gs_send, r.gs_recv), from_level)

    def own_grad_side():
        return side_copy(r.far, r.grad_oth, (r.gs_send, r.gs_recv), level)

    def each_below(body):
        def one(step, unused):
            body(level - step)
            return unused

        lax.fori_loop(1, level + 1, one, 0)

    def each_above(body):
        def one(step, unused):
            body(level + step)
            return unused

        lax.fori_loop(1, levels - level, one, 0)

    pl.semaphore_wait(barrier, greetings)
    each_below(lambda other: query_down(level, other).start())

    for part in range(PARTS):
        first.start(part, dot_plain(r.heads[span(theirs(part)), :], r.out_w[...]))
        r.own[span(part * size), :] = dot_plain(r.heads[span(mine(part)), :], r.out_w[...])
    for part in range(PARTS):
        first.middle(part, r.own[span(part * size), :])

    def early(index, unused):
        here = span(index * size)
        r.pull[here, :] = dot_rows(r.cot[here, :], r.proj_w[...])
        return unused

    lax.fori_loop(0, rows // size, early, 0)
    r.small[...] = jnp.zeros(r.small.shape, jnp.float32)
    r.fold[...] = jnp.zeros(r.fold.shape, jnp.float32)
    r.small[6:7, :] = column_sum(r.cot[...].astype(jnp.float32))

    def feed(start):
        here = span(start)
        f = dot_plain(r.c[here, :], r.fc_w[...]) + fc_b
        u, slope = gelu_and_slope(f)
        r.u[here, :] = u.astype(jnp.bfloat16)
        ef = (r.pull[here, :] * slope).astype(jnp.bfloat16)
        r.ef[here, :] = ef
        return dot_rows(ef, r.fc_w[...])

    for part in range(PARTS):
        total = first.result(part) + out_b
        h1 = r.tok[span(mine(part)), :].astype(jnp.float32) + total
        r.h1[span(part * size), :] = h1
        nhat, scale = normalize(h1)
        r.c[span(mine(part)), :] = (nhat * gain + offset).astype(jnp.bfloat16)
        c_share.copy(part, mine(part)).start()
        r.own[span(part * size), :] = feed(mine(part))
        c_share.copy(part, theirs(part)).wait_recv()
        second.start(part, feed(theirs(part)))
        r.other_two[span(part * size), :] = dot_plain(r.u[span(theirs(part)), :], r.proj_w[...]).astype(
            jnp.bfloat16
        )
        r.own_two[span(part * size), :] = dot_plain(r.u[span(mine(part)), :], r.proj_w[...])
        second.middle(part, r.own[span(part * size), :])

    r.base[...] = r.h1[...] + proj_b
    bite = 384

    def weight_blocks(blocks_ref, left_ref, right, extra=None):
        slab = blocks_ref.shape[1]
        for index in range(D // bite):
            value = dot_columns(left_ref[:, index * bite : (index + 1) * bite], right)
            if extra is not None:
                value = value + extra[index * bite : (index + 1) * bite, :]
            for place in range(bite // slab):
                blocks_ref[index * (bite // slab) + place] = value[
                    place * slab : (place + 1) * slab
                ].astype(jnp.bfloat16)

    weight_blocks(r.proj_blocks, r.cot, r.u[...])
    scatters[0].start()
    weight_blocks(r.fc_blocks, r.c, r.ef[...])
    scatters[1].start()

    def query_on(other):
        query_down(other, level).wait_recv()
        query_side(other).start()

    each_above(query_on)

    gain_sum = jnp.zeros((1, D), jnp.float32)
    offset_sum = jnp.zeros((1, D), jnp.float32)
    out_sum = jnp.zeros((1, D), jnp.float32)
    for part in range(PARTS):
        grad = second.result(part)
        nhat, scale = normalize(r.h1[span(part * size), :])
        gain_sum = gain_sum + column_sum(grad * nhat)
        offset_sum = offset_sum + column_sum(grad)
        mid = r.cot[span(mine(part)), :].astype(jnp.float32) + norm_back(grad, nhat, scale, gain)
        r.mid[span(part * size), :] = mid
        e1 = mid.astype(jnp.bfloat16)
        out_sum = out_sum + column_sum(e1.astype(jnp.float32))
        r.e1[span(mine(part)), :] = e1
        e_share.copy(part, mine(part)).start()
        r.grad[span(mine(part)), :] = dot_rows(e1, r.out_w[...]).astype(jnp.bfloat16)
    r.fold[2:3, :] = gain_sum
    r.fold[3:4, :] = offset_sum
    r.fold[4:5, :] = out_sum
    for part in range(PARTS):
        e_share.copy(part, theirs(part)).wait_recv()
        r.grad[span(theirs(part)), :] = dot_rows(r.e1[span(theirs(part)), :], r.out_w[...]).astype(jnp.bfloat16)

    doc_first = r.doc_row[0:1, 0:1]
    last = (level == levels - 1) & (side == 1)

    def prepare(index, unused):
        here = pl.ds(pl.multiple_of(index * chunk, chunk), chunk)
        grad = r.grad[here, :]
        product = grad.astype(jnp.float32) * r.attended[here, :]
        far = jnp.where(last & (r.doc_col[here, :] != doc_first), -NEGATIVE, 0.0)
        lses = [r.lse[here, head : head + 1] for head in range(heads)]
        deltas = [
            jnp.sum(jnp.where(lane_head == head, product, 0.0), axis=1, keepdims=True)
            for head in range(heads)
        ]
        r.near[here, :] = with_stats(grad, lses + deltas)
        r.far[here, :] = with_stats(grad, [lse + far for lse in lses] + deltas)
        for head in range(heads):
            r.near_lse[head, here, :] = lses[head]
            r.stat[0, head, here, :] = lses[head] + far
            r.stat[0, heads + head, here, :] = deltas[head]
        return unused

    lax.fori_loop(0, rows // chunk, prepare, 0)
    own_grad_side().start()
    each_below(lambda other: grad_down(level, other).start())
    late.start()
    weight_blocks(r.out_blocks, r.e1, r.heads[...])
    scatters[2].start()
    r.small[5:6, :] = column_sum(r.ef[...].astype(jnp.float32))

    r.mem_acc[...] = jnp.zeros(r.mem_acc.shape, jnp.float32)
    r.pulls[...] = jnp.zeros(r.pulls.shape, jnp.float32)

    def memory_back(index, unused):
        here = pl.ds(pl.multiple_of(index * chunk, chunk), chunk)
        query = r.pair[0, here, :].astype(jnp.float32)
        grad = r.grad[here, :]
        val_parts, mu_pulls, sigma_pulls = [], [], []
        for head in range(heads):
            place = memory_place(query, r.spot_rows[0:2, :], lane_head == head)
            slope = place.gap / place.spread
            square = place.gap * slope
            density = place.height * jnp.exp(-0.5 * square)
            val_parts.append(dot_columns(density.astype(jnp.bfloat16), grad))
            weighed = dot_rows(grad * head_mask[head], r.mem[:, width:]) * density
            to_centre = -jnp.sum(weighed * slope, axis=1, keepdims=True)
            to_spread = 0.5 * jnp.sum(weighed * (square - 1.0), axis=1, keepdims=True) / place.spread
            mu_pulls.append(to_centre * place.centre * (1.0 - place.centre))
            sigma_pulls.append(to_spread * SPREAD / (1.0 + jnp.exp(-place.loose)))
        mu_pull, sigma_pull = pick_heads(mu_pulls, lane_head), pick_heads(sigma_pulls, lane_head)
        r.dq[0, here, :] = mu_pull * r.spot_rows[0:1, :] + sigma_pull * r.spot_rows[1:2, :]
        r.mem_acc[...] += pick_heads(val_parts, lane_head)
        r.pulls[0:1, :] += column_sum(mu_pull * query)
        r.pulls[1:2, :] += column_sum(sigma_pull * query)
        return unused

    lax.fori_loop(0, rows // chunk, memory_back, 0)
    by_head = lax.broadcasted_iota(jnp.int32, (8, 1), 0) == lane_head
    pulls = [jnp.where(by_head, r.pulls[i : i + 1, :], 0.0) for i in range(2)]
    for index in range(2):
        spot_grad = sum(dot_rows(part, r.mem[:, :width]) for part in thirds(pulls[index]))
        r.small[8 + heads * index : 8 + heads * (index + 1), :NB] = spot_grad[:heads, :]
    key_grad = dot_columns(
        r.spots[...].astype(jnp.bfloat16), jnp.concatenate(pulls, axis=0).astype(jnp.bfloat16)
    )
    r.mem_grad[...] = jnp.concatenate([key_grad, r.mem_acc[...]], axis=1).astype(jnp.bfloat16)
    scatters[0].middle()

    r.dq[1] = jnp.zeros((rows, width), jnp.float32)
    r.dk[...] = jnp.zeros(r.dk.shape, jnp.float32)
    r.dv[...] = jnp.zeros(r.dv.shape, jnp.float32)

    def query_fold(slot, grad_ref, block_ref, own):
        if not own:
            mask_rows = block_ref[rows:, :].astype(jnp.float32)
            key_mask = jnp.concatenate([mask_rows[0:1, :half], mask_rows[1:2, :half]], axis=1)

        def part(index, unused):
            here = pl.ds(pl.multiple_of(index * chunk, chunk), chunk)
            query = r.pair[slot, here, :]
            grad = grad_ref[here, :width]
            keys = block_ref[:rows, :width]
            vals = block_ref[:rows, width:]
            if own:
                q_pos = index * chunk + lax.broadcasted_iota(jnp.int32, (chunk, rows), 0)
                k_pos = lax.broadcasted_iota(jnp.int32, (chunk, rows), 1)
                visible = (q_pos >= k_pos) & (r.doc_col[here, :] == r.doc_row[0:1, :])
            products = []
            for head in range(heads):
                scores = dot_rows(query * head_mask[head], keys)
                if own:
                    scores = jnp.where(visible, scores, NEGATIVE)
                    lse = r.near_lse[head, here, :]
                else:
                    scores = scores + key_mask
                    lse = r.stat[slot, head, here, :]
                probs = jnp.exp(scores - lse)
                pull = dot_rows(grad * head_mask[head], vals) - r.stat[slot, heads + head, here, :]
                products.append(dot_plain((probs * pull).astype(jnp.bfloat16), keys))
            r.dq[slot, here, :] = r.dq[slot, here, :] + pick_heads(products, lane_head)
            return unused

        lax.fori_loop(0, rows // chunk, part, 0)

    query_fold(0, r.near, block_of(r.kv_col, level, "keys"), True)
    other_grad_ref = None

    def own_earlier(from_level, unused):
        query_fold(0, r.near, block_of(r.kv_col, from_level, "keys"), False)
        return unused

    lax.fori_loop(0, level, own_earlier, 0)
    scatters[1].middle()
    own_grad_side().wait_recv()
    other_grad_ref = block_of(r.grad_oth, level, "grad")

    def other_stats(index, unused):
        here = pl.ds(pl.multiple_of(index * chunk, chunk), chunk)
        extended = other_grad_ref[here, :]
        for row in range(2 * heads):
            r.stat[1, row, here, :] = stat_column(extended, width, row)
        return unused

    lax.fori_loop(0, rows // chunk, other_stats, 0)

    def other_earlier(from_level, unused):
        query_fold(1, other_grad_ref, block_of(r.kv_col, from_level, "keys"), False)
        return unused

    lax.fori_loop(0, level + 1 - side, other_earlier, 0)
    r.dq_out[...] = r.dq[1].astype(jnp.bfloat16)
    dq_copy = pltpu.make_async_remote_copy(
        r.dq_out, r.dq_in, r.dq_sem.at[0], r.dq_sem.at[1], device_id=partner, device_id_type=MESH_ID
    )
    dq_copy.start()
    late.middle()

    own_block_ref = block_of(r.kv_col, level, "keys")

    def key_fold(query_ref, grad_ref, own):
        def part(index, unused):
            here = pl.ds(pl.multiple_of(index * chunk, chunk), chunk)
            keys = own_block_ref[here, :width]
            vals = own_block_ref[here, width:]
            query = query_ref[...]
            extended = grad_ref[...]
            if own:
                k_pos = index * chunk + lax.broadcasted_iota(jnp.int32, (chunk, rows), 0)
                q_pos = lax.broadcasted_iota(jnp.int32, (chunk, rows), 1)
                visible = (q_pos >= k_pos) & (r.doc_col[here, :] == r.doc_row[0:1, :])
            grad = extended[:, :width]
            stats = stat_rows(extended, width, 8)
            key_parts, val_parts = [], []
            for head in range(heads):
                scores = dot_rows(keys * head_mask[head], query)
                if own:
                    scores = jnp.where(visible, scores, NEGATIVE)
                probs = jnp.exp(scores - stats[head : head + 1, :])
                val_parts.append(dot_plain(probs.astype(jnp.bfloat16), grad))
                pull = dot_rows(vals * head_mask[head], grad) - stats[heads + head : heads + head + 1, :]
                key_parts.append(dot_plain((probs * pull).astype(jnp.bfloat16), query))
            r.dk[here, :] = r.dk[here, :] + pick_heads(key_parts, lane_head)
            r.dv[here, :] = r.dv[here, :] + pick_heads(val_parts, lane_head)
            return unused

        lax.fori_loop(0, rows // chunk, part, 0)

    @pl.when(side == 0)
    def _():
        key_fold(r.pair.at[1], block_of(r.grad_oth, level, "grad"), False)

    def later(from_level):
        grad_down(from_level, level).wait_recv()
        grad_side(from_level).start()
        key_fold(
            block_of(r.query_col, from_level, "query"), block_of(r.grad_col, from_level, "grad"), False
        )
        query_side(from_level).wait_recv()
        grad_side(from_level).wait_recv()
        key_fold(
            block_of(r.query_oth, from_level, "query"), block_of(r.grad_oth, from_level, "grad"), False
        )

    each_above(later)
    reaches = r.doc_col[...] >= (seq + 1) * rows
    r.dk[...] = jnp.where(reaches, r.dk[...], 0.0)
    r.dv[...] = jnp.where(reaches, r.dv[...], 0.0)
    key_fold(r.pair.at[0], r.near, True)
    dq_copy.wait()
    r.grads[...] = jnp.concatenate(
        [(r.dq[0] + r.dq_in[...].astype(jnp.float32)) * (DH**-0.5), r.dk[...], r.dv[...]], axis=1
    ).astype(jnp.bfloat16)

    for part in range(PARTS):
        third.start(part, dot_rows(r.grads[span(theirs(part)), :], r.qkv_w[...]))
        r.own[span(part * size), :] = dot_rows(r.grads[span(mine(part)), :], r.qkv_w[...])
    memory_part = jnp.concatenate(
        [
            jnp.concatenate(
                [jnp.zeros((width, width), jnp.float32), dot_columns(r.coeff[slot], r.mem_grad[...])], axis=1
            )
            for slot in range(4)
        ],
        axis=0,
    )
    weight_blocks(r.qkv_blocks, r.normed, r.grads[...], memory_part)
    scatters[3].start()
    for part in range(PARTS):
        third.middle(part, r.own[span(part * size), :])
    bias_row = column_sum(r.grads[...].astype(jnp.float32))
    r.small[7:8, :] = jnp.concatenate(
        [bias_row[:, :width], bias_row[:, 2 * width :], jnp.zeros((1, D - 2 * width), jnp.float32)], axis=1
    )
    scatters[2].middle()
    late.late()
    gain_sum = jnp.zeros((1, D), jnp.float32)
    offset_sum = jnp.zeros((1, D), jnp.float32)
    for part in range(PARTS):
        grad = third.result(part)
        nhat, scale = normalize(r.tok[span(mine(part)), :].astype(jnp.float32))
        gain_sum = gain_sum + column_sum(grad * nhat)
        offset_sum = offset_sum + column_sum(grad)
        out = r.mid[span(part * size), :] + norm_back(grad, nhat, scale, first_gain)
        r.tokens_out[span(mine(part)), :] = out.astype(jnp.bfloat16)
        token_share.copy(part, mine(part)).start()
    r.fold[0:1, :] = gain_sum
    r.fold[1:2, :] = offset_sum
    fold_copy = swap_with("core", r.fold, r.fold_in, (r.share_6, r.share_7), 0)
    fold_copy.start()
    scatters[3].middle()
    fold_copy.wait()
    r.small[0:5, :] = r.fold[0:5, :] + r.fold_in[0:5, :]
    small.start()
    scatters[0].finish(r.proj_share)
    scatters[1].finish(r.fc_share)
    small.middle()
    scatters[2].finish(r.out_share)
    scatters[3].finish(r.qkv_share)
    small.finish(r.small_out)
    late.finish()
    for part in range(PARTS):
        token_share.copy(part, theirs(part)).wait_recv()
        token_share.copy(part, mine(part)).wait_send()
        c_share.copy(part, mine(part)).wait_send()
        e_share.copy(part, mine(part)).wait_send()
    own_grad_side().wait_send()
    each_below(lambda other: query_down(level, other).wait_send())
    each_below(lambda other: grad_down(level, other).wait_send())
    each_above(lambda other: query_side(other).wait_send())
    each_above(lambda other: grad_side(other).wait_send())


def layer_back(levels, inputs):
    rows, width = inputs["heads"].shape
    heads = width // DH
    half = rows // 2
    size = half // PARTS
    hidden = inputs["fc_w"].shape[1]
    slab = D // (2 * levels)
    staged = levels > 8
    bf, fl = jnp.bfloat16, jnp.float32
    vmem = pl.BlockSpec(memory_space=pltpu.VMEM)
    far = pl.BlockSpec(memory_space=pl.ANY)
    dma = pltpu.SemaphoreType.DMA
    shape = jax.ShapeDtypeStruct
    outs = {
        "output": shape((rows, D), bf),
        "tokens_out": shape((rows, D), bf),
        "proj_share": shape((slab, hidden), fl),
        "fc_share": shape((slab, hidden), fl),
        "out_share": shape((slab, width), fl),
        "qkv_share": shape((slab, 3 * width), fl),
        "small_out": shape((16, D), fl),
    }
    gathered = {
        "query_col": ((levels, rows, width), bf),
        "query_oth": ((levels, rows, width), bf),
        "grad_col": ((levels, rows, LANES_OUT), bf),
        "grad_oth": ((levels, rows, LANES_OUT), bf),
    }
    scratch = {}
    out_specs = [vmem] * len(outs)
    if staged:
        for name, (dims, kind) in gathered.items():
            outs[name] = shape(dims, kind)
            out_specs.append(far)
        scratch["stage_query"] = pltpu.VMEM((rows, width), bf)
        scratch["stage_grad"] = pltpu.VMEM((rows, LANES_OUT), bf)
        scratch["stage_keys"] = pltpu.VMEM(inputs["kv_col"].shape[1:], bf)
        scratch["stage_sem"] = dma(())
    else:
        for name, (dims, kind) in gathered.items():
            scratch[name] = pltpu.VMEM(dims, kind)
    for name, dims, kind in (
        ("c", (rows, D), bf),
        ("e1", (rows, D), bf),
        ("u", (rows, hidden), bf),
        ("ef", (rows, hidden), bf),
        ("pull", (rows, hidden), fl),
        ("h1", (half, D), fl),
        ("own", (half, D), fl),
        ("base", (half, D), fl),
        ("mid", (half, D), fl),
        ("own_two", (half, D), fl),
        ("other_two", (half, D), bf),
        ("fold", (8, D), fl),
        ("fold_in", (8, D), fl),
        ("small", (16, D), fl),
        ("grad", (rows, width), bf),
        ("near", (rows, LANES_OUT), bf),
        ("far", (rows, LANES_OUT), bf),
        ("near_lse", (heads, rows, 1), fl),
        ("stat", (2, 2 * heads, rows, 1), fl),
        ("mem_acc", (NB, width), fl),
        ("pulls", (8, width), fl),
        ("mem_grad", (NB, 2 * width), bf),
        ("dq", (2, rows, width), fl),
        ("dk", (rows, width), fl),
        ("dv", (rows, width), fl),
        ("dq_out", (rows, width), bf),
        ("dq_in", (rows, width), bf),
        ("grads", (rows, 3 * width), bf),
        ("proj_blocks", (2 * levels, slab, hidden), bf),
        ("fc_blocks", (2 * levels, slab, hidden), bf),
        ("out_blocks", (2 * levels, slab, width), bf),
        ("qkv_blocks", (2 * levels, slab, 3 * width), bf),
    ):
        scratch[name] = pltpu.VMEM(dims, kind)

    def several(prefix, items):
        scratch.update({f"{prefix}_{index}": item for index, item in enumerate(items)})

    for name in ("first", "second", "third"):
        several(name, TpSum.scratch(PARTS, size, D))
    for name, columns in (("proj", hidden), ("fc", hidden), ("out", width), ("qkv", 3 * width)):
        several(name, Scatter.scratch(levels, slab, columns))
    several("small", SmallSum.scratch(levels, (16, D)))
    several("late", LateOutput.scratch(half, D))
    several("share", [dma((PARTS,))] * 8)
    for name in ("qd", "qs", "gd", "gs"):
        scratch[name + "_send"] = dma((levels,))
        scratch[name + "_recv"] = dma((levels,))
    scratch["dq_sem"] = dma((2,))
    names = [*inputs, *outs, *scratch]
    results = pl.pallas_call(
        functools.partial(back_kernel, levels, names),
        out_shape=tuple(outs.values()),
        in_specs=[far if staged and name == "kv_col" else vmem for name in inputs],
        out_specs=tuple(out_specs),
        scratch_shapes=list(scratch.values()),
        name="layer_back",
        compiler_params=pltpu.CompilerParams(
            collective_id=2, has_side_effects=True, vmem_limit_bytes=VMEM_LIMIT
        ),
    )(*inputs.values())
    return SimpleNamespace(**dict(zip(outs, results)))


def local(
    tokens,
    cotangent,
    past_states,
    doc_ids,
    cur_book,
    past_book,
    past_age,
    ln1_gain,
    ln1_bias,
    qkv_weight,
    qv_bias,
    out_weight,
    out_bias,
    ln2_gain,
    ln2_bias,
    fc_weight,
    fc_bias,
    proj_weight,
    proj_bias,
    mu_weight,
    sigma_weight,
):
    tok_rows = tokens.shape[0]
    heads_here = mu_weight.shape[0]
    head_cols = qkv_weight.shape[2]
    seq_count = lax.axis_size("seq")
    seq_index = lax.axis_index("seq")
    levels = seq_count // 2
    row_pad = ((0, 6), (0, 0))
    norm_rows = jnp.pad(jnp.stack([ln1_gain, ln1_bias]), row_pad)
    qkv_flat = qkv_weight.reshape(D, 3 * head_cols)
    bias_row = jnp.concatenate([qv_bias[0], jnp.zeros(head_cols, jnp.float32), qv_bias[1]])
    bias_rows = jnp.broadcast_to(bias_row[None], (8, 3 * head_cols))
    reaches = doc_ids >= (seq_index + 1) * tok_rows
    key_mask = jnp.where(reaches, 0.0, NEGATIVE).astype(jnp.bfloat16).reshape(2, tok_rows // 2)
    key_mask = jnp.pad(key_mask, ((0, 14), (0, 2 * head_cols - tok_rows // 2)))

    quarter = D // lax.axis_size("tp")
    columns = lax.dynamic_slice_in_dim(
        past_states, lax.axis_index("tp") * quarter, quarter, axis=1
    )
    half = SEG // 2
    marks = jnp.concatenate([past_book, past_age, jnp.zeros(14, jnp.int32)]).astype(jnp.bfloat16)
    past = jnp.concatenate(
        [
            jnp.concatenate([columns[:half], columns[half:]], axis=1),
            jnp.broadcast_to(marks[:, None], (16, 2 * quarter)),
        ]
    )
    book = jnp.broadcast_to(cur_book.astype(jnp.float32)[:, None], (8, 2 * quarter))
    spots = jnp.pad(jnp.stack([mu_weight, sigma_weight]), ((0, 0), (0, 8 - heads_here), (0, 0)))
    spots = spots.reshape(16, NB)
    table = jnp.asarray(np.stack(coefficient_tables(seq_count // BOOKS, NB, SEG), axis=1))

    normed, pair, kv_col, attended, lse, heads_out, coeff, memory, spot_rows = attention_forward(
        levels,
        tokens,
        norm_rows,
        qkv_flat,
        bias_rows,
        doc_ids,
        key_mask,
        past,
        book,
        spots,
        table,
    )
    vectors = jnp.pad(
        jnp.stack([ln2_gain, ln2_bias, out_bias, fc_bias, proj_bias, ln1_gain]), ((0, 2), (0, 0))
    )
    done = layer_back(
        levels,
        {
            "heads": heads_out,
            "tok": tokens,
            "cot": cotangent,
            "out_w": out_weight,
            "fc_w": fc_weight,
            "proj_w": proj_weight,
            "vec": vectors,
            "qkv_w": qkv_flat,
            "attended": attended,
            "lse": lse,
            "pair": pair,
            "kv_col": kv_col,
            "doc_col": doc_ids[:, None],
            "doc_row": doc_ids[None, :],
            "normed": normed,
            "coeff": coeff,
            "mem": memory,
            "spot_rows": spot_rows,
            "spots": spots,
        },
    )
    small = done.small_out
    return (
        done.output,
        done.tokens_out,
        done.qkv_share.reshape(-1, 3, head_cols),
        small[7, : 2 * head_cols].reshape(2, head_cols),
        done.out_share.T,
        small[4],
        done.fc_share,
        small[5],
        done.proj_share.T,
        small[6],
        small[0],
        small[1],
        small[2],
        small[3],
        small[8 : 8 + heads_here, :NB],
        small[8 + heads_here : 8 + 2 * heads_here, :NB],
    )


def solution(mesh):
    in_specs = (
        P("seq", None),
        P("seq", None),
        P("seq", None),
        P("seq"),
        P("seq"),
        P("seq"),
        P("seq"),
        P(),
        P(),
        P(None, None, "tp"),
        P(None, "tp"),
        P("tp", None),
        P(),
        P(),
        P(),
        P(None, "tp"),
        P("tp"),
        P("tp", None),
        P(),
        P("tp", None),
        P("tp", None),
    )
    out_specs = (
        P("seq", None),
        P("seq", None),
        P("seq", None, "tp"),
        P(None, "tp"),
        P("tp", "seq"),
        P(),
        P("seq", "tp"),
        P("tp"),
        P("tp", "seq"),
        P(),
        P(),
        P(),
        P(),
        P(),
        P("tp", None),
        P("tp", None),
    )
    return jax.shard_map(local, mesh=mesh, in_specs=in_specs, out_specs=out_specs, check_vma=False)
```

```python
import functools
from types import SimpleNamespace
from typing import NamedTuple

import ml_dtypes
import numpy as np

import jax
import jax.numpy as jnp
from jax import lax
from jax.experimental import pallas as pl
from jax.experimental.pallas import tpu as pltpu
from jax.sharding import PartitionSpec as P

D = 768
DH = 64
NB = 512
SEG = 512
BOOKS = 4


EPS = 1e-05
TAU = 0.75
RIDGE = 1.0
SPREAD = 0.01
NEGATIVE = -1e30
MESH_ID = pl.DeviceIdType.MESH
VMEM_LIMIT = 60 * 2**20


def coefficient_tables(age_count, basis_n, seg_len):
    shrink = TAU ** np.arange(age_count, dtype=np.float64)
    inside = (np.arange(seg_len) + 0.5) / seg_len
    times = shrink[:, None] * (TAU + (1.0 - TAU) * inside[None, :])
    centres = (np.arange(basis_n) + 0.5) / basis_n
    offset = (times[:, None, :] - centres[None, :, None]) * basis_n
    basis = np.exp(-0.5 * offset * offset)
    gram = np.einsum("agx,ahx->gh", basis, basis) + RIDGE * np.eye(basis_n)
    table = np.linalg.solve(gram[None], basis)
    high = table.astype(ml_dtypes.bfloat16)
    lower = (table - high.astype(np.float64)).astype(ml_dtypes.bfloat16)
    return high, lower


LANES_OUT = 256


def head_of_lane(width):
    return lax.broadcasted_iota(jnp.int32, (1, width), 1) // DH


def head_masks(width):
    lane_head = head_of_lane(width)
    return [(lane_head == head).astype(jnp.float32).astype(jnp.bfloat16) for head in range(width // DH)]


def pick_heads(per_head, lane_head):
    chosen = per_head[0]
    for head in range(1, len(per_head)):
        chosen = jnp.where(lane_head == head, per_head[head], chosen)
    return chosen


def dot_rows(left, right):
    return lax.dot_general(left, right, (((1,), (1,)), ((), ())), preferred_element_type=jnp.float32)


def dot_plain(left, right):
    return lax.dot_general(left, right, (((1,), (0,)), ((), ())), preferred_element_type=jnp.float32)


def thirds(value):
    first = value.astype(jnp.bfloat16)
    rest = value - first.astype(jnp.float32)
    second = rest.astype(jnp.bfloat16)
    third = (rest - second.astype(jnp.float32)).astype(jnp.bfloat16)
    return first, second, third


def with_stats(block, stats):
    rows, width = block.shape
    spare = LANES_OUT - width
    lane = lax.broadcasted_iota(jnp.int32, (1, spare), 1)
    tail = jnp.zeros((rows, spare), jnp.float32)
    for index, column in enumerate(stats):
        for part, value in enumerate(thirds(column)):
            tail = jnp.where(lane == 3 * index + part, value.astype(jnp.float32), tail)
    return jnp.concatenate([block, tail.astype(jnp.bfloat16)], axis=1)


def stat_column(extended, width, index):
    lane = lax.broadcasted_iota(jnp.int32, (1, LANES_OUT), 1)
    start = width + 3 * index
    mine = (lane >= start) & (lane < start + 3)
    return jnp.sum(jnp.where(mine, extended.astype(jnp.float32), 0.0), axis=1, keepdims=True)


def stat_rows(extended, width, count):
    row = lax.broadcasted_iota(jnp.int32, (count, LANES_OUT), 0)
    lane = lax.broadcasted_iota(jnp.int32, (count, LANES_OUT), 1)
    start = width + 3 * row
    chooser = ((lane >= start) & (lane < start + 3)).astype(jnp.float32).astype(jnp.bfloat16)
    return dot_rows(chooser, extended)


def greet(levels, whole_tp=False):
    seq, tp = lax.axis_index("seq"), lax.axis_index("tp")
    level, side = seq // 2, seq % 2
    barrier = pltpu.get_barrier_semaphore()
    pl.semaphore_signal(barrier, inc=1, device_id=(2 * level + 1 - side, tp), device_id_type=MESH_ID)

    def one(step, unused):
        other = lax.rem(level + step, levels)
        pl.semaphore_signal(barrier, inc=1, device_id=(2 * other + side, tp), device_id_type=MESH_ID)
        return unused

    lax.fori_loop(1, levels, one, 0)
    if not whole_tp:
        return barrier, levels
    greet_tp()
    return barrier, levels + 2


class MemoryPlace(NamedTuple):
    loose: jax.Array
    centre: jax.Array
    spread: jax.Array
    height: jax.Array
    gap: jax.Array


def memory_place(query, spot_rows, in_head):
    width_sq = 1.0 / (NB * NB)
    centre = 1.0 / (
        1.0 + jnp.exp(-jnp.sum(jnp.where(in_head, query * spot_rows[0:1, :], 0.0), axis=1, keepdims=True))
    )
    loose = jnp.sum(jnp.where(in_head, query * spot_rows[1:2, :], 0.0), axis=1, keepdims=True)
    soft = jnp.maximum(loose, 0.0) + jnp.log(1.0 + jnp.exp(-jnp.abs(loose)))
    spread = SPREAD * soft + width_sq
    height = (1.0 / NB) * lax.rsqrt(spread)
    centres = (lax.broadcasted_iota(jnp.int32, (1, NB), 1).astype(jnp.float32) + 0.5) / NB
    return MemoryPlace(loose, centre, spread, height, centre - centres)


def doc_vectors(doc_ref):
    row = doc_ref[...].astype(jnp.float32)
    return row, jnp.transpose(jnp.broadcast_to(row, (128, row.shape[1])))[:, 0:1]


def spot_rows_of(mu_ref, sigma_ref):
    fill = jnp.zeros((8 - mu_ref.shape[0], mu_ref.shape[1]), jnp.float32)
    return [jnp.concatenate([ref[...], fill], axis=0) for ref in (mu_ref, sigma_ref)]


def forward_kernel(
    levels,
    tok_ref,
    gain_ref,
    offset_ref,
    weight_ref,
    bias_ref,
    doc_ref,
    past_ref,
    book_ref,
    past_book_ref,
    past_age_ref,
    mu_ref,
    sigma_ref,
    table_ref,
    normed_ref,
    pair_ref,
    kv_out_ref,
    out_ref,
    lse_ref,
    heads_ref,
    coeff_ref,
    mem_ref,
    spot_row_ref,
    query_col_ref,
    top_ref,
    total_ref,
    acc_ref,
    part_ref,
    part_in_ref,
    kv_send,
    kv_recv,
    pair_sem,
    part_sem,
    past_col_ref,
    past_oth_ref,
    table_in_ref,
    past_up,
    past_down,
    past_side,
    coeff_sems,
    table_sem,
    doc_col_ref,
    read_ref,
    query_down,
):
    seq, tp = lax.axis_index("seq"), lax.axis_index("tp")
    level, side = seq // 2, seq % 2
    rows = tok_ref.shape[0]
    width = pair_ref.shape[2]
    heads = width // DH
    partner = (2 * level + 1 - side, tp)
    lane_head = head_of_lane(width)
    head_mask = head_masks(width)
    barrier, greetings = greet(levels, True)

    chunk = rows // 2
    time_half = rows // 2
    mark_row = lax.broadcasted_iota(jnp.int32, (16, 2 * width), 0)
    past_col_ref[level, time_half:, :] = jnp.where(
        mark_row == 0,
        past_book_ref[...].astype(jnp.float32),
        jnp.where(mark_row == 1, past_age_ref[...].astype(jnp.float32), 0.0),
    ).astype(jnp.bfloat16)
    for quarter in range(4):

        @pl.when(tp == quarter)
        def _(quarter=quarter):
            columns = past_ref[:, quarter * width : (quarter + 1) * width]
            past_col_ref[level, :time_half, :] = jnp.concatenate(
                [columns[:time_half], columns[time_half:]], axis=1
            )

    def past_copy(direction, from_level):
        block = past_col_ref.at[from_level]
        if direction == "side":
            sems, target, place = past_side, partner, past_oth_ref.at[from_level]
        elif direction == "up":
            sems, target, place = past_up, (lax.rem(2 * level + 2, 2 * levels) + side, tp), block
        else:
            sems, target, place = past_down, (lax.rem(2 * (level + levels - 1), 2 * levels) + side, tp), block
        return pltpu.make_async_remote_copy(
            block,
            place,
            sems.at[0, from_level],
            sems.at[1, from_level],
            device_id=target,
            device_id_type=MESH_ID,
        )

    pl.semaphore_wait(barrier, greetings)

    def pass_past(from_level, up, down):
        past_copy("side", from_level).start()
        if up:

            @pl.when(level < levels - 1)
            def _():
                past_copy("up", from_level).start()

        if down:

            @pl.when(level > 0)
            def _():
                past_copy("down", from_level).start()

    pass_past(level, True, True)

    doc_row, doc_column = doc_vectors(doc_ref)
    doc_col_ref[...] = doc_column
    bias = jnp.concatenate(
        [bias_ref[0:1, :], jnp.zeros((1, width), jnp.float32), bias_ref[1:2, :]], axis=1
    )

    def project(index, unused):
        here = pl.ds(pl.multiple_of(index * chunk, chunk), chunk)
        x = tok_ref[here, :].astype(jnp.float32)
        centred = x - jnp.mean(x, axis=1, keepdims=True)
        variance = jnp.mean(centred * centred, axis=1, keepdims=True)
        a = centred * lax.rsqrt(variance + EPS) * gain_ref[...][None, :] + offset_ref[...][None, :]
        a = a.astype(jnp.bfloat16)
        normed_ref[here, :] = a
        mixed = (dot_plain(a, weight_ref[...]) + bias).astype(jnp.bfloat16)
        query = mixed[:, :width] * jnp.bfloat16(DH**-0.5)
        pair_ref[0, here, :] = query
        kv_out_ref[level, here, :] = mixed[:, width:]
        return unused

    lax.fori_loop(0, rows // chunk, project, 0)
    hidden = jnp.where(doc_row >= ((seq + 1) * rows).astype(jnp.float32), 0.0, NEGATIVE)
    mask_rows = jnp.where(
        mark_row[:, : rows // 2] == 0,
        hidden[:, : rows // 2],
        jnp.where(mark_row[:, : rows // 2] == 1, hidden[:, rows // 2 :], 0.0),
    )
    kv_out_ref[level, rows:, :] = jnp.concatenate(
        [mask_rows, jnp.zeros((16, 2 * width - rows // 2), jnp.float32)], axis=1
    ).astype(jnp.bfloat16)

    pair_copy = pltpu.make_async_remote_copy(
        pair_ref.at[0], pair_ref.at[1], pair_sem.at[0], pair_sem.at[1], device_id=partner, device_id_type=MESH_ID
    )
    pair_copy.start()

    def kv_copy(from_level):
        return pltpu.make_async_remote_copy(
            kv_out_ref.at[from_level],
            kv_out_ref.at[from_level],
            kv_send.at[from_level],
            kv_recv.at[from_level],
            device_id=(lax.rem(2 * level + 2, 2 * levels) + side, tp),
            device_id_type=MESH_ID,
        )

    def down_copy(from_level, to_level):
        return pltpu.make_async_remote_copy(
            pair_ref.at[0],
            query_col_ref.at[from_level],
            query_down.at[0, to_level],
            query_down.at[1, from_level],
            device_id=(2 * to_level + side, tp),
            device_id_type=MESH_ID,
        )

    def each_below(body):
        def one(step, unused):
            body(level - step)
            return unused

        lax.fori_loop(1, level + 1, one, 0)

    def each_above(body):
        def one(step, unused):
            body(level + step)
            return unused

        lax.fori_loop(1, levels - level, one, 0)

    @pl.when(level < levels - 1)
    def _():
        kv_copy(level).start()


    top_ref[...] = jnp.full(top_ref.shape, NEGATIVE, jnp.float32)
    total_ref[...] = jnp.zeros(total_ref.shape, jnp.float32)
    acc_ref[...] = jnp.zeros(acc_ref.shape, jnp.float32)

    doc_first = doc_row[0:1, 0:1]
    def reach_of(here):
        docs = doc_col_ref[here, :]
        last = (level == levels - 1) & (side == 1)
        return jnp.where(last & (docs != doc_first), NEGATIVE, 0.0)

    def fold(slot, from_level, mask_kind):
        mask_rows = kv_out_ref[from_level, rows:, :].astype(jnp.float32)
        key_mask = jnp.concatenate([mask_rows[0:1, : rows // 2], mask_rows[1:2, : rows // 2]], axis=1)

        def part(index, unused):
            here = pl.ds(pl.multiple_of(index * chunk, chunk), chunk)
            query = pair_ref[slot, here, :]
            keys = kv_out_ref[from_level, :rows, :width]
            vals = kv_out_ref[from_level, :rows, width:]
            if mask_kind == "own":
                q_pos = index * chunk + lax.broadcasted_iota(jnp.int32, (chunk, rows), 0)
                k_pos = lax.broadcasted_iota(jnp.int32, (chunk, rows), 1)
                visible = (q_pos >= k_pos) & (doc_col_ref[here, :] == doc_row)
            products, scales = [], []
            for head in range(heads):
                scores = dot_rows(query * head_mask[head], keys)
                old_top = top_ref[slot, head, here, :]
                if mask_kind == "own":
                    scores = jnp.where(visible, scores, NEGATIVE)
                    reach = 0.0
                else:
                    scores = scores + key_mask
                    reach = jnp.where(slot == 0, reach_of(here), 0.0)
                new_top = jnp.maximum(old_top, jnp.max(scores, axis=1, keepdims=True) + reach)
                weights = jnp.exp(scores - (new_top - reach))
                scale = jnp.exp(old_top - new_top)
                top_ref[slot, head, here, :] = new_top
                total_ref[slot, head, here, :] = total_ref[slot, head, here, :] * scale + jnp.sum(
                    weights, axis=1, keepdims=True
                )
                products.append(dot_plain(weights.astype(jnp.bfloat16), vals))
                scales.append(scale)
            acc_ref[slot, here, :] = acc_ref[slot, here, :] * pick_heads(scales, lane_head) + pick_heads(
                products, lane_head
            )
            return unused

        lax.fori_loop(0, rows // chunk, part, 0)

    fold(0, level, "own")
    pair_copy.wait()

    @pl.when(side == 0)
    def _():
        fold(1, level, "off")

    def keys_arrived(step):
        from_level = level - step
        kv_copy(from_level).wait_recv()

        @pl.when(level < levels - 1)
        def _():
            kv_copy(from_level).start()

        def both(slot, inner):
            fold(1 - slot, from_level, "off")
            return inner

        lax.fori_loop(0, 2, both, 0)

    def arrived(step, unused):
        @pl.when(level >= step)
        def _():
            past_copy("up", level - step).wait_recv()
            pass_past(level - step, True, False)

        @pl.when(level + step < levels)
        def _():
            past_copy("down", level + step).wait_recv()
            pass_past(level + step, False, True)

        @pl.when(step == 1)
        def _():
            each_below(lambda other: down_copy(level, other).start())

        @pl.when((level >= step) & (step < levels - 1))
        def _():
            keys_arrived(step)

        return unused

    lax.fori_loop(1, levels, arrived, 0)

    def from_side(other, unused):
        past_copy("side", other).wait_recv()
        return unused

    lax.fori_loop(0, levels, from_side, 0)
    own_book = book_ref[...].astype(jnp.float32)
    ages = table_ref.shape[0]

    def one_age(age, total):
        table_copy = pltpu.make_async_copy(table_ref.at[age], table_in_ref, table_sem)
        table_copy.start()

        def one_level(other, found):
            for blocks_ref in (past_col_ref, past_oth_ref):
                mark = blocks_ref[other, time_half:, :].astype(jnp.float32)
                chosen = (mark[0:1, :] == own_book) & (mark[1:2, :] == age.astype(jnp.float32))
                found = jnp.where(chosen, blocks_ref[other, :time_half, :].astype(jnp.float32), found)
            return found

        found = lax.fori_loop(
            0, levels, one_level, jnp.zeros((time_half, 2 * width), jnp.float32)
        ).astype(jnp.bfloat16)
        table_copy.wait()
        for index in range(2):
            table = table_in_ref[index]
            total = total + (
                dot_plain(table[:, :time_half], found)[:, :width]
                + dot_plain(table[:, time_half:], found)[:, width:]
            )
        return total

    coeff = lax.fori_loop(0, ages, one_age, jnp.zeros((NB, width), jnp.float32))
    coeff_ref[tp] = coeff.astype(jnp.bfloat16)

    def coeff_copy(kind, slot, index):
        return swap_with(kind, coeff_ref.at[slot], coeff_ref.at[slot], (coeff_sems.at[0], coeff_sems.at[1]), index)

    core_mate, chip_mate = tp + 1 - 2 * (tp % 2), lax.rem(tp + 2, 4)
    coeff_copy("chip", tp, 0).start()
    coeff_copy("core", tp, 1).start()


    @pl.when(level == levels - 1)
    def _():
        kv_copy(0).wait_recv()
        fold(1, 0, "off")

    def finish(index, unused):
        here = pl.ds(pl.multiple_of(index * chunk, chunk), chunk)
        totals = [total_ref[1, head, here, :] for head in range(heads)]
        tops = [top_ref[1, head, here, :] for head in range(heads)]
        some = [value > 0.0 for value in totals]
        inverse = [jnp.where(ok, 1.0 / jnp.where(ok, value, 1.0), 0.0) for ok, value in zip(some, totals)]
        logs = [
            jnp.where(ok, top + jnp.log(jnp.where(ok, value, 1.0)), NEGATIVE)
            for ok, top, value in zip(some, tops, totals)
        ]
        share = (acc_ref[1, here, :] * pick_heads(inverse, lane_head)).astype(jnp.bfloat16)
        part_ref[here, :] = with_stats(share, logs)
        return unused

    lax.fori_loop(0, rows // chunk, finish, 0)
    part_copy = pltpu.make_async_remote_copy(
        part_ref, part_in_ref, part_sem.at[0], part_sem.at[1], device_id=partner, device_id_type=MESH_ID
    )
    part_copy.start()

    @pl.when(level == levels - 1)
    def _():
        fold(0, 0, "off")

    coeff_copy("chip", chip_mate, 0).wait_recv()
    coeff_copy("core", chip_mate, 2).start()
    coeff_copy("core", core_mate, 1).wait_recv()
    coeff_copy("core", lax.rem(core_mate + 2, 4), 2).wait_recv()
    memory = jnp.zeros((NB, 2 * width), jnp.float32)
    for slot in range(4):
        memory = memory + dot_plain(
            coeff_ref[slot], weight_ref[slot * width : (slot + 1) * width, width:]
        )
    mem_ref[...] = memory.astype(jnp.bfloat16)
    for index, spots in enumerate(spot_rows_of(mu_ref, sigma_ref)):
        row = sum(dot_plain(third, mem_ref[:, :width]) for third in thirds(spots))
        spot_row_ref[index : index + 1, :] = pick_heads(
            [row[head : head + 1, :] for head in range(heads)], lane_head
        )

    def read_memory(index, unused):
        here = pl.ds(pl.multiple_of(index * chunk, chunk), chunk)
        query = pair_ref[0, here, :].astype(jnp.float32)
        reads = []
        for head in range(heads):
            place = memory_place(query, spot_row_ref[0:2, :], lane_head == head)
            density = place.height * jnp.exp(place.gap * place.gap * (-0.5 / place.spread))
            reads.append(dot_plain(density.astype(jnp.bfloat16), mem_ref[:, width:]))
        read_ref[here, :] = pick_heads(reads, lane_head)
        return unused

    lax.fori_loop(0, rows // chunk, read_memory, 0)

    part_copy.wait()

    def merge(index, unused):
        here = pl.ds(pl.multiple_of(index * chunk, chunk), chunk)
        reach = reach_of(here)
        received = part_in_ref[here, :]
        mine, theirs, columns = [], [], []
        for head in range(heads):
            total = total_ref[0, head, here, :]
            own_log = top_ref[0, head, here, :] + jnp.log(total)
            other_log = stat_column(received, width, head) + reach
            high = jnp.maximum(own_log, other_log)
            both_log = high + jnp.log(jnp.exp(own_log - high) + jnp.exp(other_log - high))
            mine.append(jnp.exp(own_log - both_log) / total)
            theirs.append(jnp.exp(other_log - both_log))
            columns.append(both_log)
        attended = acc_ref[0, here, :] * pick_heads(mine, lane_head) + received[:, :width].astype(
            jnp.float32
        ) * pick_heads(theirs, lane_head)
        out_ref[here, :] = attended
        heads_ref[here, :] = (attended + read_ref[here, :]).astype(jnp.bfloat16)
        lane = lax.broadcasted_iota(jnp.int32, (1, 8), 1)
        packed = jnp.zeros((chunk, 8), jnp.float32)
        for head in range(heads):
            packed = jnp.where(lane == head, columns[head], packed)
        lse_ref[here, :] = packed
        return unused

    lax.fori_loop(0, rows // chunk, merge, 0)

    each_below(lambda other: down_copy(level, other).wait_send())
    each_above(lambda other: down_copy(other, level).wait_recv())
    coeff_copy("chip", tp, 0).wait_send()
    coeff_copy("core", tp, 1).wait_send()
    coeff_copy("core", chip_mate, 2).wait_send()

    def past_sent(other, unused):
        past_copy("side", other).wait_send()

        @pl.when((level < levels - 1) & (other <= level))
        def _():
            past_copy("up", other).wait_send()

        @pl.when((level > 0) & (other >= level))
        def _():
            past_copy("down", other).wait_send()

        return unused

    lax.fori_loop(0, levels, past_sent, 0)

    @pl.when(level < levels - 1)
    def _():
        def sent_up(from_level, unused):
            kv_copy(from_level).wait_send()
            return unused

        lax.fori_loop(0, level + 1, sent_up, 0)


def attention_forward(
    levels,
    tokens,
    gain,
    offset,
    weight,
    bias,
    doc_row,
    past,
    book,
    past_book,
    past_age,
    mu_weight,
    sigma_weight,
    table,
):
    rows = tokens.shape[0]
    width = weight.shape[1] // 3
    heads = width // DH
    vmem = pl.BlockSpec(memory_space=pltpu.VMEM)
    far = pl.BlockSpec(memory_space=pl.ANY) if levels > 8 else vmem
    dma = pltpu.SemaphoreType.DMA
    return pl.pallas_call(
        functools.partial(forward_kernel, levels),
        out_shape=(
            jax.ShapeDtypeStruct((rows, D), jnp.bfloat16),
            jax.ShapeDtypeStruct((2, rows, width), jnp.bfloat16),
            jax.ShapeDtypeStruct((levels, rows + 16, 2 * width), jnp.bfloat16),
            jax.ShapeDtypeStruct((rows, width), jnp.float32),
            jax.ShapeDtypeStruct((rows, 8), jnp.float32),
            jax.ShapeDtypeStruct((rows, width), jnp.bfloat16),
            jax.ShapeDtypeStruct((4, NB, width), jnp.bfloat16),
            jax.ShapeDtypeStruct((NB, 2 * width), jnp.bfloat16),
            jax.ShapeDtypeStruct((8, width), jnp.float32),
            jax.ShapeDtypeStruct((levels, rows, width), jnp.bfloat16),
        ),
        in_specs=[vmem] * 12 + [pl.BlockSpec(memory_space=pl.ANY)],
        out_specs=(vmem,) * 9 + (far,),
        scratch_shapes=[
            pltpu.VMEM((2, heads, rows, 1), jnp.float32),
            pltpu.VMEM((2, heads, rows, 1), jnp.float32),
            pltpu.VMEM((2, rows, width), jnp.float32),
            pltpu.VMEM((rows, LANES_OUT), jnp.bfloat16),
            pltpu.VMEM((rows, LANES_OUT), jnp.bfloat16),
            dma((levels,)),
            dma((levels,)),
            dma((2,)),
            dma((2,)),
            pltpu.VMEM((levels, SEG // 2 + 16, 2 * width), jnp.bfloat16),
            pltpu.VMEM((levels, SEG // 2 + 16, 2 * width), jnp.bfloat16),
            pltpu.VMEM(table.shape[1:], jnp.bfloat16),
            dma((2, levels)),
            dma((2, levels)),
            dma((2, levels)),
            dma((2, 3)),
            dma(()),
            pltpu.VMEM((rows, 1), jnp.float32),
            pltpu.VMEM((rows, width), jnp.float32),
            dma((2, levels)),
        ],
        name="attention_forward",
        compiler_params=pltpu.CompilerParams(
            collective_id=1, has_side_effects=True, vmem_limit_bytes=VMEM_LIMIT
        ),
    )(
        tokens,
        gain,
        offset,
        weight,
        bias,
        doc_row,
        past,
        book,
        past_book,
        past_age,
        mu_weight,
        sigma_weight,
        table,
    )


def column_copy(block_ref, from_level, landing_ref, send_sem, recv_sem, to_level):
    seq, tp = lax.axis_index("seq"), lax.axis_index("tp")
    return pltpu.make_async_remote_copy(
        block_ref,
        landing_ref.at[from_level],
        send_sem.at[to_level],
        recv_sem.at[from_level],
        device_id=(2 * to_level + seq % 2, tp),
        device_id_type=MESH_ID,
    )


class Scatter:
    def __init__(self, levels, blocks, plane_in, plane_sum, column_in, sems):
        self.levels, self.blocks = levels, blocks
        self.plane_in, self.plane_sum, self.column_in = plane_in, plane_sum, column_in
        self.plane_send, self.plane_recv, self.column_send, self.column_recv = sems
        seq, tp = lax.axis_index("seq"), lax.axis_index("tp")
        self.level, self.side, self.tp = seq // 2, seq % 2, tp

    def plane_copy(self, to_level):
        return pltpu.make_async_remote_copy(
            self.blocks.at[2 * to_level + 1 - self.side],
            self.plane_in.at[to_level],
            self.plane_send.at[to_level],
            self.plane_recv.at[to_level],
            device_id=(2 * self.level + 1 - self.side, self.tp),
            device_id_type=MESH_ID,
        )

    def swap_copy(self, from_level, to_level):
        return column_copy(
            self.plane_sum.at[to_level], from_level, self.column_in, self.column_send, self.column_recv, to_level
        )

    def loop(self, first, body):
        def one(step, unused):
            body(lax.rem(self.level + step, self.levels))
            return unused

        lax.fori_loop(first, self.levels, one, 0)

    def start(self):
        self.loop(0, lambda other: self.plane_copy(other).start())

    def middle(self):
        def one(other):
            self.plane_copy(other).wait_recv()
            total = self.blocks[2 * other + self.side].astype(jnp.float32) + self.plane_in[other].astype(
                jnp.float32
            )
            self.plane_sum[other] = total.astype(jnp.bfloat16)
            self.swap_copy(self.level, other).start()

        self.loop(1, one)

    def finish(self, out_ref):
        self.plane_copy(self.level).wait_recv()
        out_ref[...] = self.blocks[2 * self.level + self.side].astype(jnp.float32) + self.plane_in[
            self.level
        ].astype(jnp.float32)

        def one(other):
            self.swap_copy(other, self.level).wait_recv()
            out_ref[...] += self.column_in[other].astype(jnp.float32)

        self.loop(1, one)
        self.loop(0, lambda other: self.plane_copy(other).wait_send())
        self.loop(1, lambda other: self.swap_copy(self.level, other).wait_send())

    @staticmethod
    def scratch(levels, rows, width):
        buffer = pltpu.VMEM((levels, rows, width), jnp.bfloat16)
        return [buffer] * 3 + [pltpu.SemaphoreType.DMA((levels,))] * 4


class SmallSum:
    def __init__(self, levels, small, plane_in, column_in, sems):
        self.levels, self.small, self.plane_in, self.column_in = levels, small, plane_in, column_in
        self.plane_sem, self.column_send, self.column_recv = sems
        seq, tp = lax.axis_index("seq"), lax.axis_index("tp")
        self.level, self.side, self.tp = seq // 2, seq % 2, tp

    def plane_copy(self):
        return pltpu.make_async_remote_copy(
            self.small,
            self.plane_in,
            self.plane_sem.at[0],
            self.plane_sem.at[1],
            device_id=(2 * self.level + 1 - self.side, self.tp),
            device_id_type=MESH_ID,
        )

    def swap_copy(self, from_level, to_level):
        return column_copy(
            self.column_in.at[from_level], from_level, self.column_in, self.column_send, self.column_recv, to_level
        )

    def loop(self, body):
        def one(step, unused):
            body(lax.rem(self.level + step, self.levels))
            return unused

        lax.fori_loop(1, self.levels, one, 0)

    def start(self):
        self.plane_copy().start()

    def middle(self):
        self.plane_copy().wait()
        self.column_in[self.level] = self.small[...] + self.plane_in[...]
        self.loop(lambda other: self.swap_copy(self.level, other).start())

    def finish(self, out_ref):
        self.loop(lambda other: self.swap_copy(other, self.level).wait_recv())
        self.loop(lambda other: self.swap_copy(self.level, other).wait_send())
        out_ref[...] = self.column_in[0]

        def one(other, unused):
            out_ref[...] += self.column_in[other]
            return unused

        lax.fori_loop(1, self.levels, one, 0)

    @staticmethod
    def scratch(levels, shape):
        dma = pltpu.SemaphoreType.DMA
        return [
            pltpu.VMEM(shape, jnp.float32),
            pltpu.VMEM((levels,) + shape, jnp.float32),
            dma((2,)),
            dma((levels,)),
            dma((levels,)),
        ]


def tp_partner(kind):
    seq, tp = lax.axis_index("seq"), lax.axis_index("tp")
    if kind == "core":
        return (seq, tp + 1 - 2 * (tp % 2))
    return (seq, lax.rem(tp + 2, 4))


def greet_tp():
    barrier = pltpu.get_barrier_semaphore()
    for kind in ("core", "chip"):
        pl.semaphore_signal(barrier, inc=1, device_id=tp_partner(kind), device_id_type=MESH_ID)
    return barrier, 2


def swap_with(kind, source, target, sems, index):
    send, recv = sems
    return pltpu.make_async_remote_copy(
        source, target, send.at[index], recv.at[index], device_id=tp_partner(kind), device_id_type=MESH_ID
    )


class TpSum:
    def __init__(self, core_out, core_in, chip_out, chip_in, sems):
        self.core_out, self.core_in, self.chip_out, self.chip_in = core_out, core_in, chip_out, chip_in
        self.core_sems, self.chip_sems = sems[:2], sems[2:]

    def core_copy(self, part):
        return swap_with("core", self.core_out.at[part], self.core_in.at[part], self.core_sems, part)

    def chip_copy(self, part):
        return swap_with("chip", self.chip_out.at[part], self.chip_in.at[part], self.chip_sems, part)

    def start(self, part, for_other_core):
        self.core_out[part] = for_other_core.astype(jnp.bfloat16)
        self.core_copy(part).start()

    def middle(self, part, own):
        self.core_copy(part).wait()
        self.chip_out[part] = (own + self.core_in[part].astype(jnp.float32)).astype(jnp.bfloat16)
        self.chip_copy(part).start()

    def result(self, part):
        self.chip_copy(part).wait()
        return self.chip_out[part].astype(jnp.float32) + self.chip_in[part].astype(jnp.float32)

    @staticmethod
    def scratch(parts, rows, width):
        buffer = pltpu.VMEM((parts, rows, width), jnp.bfloat16)
        return [buffer] * 4 + [pltpu.SemaphoreType.DMA((parts,))] * 4

    COUNT = 8


class RowShare:
    def __init__(self, whole, rows, sems):
        self.whole, self.rows, self.sems = whole, rows, sems

    def copy(self, part, start):
        here = self.whole.at[pl.ds(pl.multiple_of(start, self.rows), self.rows), :]
        return swap_with("core", here, here, self.sems, part)


def normalize(v):
    centred = v - jnp.mean(v, axis=1, keepdims=True)
    scale = lax.rsqrt(jnp.mean(centred * centred, axis=1, keepdims=True) + EPS)
    return centred * scale, scale


def norm_back(grad, nhat, scale, gain):
    inner = grad * gain
    return (
        inner
        - jnp.mean(inner, axis=1, keepdims=True)
        - nhat * jnp.mean(inner * nhat, axis=1, keepdims=True)
    ) * scale


def gelu_and_slope(f):
    root = (2.0 / np.pi) ** 0.5
    square = f * f
    bend = jnp.tanh(root * f * (1.0 + 0.044715 * square))
    half = 0.5 * (1.0 + bend)
    slope = half + 0.5 * f * (1.0 - bend * bend) * (root * (1.0 + 3.0 * 0.044715 * square))
    return f * half, slope


def dot_columns(left, right):
    return lax.dot_general(left, right, (((0,), (0,)), ((), ())), preferred_element_type=jnp.float32)


def column_sum(v):
    return jnp.sum(v, axis=0, keepdims=True)


class LateOutput:
    def __init__(self, base, own, other, whole, sems):
        self.base, self.own, self.other, self.whole = base, own, other, whole
        self.half = own.shape[0]
        self.core_in, self.chip_out, self.chip_in = sems[:3]
        self.core_sems, self.chip_sems, self.share_sems = sems[3:5], sems[5:7], sems[7:9]
        self.share = RowShare(whole, self.half, self.share_sems)
        self.core = lax.axis_index("tp") % 2

    COUNT = 9

    def core_copy(self):
        return swap_with("core", self.other, self.core_in, self.core_sems, 0)

    def chip_copy(self):
        return swap_with("chip", self.chip_out, self.chip_in, self.chip_sems, 0)

    def start(self):
        self.core_copy().start()

    def middle(self):
        self.core_copy().wait()
        self.chip_out[...] = (self.own[...] + self.core_in[...].astype(jnp.float32)).astype(jnp.bfloat16)
        self.chip_copy().start()

    def late(self):
        self.chip_copy().wait()
        total = self.chip_out[...].astype(jnp.float32) + self.chip_in[...].astype(jnp.float32)
        here = pl.ds(pl.multiple_of(self.core * self.half, self.half), self.half)
        self.whole[here, :] = (self.base[...] + total).astype(jnp.bfloat16)
        self.share.copy(0, self.core * self.half).start()

    def finish(self):
        self.share.copy(0, (1 - self.core) * self.half).wait_recv()
        self.share.copy(0, self.core * self.half).wait_send()

    @staticmethod
    def scratch(half, width):
        buffer = pltpu.VMEM((half, width), jnp.bfloat16)
        return [buffer] * 3 + [pltpu.SemaphoreType.DMA((1,))] * 6


PARTS = 2


def back_kernel(levels, names, *refs):
    r = SimpleNamespace(**dict(zip(names, refs)))
    seq, tp = lax.axis_index("seq"), lax.axis_index("tp")
    level, side, core = seq // 2, seq % 2, tp % 2
    rows, width = r.heads.shape
    heads = width // DH
    half = rows // 2
    size = half // PARTS
    partner = (2 * level + 1 - side, tp)
    lane_head = head_of_lane(width)
    head_mask = head_masks(width)
    chunk = rows // 2
    staged = hasattr(r, "stage_query")

    first, second, third = (
        TpSum(*(getattr(r, f"{name}_{i}") for i in range(4)), [getattr(r, f"{name}_{i}") for i in range(4, 8)])
        for name in ("first", "second", "third")
    )
    scatters = [
        Scatter(
            levels,
            getattr(r, f"{name}_blocks"),
            *(getattr(r, f"{name}_{i}") for i in range(3)),
            [getattr(r, f"{name}_{i}") for i in range(3, 7)],
        )
        for name in ("proj", "fc", "out", "qkv")
    ]
    small = SmallSum(levels, r.small, r.small_0, r.small_1, (r.small_2, r.small_3, r.small_4))
    late = LateOutput(
        r.base, r.own_two, r.other_two, r.output, [getattr(r, f"late_{i}") for i in range(LateOutput.COUNT)]
    )
    c_share = RowShare(r.c, size, (r.share_0, r.share_1))
    e_share = RowShare(r.e1, size, (r.share_2, r.share_3))
    token_share = RowShare(r.tokens_out, size, (r.share_4, r.share_5))
    gain, offset, out_b, fc_b, proj_b, first_gain = (
        ref[...][None, :] for ref in (r.ln2_gain, r.ln2_bias, r.out_b, r.fc_b, r.proj_b, r.ln1_gain)
    )
    barrier, greetings = greet(levels, True)

    def span(start, count=size):
        return pl.ds(pl.multiple_of(start, size), count)

    def mine(part):
        return core * half + part * size

    def theirs(part):
        return (1 - core) * half + part * size

    def block_of(blocks_ref, from_level, place):
        if not staged:
            return blocks_ref.at[from_level]
        target = getattr(r, "stage_" + place)
        copy = pltpu.make_async_copy(blocks_ref.at[from_level], target, r.stage_sem)
        copy.start()
        copy.wait()
        return target

    def down_copy(source_ref, landing_ref, sems, from_level, to_level):
        send, recv = sems
        return pltpu.make_async_remote_copy(
            source_ref,
            landing_ref.at[from_level],
            send.at[to_level],
            recv.at[from_level],
            device_id=(2 * to_level + side, tp),
            device_id_type=MESH_ID,
        )

    def side_copy(source_ref, landing_ref, sems, from_level):
        send, recv = sems
        return pltpu.make_async_remote_copy(
            source_ref,
            landing_ref.at[from_level],
            send.at[from_level],
            recv.at[from_level],
            device_id=partner,
            device_id_type=MESH_ID,
        )

    def query_side(from_level):
        return side_copy(r.query_col.at[from_level], r.query_oth, (r.qs_send, r.qs_recv), from_level)

    def grad_down(from_level, to_level):
        return down_copy(r.far, r.grad_col, (r.gd_send, r.gd_recv), from_level, to_level)

    def grad_side(from_level):
        return side_copy(r.grad_col.at[from_level], r.grad_oth, (r.gs_send, r.gs_recv), from_level)

    def own_grad_side():
        return side_copy(r.far, r.grad_oth, (r.gs_send, r.gs_recv), level)

    def each_below(body):
        def one(step, unused):
            body(level - step)
            return unused

        lax.fori_loop(1, level + 1, one, 0)

    def each_above(body):
        def one(step, unused):
            body(level + step)
            return unused

        lax.fori_loop(1, levels - level, one, 0)

    pl.semaphore_wait(barrier, greetings)

    each_above(lambda other: query_side(other).start())

    for part in range(PARTS):
        first.start(part, dot_plain(r.heads[span(theirs(part)), :], r.out_w[...]))
        r.own[span(part * size), :] = dot_plain(r.heads[span(mine(part)), :], r.out_w[...])
    for part in range(PARTS):
        first.middle(part, r.own[span(part * size), :])

    def early(index, unused):
        here = span(index * size)
        r.pull[here, :] = dot_rows(r.cot[here, :], r.proj_w[...])
        return unused

    lax.fori_loop(0, rows // size, early, 0)
    r.small[...] = jnp.zeros(r.small.shape, jnp.float32)
    r.fold[...] = jnp.zeros(r.fold.shape, jnp.float32)
    r.small[6:7, :] = column_sum(r.cot[...].astype(jnp.float32))

    def feed(start):
        here = span(start)
        f = dot_plain(r.c[here, :], r.fc_w[...]) + fc_b
        u, slope = gelu_and_slope(f)
        r.u[here, :] = u.astype(jnp.bfloat16)
        ef = (r.pull[here, :] * slope).astype(jnp.bfloat16)
        r.ef[here, :] = ef
        return dot_rows(ef, r.fc_w[...])

    for part in range(PARTS):
        total = first.result(part) + out_b
        h1 = r.tok[span(mine(part)), :].astype(jnp.float32) + total
        r.h1[span(part * size), :] = h1
        nhat, scale = normalize(h1)
        r.c[span(mine(part)), :] = (nhat * gain + offset).astype(jnp.bfloat16)
        c_share.copy(part, mine(part)).start()
        r.own[span(part * size), :] = feed(mine(part))
        c_share.copy(part, theirs(part)).wait_recv()
        second.start(part, feed(theirs(part)))
        r.other_two[span(part * size), :] = dot_plain(r.u[span(theirs(part)), :], r.proj_w[...]).astype(
            jnp.bfloat16
        )
        r.own_two[span(part * size), :] = dot_plain(r.u[span(mine(part)), :], r.proj_w[...])
        second.middle(part, r.own[span(part * size), :])

    r.base[...] = r.h1[...] + proj_b
    bite = 384

    def weight_blocks(blocks_ref, left_ref, right, extra=None):
        slab = blocks_ref.shape[1]
        for index in range(D // bite):
            value = dot_columns(left_ref[:, index * bite : (index + 1) * bite], right)
            if extra is not None:
                value = value + extra[index * bite : (index + 1) * bite, :]
            for place in range(bite // slab):
                blocks_ref[index * (bite // slab) + place] = value[
                    place * slab : (place + 1) * slab
                ].astype(jnp.bfloat16)

    weight_blocks(r.proj_blocks, r.cot, r.u[...])
    scatters[0].start()
    weight_blocks(r.fc_blocks, r.c, r.ef[...])
    scatters[1].start()

    gain_sum = jnp.zeros((1, D), jnp.float32)
    offset_sum = jnp.zeros((1, D), jnp.float32)
    out_sum = jnp.zeros((1, D), jnp.float32)
    for part in range(PARTS):
        grad = second.result(part)
        nhat, scale = normalize(r.h1[span(part * size), :])
        gain_sum = gain_sum + column_sum(grad * nhat)
        offset_sum = offset_sum + column_sum(grad)
        mid = r.cot[span(mine(part)), :].astype(jnp.float32) + norm_back(grad, nhat, scale, gain)
        r.mid[span(part * size), :] = mid
        e1 = mid.astype(jnp.bfloat16)
        out_sum = out_sum + column_sum(e1.astype(jnp.float32))
        r.e1[span(mine(part)), :] = e1
        e_share.copy(part, mine(part)).start()
        r.grad[span(mine(part)), :] = dot_rows(e1, r.out_w[...]).astype(jnp.bfloat16)
    r.fold[2:3, :] = gain_sum
    r.fold[3:4, :] = offset_sum
    r.fold[4:5, :] = out_sum
    for part in range(PARTS):
        e_share.copy(part, theirs(part)).wait_recv()
        r.grad[span(theirs(part)), :] = dot_rows(r.e1[span(theirs(part)), :], r.out_w[...]).astype(jnp.bfloat16)

    doc_row, doc_column = doc_vectors(r.doc)
    r.doc_col[...] = doc_column
    doc_first = doc_row[0:1, 0:1]
    last = (level == levels - 1) & (side == 1)

    def prepare(index, unused):
        here = pl.ds(pl.multiple_of(index * chunk, chunk), chunk)
        grad = r.grad[here, :]
        product = grad.astype(jnp.float32) * r.attended[here, :]
        far = jnp.where(last & (r.doc_col[here, :] != doc_first), -NEGATIVE, 0.0)
        lses = [r.lse[here, head : head + 1] for head in range(heads)]
        deltas = [
            jnp.sum(jnp.where(lane_head == head, product, 0.0), axis=1, keepdims=True)
            for head in range(heads)
        ]
        r.near[here, :] = with_stats(grad, lses + deltas)
        r.far[here, :] = with_stats(grad, [lse + far for lse in lses] + deltas)
        for head in range(heads):
            r.near_lse[head, here, :] = lses[head]
            r.stat[0, head, here, :] = lses[head] + far
            r.stat[0, heads + head, here, :] = deltas[head]
        return unused

    lax.fori_loop(0, rows // chunk, prepare, 0)
    own_grad_side().start()
    each_below(lambda other: grad_down(level, other).start())
    late.start()
    weight_blocks(r.out_blocks, r.e1, r.heads[...])
    scatters[2].start()
    r.small[5:6, :] = column_sum(r.ef[...].astype(jnp.float32))

    r.mem_acc[...] = jnp.zeros(r.mem_acc.shape, jnp.float32)
    r.pulls[...] = jnp.zeros(r.pulls.shape, jnp.float32)

    def memory_back(index, unused):
        here = pl.ds(pl.multiple_of(index * chunk, chunk), chunk)
        query = r.pair[0, here, :].astype(jnp.float32)
        grad = r.grad[here, :]
        val_parts, mu_pulls, sigma_pulls = [], [], []
        for head in range(heads):
            place = memory_place(query, r.spot_rows[0:2, :], lane_head == head)
            slope = place.gap / place.spread
            square = place.gap * slope
            density = place.height * jnp.exp(-0.5 * square)
            val_parts.append(dot_columns(density.astype(jnp.bfloat16), grad))
            weighed = dot_rows(grad * head_mask[head], r.mem[:, width:]) * density
            to_centre = -jnp.sum(weighed * slope, axis=1, keepdims=True)
            to_spread = 0.5 * jnp.sum(weighed * (square - 1.0), axis=1, keepdims=True) / place.spread
            mu_pulls.append(to_centre * place.centre * (1.0 - place.centre))
            sigma_pulls.append(to_spread * SPREAD / (1.0 + jnp.exp(-place.loose)))
        mu_pull, sigma_pull = pick_heads(mu_pulls, lane_head), pick_heads(sigma_pulls, lane_head)
        r.dq[0, here, :] = mu_pull * r.spot_rows[0:1, :] + sigma_pull * r.spot_rows[1:2, :]
        r.mem_acc[...] += pick_heads(val_parts, lane_head)
        r.pulls[0:1, :] += column_sum(mu_pull * query)
        r.pulls[1:2, :] += column_sum(sigma_pull * query)
        return unused

    lax.fori_loop(0, rows // chunk, memory_back, 0)
    by_head = lax.broadcasted_iota(jnp.int32, (8, 1), 0) == lane_head
    pulls = [jnp.where(by_head, r.pulls[i : i + 1, :], 0.0) for i in range(2)]
    for index in range(2):
        spot_grad = sum(dot_rows(part, r.mem[:, :width]) for part in thirds(pulls[index]))
        r.small[8 + heads * index : 8 + heads * (index + 1), :NB] = spot_grad[:heads, :]
    key_grad = dot_columns(
        jnp.concatenate(spot_rows_of(r.mu_w, r.sigma_w), axis=0).astype(jnp.bfloat16), jnp.concatenate(pulls, axis=0).astype(jnp.bfloat16)
    )
    r.mem_grad[...] = jnp.concatenate([key_grad, r.mem_acc[...]], axis=1).astype(jnp.bfloat16)
    scatters[0].middle()

    r.dq[1] = jnp.zeros((rows, width), jnp.float32)
    r.dk[...] = jnp.zeros(r.dk.shape, jnp.float32)
    r.dv[...] = jnp.zeros(r.dv.shape, jnp.float32)

    def query_fold(slot, grad_ref, block_ref, own):
        if not own:
            mask_rows = block_ref[rows:, :].astype(jnp.float32)
            key_mask = jnp.concatenate([mask_rows[0:1, :half], mask_rows[1:2, :half]], axis=1)

        def part(index, unused):
            here = pl.ds(pl.multiple_of(index * chunk, chunk), chunk)
            query = r.pair[slot, here, :]
            grad = grad_ref[here, :width]
            keys = block_ref[:rows, :width]
            vals = block_ref[:rows, width:]
            if own:
                q_pos = index * chunk + lax.broadcasted_iota(jnp.int32, (chunk, rows), 0)
                k_pos = lax.broadcasted_iota(jnp.int32, (chunk, rows), 1)
                visible = (q_pos >= k_pos) & (r.doc_col[here, :] == doc_row)
            products = []
            for head in range(heads):
                scores = dot_rows(query * head_mask[head], keys)
                if own:
                    scores = jnp.where(visible, scores, NEGATIVE)
                    lse = r.near_lse[head, here, :]
                else:
                    scores = scores + key_mask
                    lse = r.stat[slot, head, here, :]
                probs = jnp.exp(scores - lse)
                pull = dot_rows(grad * head_mask[head], vals) - r.stat[slot, heads + head, here, :]
                products.append(dot_plain((probs * pull).astype(jnp.bfloat16), keys))
            r.dq[slot, here, :] = r.dq[slot, here, :] + pick_heads(products, lane_head)
            return unused

        lax.fori_loop(0, rows // chunk, part, 0)

    query_fold(0, r.near, block_of(r.kv_col, level, "keys"), True)
    other_grad_ref = None

    def own_earlier(from_level, unused):
        query_fold(0, r.near, block_of(r.kv_col, from_level, "keys"), False)
        return unused

    lax.fori_loop(0, level, own_earlier, 0)
    scatters[1].middle()
    own_grad_side().wait_recv()
    other_grad_ref = block_of(r.grad_oth, level, "grad")

    def other_stats(index, unused):
        here = pl.ds(pl.multiple_of(index * chunk, chunk), chunk)
        extended = other_grad_ref[here, :]
        for row in range(2 * heads):
            r.stat[1, row, here, :] = stat_column(extended, width, row)
        return unused

    lax.fori_loop(0, rows // chunk, other_stats, 0)

    def other_earlier(from_level, unused):
        query_fold(1, other_grad_ref, block_of(r.kv_col, from_level, "keys"), False)
        return unused

    lax.fori_loop(0, level + 1 - side, other_earlier, 0)
    r.dq_out[...] = r.dq[1].astype(jnp.bfloat16)
    dq_copy = pltpu.make_async_remote_copy(
        r.dq_out, r.dq_in, r.dq_sem.at[0], r.dq_sem.at[1], device_id=partner, device_id_type=MESH_ID
    )
    dq_copy.start()
    late.middle()

    own_block_ref = block_of(r.kv_col, level, "keys")

    def key_fold(query_ref, grad_ref, own):
        def part(index, unused):
            here = pl.ds(pl.multiple_of(index * chunk, chunk), chunk)
            keys = own_block_ref[here, :width]
            vals = own_block_ref[here, width:]
            query = query_ref[...]
            extended = grad_ref[...]
            if own:
                k_pos = index * chunk + lax.broadcasted_iota(jnp.int32, (chunk, rows), 0)
                q_pos = lax.broadcasted_iota(jnp.int32, (chunk, rows), 1)
                visible = (q_pos >= k_pos) & (r.doc_col[here, :] == doc_row)
            grad = extended[:, :width]
            stats = stat_rows(extended, width, 8)
            key_parts, val_parts = [], []
            for head in range(heads):
                scores = dot_rows(keys * head_mask[head], query)
                if own:
                    scores = jnp.where(visible, scores, NEGATIVE)
                probs = jnp.exp(scores - stats[head : head + 1, :])
                val_parts.append(dot_plain(probs.astype(jnp.bfloat16), grad))
                pull = dot_rows(vals * head_mask[head], grad) - stats[heads + head : heads + head + 1, :]
                key_parts.append(dot_plain((probs * pull).astype(jnp.bfloat16), query))
            r.dk[here, :] = r.dk[here, :] + pick_heads(key_parts, lane_head)
            r.dv[here, :] = r.dv[here, :] + pick_heads(val_parts, lane_head)
            return unused

        lax.fori_loop(0, rows // chunk, part, 0)

    @pl.when(side == 0)
    def _():
        key_fold(r.pair.at[1], block_of(r.grad_oth, level, "grad"), False)

    def later(from_level):
        grad_down(from_level, level).wait_recv()
        grad_side(from_level).start()
        key_fold(
            block_of(r.query_col, from_level, "query"), block_of(r.grad_col, from_level, "grad"), False
        )
        query_side(from_level).wait_recv()
        grad_side(from_level).wait_recv()
        key_fold(
            block_of(r.query_oth, from_level, "query"), block_of(r.grad_oth, from_level, "grad"), False
        )

    each_above(later)
    reaches = r.doc_col[...] >= ((seq + 1) * rows).astype(jnp.float32)
    r.dk[...] = jnp.where(reaches, r.dk[...], 0.0)
    r.dv[...] = jnp.where(reaches, r.dv[...], 0.0)
    key_fold(r.pair.at[0], r.near, True)
    dq_copy.wait()
    r.grads[...] = jnp.concatenate(
        [(r.dq[0] + r.dq_in[...].astype(jnp.float32)) * (DH**-0.5), r.dk[...], r.dv[...]], axis=1
    ).astype(jnp.bfloat16)

    for part in range(PARTS):
        third.start(part, dot_rows(r.grads[span(theirs(part)), :], r.qkv_w[...]))
        r.own[span(part * size), :] = dot_rows(r.grads[span(mine(part)), :], r.qkv_w[...])
    memory_part = jnp.concatenate(
        [
            jnp.concatenate(
                [jnp.zeros((width, width), jnp.float32), dot_columns(r.coeff[slot], r.mem_grad[...])], axis=1
            )
            for slot in range(4)
        ],
        axis=0,
    )
    weight_blocks(r.qkv_blocks, r.normed, r.grads[...], memory_part)
    scatters[3].start()
    for part in range(PARTS):
        third.middle(part, r.own[span(part * size), :])
    bias_row = column_sum(r.grads[...].astype(jnp.float32))
    r.small[7:8, :] = jnp.concatenate(
        [bias_row[:, :width], bias_row[:, 2 * width :], jnp.zeros((1, D - 2 * width), jnp.float32)], axis=1
    )

    gain_sum = jnp.zeros((1, D), jnp.float32)
    offset_sum = jnp.zeros((1, D), jnp.float32)
    for part in range(PARTS):
        for start, grad in (
            (mine(part), r.own[span(part * size), :]),
            (theirs(part), third.core_out[part].astype(jnp.float32)),
        ):
            nhat, scale = normalize(r.tok[span(start), :].astype(jnp.float32))
            gain_sum = gain_sum + column_sum(grad * nhat)
            offset_sum = offset_sum + column_sum(grad)
    r.fold[0:1, :] = gain_sum
    r.fold[1:2, :] = offset_sum
    fold_copy = swap_with("core", r.fold, r.fold_in, (r.share_6, r.share_7), 0)
    fold_copy.start()
    scatters[2].middle()
    late.late()
    fold_copy.wait()
    r.chip_fold[...] = r.fold[...] + r.fold_in[...]
    chip_copy = swap_with("chip", r.chip_fold, r.chip_fold_in, (r.share_8, r.share_9), 0)
    chip_copy.start()

    def norm_part(part):
        grad = third.result(part)
        nhat, scale = normalize(r.tok[span(mine(part)), :].astype(jnp.float32))
        out = r.mid[span(part * size), :] + norm_back(grad, nhat, scale, first_gain)
        r.tokens_out[span(mine(part)), :] = out.astype(jnp.bfloat16)
        token_share.copy(part, mine(part)).start()

    for part in range(PARTS - 1):
        norm_part(part)
    chip_copy.wait()
    r.small[0:2, :] = r.chip_fold[0:2, :] + r.chip_fold_in[0:2, :]
    r.small[2:5, :] = r.chip_fold[2:5, :]
    small.start()
    scatters[3].middle()
    norm_part(PARTS - 1)
    scatters[0].finish(r.proj_share)
    scatters[1].finish(r.fc_share)
    small.middle()
    scatters[2].finish(r.out_share)
    scatters[3].finish(r.qkv_share)
    small.finish(r.small_out)
    late.finish()
    for part in range(PARTS):
        token_share.copy(part, theirs(part)).wait_recv()
        token_share.copy(part, mine(part)).wait_send()
        c_share.copy(part, mine(part)).wait_send()
        e_share.copy(part, mine(part)).wait_send()
    own_grad_side().wait_send()
    each_below(lambda other: grad_down(level, other).wait_send())
    each_above(lambda other: grad_side(other).wait_send())
    each_above(lambda other: query_side(other).wait_send())


def layer_back(levels, inputs):
    rows, width = inputs["heads"].shape
    heads = width // DH
    half = rows // 2
    size = half // PARTS
    hidden = inputs["fc_w"].shape[1]
    slab = D // (2 * levels)
    staged = levels > 8
    bf, fl = jnp.bfloat16, jnp.float32
    vmem = pl.BlockSpec(memory_space=pltpu.VMEM)
    far = pl.BlockSpec(memory_space=pl.ANY)
    dma = pltpu.SemaphoreType.DMA
    shape = jax.ShapeDtypeStruct
    outs = {
        "output": shape((rows, D), bf),
        "tokens_out": shape((rows, D), bf),
        "proj_share": shape((slab, hidden), fl),
        "fc_share": shape((slab, hidden), fl),
        "out_share": shape((slab, width), fl),
        "qkv_share": shape((slab, 3 * width), fl),
        "small_out": shape((16, D), fl),
    }
    gathered = {
        "query_oth": ((levels, rows, width), bf),
        "grad_col": ((levels, rows, LANES_OUT), bf),
        "grad_oth": ((levels, rows, LANES_OUT), bf),
    }
    scratch = {}
    out_specs = [vmem] * len(outs)
    if staged:
        for name, (dims, kind) in gathered.items():
            outs[name] = shape(dims, kind)
            out_specs.append(far)
        scratch["stage_query"] = pltpu.VMEM((rows, width), bf)
        scratch["stage_grad"] = pltpu.VMEM((rows, LANES_OUT), bf)
        scratch["stage_keys"] = pltpu.VMEM(inputs["kv_col"].shape[1:], bf)
        scratch["stage_sem"] = dma(())
    else:
        for name, (dims, kind) in gathered.items():
            scratch[name] = pltpu.VMEM(dims, kind)
    for name, dims, kind in (
        ("c", (rows, D), bf),
        ("e1", (rows, D), bf),
        ("u", (rows, hidden), bf),
        ("ef", (rows, hidden), bf),
        ("pull", (rows, hidden), fl),
        ("h1", (half, D), fl),
        ("own", (half, D), fl),
        ("base", (half, D), fl),
        ("mid", (half, D), fl),
        ("own_two", (half, D), fl),
        ("other_two", (half, D), bf),
        ("fold", (8, D), fl),
        ("fold_in", (8, D), fl),
        ("chip_fold", (8, D), fl),
        ("chip_fold_in", (8, D), fl),
        ("small", (16, D), fl),
        ("grad", (rows, width), bf),
        ("near", (rows, LANES_OUT), bf),
        ("far", (rows, LANES_OUT), bf),
        ("doc_col", (rows, 1), fl),
        ("near_lse", (heads, rows, 1), fl),
        ("stat", (2, 2 * heads, rows, 1), fl),
        ("mem_acc", (NB, width), fl),
        ("pulls", (8, width), fl),
        ("mem_grad", (NB, 2 * width), bf),
        ("dq", (2, rows, width), fl),
        ("dk", (rows, width), fl),
        ("dv", (rows, width), fl),
        ("dq_out", (rows, width), bf),
        ("dq_in", (rows, width), bf),
        ("grads", (rows, 3 * width), bf),
        ("proj_blocks", (2 * levels, slab, hidden), bf),
        ("fc_blocks", (2 * levels, slab, hidden), bf),
        ("out_blocks", (2 * levels, slab, width), bf),
        ("qkv_blocks", (2 * levels, slab, 3 * width), bf),
    ):
        scratch[name] = pltpu.VMEM(dims, kind)

    def several(prefix, items):
        scratch.update({f"{prefix}_{index}": item for index, item in enumerate(items)})

    for name in ("first", "second", "third"):
        several(name, TpSum.scratch(PARTS, size, D))
    for name, columns in (("proj", hidden), ("fc", hidden), ("out", width), ("qkv", 3 * width)):
        several(name, Scatter.scratch(levels, slab, columns))
    several("small", SmallSum.scratch(levels, (16, D)))
    several("late", LateOutput.scratch(half, D))
    several("share", [dma((PARTS,))] * 10)
    for name in ("qs", "gd", "gs"):
        scratch[name + "_send"] = dma((levels,))
        scratch[name + "_recv"] = dma((levels,))
    scratch["dq_sem"] = dma((2,))
    names = [*inputs, *outs, *scratch]
    results = pl.pallas_call(
        functools.partial(back_kernel, levels, names),
        out_shape=tuple(outs.values()),
        in_specs=[far if staged and name in ("kv_col", "query_col") else vmem for name in inputs],
        out_specs=tuple(out_specs),
        scratch_shapes=list(scratch.values()),
        name="layer_back",
        compiler_params=pltpu.CompilerParams(
            collective_id=2, has_side_effects=True, vmem_limit_bytes=VMEM_LIMIT
        ),
    )(*inputs.values())
    return SimpleNamespace(**dict(zip(outs, results)))


def unpack_kernel(output_ref, tokens_ref, proj_ref, fc_ref, out_ref, qkv_ref, small_ref, *outs):
    slab, width = out_ref.shape

    def turned(ref):
        fill = jnp.zeros((128 - slab, ref.shape[1]), jnp.float32)
        return jnp.transpose(jnp.concatenate([ref[...], fill], axis=0))[:, :slab]

    output_out, tokens_out, qkv_out, qv_out, out_out, out_b, fc_out, fc_b, proj_out, proj_b, *rest = outs
    output_out[...] = output_ref[...]
    tokens_out[...] = tokens_ref[...]
    for index in range(3):
        qkv_out[:, index, :] = qkv_ref[:, index * width : (index + 1) * width]
    for index in range(2):
        qv_out[index : index + 1, :] = small_ref[7:8, index * width : (index + 1) * width]
    out_out[...] = turned(out_ref)
    fc_out[...] = fc_ref[...]
    proj_out[...] = turned(proj_ref)
    for row, ref in zip((4, 5, 6, 0, 1, 2, 3), (out_b, fc_b, proj_b, *rest[:4])):
        ref[...] = small_ref[row, :]
    heads = rest[4].shape[0]
    rest[4][...] = small_ref[8 : 8 + heads, :NB]
    rest[5][...] = small_ref[8 + heads : 8 + 2 * heads, :NB]


def unpack(done, heads):
    slab, width = done.out_share.shape
    hidden = done.fc_share.shape[1]
    vmem = pl.BlockSpec(memory_space=pltpu.VMEM)

    def full(*dims):
        return jax.ShapeDtypeStruct(dims, jnp.float32)

    row = full(D)
    return pl.pallas_call(
        unpack_kernel,
        out_shape=(
            jax.ShapeDtypeStruct(done.output.shape, jnp.bfloat16),
            jax.ShapeDtypeStruct(done.output.shape, jnp.bfloat16),
            full(slab, 3, width),
            full(2, width),
            full(width, slab),
            row,
            full(slab, hidden),
            row,
            full(hidden, slab),
            row,
            row,
            row,
            row,
            row,
            full(heads, NB),
            full(heads, NB),
        ),
        in_specs=[vmem] * 7,
        out_specs=(vmem,) * 16,
        name="unpack",
        compiler_params=pltpu.CompilerParams(vmem_limit_bytes=VMEM_LIMIT),
    )(
        done.output,
        done.tokens_out,
        done.proj_share,
        done.fc_share,
        done.out_share,
        done.qkv_share,
        done.small_out,
    )


def local(
    tokens,
    cotangent,
    past_states,
    doc_ids,
    cur_book,
    past_book,
    past_age,
    ln1_gain,
    ln1_bias,
    qkv_weight,
    qv_bias,
    out_weight,
    out_bias,
    ln2_gain,
    ln2_bias,
    fc_weight,
    fc_bias,
    proj_weight,
    proj_bias,
    mu_weight,
    sigma_weight,
):
    heads_here = mu_weight.shape[0]
    head_cols = qkv_weight.shape[2]
    seq_count = lax.axis_size("seq")
    levels = seq_count // 2
    qkv_flat = qkv_weight.reshape(D, 3 * head_cols)
    doc_row = doc_ids[None, :]
    table = jnp.asarray(np.stack(coefficient_tables(seq_count // BOOKS, NB, SEG), axis=1))
    normed, pair, kv_col, attended, lse, heads_out, coeff, memory, spot_rows, query_col = (
        attention_forward(
        levels,
        tokens,
        ln1_gain,
        ln1_bias,
        qkv_flat,
        qv_bias,
        doc_row,
        past_states,
        cur_book[None],
        past_book[None],
        past_age[None],
        mu_weight,
        sigma_weight,
        table,
        )
    )
    done = layer_back(
        levels,
        {
            "heads": heads_out,
            "tok": tokens,
            "cot": cotangent,
            "out_w": out_weight,
            "fc_w": fc_weight,
            "proj_w": proj_weight,
            "ln1_gain": ln1_gain,
            "ln2_gain": ln2_gain,
            "ln2_bias": ln2_bias,
            "out_b": out_bias,
            "fc_b": fc_bias,
            "proj_b": proj_bias,
            "qkv_w": qkv_flat,
            "attended": attended,
            "lse": lse,
            "pair": pair,
            "kv_col": kv_col,
            "query_col": query_col,
            "doc": doc_row,
            "normed": normed,
            "coeff": coeff,
            "mem": memory,
            "spot_rows": spot_rows,
            "mu_w": mu_weight,
            "sigma_w": sigma_weight,
        },
    )
    return unpack(done, heads_here)


def solution(mesh):
    in_specs = (
        P("seq", None),
        P("seq", None),
        P("seq", None),
        P("seq"),
        P("seq"),
        P("seq"),
        P("seq"),
        P(),
        P(),
        P(None, None, "tp"),
        P(None, "tp"),
        P("tp", None),
        P(),
        P(),
        P(),
        P(None, "tp"),
        P("tp"),
        P("tp", None),
        P(),
        P("tp", None),
        P("tp", None),
    )
    out_specs = (
        P("seq", None),
        P("seq", None),
        P("seq", None, "tp"),
        P(None, "tp"),
        P("tp", "seq"),
        P(),
        P("seq", "tp"),
        P("tp"),
        P("tp", "seq"),
        P(),
        P(),
        P(),
        P(),
        P(),
        P("tp", None),
        P("tp", None),
    )
    return jax.shard_map(local, mesh=mesh, in_specs=in_specs, out_specs=out_specs, check_vma=False)
```

```python
import functools
from types import SimpleNamespace
from typing import NamedTuple

import ml_dtypes
import numpy as np

import jax
import jax.numpy as jnp
from jax import lax
from jax.experimental import pallas as pl
from jax.experimental.pallas import tpu as pltpu
from jax.sharding import PartitionSpec as P

D = 768
DH = 64
NB = 512
SEG = 512
BOOKS = 4


EPS = 1e-05
TAU = 0.75
RIDGE = 1.0
SPREAD = 0.01
NEGATIVE = -1e30
MESH_ID = pl.DeviceIdType.MESH
VMEM_LIMIT = 62 * 2**20


def coefficient_tables(age_count, basis_n, seg_len):
    shrink = TAU ** np.arange(age_count, dtype=np.float64)
    inside = (np.arange(seg_len) + 0.5) / seg_len
    times = shrink[:, None] * (TAU + (1.0 - TAU) * inside[None, :])
    centres = (np.arange(basis_n) + 0.5) / basis_n
    offset = (times[:, None, :] - centres[None, :, None]) * basis_n
    basis = np.exp(-0.5 * offset * offset)
    gram = np.einsum("agx,ahx->gh", basis, basis) + RIDGE * np.eye(basis_n)
    table = np.linalg.solve(gram[None], basis)
    high = table.astype(ml_dtypes.bfloat16)
    lower = (table - high.astype(np.float64)).astype(ml_dtypes.bfloat16)
    return high, lower


LANES_OUT = 256


def head_of_lane(width):
    return lax.broadcasted_iota(jnp.int32, (1, width), 1) // DH


def head_masks(width):
    lane_head = head_of_lane(width)
    return [(lane_head == head).astype(jnp.float32).astype(jnp.bfloat16) for head in range(width // DH)]


def pick_heads(per_head, lane_head):
    chosen = per_head[0]
    for head in range(1, len(per_head)):
        chosen = jnp.where(lane_head == head, per_head[head], chosen)
    return chosen


def dot_rows(left, right):
    return lax.dot_general(left, right, (((1,), (1,)), ((), ())), preferred_element_type=jnp.float32)


def dot_plain(left, right):
    return lax.dot_general(left, right, (((1,), (0,)), ((), ())), preferred_element_type=jnp.float32)


def thirds(value):
    first = value.astype(jnp.bfloat16)
    rest = value - first.astype(jnp.float32)
    second = rest.astype(jnp.bfloat16)
    third = (rest - second.astype(jnp.float32)).astype(jnp.bfloat16)
    return first, second, third


def with_stats(block, stats):
    rows, width = block.shape
    spare = LANES_OUT - width
    lane = lax.broadcasted_iota(jnp.int32, (1, spare), 1)
    tail = jnp.zeros((rows, spare), jnp.float32)
    for index, column in enumerate(stats):
        for part, value in enumerate(thirds(column)):
            tail = jnp.where(lane == 3 * index + part, value.astype(jnp.float32), tail)
    return jnp.concatenate([block, tail.astype(jnp.bfloat16)], axis=1)


def stat_column(extended, width, index):
    lane = lax.broadcasted_iota(jnp.int32, (1, LANES_OUT), 1)
    start = width + 3 * index
    mine = (lane >= start) & (lane < start + 3)
    return jnp.sum(jnp.where(mine, extended.astype(jnp.float32), 0.0), axis=1, keepdims=True)


def stats_as_rows(stats):
    lane = lax.broadcasted_iota(jnp.int32, (1, 128), 1)
    spread = jnp.zeros((stats[0].shape[0], 128), jnp.float32)
    for index, column in enumerate(stats):
        for part, value in enumerate(thirds(column)):
            spread = jnp.where(lane == 3 * index + part, value.astype(jnp.float32), spread)
    row = lax.broadcasted_iota(jnp.int32, (8, 128), 0)
    lane = lax.broadcasted_iota(jnp.int32, (8, 128), 1)
    chooser = ((lane >= 3 * row) & (lane < 3 * row + 3)).astype(jnp.float32).astype(jnp.bfloat16)
    return dot_rows(chooser, spread.astype(jnp.bfloat16))


def packed(block):
    half = block.shape[0] // 2
    return jnp.concatenate([block[:half], block[half:]], axis=1)


def greet(levels, whole_tp=False):
    seq, tp = lax.axis_index("seq"), lax.axis_index("tp")
    level, side = seq // 2, seq % 2
    barrier = pltpu.get_barrier_semaphore()
    pl.semaphore_signal(barrier, inc=1, device_id=(2 * level + 1 - side, tp), device_id_type=MESH_ID)

    def one(step, unused):
        other = lax.rem(level + step, levels)
        pl.semaphore_signal(barrier, inc=1, device_id=(2 * other + side, tp), device_id_type=MESH_ID)
        return unused

    lax.fori_loop(1, levels, one, 0)
    if not whole_tp:
        return barrier, levels
    greet_tp()
    return barrier, levels + 2


class MemoryPlace(NamedTuple):
    loose: jax.Array
    centre: jax.Array
    spread: jax.Array
    height: jax.Array
    gap: jax.Array


def memory_place(query, spot_rows, in_head):
    width_sq = 1.0 / (NB * NB)
    centre = 1.0 / (
        1.0 + jnp.exp(-jnp.sum(jnp.where(in_head, query * spot_rows[0:1, :], 0.0), axis=1, keepdims=True))
    )
    loose = jnp.sum(jnp.where(in_head, query * spot_rows[1:2, :], 0.0), axis=1, keepdims=True)
    soft = jnp.maximum(loose, 0.0) + jnp.log(1.0 + jnp.exp(-jnp.abs(loose)))
    spread = SPREAD * soft + width_sq
    height = (1.0 / NB) * lax.rsqrt(spread)
    centres = (lax.broadcasted_iota(jnp.int32, (1, NB), 1).astype(jnp.float32) + 0.5) / NB
    return MemoryPlace(loose, centre, spread, height, centre - centres)


def doc_vectors(doc_ref):
    row = doc_ref[...].astype(jnp.float32)
    return row, jnp.transpose(jnp.broadcast_to(row, (128, row.shape[1])))[:, 0:1]


def spot_rows_of(mu_ref, sigma_ref):
    fill = jnp.zeros((8 - mu_ref.shape[0], mu_ref.shape[1]), jnp.float32)
    return [jnp.concatenate([ref[...], fill], axis=0) for ref in (mu_ref, sigma_ref)]


def forward_kernel(
    levels,
    tok_ref,
    gain_ref,
    offset_ref,
    weight_ref,
    bias_ref,
    doc_ref,
    past_ref,
    book_ref,
    past_book_ref,
    past_age_ref,
    mu_ref,
    sigma_ref,
    table_ref,
    normed_ref,
    pair_ref,
    kv_out_ref,
    out_ref,
    lse_ref,
    heads_ref,
    coeff_ref,
    mem_ref,
    spot_row_ref,
    query_col_ref,
    top_ref,
    total_ref,
    acc_ref,
    part_ref,
    part_in_ref,
    kv_send,
    kv_recv,
    pair_sem,
    part_sem,
    past_col_ref,
    past_oth_ref,
    table_in_ref,
    past_up,
    past_down,
    past_side,
    coeff_sems,
    table_sem,
    doc_col_ref,
    read_ref,
    pack_ref,
    query_down,
):
    seq, tp = lax.axis_index("seq"), lax.axis_index("tp")
    level, side = seq // 2, seq % 2
    rows = tok_ref.shape[0]
    width = pair_ref.shape[2]
    heads = width // DH
    partner = (2 * level + 1 - side, tp)
    lane_head = head_of_lane(width)
    head_mask = head_masks(width)
    barrier, greetings = greet(levels, True)

    chunk = rows // 2
    time_half = rows // 2
    mark_row = lax.broadcasted_iota(jnp.int32, (16, 2 * width), 0)
    past_col_ref[level, time_half:, :] = jnp.where(
        mark_row == 0,
        past_book_ref[...].astype(jnp.float32),
        jnp.where(mark_row == 1, past_age_ref[...].astype(jnp.float32), 0.0),
    ).astype(jnp.bfloat16)
    for quarter in range(4):

        @pl.when(tp == quarter)
        def _(quarter=quarter):
            columns = past_ref[:, quarter * width : (quarter + 1) * width]
            past_col_ref[level, :time_half, :] = jnp.concatenate(
                [columns[:time_half], columns[time_half:]], axis=1
            )

    def past_copy(direction, from_level):
        block = past_col_ref.at[from_level]
        if direction == "side":
            sems, target, place = past_side, partner, past_oth_ref.at[from_level]
        elif direction == "up":
            sems, target, place = past_up, (lax.rem(2 * level + 2, 2 * levels) + side, tp), block
        else:
            sems, target, place = past_down, (lax.rem(2 * (level + levels - 1), 2 * levels) + side, tp), block
        return pltpu.make_async_remote_copy(
            block,
            place,
            sems.at[0, from_level],
            sems.at[1, from_level],
            device_id=target,
            device_id_type=MESH_ID,
        )

    pl.semaphore_wait(barrier, greetings)

    def pass_past(from_level, up, down):
        past_copy("side", from_level).start()
        if up:

            @pl.when(level < levels - 1)
            def _():
                past_copy("up", from_level).start()

        if down:

            @pl.when(level > 0)
            def _():
                past_copy("down", from_level).start()

    pass_past(level, True, True)

    doc_row, doc_column = doc_vectors(doc_ref)
    doc_col_ref[...] = doc_column
    bias = jnp.concatenate(
        [bias_ref[0:1, :], jnp.zeros((1, width), jnp.float32), bias_ref[1:2, :]], axis=1
    )

    def project(index, unused):
        here = pl.ds(pl.multiple_of(index * chunk, chunk), chunk)
        x = tok_ref[here, :].astype(jnp.float32)
        centred = x - jnp.mean(x, axis=1, keepdims=True)
        variance = jnp.mean(centred * centred, axis=1, keepdims=True)
        a = centred * lax.rsqrt(variance + EPS) * gain_ref[...][None, :] + offset_ref[...][None, :]
        a = a.astype(jnp.bfloat16)
        normed_ref[here, :] = a
        mixed = jnp.concatenate([dot_plain(a, weight_ref[index]) for index in range(3)], axis=1)
        mixed = (mixed + bias).astype(jnp.bfloat16)
        query = mixed[:, :width] * jnp.bfloat16(DH**-0.5)
        pair_ref[0, here, :] = query
        kv_out_ref[level, here, :] = mixed[:, width:]
        return unused

    lax.fori_loop(0, rows // chunk, project, 0)
    hidden = jnp.where(doc_row >= ((seq + 1) * rows).astype(jnp.float32), 0.0, NEGATIVE)
    mask_rows = jnp.where(
        mark_row[:, : rows // 2] == 0,
        hidden[:, : rows // 2],
        jnp.where(mark_row[:, : rows // 2] == 1, hidden[:, rows // 2 :], 0.0),
    )
    kv_out_ref[level, rows:, :] = jnp.concatenate(
        [mask_rows, jnp.zeros((16, 2 * width - rows // 2), jnp.float32)], axis=1
    ).astype(jnp.bfloat16)

    pair_copy = pltpu.make_async_remote_copy(
        pair_ref.at[0], pair_ref.at[1], pair_sem.at[0], pair_sem.at[1], device_id=partner, device_id_type=MESH_ID
    )
    pair_copy.start()

    def kv_copy(from_level):
        return pltpu.make_async_remote_copy(
            kv_out_ref.at[from_level],
            kv_out_ref.at[from_level],
            kv_send.at[from_level],
            kv_recv.at[from_level],
            device_id=(lax.rem(2 * level + 2, 2 * levels) + side, tp),
            device_id_type=MESH_ID,
        )

    pack_ref[...] = packed(pair_ref[0])

    def down_copy(from_level, to_level):
        return pltpu.make_async_remote_copy(
            pack_ref,
            query_col_ref.at[from_level],
            query_down.at[0, to_level],
            query_down.at[1, from_level],
            device_id=(2 * to_level + side, tp),
            device_id_type=MESH_ID,
        )

    def each_below(body):
        def one(step, unused):
            body(level - step)
            return unused

        lax.fori_loop(1, level + 1, one, 0)

    def each_above(body):
        def one(step, unused):
            body(level + step)
            return unused

        lax.fori_loop(1, levels - level, one, 0)

    @pl.when(level < levels - 1)
    def _():
        kv_copy(level).start()


    top_ref[...] = jnp.full(top_ref.shape, NEGATIVE, jnp.float32)
    total_ref[...] = jnp.zeros(total_ref.shape, jnp.float32)
    acc_ref[...] = jnp.zeros(acc_ref.shape, jnp.float32)

    doc_first = doc_row[0:1, 0:1]
    def reach_of(here):
        docs = doc_col_ref[here, :]
        last = (level == levels - 1) & (side == 1)
        return jnp.where(last & (docs != doc_first), NEGATIVE, 0.0)

    def fold(slot, from_level, mask_kind):
        mask_rows = kv_out_ref[from_level, rows:, :].astype(jnp.float32)
        key_mask = jnp.concatenate([mask_rows[0:1, : rows // 2], mask_rows[1:2, : rows // 2]], axis=1)

        def part(index, unused):
            here = pl.ds(pl.multiple_of(index * chunk, chunk), chunk)
            query = pair_ref[slot, here, :]
            keys = kv_out_ref[from_level, :rows, :width]
            vals = kv_out_ref[from_level, :rows, width:]
            if mask_kind == "own":
                q_pos = index * chunk + lax.broadcasted_iota(jnp.int32, (chunk, rows), 0)
                k_pos = lax.broadcasted_iota(jnp.int32, (chunk, rows), 1)
                visible = (q_pos >= k_pos) & (doc_col_ref[here, :] == doc_row)
            products, scales = [], []
            for head in range(heads):
                scores = dot_rows(query * head_mask[head], keys)
                old_top = top_ref[slot, head, here, :]
                if mask_kind == "own":
                    scores = jnp.where(visible, scores, NEGATIVE)
                    reach = 0.0
                else:
                    scores = scores + key_mask
                    reach = jnp.where(slot == 0, reach_of(here), 0.0)
                new_top = jnp.maximum(old_top, jnp.max(scores, axis=1, keepdims=True) + reach)
                weights = jnp.exp(scores - (new_top - reach))
                scale = jnp.exp(old_top - new_top)
                top_ref[slot, head, here, :] = new_top
                total_ref[slot, head, here, :] = total_ref[slot, head, here, :] * scale + jnp.sum(
                    weights, axis=1, keepdims=True
                )
                products.append(dot_plain(weights.astype(jnp.bfloat16), vals))
                scales.append(scale)
            acc_ref[slot, here, :] = acc_ref[slot, here, :] * pick_heads(scales, lane_head) + pick_heads(
                products, lane_head
            )
            return unused

        lax.fori_loop(0, rows // chunk, part, 0)

    fold(0, level, "own")
    pair_copy.wait()

    @pl.when(side == 0)
    def _():
        fold(1, level, "off")

    def keys_arrived(step):
        from_level = level - step
        kv_copy(from_level).wait_recv()

        @pl.when(level < levels - 1)
        def _():
            kv_copy(from_level).start()

        def both(slot, inner):
            fold(1 - slot, from_level, "off")
            return inner

        lax.fori_loop(0, 2, both, 0)

    def arrived(step, unused):
        @pl.when(level >= step)
        def _():
            past_copy("up", level - step).wait_recv()
            pass_past(level - step, True, False)

        @pl.when(level + step < levels)
        def _():
            past_copy("down", level + step).wait_recv()
            pass_past(level + step, False, True)

        @pl.when(step == 1)
        def _():
            each_below(lambda other: down_copy(level, other).start())

        @pl.when((level >= step) & (step < levels - 1))
        def _():
            keys_arrived(step)

        return unused

    lax.fori_loop(1, levels, arrived, 0)

    def from_side(other, unused):
        past_copy("side", other).wait_recv()
        return unused

    lax.fori_loop(0, levels, from_side, 0)
    own_book = book_ref[...].astype(jnp.float32)
    ages = table_ref.shape[0]

    def one_age(age, total):
        table_copy = pltpu.make_async_copy(table_ref.at[age], table_in_ref, table_sem)
        table_copy.start()

        def one_level(other, found):
            for blocks_ref in (past_col_ref, past_oth_ref):
                mark = blocks_ref[other, time_half:, :].astype(jnp.float32)
                chosen = (mark[0:1, :] == own_book) & (mark[1:2, :] == age.astype(jnp.float32))
                found = jnp.where(chosen, blocks_ref[other, :time_half, :].astype(jnp.float32), found)
            return found

        found = lax.fori_loop(
            0, levels, one_level, jnp.zeros((time_half, 2 * width), jnp.float32)
        ).astype(jnp.bfloat16)
        table_copy.wait()
        for index in range(2):
            table = table_in_ref[index]
            total = total + (
                dot_plain(table[:, :time_half], found)[:, :width]
                + dot_plain(table[:, time_half:], found)[:, width:]
            )
        return total

    coeff = lax.fori_loop(0, ages, one_age, jnp.zeros((NB, width), jnp.float32))
    coeff_ref[tp] = coeff.astype(jnp.bfloat16)

    def coeff_copy(kind, slot, index):
        return swap_with(kind, coeff_ref.at[slot], coeff_ref.at[slot], (coeff_sems.at[0], coeff_sems.at[1]), index)

    core_mate, chip_mate = tp + 1 - 2 * (tp % 2), lax.rem(tp + 2, 4)
    coeff_copy("chip", tp, 0).start()
    coeff_copy("core", tp, 1).start()


    @pl.when(level == levels - 1)
    def _():
        kv_copy(0).wait_recv()
        fold(1, 0, "off")

    def finish(index, unused):
        here = pl.ds(pl.multiple_of(index * chunk, chunk), chunk)
        totals = [total_ref[1, head, here, :] for head in range(heads)]
        tops = [top_ref[1, head, here, :] for head in range(heads)]
        some = [value > 0.0 for value in totals]
        inverse = [jnp.where(ok, 1.0 / jnp.where(ok, value, 1.0), 0.0) for ok, value in zip(some, totals)]
        logs = [
            jnp.where(ok, top + jnp.log(jnp.where(ok, value, 1.0)), NEGATIVE)
            for ok, top, value in zip(some, tops, totals)
        ]
        share = (acc_ref[1, here, :] * pick_heads(inverse, lane_head)).astype(jnp.bfloat16)
        part_ref[here, :] = with_stats(share, logs)
        return unused

    lax.fori_loop(0, rows // chunk, finish, 0)
    part_copy = pltpu.make_async_remote_copy(
        part_ref, part_in_ref, part_sem.at[0], part_sem.at[1], device_id=partner, device_id_type=MESH_ID
    )
    part_copy.start()

    @pl.when(level == levels - 1)
    def _():
        fold(0, 0, "off")

    coeff_copy("chip", chip_mate, 0).wait_recv()
    coeff_copy("core", chip_mate, 2).start()
    coeff_copy("core", core_mate, 1).wait_recv()
    coeff_copy("core", lax.rem(core_mate + 2, 4), 2).wait_recv()
    memory = jnp.zeros((NB, 2 * width), jnp.float32)
    for slot in range(4):
        here = slice(slot * width, (slot + 1) * width)
        memory = memory + jnp.concatenate(
            [dot_plain(coeff_ref[slot], weight_ref[index, here, :]) for index in (1, 2)], axis=1
        )
    mem_ref[...] = memory.astype(jnp.bfloat16)
    for index, spots in enumerate(spot_rows_of(mu_ref, sigma_ref)):
        row = sum(dot_plain(third, mem_ref[:, :width]) for third in thirds(spots))
        spot_row_ref[index : index + 1, :] = pick_heads(
            [row[head : head + 1, :] for head in range(heads)], lane_head
        )

    def read_memory(index, unused):
        here = pl.ds(pl.multiple_of(index * chunk, chunk), chunk)
        query = pair_ref[0, here, :].astype(jnp.float32)
        reads = []
        for head in range(heads):
            place = memory_place(query, spot_row_ref[0:2, :], lane_head == head)
            density = place.height * jnp.exp(place.gap * place.gap * (-0.5 / place.spread))
            reads.append(dot_plain(density.astype(jnp.bfloat16), mem_ref[:, width:]))
        read_ref[here, :] = pick_heads(reads, lane_head)
        return unused

    lax.fori_loop(0, rows // chunk, read_memory, 0)

    part_copy.wait()

    def merge(index, unused):
        here = pl.ds(pl.multiple_of(index * chunk, chunk), chunk)
        reach = reach_of(here)
        received = part_in_ref[here, :]
        mine, theirs, columns = [], [], []
        for head in range(heads):
            total = total_ref[0, head, here, :]
            own_log = top_ref[0, head, here, :] + jnp.log(total)
            other_log = stat_column(received, width, head) + reach
            high = jnp.maximum(own_log, other_log)
            both_log = high + jnp.log(jnp.exp(own_log - high) + jnp.exp(other_log - high))
            mine.append(jnp.exp(own_log - both_log) / total)
            theirs.append(jnp.exp(other_log - both_log))
            columns.append(both_log)
        attended = acc_ref[0, here, :] * pick_heads(mine, lane_head) + received[:, :width].astype(
            jnp.float32
        ) * pick_heads(theirs, lane_head)
        out_ref[here, :] = attended
        heads_ref[here, :] = (attended + read_ref[here, :]).astype(jnp.bfloat16)
        lane = lax.broadcasted_iota(jnp.int32, (1, 8), 1)
        packed = jnp.zeros((chunk, 8), jnp.float32)
        for head in range(heads):
            packed = jnp.where(lane == head, columns[head], packed)
        lse_ref[here, :] = packed
        return unused

    lax.fori_loop(0, rows // chunk, merge, 0)

    each_below(lambda other: down_copy(level, other).wait_send())
    each_above(lambda other: down_copy(other, level).wait_recv())
    coeff_copy("chip", tp, 0).wait_send()
    coeff_copy("core", tp, 1).wait_send()
    coeff_copy("core", chip_mate, 2).wait_send()

    def past_sent(other, unused):
        past_copy("side", other).wait_send()

        @pl.when((level < levels - 1) & (other <= level))
        def _():
            past_copy("up", other).wait_send()

        @pl.when((level > 0) & (other >= level))
        def _():
            past_copy("down", other).wait_send()

        return unused

    lax.fori_loop(0, levels, past_sent, 0)

    @pl.when(level < levels - 1)
    def _():
        def sent_up(from_level, unused):
            kv_copy(from_level).wait_send()
            return unused

        lax.fori_loop(0, level + 1, sent_up, 0)


def attention_forward(
    levels,
    tokens,
    gain,
    offset,
    weight,
    bias,
    doc_row,
    past,
    book,
    past_book,
    past_age,
    mu_weight,
    sigma_weight,
    table,
):
    rows = tokens.shape[0]
    width = weight.shape[2]
    heads = width // DH
    vmem = pl.BlockSpec(memory_space=pltpu.VMEM)
    far = pl.BlockSpec(memory_space=pl.ANY) if levels > 8 else vmem
    dma = pltpu.SemaphoreType.DMA
    return pl.pallas_call(
        functools.partial(forward_kernel, levels),
        out_shape=(
            jax.ShapeDtypeStruct((rows, D), jnp.bfloat16),
            jax.ShapeDtypeStruct((2, rows, width), jnp.bfloat16),
            jax.ShapeDtypeStruct((levels, rows + 16, 2 * width), jnp.bfloat16),
            jax.ShapeDtypeStruct((rows, width), jnp.float32),
            jax.ShapeDtypeStruct((rows, 8), jnp.float32),
            jax.ShapeDtypeStruct((rows, width), jnp.bfloat16),
            jax.ShapeDtypeStruct((4, NB, width), jnp.bfloat16),
            jax.ShapeDtypeStruct((NB, 2 * width), jnp.bfloat16),
            jax.ShapeDtypeStruct((8, width), jnp.float32),
            jax.ShapeDtypeStruct((levels, rows // 2, 2 * width), jnp.bfloat16),
        ),
        in_specs=[vmem] * 12 + [pl.BlockSpec(memory_space=pl.ANY)],
        out_specs=(vmem,) * 9 + (far,),
        scratch_shapes=[
            pltpu.VMEM((2, heads, rows, 1), jnp.float32),
            pltpu.VMEM((2, heads, rows, 1), jnp.float32),
            pltpu.VMEM((2, rows, width), jnp.float32),
            pltpu.VMEM((rows, LANES_OUT), jnp.bfloat16),
            pltpu.VMEM((rows, LANES_OUT), jnp.bfloat16),
            dma((levels,)),
            dma((levels,)),
            dma((2,)),
            dma((2,)),
            pltpu.VMEM((levels, SEG // 2 + 16, 2 * width), jnp.bfloat16),
            pltpu.VMEM((levels, SEG // 2 + 16, 2 * width), jnp.bfloat16),
            pltpu.VMEM(table.shape[1:], jnp.bfloat16),
            dma((2, levels)),
            dma((2, levels)),
            dma((2, levels)),
            dma((2, 3)),
            dma(()),
            pltpu.VMEM((rows, 1), jnp.float32),
            pltpu.VMEM((rows, width), jnp.float32),
            pltpu.VMEM((rows // 2, 2 * width), jnp.bfloat16),
            dma((2, levels)),
        ],
        name="attention_forward",
        compiler_params=pltpu.CompilerParams(
            collective_id=1, has_side_effects=True, vmem_limit_bytes=VMEM_LIMIT
        ),
    )(
        tokens,
        gain,
        offset,
        weight,
        bias,
        doc_row,
        past,
        book,
        past_book,
        past_age,
        mu_weight,
        sigma_weight,
        table,
    )


def column_copy(block_ref, from_level, landing_ref, send_sem, recv_sem, to_level):
    seq, tp = lax.axis_index("seq"), lax.axis_index("tp")
    return pltpu.make_async_remote_copy(
        block_ref,
        landing_ref.at[from_level],
        send_sem.at[to_level],
        recv_sem.at[from_level],
        device_id=(2 * to_level + seq % 2, tp),
        device_id_type=MESH_ID,
    )


class Scatter:
    def __init__(self, levels, blocks, plane_in, plane_sum, column_in, sems):
        self.levels, self.blocks = levels, blocks
        self.plane_in, self.plane_sum, self.column_in = plane_in, plane_sum, column_in
        self.plane_send, self.plane_recv, self.column_send, self.column_recv = sems
        seq, tp = lax.axis_index("seq"), lax.axis_index("tp")
        self.level, self.side, self.tp = seq // 2, seq % 2, tp

    def plane_copy(self, to_level):
        return pltpu.make_async_remote_copy(
            self.blocks.at[2 * to_level + 1 - self.side],
            self.plane_in.at[to_level],
            self.plane_send.at[to_level],
            self.plane_recv.at[to_level],
            device_id=(2 * self.level + 1 - self.side, self.tp),
            device_id_type=MESH_ID,
        )

    def swap_copy(self, from_level, to_level):
        return column_copy(
            self.plane_sum.at[to_level], from_level, self.column_in, self.column_send, self.column_recv, to_level
        )

    def loop(self, first, body):
        def one(step, unused):
            body(lax.rem(self.level + step, self.levels))
            return unused

        lax.fori_loop(first, self.levels, one, 0)

    def start(self):
        self.loop(1, lambda other: self.plane_copy(other).start())
        self.plane_copy(self.level).start()

    def middle(self):
        def one(other):
            self.plane_copy(other).wait_recv()
            total = self.blocks[2 * other + self.side].astype(jnp.float32) + self.plane_in[other].astype(
                jnp.float32
            )
            self.plane_sum[other] = total.astype(jnp.bfloat16)
            self.swap_copy(self.level, other).start()

        self.loop(1, one)

    def finish(self, out_ref):
        self.plane_copy(self.level).wait_recv()
        out_ref[...] = self.blocks[2 * self.level + self.side].astype(jnp.float32) + self.plane_in[
            self.level
        ].astype(jnp.float32)

        def one(other):
            self.swap_copy(other, self.level).wait_recv()
            out_ref[...] += self.column_in[other].astype(jnp.float32)

        self.loop(1, one)
        self.loop(0, lambda other: self.plane_copy(other).wait_send())
        self.loop(1, lambda other: self.swap_copy(self.level, other).wait_send())

    @staticmethod
    def scratch(levels, rows, width):
        buffer = pltpu.VMEM((levels, rows, width), jnp.bfloat16)
        return [buffer] * 3 + [pltpu.SemaphoreType.DMA((levels,))] * 4


class SmallSum:
    def __init__(self, levels, small, plane_in, column_in, sems):
        self.levels, self.small, self.plane_in, self.column_in = levels, small, plane_in, column_in
        self.plane_sem, self.column_send, self.column_recv = sems
        seq, tp = lax.axis_index("seq"), lax.axis_index("tp")
        self.level, self.side, self.tp = seq // 2, seq % 2, tp

    def plane_copy(self):
        return pltpu.make_async_remote_copy(
            self.small,
            self.plane_in,
            self.plane_sem.at[0],
            self.plane_sem.at[1],
            device_id=(2 * self.level + 1 - self.side, self.tp),
            device_id_type=MESH_ID,
        )

    def swap_copy(self, from_level, to_level):
        return column_copy(
            self.column_in.at[from_level], from_level, self.column_in, self.column_send, self.column_recv, to_level
        )

    def loop(self, body):
        def one(step, unused):
            body(lax.rem(self.level + step, self.levels))
            return unused

        lax.fori_loop(1, self.levels, one, 0)

    def start(self):
        self.plane_copy().start()

    def middle(self):
        self.plane_copy().wait()
        self.column_in[self.level] = self.small[...] + self.plane_in[...]
        self.loop(lambda other: self.swap_copy(self.level, other).start())

    def finish(self, out_ref):
        self.loop(lambda other: self.swap_copy(other, self.level).wait_recv())
        self.loop(lambda other: self.swap_copy(self.level, other).wait_send())
        out_ref[...] = self.column_in[0]

        def one(other, unused):
            out_ref[...] += self.column_in[other]
            return unused

        lax.fori_loop(1, self.levels, one, 0)

    @staticmethod
    def scratch(levels, shape):
        dma = pltpu.SemaphoreType.DMA
        return [
            pltpu.VMEM(shape, jnp.float32),
            pltpu.VMEM((levels,) + shape, jnp.float32),
            dma((2,)),
            dma((levels,)),
            dma((levels,)),
        ]


def tp_partner(kind):
    seq, tp = lax.axis_index("seq"), lax.axis_index("tp")
    if kind == "core":
        return (seq, tp + 1 - 2 * (tp % 2))
    return (seq, lax.rem(tp + 2, 4))


def greet_tp():
    barrier = pltpu.get_barrier_semaphore()
    for kind in ("core", "chip"):
        pl.semaphore_signal(barrier, inc=1, device_id=tp_partner(kind), device_id_type=MESH_ID)
    return barrier, 2


def swap_with(kind, source, target, sems, index):
    send, recv = sems
    return pltpu.make_async_remote_copy(
        source, target, send.at[index], recv.at[index], device_id=tp_partner(kind), device_id_type=MESH_ID
    )


class TpSum:
    def __init__(self, core_out, core_in, chip_out, chip_in, sems):
        self.core_out, self.core_in, self.chip_out, self.chip_in = core_out, core_in, chip_out, chip_in
        self.core_sems, self.chip_sems = sems[:2], sems[2:]

    def core_copy(self, part):
        return swap_with("core", self.core_out.at[part], self.core_in.at[part], self.core_sems, part)

    def chip_copy(self, part):
        return swap_with("chip", self.chip_out.at[part], self.chip_in.at[part], self.chip_sems, part)

    def start(self, part, for_other_core):
        self.core_out[part] = for_other_core.astype(jnp.bfloat16)
        self.core_copy(part).start()

    def middle(self, part, own):
        self.core_copy(part).wait()
        self.chip_out[part] = (own + self.core_in[part].astype(jnp.float32)).astype(jnp.bfloat16)
        self.chip_copy(part).start()

    def result(self, part):
        self.chip_copy(part).wait()
        return self.chip_out[part].astype(jnp.float32) + self.chip_in[part].astype(jnp.float32)

    @staticmethod
    def scratch(parts, rows, width):
        buffer = pltpu.VMEM((parts, rows, width), jnp.bfloat16)
        return [buffer] * 4 + [pltpu.SemaphoreType.DMA((parts,))] * 4

    COUNT = 8


class RowShare:
    def __init__(self, whole, rows, sems):
        self.whole, self.rows, self.sems = whole, rows, sems

    def copy(self, part, start):
        here = self.whole.at[pl.ds(pl.multiple_of(start, self.rows), self.rows), :]
        return swap_with("core", here, here, self.sems, part)


def normalize(v):
    centred = v - jnp.mean(v, axis=1, keepdims=True)
    scale = lax.rsqrt(jnp.mean(centred * centred, axis=1, keepdims=True) + EPS)
    return centred * scale, scale


def norm_back(grad, nhat, scale, gain):
    inner = grad * gain
    return (
        inner
        - jnp.mean(inner, axis=1, keepdims=True)
        - nhat * jnp.mean(inner * nhat, axis=1, keepdims=True)
    ) * scale


def gelu_and_slope(f):
    root = (2.0 / np.pi) ** 0.5
    square = f * f
    bend = jnp.tanh(root * f * (1.0 + 0.044715 * square))
    half = 0.5 * (1.0 + bend)
    slope = half + 0.5 * f * (1.0 - bend * bend) * (root * (1.0 + 3.0 * 0.044715 * square))
    return f * half, slope


def dot_columns(left, right):
    return lax.dot_general(left, right, (((0,), (0,)), ((), ())), preferred_element_type=jnp.float32)


def column_sum(v):
    return jnp.sum(v, axis=0, keepdims=True)


class LateOutput:
    def __init__(self, base, own, other, whole, sems):
        self.base, self.own, self.other, self.whole = base, own, other, whole
        self.half = own.shape[0]
        self.core_in, self.chip_out, self.chip_in = sems[:3]
        self.core_sems, self.chip_sems, self.share_sems = sems[3:5], sems[5:7], sems[7:9]
        self.share = RowShare(whole, self.half, self.share_sems)
        self.core = lax.axis_index("tp") % 2

    COUNT = 9

    def core_copy(self):
        return swap_with("core", self.other, self.core_in, self.core_sems, 0)

    def chip_copy(self):
        return swap_with("chip", self.chip_out, self.chip_in, self.chip_sems, 0)

    def start(self):
        self.core_copy().start()

    def middle(self):
        self.core_copy().wait()
        self.chip_out[...] = (self.own[...] + self.core_in[...].astype(jnp.float32)).astype(jnp.bfloat16)
        self.chip_copy().start()

    def late(self):
        self.chip_copy().wait()
        total = self.chip_out[...].astype(jnp.float32) + self.chip_in[...].astype(jnp.float32)
        here = pl.ds(pl.multiple_of(self.core * self.half, self.half), self.half)
        self.whole[here, :] = (self.base[...] + total).astype(jnp.bfloat16)
        self.share.copy(0, self.core * self.half).start()

    def finish(self):
        self.share.copy(0, (1 - self.core) * self.half).wait_recv()
        self.share.copy(0, self.core * self.half).wait_send()

    @staticmethod
    def scratch(half, width):
        buffer = pltpu.VMEM((half, width), jnp.bfloat16)
        return [buffer] * 3 + [pltpu.SemaphoreType.DMA((1,))] * 6


PARTS = 2


def back_kernel(levels, names, *refs):
    r = SimpleNamespace(**dict(zip(names, refs)))
    seq, tp = lax.axis_index("seq"), lax.axis_index("tp")
    level, side, core = seq // 2, seq % 2, tp % 2
    rows, width = r.heads.shape
    heads = width // DH
    half = rows // 2
    size = half // PARTS
    partner = (2 * level + 1 - side, tp)
    lane_head = head_of_lane(width)
    head_mask = head_masks(width)
    chunk = rows
    staged = hasattr(r, "stage_query")

    first, second, third = (
        TpSum(*(getattr(r, f"{name}_{i}") for i in range(4)), [getattr(r, f"{name}_{i}") for i in range(4, 8)])
        for name in ("first", "second", "third")
    )
    scatters = [
        Scatter(
            levels,
            getattr(r, f"{name}_blocks"),
            *(getattr(r, f"{name}_{i}") for i in range(3)),
            [getattr(r, f"{name}_{i}") for i in range(3, 7)],
        )
        for name in ("proj", "fc", "mix", "kv")
    ]
    small = SmallSum(levels, r.small, r.small_0, r.small_1, (r.small_2, r.small_3, r.small_4))
    late = LateOutput(
        r.base, r.own_two, r.other_two, r.output, [getattr(r, f"late_{i}") for i in range(LateOutput.COUNT)]
    )
    c_share = RowShare(r.c, size, (r.share_0, r.share_1))
    e_share = RowShare(r.e1, size, (r.share_2, r.share_3))
    token_share = RowShare(r.tokens_out, size, (r.share_4, r.share_5))
    gain, offset, out_b, fc_b, proj_b, first_gain = (
        ref[...][None, :] for ref in (r.ln2_gain, r.ln2_bias, r.out_b, r.fc_b, r.proj_b, r.ln1_gain)
    )
    barrier, greetings = greet(levels, True)

    def span(start, count=size):
        return pl.ds(pl.multiple_of(start, size), count)

    def mine(part):
        return core * half + part * size

    def theirs(part):
        return (1 - core) * half + part * size

    def block_of(blocks_ref, from_level, place):
        if not staged:
            return blocks_ref.at[from_level]
        target = getattr(r, "stage_" + place)
        copy = pltpu.make_async_copy(blocks_ref.at[from_level], target, r.stage_sem)
        copy.start()
        copy.wait()
        return target

    def down_copy(source_ref, landing_ref, sems, from_level, to_level):
        send, recv = sems
        return pltpu.make_async_remote_copy(
            source_ref,
            landing_ref.at[from_level],
            send.at[to_level],
            recv.at[from_level],
            device_id=(2 * to_level + side, tp),
            device_id_type=MESH_ID,
        )

    def side_copy(source_ref, landing_ref, sems, from_level):
        send, recv = sems
        return pltpu.make_async_remote_copy(
            source_ref,
            landing_ref.at[from_level],
            send.at[from_level],
            recv.at[from_level],
            device_id=partner,
            device_id_type=MESH_ID,
        )

    def query_side(from_level):
        return side_copy(r.query_col.at[from_level], r.query_oth, (r.qs_send, r.qs_recv), from_level)

    def grad_down(from_level, to_level):
        return (
            down_copy(r.pack, r.grad_col, (r.gd_send, r.gd_recv), from_level, to_level),
            down_copy(r.far_rows, r.rows_col, (r.rd_send, r.rd_recv), from_level, to_level),
        )

    def grad_side(from_level):
        return (
            side_copy(r.grad_col.at[from_level], r.grad_oth, (r.gs_send, r.gs_recv), from_level),
            side_copy(r.rows_col.at[from_level], r.rows_oth, (r.rs_send, r.rs_recv), from_level),
        )

    def own_grad_side():
        return (
            side_copy(r.pack, r.grad_oth, (r.gs_send, r.gs_recv), level),
            side_copy(r.far_rows, r.rows_oth, (r.rs_send, r.rs_recv), level),
        )

    def start_all(copies):
        for copy in copies:
            copy.start()

    def wait_recv_all(copies):
        for copy in copies:
            copy.wait_recv()

    def wait_send_all(copies):
        for copy in copies:
            copy.wait_send()

    def opened(block_ref, target):
        target[:half, :] = block_ref[:, :width]
        target[half:, :] = block_ref[:, width:]
        return target

    def each_below(body):
        def one(step, unused):
            body(level - step)
            return unused

        lax.fori_loop(1, level + 1, one, 0)

    def each_above(body):
        def one(step, unused):
            body(level + step)
            return unused

        lax.fori_loop(1, levels - level, one, 0)

    pl.semaphore_wait(barrier, greetings)

    each_above(lambda other: query_side(other).start())

    for part in range(PARTS):
        first.start(part, dot_plain(r.heads[span(theirs(part)), :], r.out_w[...]))
        r.own[span(part * size), :] = dot_plain(r.heads[span(mine(part)), :], r.out_w[...])
    for part in range(PARTS):
        first.middle(part, r.own[span(part * size), :])

    def early(index, unused):
        here = span(index * size)
        r.pull[here, :] = dot_rows(r.cot[here, :], r.proj_w[...])
        return unused

    lax.fori_loop(0, rows // size, early, 0)
    r.small[...] = jnp.zeros(r.small.shape, jnp.float32)
    r.fold[...] = jnp.zeros(r.fold.shape, jnp.float32)
    r.small[6:7, :] = column_sum(r.cot[...].astype(jnp.float32))

    def feed(start):
        here = span(start)
        f = dot_plain(r.c[here, :], r.fc_w[...]) + fc_b
        u, slope = gelu_and_slope(f)
        r.u[here, :] = u.astype(jnp.bfloat16)
        ef = (r.pull[here, :] * slope).astype(jnp.bfloat16)
        r.ef[here, :] = ef
        return dot_rows(ef, r.fc_w[...])

    for part in range(PARTS):
        total = first.result(part) + out_b
        h1 = r.tok[span(mine(part)), :].astype(jnp.float32) + total
        r.h1[span(part * size), :] = h1
        nhat, scale = normalize(h1)
        r.c[span(mine(part)), :] = (nhat * gain + offset).astype(jnp.bfloat16)
        c_share.copy(part, mine(part)).start()
        r.own[span(part * size), :] = feed(mine(part))
        c_share.copy(part, theirs(part)).wait_recv()
        second.start(part, feed(theirs(part)))
        r.other_two[span(part * size), :] = dot_plain(r.u[span(theirs(part)), :], r.proj_w[...]).astype(
            jnp.bfloat16
        )
        r.own_two[span(part * size), :] = dot_plain(r.u[span(mine(part)), :], r.proj_w[...])
        second.middle(part, r.own[span(part * size), :])

    r.base[...] = r.h1[...] + proj_b
    bite = 384

    def weight_blocks(blocks_ref, left_ref, right, extra=None, place_of=0):
        slab, columns = blocks_ref.shape[1], right.shape[1]
        for index in range(D // bite):
            value = dot_columns(left_ref[:, index * bite : (index + 1) * bite], right)
            if extra is not None:
                start = index * bite + extra
                value = value + r.pull[:bite, start : start + columns]
            for place in range(bite // slab):
                blocks_ref[
                    index * (bite // slab) + place, :, place_of * columns : (place_of + 1) * columns
                ] = value[place * slab : (place + 1) * slab].astype(jnp.bfloat16)

    weight_blocks(r.proj_blocks, r.cot, r.u[...])
    scatters[0].start()
    weight_blocks(r.fc_blocks, r.c, r.ef[...])
    scatters[1].start()

    gain_sum = jnp.zeros((1, D), jnp.float32)
    offset_sum = jnp.zeros((1, D), jnp.float32)
    out_sum = jnp.zeros((1, D), jnp.float32)
    for part in range(PARTS):
        grad = second.result(part)
        nhat, scale = normalize(r.h1[span(part * size), :])
        gain_sum = gain_sum + column_sum(grad * nhat)
        offset_sum = offset_sum + column_sum(grad)
        mid = r.cot[span(mine(part)), :].astype(jnp.float32) + norm_back(grad, nhat, scale, gain)
        r.mid[span(part * size), :] = mid
        e1 = mid.astype(jnp.bfloat16)
        out_sum = out_sum + column_sum(e1.astype(jnp.float32))
        r.e1[span(mine(part)), :] = e1
        e_share.copy(part, mine(part)).start()
        r.grad[span(mine(part)), :] = dot_rows(e1, r.out_w[...]).astype(jnp.bfloat16)
    r.fold[2:3, :] = gain_sum
    r.fold[3:4, :] = offset_sum
    r.fold[4:5, :] = out_sum
    for part in range(PARTS):
        e_share.copy(part, theirs(part)).wait_recv()
        r.grad[span(theirs(part)), :] = dot_rows(r.e1[span(theirs(part)), :], r.out_w[...]).astype(jnp.bfloat16)

    r.pack[...] = packed(r.grad[...])
    own_grad_side()[0].start()
    each_below(lambda other: grad_down(level, other)[0].start())
    doc_row, doc_column = doc_vectors(r.doc)
    r.doc_col[...] = doc_column
    doc_first = doc_row[0:1, 0:1]
    last = (level == levels - 1) & (side == 1)

    def prepare(index, unused):
        here = pl.ds(pl.multiple_of(index * chunk, chunk), chunk)
        grad = r.grad[here, :]
        product = grad.astype(jnp.float32) * r.attended[here, :]
        far = jnp.where(last & (r.doc_col[here, :] != doc_first), -NEGATIVE, 0.0)
        lses = [r.lse[here, head : head + 1] for head in range(heads)]
        deltas = [
            jnp.sum(jnp.where(lane_head == head, product, 0.0), axis=1, keepdims=True)
            for head in range(heads)
        ]
        r.near_rows[:, here] = stats_as_rows(lses + deltas)
        r.far_rows[:, here] = stats_as_rows([lse + far for lse in lses] + deltas)
        for head in range(heads):
            r.near_lse[head, here, :] = lses[head]
            r.stat[0, head, here, :] = lses[head] + far
            r.stat[0, heads + head, here, :] = deltas[head]
        return unused

    lax.fori_loop(0, rows // chunk, prepare, 0)
    own_grad_side()[1].start()
    each_below(lambda other: grad_down(level, other)[1].start())
    late.start()
    r.small[5:6, :] = column_sum(r.ef[...].astype(jnp.float32))

    r.mem_acc[...] = jnp.zeros(r.mem_acc.shape, jnp.float32)
    r.pulls[...] = jnp.zeros(r.pulls.shape, jnp.float32)

    def memory_back(index, unused):
        here = pl.ds(pl.multiple_of(index * chunk, chunk), chunk)
        query = r.pair[0, here, :].astype(jnp.float32)
        grad = r.grad[here, :]
        val_parts, mu_pulls, sigma_pulls = [], [], []
        for head in range(heads):
            place = memory_place(query, r.spot_rows[0:2, :], lane_head == head)
            slope = place.gap / place.spread
            square = place.gap * slope
            density = place.height * jnp.exp(-0.5 * square)
            val_parts.append(dot_columns(density.astype(jnp.bfloat16), grad))
            weighed = dot_rows(grad * head_mask[head], r.mem[:, width:]) * density
            to_centre = -jnp.sum(weighed * slope, axis=1, keepdims=True)
            to_spread = 0.5 * jnp.sum(weighed * (square - 1.0), axis=1, keepdims=True) / place.spread
            mu_pulls.append(to_centre * place.centre * (1.0 - place.centre))
            sigma_pulls.append(to_spread * SPREAD / (1.0 + jnp.exp(-place.loose)))
        mu_pull, sigma_pull = pick_heads(mu_pulls, lane_head), pick_heads(sigma_pulls, lane_head)
        r.dq[0, here, :] = mu_pull * r.spot_rows[0:1, :] + sigma_pull * r.spot_rows[1:2, :]
        r.mem_acc[...] += pick_heads(val_parts, lane_head)
        r.pulls[0:1, :] += column_sum(mu_pull * query)
        r.pulls[1:2, :] += column_sum(sigma_pull * query)
        return unused

    lax.fori_loop(0, rows // chunk, memory_back, 0)
    by_head = lax.broadcasted_iota(jnp.int32, (8, 1), 0) == lane_head
    pulls = [jnp.where(by_head, r.pulls[i : i + 1, :], 0.0) for i in range(2)]
    for index in range(2):
        spot_grad = sum(dot_rows(part, r.mem[:, :width]) for part in thirds(pulls[index]))
        r.small[8 + heads * index : 8 + heads * (index + 1), :NB] = spot_grad[:heads, :]
    key_grad = dot_columns(
        jnp.concatenate(spot_rows_of(r.mu_w, r.sigma_w), axis=0).astype(jnp.bfloat16), jnp.concatenate(pulls, axis=0).astype(jnp.bfloat16)
    )
    r.mem_grad[...] = jnp.concatenate([key_grad, r.mem_acc[...]], axis=1).astype(jnp.bfloat16)
    for slot in range(4):
        r.pull[
            (slot % 2) * width : (slot % 2 + 1) * width,
            2 * width * (slot // 2) : 2 * width * (slot // 2 + 1),
        ] = dot_columns(r.coeff[slot], r.mem_grad[...])
    scatters[0].middle()

    r.dq[1] = jnp.zeros((rows, width), jnp.float32)
    r.dk[...] = jnp.zeros(r.dk.shape, jnp.float32)
    r.dv[...] = jnp.zeros(r.dv.shape, jnp.float32)

    def query_fold(slot, grad_ref, block_ref, own):
        if not own:
            mask_rows = block_ref[rows:, :].astype(jnp.float32)
            key_mask = jnp.concatenate([mask_rows[0:1, :half], mask_rows[1:2, :half]], axis=1)

        def part(index, unused):
            here = pl.ds(pl.multiple_of(index * chunk, chunk), chunk)
            query = r.pair[slot, here, :]
            grad = grad_ref[here, :]
            keys = block_ref[:rows, :width]
            vals = block_ref[:rows, width:]
            if own:
                q_pos = index * chunk + lax.broadcasted_iota(jnp.int32, (chunk, rows), 0)
                k_pos = lax.broadcasted_iota(jnp.int32, (chunk, rows), 1)
                visible = (q_pos >= k_pos) & (r.doc_col[here, :] == doc_row)
            products = []
            for head in range(heads):
                scores = dot_rows(query * head_mask[head], keys)
                if own:
                    scores = jnp.where(visible, scores, NEGATIVE)
                    lse = r.near_lse[head, here, :]
                else:
                    scores = scores + key_mask
                    lse = r.stat[slot, head, here, :]
                probs = jnp.exp(scores - lse)
                pull = dot_rows(grad * head_mask[head], vals) - r.stat[slot, heads + head, here, :]
                products.append(dot_plain((probs * pull).astype(jnp.bfloat16), keys))
            r.dq[slot, here, :] = r.dq[slot, here, :] + pick_heads(products, lane_head)
            return unused

        lax.fori_loop(0, rows // chunk, part, 0)

    query_fold(0, r.grad, block_of(r.kv_col, level, "keys"), True)

    def own_earlier(from_level, unused):
        query_fold(0, r.grad, block_of(r.kv_col, from_level, "keys"), False)
        return unused

    lax.fori_loop(0, level, own_earlier, 0)
    scatters[1].middle()
    wait_recv_all(own_grad_side())
    other_grad_ref = opened(block_of(r.grad_oth, level, "grad"), r.other_grad)
    other_columns = jnp.transpose(
        jnp.concatenate([r.rows_oth[level], jnp.zeros((120, rows), jnp.float32)], axis=0)
    )
    for row in range(2 * heads):
        r.stat[1, row] = other_columns[:, row : row + 1]

    def other_earlier(from_level, unused):
        query_fold(1, other_grad_ref, block_of(r.kv_col, from_level, "keys"), False)
        return unused

    lax.fori_loop(0, level + 1 - side, other_earlier, 0)
    r.dq_out[...] = r.dq[1].astype(jnp.bfloat16)
    dq_copy = pltpu.make_async_remote_copy(
        r.dq_out, r.dq_in, r.dq_sem.at[0], r.dq_sem.at[1], device_id=partner, device_id_type=MESH_ID
    )
    dq_copy.start()
    late.middle()

    own_block_ref = block_of(r.kv_col, level, "keys")

    def key_fold(query_ref, grad_ref, stats, own):
        def part(index, unused):
            here = pl.ds(pl.multiple_of(index * chunk, chunk), chunk)
            keys = own_block_ref[here, :width]
            vals = own_block_ref[here, width:]
            query = query_ref[...]
            grad = grad_ref[...]
            if own:
                k_pos = index * chunk + lax.broadcasted_iota(jnp.int32, (chunk, rows), 0)
                q_pos = lax.broadcasted_iota(jnp.int32, (chunk, rows), 1)
                visible = (q_pos >= k_pos) & (r.doc_col[here, :] == doc_row)
            key_parts, val_parts = [], []
            for head in range(heads):
                scores = dot_rows(keys * head_mask[head], query)
                if own:
                    scores = jnp.where(visible, scores, NEGATIVE)
                probs = jnp.exp(scores - stats[head : head + 1, :])
                val_parts.append(dot_plain(probs.astype(jnp.bfloat16), grad))
                pull = dot_rows(vals * head_mask[head], grad) - stats[heads + head : heads + head + 1, :]
                key_parts.append(dot_plain((probs * pull).astype(jnp.bfloat16), query))
            r.dk[here, :] = r.dk[here, :] + pick_heads(key_parts, lane_head)
            r.dv[here, :] = r.dv[here, :] + pick_heads(val_parts, lane_head)
            return unused

        lax.fori_loop(0, rows // chunk, part, 0)

    @pl.when(side == 0)
    def _():
        key_fold(r.pair.at[1], r.other_grad, r.rows_oth[level], False)

    def later(from_level):
        wait_recv_all(grad_down(from_level, level))
        start_all(grad_side(from_level))
        key_fold(
            opened(block_of(r.query_col, from_level, "query"), r.open_query),
            opened(block_of(r.grad_col, from_level, "grad"), r.open_grad),
            r.rows_col[from_level],
            False,
        )
        query_side(from_level).wait_recv()
        wait_recv_all(grad_side(from_level))
        key_fold(
            opened(block_of(r.query_oth, from_level, "query"), r.open_query),
            opened(block_of(r.grad_oth, from_level, "grad"), r.open_grad),
            r.rows_oth[from_level],
            False,
        )

    dq_copy.wait()
    r.grads[0] = ((r.dq[0] + r.dq_in[...].astype(jnp.float32)) * (DH**-0.5)).astype(jnp.bfloat16)
    weight_blocks(r.mix_blocks, r.normed, r.grads[0], None, 0)
    weight_blocks(r.mix_blocks, r.e1, r.heads[...], None, 1)
    scatters[2].start()
    each_above(later)
    scatters[2].middle()
    reaches = r.doc_col[...] >= ((seq + 1) * rows).astype(jnp.float32)
    r.dk[...] = jnp.where(reaches, r.dk[...], 0.0)
    r.dv[...] = jnp.where(reaches, r.dv[...], 0.0)
    key_fold(r.pair.at[0], r.grad, r.near_rows[...], True)
    r.grads[1] = r.dk[...].astype(jnp.bfloat16)
    r.grads[2] = r.dv[...].astype(jnp.bfloat16)

    def norm_grad(start):
        return sum(dot_rows(r.grads[index, span(start), :], r.qkv_w[index]) for index in range(3))

    for part in range(PARTS):
        third.start(part, norm_grad(theirs(part)))
        r.own[span(part * size), :] = norm_grad(mine(part))
    for index in range(2):
        weight_blocks(
            r.kv_blocks,
            r.normed,
            r.grads[1 + index],
            index * width,
            index,
        )
    scatters[3].start()
    for part in range(PARTS):
        third.middle(part, r.own[span(part * size), :])
    r.small[7:8, :] = jnp.concatenate(
        [column_sum(r.grads[index].astype(jnp.float32)) for index in (0, 2)]
        + [jnp.zeros((1, D - 2 * width), jnp.float32)],
        axis=1,
    )

    gain_sum = jnp.zeros((1, D), jnp.float32)
    offset_sum = jnp.zeros((1, D), jnp.float32)
    for part in range(PARTS):
        for start, grad in (
            (mine(part), r.own[span(part * size), :]),
            (theirs(part), third.core_out[part].astype(jnp.float32)),
        ):
            nhat, scale = normalize(r.tok[span(start), :].astype(jnp.float32))
            gain_sum = gain_sum + column_sum(grad * nhat)
            offset_sum = offset_sum + column_sum(grad)
    r.fold[0:1, :] = gain_sum
    r.fold[1:2, :] = offset_sum
    fold_copy = swap_with("core", r.fold, r.fold_in, (r.share_6, r.share_7), 0)
    fold_copy.start()
    late.late()
    fold_copy.wait()
    r.chip_fold[...] = r.fold[...] + r.fold_in[...]
    chip_copy = swap_with("chip", r.chip_fold, r.chip_fold_in, (r.share_8, r.share_9), 0)
    chip_copy.start()
    scatters[3].middle()

    def norm_part(part):
        grad = third.result(part)
        nhat, scale = normalize(r.tok[span(mine(part)), :].astype(jnp.float32))
        out = r.mid[span(part * size), :] + norm_back(grad, nhat, scale, first_gain)
        r.tokens_out[span(mine(part)), :] = out.astype(jnp.bfloat16)
        token_share.copy(part, mine(part)).start()

    chip_copy.wait()
    r.small[0:2, :] = r.chip_fold[0:2, :] + r.chip_fold_in[0:2, :]
    r.small[2:5, :] = r.chip_fold[2:5, :]
    small.start()
    norm_part(0)
    small.middle()
    for part in range(1, PARTS):
        norm_part(part)
    scatters[0].finish(r.proj_share)
    scatters[1].finish(r.fc_share)
    scatters[2].finish(r.mix_share)
    scatters[3].finish(r.kv_share)
    small.finish(r.small_out)
    late.finish()
    for part in range(PARTS):
        token_share.copy(part, theirs(part)).wait_recv()
        token_share.copy(part, mine(part)).wait_send()
        c_share.copy(part, mine(part)).wait_send()
        e_share.copy(part, mine(part)).wait_send()
    wait_send_all(own_grad_side())
    each_below(lambda other: wait_send_all(grad_down(level, other)))
    each_above(lambda other: wait_send_all(grad_side(other)))
    each_above(lambda other: query_side(other).wait_send())


def layer_back(levels, inputs):
    rows, width = inputs["heads"].shape
    heads = width // DH
    half = rows // 2
    size = half // PARTS
    hidden = inputs["fc_w"].shape[1]
    slab = D // (2 * levels)
    staged = levels > 8
    bf, fl = jnp.bfloat16, jnp.float32
    vmem = pl.BlockSpec(memory_space=pltpu.VMEM)
    far = pl.BlockSpec(memory_space=pl.ANY)
    dma = pltpu.SemaphoreType.DMA
    shape = jax.ShapeDtypeStruct
    outs = {
        "output": shape((rows, D), bf),
        "tokens_out": shape((rows, D), bf),
        "proj_share": shape((slab, hidden), fl),
        "fc_share": shape((slab, hidden), fl),
        "mix_share": shape((slab, 2 * width), fl),
        "kv_share": shape((slab, 2 * width), fl),
        "small_out": shape((16, D), fl),
    }
    gathered = {
        "query_oth": ((levels, half, 2 * width), bf),
        "grad_col": ((levels, half, 2 * width), bf),
        "grad_oth": ((levels, half, 2 * width), bf),
    }
    scratch = {}
    out_specs = [vmem] * len(outs)
    if staged:
        for name, (dims, kind) in gathered.items():
            outs[name] = shape(dims, kind)
            out_specs.append(far)
        scratch["stage_query"] = pltpu.VMEM((half, 2 * width), bf)
        scratch["stage_grad"] = pltpu.VMEM((half, 2 * width), bf)
        scratch["stage_keys"] = pltpu.VMEM(inputs["kv_col"].shape[1:], bf)
        scratch["stage_sem"] = dma(())
    else:
        for name, (dims, kind) in gathered.items():
            scratch[name] = pltpu.VMEM(dims, kind)
    for name, dims, kind in (
        ("c", (rows, D), bf),
        ("e1", (rows, D), bf),
        ("u", (rows, hidden), bf),
        ("ef", (rows, hidden), bf),
        ("pull", (rows, hidden), fl),
        ("h1", (half, D), fl),
        ("own", (half, D), fl),
        ("base", (half, D), fl),
        ("mid", (half, D), fl),
        ("own_two", (half, D), fl),
        ("other_two", (half, D), bf),
        ("fold", (8, D), fl),
        ("fold_in", (8, D), fl),
        ("chip_fold", (8, D), fl),
        ("chip_fold_in", (8, D), fl),
        ("small", (16, D), fl),
        ("grad", (rows, width), bf),
        ("pack", (half, 2 * width), bf),
        ("near_rows", (8, rows), fl),
        ("far_rows", (8, rows), fl),
        ("rows_col", (levels, 8, rows), fl),
        ("rows_oth", (levels, 8, rows), fl),
        ("other_grad", (rows, width), bf),
        ("open_query", (rows, width), bf),
        ("open_grad", (rows, width), bf),
        ("doc_col", (rows, 1), fl),
        ("near_lse", (heads, rows, 1), fl),
        ("stat", (2, 2 * heads, rows, 1), fl),
        ("mem_acc", (NB, width), fl),
        ("pulls", (8, width), fl),
        ("mem_grad", (NB, 2 * width), bf),
        ("dq", (2, rows, width), fl),
        ("dk", (rows, width), fl),
        ("dv", (rows, width), fl),
        ("dq_out", (rows, width), bf),
        ("dq_in", (rows, width), bf),
        ("grads", (3, rows, width), bf),
        ("proj_blocks", (2 * levels, slab, hidden), bf),
        ("fc_blocks", (2 * levels, slab, hidden), bf),
        ("mix_blocks", (2 * levels, slab, 2 * width), bf),
        ("kv_blocks", (2 * levels, slab, 2 * width), bf),
    ):
        scratch[name] = pltpu.VMEM(dims, kind)

    def several(prefix, items):
        scratch.update({f"{prefix}_{index}": item for index, item in enumerate(items)})

    for name in ("first", "second", "third"):
        several(name, TpSum.scratch(PARTS, size, D))
    for name, columns in (("proj", hidden), ("fc", hidden), ("mix", 2 * width), ("kv", 2 * width)):
        several(name, Scatter.scratch(levels, slab, columns))
    several("small", SmallSum.scratch(levels, (16, D)))
    several("late", LateOutput.scratch(half, D))
    several("share", [dma((PARTS,))] * 10)
    for name in ("qs", "gd", "gs", "rd", "rs"):
        scratch[name + "_send"] = dma((levels,))
        scratch[name + "_recv"] = dma((levels,))
    scratch["dq_sem"] = dma((2,))
    names = [*inputs, *outs, *scratch]
    results = pl.pallas_call(
        functools.partial(back_kernel, levels, names),
        out_shape=tuple(outs.values()),
        in_specs=[far if staged and name in ("kv_col", "query_col") else vmem for name in inputs],
        out_specs=tuple(out_specs),
        scratch_shapes=list(scratch.values()),
        name="layer_back",
        compiler_params=pltpu.CompilerParams(
            collective_id=2, has_side_effects=True, vmem_limit_bytes=VMEM_LIMIT
        ),
    )(*inputs.values())
    return SimpleNamespace(**dict(zip(outs, results)))


def unpack_kernel(output_ref, tokens_ref, proj_ref, fc_ref, mix_ref, kv_ref, small_ref, *outs):
    slab, width = kv_ref.shape[0], kv_ref.shape[1] // 2
    output_out, tokens_out, qkv_out, qv_out, out_out, out_b, fc_out, fc_b, proj_out, proj_b, *rest = outs
    output_out[...] = output_ref[...]
    tokens_out[...] = tokens_ref[...]
    qkv_out[0] = mix_ref[:, :width]
    for index in range(2):
        qkv_out[1 + index] = kv_ref[:, index * width : (index + 1) * width]
        qv_out[index : index + 1, :] = small_ref[7:8, index * width : (index + 1) * width]
    fill = jnp.zeros((128 - slab, width), jnp.float32)
    out_out[...] = jnp.transpose(jnp.concatenate([mix_ref[:, width:], fill], axis=0))[:, :slab]
    fc_out[...] = fc_ref[...]
    proj_out[...] = proj_ref[...]
    for row, ref in zip((4, 5, 6, 0, 1, 2, 3), (out_b, fc_b, proj_b, *rest[:4])):
        ref[...] = small_ref[row, :]
    heads = rest[4].shape[0]
    rest[4][...] = small_ref[8 : 8 + heads, :NB]
    rest[5][...] = small_ref[8 + heads : 8 + 2 * heads, :NB]


def unpack(done, heads):
    slab, width = done.kv_share.shape[0], done.kv_share.shape[1] // 2
    hidden = done.fc_share.shape[1]
    vmem = pl.BlockSpec(memory_space=pltpu.VMEM)

    def full(*dims):
        return jax.ShapeDtypeStruct(dims, jnp.float32)

    row = full(D)
    results = pl.pallas_call(
        unpack_kernel,
        out_shape=(
            jax.ShapeDtypeStruct(done.output.shape, jnp.bfloat16),
            jax.ShapeDtypeStruct(done.output.shape, jnp.bfloat16),
            full(3, slab, width),
            full(2, width),
            full(width, slab),
            row,
            full(slab, hidden),
            row,
            full(slab, hidden),
            row,
            row,
            row,
            row,
            row,
            full(heads, NB),
            full(heads, NB),
        ),
        in_specs=[vmem] * 7,
        out_specs=(vmem,) * 16,
        name="unpack",
        compiler_params=pltpu.CompilerParams(vmem_limit_bytes=VMEM_LIMIT),
    )(
        done.output,
        done.tokens_out,
        done.proj_share,
        done.fc_share,
        done.mix_share,
        done.kv_share,
        done.small_out,
    )
    results = list(results)
    results[2] = jnp.transpose(results[2], (1, 0, 2))
    results[8] = results[8].T
    return tuple(results)


def local(
    tokens,
    cotangent,
    past_states,
    doc_ids,
    cur_book,
    past_book,
    past_age,
    ln1_gain,
    ln1_bias,
    qkv_weight,
    qv_bias,
    out_weight,
    out_bias,
    ln2_gain,
    ln2_bias,
    fc_weight,
    fc_bias,
    proj_weight,
    proj_bias,
    mu_weight,
    sigma_weight,
):
    heads_here = mu_weight.shape[0]
    seq_count = lax.axis_size("seq")
    levels = seq_count // 2
    qkv_by_kind = jnp.transpose(qkv_weight, (1, 0, 2))
    doc_row = doc_ids[None, :]
    table = jnp.asarray(np.stack(coefficient_tables(seq_count // BOOKS, NB, SEG), axis=1))
    normed, pair, kv_col, attended, lse, heads_out, coeff, memory, spot_rows, query_col = (
        attention_forward(
        levels,
        tokens,
        ln1_gain,
        ln1_bias,
        qkv_by_kind,
        qv_bias,
        doc_row,
        past_states,
        cur_book[None],
        past_book[None],
        past_age[None],
        mu_weight,
        sigma_weight,
        table,
        )
    )
    done = layer_back(
        levels,
        {
            "heads": heads_out,
            "tok": tokens,
            "cot": cotangent,
            "out_w": out_weight,
            "fc_w": fc_weight,
            "proj_w": proj_weight,
            "ln1_gain": ln1_gain,
            "ln2_gain": ln2_gain,
            "ln2_bias": ln2_bias,
            "out_b": out_bias,
            "fc_b": fc_bias,
            "proj_b": proj_bias,
            "qkv_w": qkv_by_kind,
            "attended": attended,
            "lse": lse,
            "pair": pair,
            "kv_col": kv_col,
            "query_col": query_col,
            "doc": doc_row,
            "normed": normed,
            "coeff": coeff,
            "mem": memory,
            "spot_rows": spot_rows,
            "mu_w": mu_weight,
            "sigma_w": sigma_weight,
        },
    )
    return unpack(done, heads_here)


def solution(mesh):
    in_specs = (
        P("seq", None),
        P("seq", None),
        P("seq", None),
        P("seq"),
        P("seq"),
        P("seq"),
        P("seq"),
        P(),
        P(),
        P(None, None, "tp"),
        P(None, "tp"),
        P("tp", None),
        P(),
        P(),
        P(),
        P(None, "tp"),
        P("tp"),
        P("tp", None),
        P(),
        P("tp", None),
        P("tp", None),
    )
    out_specs = (
        P("seq", None),
        P("seq", None),
        P("seq", None, "tp"),
        P(None, "tp"),
        P("tp", "seq"),
        P(),
        P("seq", "tp"),
        P("tp"),
        P("tp", "seq"),
        P(),
        P(),
        P(),
        P(),
        P(),
        P("tp", None),
        P("tp", None),
    )
    return jax.shard_map(local, mesh=mesh, in_specs=in_specs, out_specs=out_specs, check_vma=False)
```

```python
import functools
from types import SimpleNamespace
from typing import NamedTuple

import ml_dtypes
import numpy as np

import jax
import jax.numpy as jnp
from jax import lax
from jax.experimental import pallas as pl
from jax.experimental.pallas import tpu as pltpu
from jax.sharding import PartitionSpec as P

D = 768
DH = 64
NB = 512
SEG = 512
BOOKS = 4


EPS = 1e-05
TAU = 0.75
RIDGE = 1.0
SPREAD = 0.01
NEGATIVE = -1e30
MESH_ID = pl.DeviceIdType.MESH
VMEM_LIMIT = 62 * 2**20


def coefficient_tables(age_count, basis_n, seg_len):
    shrink = TAU ** np.arange(age_count, dtype=np.float64)
    inside = (np.arange(seg_len) + 0.5) / seg_len
    times = shrink[:, None] * (TAU + (1.0 - TAU) * inside[None, :])
    centres = (np.arange(basis_n) + 0.5) / basis_n
    offset = (times[:, None, :] - centres[None, :, None]) * basis_n
    basis = np.exp(-0.5 * offset * offset)
    gram = np.einsum("agx,ahx->gh", basis, basis) + RIDGE * np.eye(basis_n)
    table = np.linalg.solve(gram[None], basis)
    high = table.astype(ml_dtypes.bfloat16)
    lower = (table - high.astype(np.float64)).astype(ml_dtypes.bfloat16)
    return high, lower


LANES_OUT = 256


def head_of_lane(width):
    return lax.broadcasted_iota(jnp.int32, (1, width), 1) // DH


def head_masks(width):
    lane_head = head_of_lane(width)
    return [(lane_head == head).astype(jnp.float32).astype(jnp.bfloat16) for head in range(width // DH)]


def pick_heads(per_head, lane_head):
    chosen = per_head[0]
    for head in range(1, len(per_head)):
        chosen = jnp.where(lane_head == head, per_head[head], chosen)
    return chosen


def dot_rows(left, right):
    return lax.dot_general(left, right, (((1,), (1,)), ((), ())), preferred_element_type=jnp.float32)


def dot_plain(left, right):
    return lax.dot_general(left, right, (((1,), (0,)), ((), ())), preferred_element_type=jnp.float32)


def thirds(value):
    first = value.astype(jnp.bfloat16)
    rest = value - first.astype(jnp.float32)
    second = rest.astype(jnp.bfloat16)
    third = (rest - second.astype(jnp.float32)).astype(jnp.bfloat16)
    return first, second, third


def with_stats(block, stats):
    rows, width = block.shape
    spare = LANES_OUT - width
    lane = lax.broadcasted_iota(jnp.int32, (1, spare), 1)
    tail = jnp.zeros((rows, spare), jnp.float32)
    for index, column in enumerate(stats):
        for part, value in enumerate(thirds(column)):
            tail = jnp.where(lane == 3 * index + part, value.astype(jnp.float32), tail)
    return jnp.concatenate([block, tail.astype(jnp.bfloat16)], axis=1)


def stat_column(extended, width, index):
    lane = lax.broadcasted_iota(jnp.int32, (1, LANES_OUT), 1)
    start = width + 3 * index
    mine = (lane >= start) & (lane < start + 3)
    return jnp.sum(jnp.where(mine, extended.astype(jnp.float32), 0.0), axis=1, keepdims=True)


def stats_as_rows(stats):
    lane = lax.broadcasted_iota(jnp.int32, (1, 128), 1)
    spread = jnp.zeros((stats[0].shape[0], 128), jnp.float32)
    for index, column in enumerate(stats):
        for part, value in enumerate(thirds(column)):
            spread = jnp.where(lane == 3 * index + part, value.astype(jnp.float32), spread)
    row = lax.broadcasted_iota(jnp.int32, (8, 128), 0)
    lane = lax.broadcasted_iota(jnp.int32, (8, 128), 1)
    chooser = ((lane >= 3 * row) & (lane < 3 * row + 3)).astype(jnp.float32).astype(jnp.bfloat16)
    return dot_rows(chooser, spread.astype(jnp.bfloat16))


def packed(block):
    half = block.shape[0] // 2
    return jnp.concatenate([block[:half], block[half:]], axis=1)


def greet(levels, whole_tp=False):
    seq, tp = lax.axis_index("seq"), lax.axis_index("tp")
    level, side = seq // 2, seq % 2
    barrier = pltpu.get_barrier_semaphore()
    pl.semaphore_signal(barrier, inc=1, device_id=(2 * level + 1 - side, tp), device_id_type=MESH_ID)

    def one(step, unused):
        other = lax.rem(level + step, levels)
        pl.semaphore_signal(barrier, inc=1, device_id=(2 * other + side, tp), device_id_type=MESH_ID)
        return unused

    lax.fori_loop(1, levels, one, 0)
    if not whole_tp:
        return barrier, levels
    greet_tp()
    return barrier, levels + 2


class MemoryPlace(NamedTuple):
    loose: jax.Array
    centre: jax.Array
    spread: jax.Array
    height: jax.Array
    gap: jax.Array


def memory_place(query, spot_rows, in_head):
    width_sq = 1.0 / (NB * NB)
    centre = 1.0 / (
        1.0 + jnp.exp(-jnp.sum(jnp.where(in_head, query * spot_rows[0:1, :], 0.0), axis=1, keepdims=True))
    )
    loose = jnp.sum(jnp.where(in_head, query * spot_rows[1:2, :], 0.0), axis=1, keepdims=True)
    soft = jnp.maximum(loose, 0.0) + jnp.log(1.0 + jnp.exp(-jnp.abs(loose)))
    spread = SPREAD * soft + width_sq
    height = (1.0 / NB) * lax.rsqrt(spread)
    centres = (lax.broadcasted_iota(jnp.int32, (1, NB), 1).astype(jnp.float32) + 0.5) / NB
    return MemoryPlace(loose, centre, spread, height, centre - centres)


def doc_vectors(doc_ref):
    row = doc_ref[...].astype(jnp.float32)
    return row, jnp.transpose(jnp.broadcast_to(row, (128, row.shape[1])))[:, 0:1]


def spot_rows_of(mu_ref, sigma_ref):
    fill = jnp.zeros((8 - mu_ref.shape[0], mu_ref.shape[1]), jnp.float32)
    return [jnp.concatenate([ref[...], fill], axis=0) for ref in (mu_ref, sigma_ref)]


def forward_kernel(
    levels,
    tok_ref,
    gain_ref,
    offset_ref,
    weight_ref,
    bias_ref,
    doc_ref,
    past_ref,
    book_ref,
    past_book_ref,
    past_age_ref,
    mu_ref,
    sigma_ref,
    table_ref,
    normed_ref,
    pair_ref,
    kv_out_ref,
    out_ref,
    lse_ref,
    heads_ref,
    coeff_ref,
    mem_ref,
    spot_row_ref,
    query_col_ref,
    top_ref,
    total_ref,
    acc_ref,
    part_ref,
    part_in_ref,
    kv_send,
    kv_recv,
    pair_sem,
    part_sem,
    past_col_ref,
    past_oth_ref,
    table_in_ref,
    past_up,
    past_down,
    past_side,
    coeff_sems,
    table_sem,
    doc_col_ref,
    read_ref,
    pack_ref,
    query_down,
):
    seq, tp = lax.axis_index("seq"), lax.axis_index("tp")
    level, side = seq // 2, seq % 2
    rows = tok_ref.shape[0]
    width = pair_ref.shape[2]
    heads = width // DH
    partner = (2 * level + 1 - side, tp)
    lane_head = head_of_lane(width)
    head_mask = head_masks(width)
    barrier, greetings = greet(levels, True)

    chunk = rows // 2
    time_half = rows // 2
    mark_row = lax.broadcasted_iota(jnp.int32, (16, 2 * width), 0)
    past_col_ref[level, time_half:, :] = jnp.where(
        mark_row == 0,
        past_book_ref[...].astype(jnp.float32),
        jnp.where(mark_row == 1, past_age_ref[...].astype(jnp.float32), 0.0),
    ).astype(jnp.bfloat16)
    for quarter in range(4):

        @pl.when(tp == quarter)
        def _(quarter=quarter):
            columns = past_ref[:, quarter * width : (quarter + 1) * width]
            past_col_ref[level, :time_half, :] = jnp.concatenate(
                [columns[:time_half], columns[time_half:]], axis=1
            )

    def past_copy(direction, from_level):
        block = past_col_ref.at[from_level]
        if direction == "side":
            sems, target, place = past_side, partner, past_oth_ref.at[from_level]
        elif direction == "up":
            sems, target, place = past_up, (lax.rem(2 * level + 2, 2 * levels) + side, tp), block
        else:
            sems, target, place = past_down, (lax.rem(2 * (level + levels - 1), 2 * levels) + side, tp), block
        return pltpu.make_async_remote_copy(
            block,
            place,
            sems.at[0, from_level],
            sems.at[1, from_level],
            device_id=target,
            device_id_type=MESH_ID,
        )

    pl.semaphore_wait(barrier, greetings)

    def pass_past(from_level, up, down):
        past_copy("side", from_level).start()
        if up:

            @pl.when(level < levels - 1)
            def _():
                past_copy("up", from_level).start()

        if down:

            @pl.when(level > 0)
            def _():
                past_copy("down", from_level).start()

    pass_past(level, True, True)

    doc_row, doc_column = doc_vectors(doc_ref)
    doc_col_ref[...] = doc_column
    bias = jnp.concatenate(
        [bias_ref[0:1, :], jnp.zeros((1, width), jnp.float32), bias_ref[1:2, :]], axis=1
    )

    def project(index, unused):
        here = pl.ds(pl.multiple_of(index * chunk, chunk), chunk)
        x = tok_ref[here, :].astype(jnp.float32)
        centred = x - jnp.mean(x, axis=1, keepdims=True)
        variance = jnp.mean(centred * centred, axis=1, keepdims=True)
        a = centred * lax.rsqrt(variance + EPS) * gain_ref[...][None, :] + offset_ref[...][None, :]
        a = a.astype(jnp.bfloat16)
        normed_ref[here, :] = a
        mixed = jnp.concatenate([dot_plain(a, weight_ref[index]) for index in range(3)], axis=1)
        mixed = (mixed + bias).astype(jnp.bfloat16)
        query = mixed[:, :width] * jnp.bfloat16(DH**-0.5)
        pair_ref[0, here, :] = query
        kv_out_ref[level, here, :] = mixed[:, width:]
        return unused

    lax.fori_loop(0, rows // chunk, project, 0)
    hidden = jnp.where(doc_row >= ((seq + 1) * rows).astype(jnp.float32), 0.0, NEGATIVE)
    mask_rows = jnp.where(
        mark_row[:, : rows // 2] == 0,
        hidden[:, : rows // 2],
        jnp.where(mark_row[:, : rows // 2] == 1, hidden[:, rows // 2 :], 0.0),
    )
    kv_out_ref[level, rows:, :] = jnp.concatenate(
        [mask_rows, jnp.zeros((16, 2 * width - rows // 2), jnp.float32)], axis=1
    ).astype(jnp.bfloat16)

    pair_copy = pltpu.make_async_remote_copy(
        pair_ref.at[0], pair_ref.at[1], pair_sem.at[0], pair_sem.at[1], device_id=partner, device_id_type=MESH_ID
    )
    pair_copy.start()

    def kv_copy(from_level):
        return pltpu.make_async_remote_copy(
            kv_out_ref.at[from_level],
            kv_out_ref.at[from_level],
            kv_send.at[from_level],
            kv_recv.at[from_level],
            device_id=(lax.rem(2 * level + 2, 2 * levels) + side, tp),
            device_id_type=MESH_ID,
        )

    pack_ref[...] = packed(pair_ref[0])

    def down_copy(from_level, to_level):
        return pltpu.make_async_remote_copy(
            pack_ref,
            query_col_ref.at[from_level],
            query_down.at[0, to_level],
            query_down.at[1, from_level],
            device_id=(2 * to_level + side, tp),
            device_id_type=MESH_ID,
        )

    def each_below(body):
        def one(step, unused):
            body(level - step)
            return unused

        lax.fori_loop(1, level + 1, one, 0)

    def each_above(body):
        def one(step, unused):
            body(level + step)
            return unused

        lax.fori_loop(1, levels - level, one, 0)

    @pl.when(level < levels - 1)
    def _():
        kv_copy(level).start()


    top_ref[...] = jnp.full(top_ref.shape, NEGATIVE, jnp.float32)
    total_ref[...] = jnp.zeros(total_ref.shape, jnp.float32)
    acc_ref[...] = jnp.zeros(acc_ref.shape, jnp.float32)

    doc_first = doc_row[0:1, 0:1]
    def reach_of(here):
        docs = doc_col_ref[here, :]
        last = (level == levels - 1) & (side == 1)
        return jnp.where(last & (docs != doc_first), NEGATIVE, 0.0)

    def fold(slot, from_level, mask_kind):
        mask_rows = kv_out_ref[from_level, rows:, :].astype(jnp.float32)
        key_mask = jnp.concatenate([mask_rows[0:1, : rows // 2], mask_rows[1:2, : rows // 2]], axis=1)

        def part(index, unused):
            here = pl.ds(pl.multiple_of(index * chunk, chunk), chunk)
            query = pair_ref[slot, here, :]
            keys = kv_out_ref[from_level, :rows, :width]
            vals = kv_out_ref[from_level, :rows, width:]
            if mask_kind == "own":
                q_pos = index * chunk + lax.broadcasted_iota(jnp.int32, (chunk, rows), 0)
                k_pos = lax.broadcasted_iota(jnp.int32, (chunk, rows), 1)
                visible = (q_pos >= k_pos) & (doc_col_ref[here, :] == doc_row)
            products, scales = [], []
            for head in range(heads):
                scores = dot_rows(query * head_mask[head], keys)
                old_top = top_ref[slot, head, here, :]
                if mask_kind == "own":
                    scores = jnp.where(visible, scores, NEGATIVE)
                    reach = 0.0
                else:
                    scores = scores + key_mask
                    reach = jnp.where(slot == 0, reach_of(here), 0.0)
                new_top = jnp.maximum(old_top, jnp.max(scores, axis=1, keepdims=True) + reach)
                weights = jnp.exp(scores - (new_top - reach))
                scale = jnp.exp(old_top - new_top)
                top_ref[slot, head, here, :] = new_top
                total_ref[slot, head, here, :] = total_ref[slot, head, here, :] * scale + jnp.sum(
                    weights, axis=1, keepdims=True
                )
                products.append(dot_plain(weights.astype(jnp.bfloat16), vals))
                scales.append(scale)
            acc_ref[slot, here, :] = acc_ref[slot, here, :] * pick_heads(scales, lane_head) + pick_heads(
                products, lane_head
            )
            return unused

        lax.fori_loop(0, rows // chunk, part, 0)

    fold(0, level, "own")
    pair_copy.wait()

    @pl.when(side == 0)
    def _():
        fold(1, level, "off")

    def keys_arrived(step):
        from_level = level - step
        kv_copy(from_level).wait_recv()

        @pl.when(level < levels - 1)
        def _():
            kv_copy(from_level).start()

        def both(slot, inner):
            fold(1 - slot, from_level, "off")
            return inner

        lax.fori_loop(0, 2, both, 0)

    def past_arrived(step, unused):
        @pl.when(level >= step)
        def _():
            past_copy("up", level - step).wait_recv()
            pass_past(level - step, True, False)

        @pl.when(level + step < levels)
        def _():
            past_copy("down", level + step).wait_recv()
            pass_past(level + step, False, True)

        return unused

    lax.fori_loop(1, levels, past_arrived, 0)
    each_below(lambda other: down_copy(level, other).start())

    def arrived(step, unused):
        keys_arrived(step)
        return unused

    lax.fori_loop(1, jnp.minimum(level, 1) + 1, arrived, 0)

    def from_side(other, unused):
        past_copy("side", other).wait_recv()
        return unused

    lax.fori_loop(0, levels, from_side, 0)
    own_book = book_ref[...].astype(jnp.float32)
    ages = table_ref.shape[0]

    def one_age(age, total):
        table_copy = pltpu.make_async_copy(table_ref.at[age], table_in_ref, table_sem)
        table_copy.start()

        def one_level(other, found):
            for blocks_ref in (past_col_ref, past_oth_ref):
                mark = blocks_ref[other, time_half:, :].astype(jnp.float32)
                chosen = (mark[0:1, :] == own_book) & (mark[1:2, :] == age.astype(jnp.float32))
                found = jnp.where(chosen, blocks_ref[other, :time_half, :].astype(jnp.float32), found)
            return found

        found = lax.fori_loop(
            0, levels, one_level, jnp.zeros((time_half, 2 * width), jnp.float32)
        ).astype(jnp.bfloat16)
        table_copy.wait()
        for index in range(2):
            table = table_in_ref[index]
            total = total + (
                dot_plain(table[:, :time_half], found)[:, :width]
                + dot_plain(table[:, time_half:], found)[:, width:]
            )
        return total

    coeff = lax.fori_loop(0, ages, one_age, jnp.zeros((NB, width), jnp.float32))
    coeff_ref[tp] = coeff.astype(jnp.bfloat16)

    def coeff_copy(kind, slot, index):
        return swap_with(kind, coeff_ref.at[slot], coeff_ref.at[slot], (coeff_sems.at[0], coeff_sems.at[1]), index)

    core_mate, chip_mate = tp + 1 - 2 * (tp % 2), lax.rem(tp + 2, 4)
    coeff_copy("chip", tp, 0).start()
    coeff_copy("core", tp, 1).start()
    lax.fori_loop(2, jnp.minimum(level, levels - 2) + 1, arrived, 0)


    @pl.when(level == levels - 1)
    def _():
        kv_copy(0).wait_recv()
        fold(1, 0, "off")

    def finish(index, unused):
        here = pl.ds(pl.multiple_of(index * chunk, chunk), chunk)
        totals = [total_ref[1, head, here, :] for head in range(heads)]
        tops = [top_ref[1, head, here, :] for head in range(heads)]
        some = [value > 0.0 for value in totals]
        inverse = [jnp.where(ok, 1.0 / jnp.where(ok, value, 1.0), 0.0) for ok, value in zip(some, totals)]
        logs = [
            jnp.where(ok, top + jnp.log(jnp.where(ok, value, 1.0)), NEGATIVE)
            for ok, top, value in zip(some, tops, totals)
        ]
        share = (acc_ref[1, here, :] * pick_heads(inverse, lane_head)).astype(jnp.bfloat16)
        part_ref[here, :] = with_stats(share, logs)
        return unused

    lax.fori_loop(0, rows // chunk, finish, 0)
    part_copy = pltpu.make_async_remote_copy(
        part_ref, part_in_ref, part_sem.at[0], part_sem.at[1], device_id=partner, device_id_type=MESH_ID
    )
    part_copy.start()

    @pl.when(level == levels - 1)
    def _():
        fold(0, 0, "off")

    coeff_copy("chip", chip_mate, 0).wait_recv()
    coeff_copy("core", chip_mate, 2).start()
    coeff_copy("core", core_mate, 1).wait_recv()
    coeff_copy("core", lax.rem(core_mate + 2, 4), 2).wait_recv()
    memory = jnp.zeros((NB, 2 * width), jnp.float32)
    for slot in range(4):
        here = slice(slot * width, (slot + 1) * width)
        memory = memory + jnp.concatenate(
            [dot_plain(coeff_ref[slot], weight_ref[index, here, :]) for index in (1, 2)], axis=1
        )
    mem_ref[...] = memory.astype(jnp.bfloat16)
    for index, spots in enumerate(spot_rows_of(mu_ref, sigma_ref)):
        row = sum(dot_plain(third, mem_ref[:, :width]) for third in thirds(spots))
        spot_row_ref[index : index + 1, :] = pick_heads(
            [row[head : head + 1, :] for head in range(heads)], lane_head
        )

    def read_memory(index, unused):
        here = pl.ds(pl.multiple_of(index * chunk, chunk), chunk)
        query = pair_ref[0, here, :].astype(jnp.float32)
        reads = []
        for head in range(heads):
            place = memory_place(query, spot_row_ref[0:2, :], lane_head == head)
            density = place.height * jnp.exp(place.gap * place.gap * (-0.5 / place.spread))
            reads.append(dot_plain(density.astype(jnp.bfloat16), mem_ref[:, width:]))
        read_ref[here, :] = pick_heads(reads, lane_head)
        return unused

    lax.fori_loop(0, rows // chunk, read_memory, 0)

    part_copy.wait()

    def merge(index, unused):
        here = pl.ds(pl.multiple_of(index * chunk, chunk), chunk)
        reach = reach_of(here)
        received = part_in_ref[here, :]
        mine, theirs, columns = [], [], []
        for head in range(heads):
            total = total_ref[0, head, here, :]
            own_log = top_ref[0, head, here, :] + jnp.log(total)
            other_log = stat_column(received, width, head) + reach
            high = jnp.maximum(own_log, other_log)
            both_log = high + jnp.log(jnp.exp(own_log - high) + jnp.exp(other_log - high))
            mine.append(jnp.exp(own_log - both_log) / total)
            theirs.append(jnp.exp(other_log - both_log))
            columns.append(both_log)
        attended = acc_ref[0, here, :] * pick_heads(mine, lane_head) + received[:, :width].astype(
            jnp.float32
        ) * pick_heads(theirs, lane_head)
        out_ref[here, :] = attended
        heads_ref[here, :] = (attended + read_ref[here, :]).astype(jnp.bfloat16)
        lane = lax.broadcasted_iota(jnp.int32, (1, 8), 1)
        packed = jnp.zeros((chunk, 8), jnp.float32)
        for head in range(heads):
            packed = jnp.where(lane == head, columns[head], packed)
        lse_ref[here, :] = packed
        return unused

    lax.fori_loop(0, rows // chunk, merge, 0)

    each_below(lambda other: down_copy(level, other).wait_send())
    each_above(lambda other: down_copy(other, level).wait_recv())
    coeff_copy("chip", tp, 0).wait_send()
    coeff_copy("core", tp, 1).wait_send()
    coeff_copy("core", chip_mate, 2).wait_send()

    def past_sent(other, unused):
        past_copy("side", other).wait_send()

        @pl.when((level < levels - 1) & (other <= level))
        def _():
            past_copy("up", other).wait_send()

        @pl.when((level > 0) & (other >= level))
        def _():
            past_copy("down", other).wait_send()

        return unused

    lax.fori_loop(0, levels, past_sent, 0)

    @pl.when(level < levels - 1)
    def _():
        def sent_up(from_level, unused):
            kv_copy(from_level).wait_send()
            return unused

        lax.fori_loop(0, level + 1, sent_up, 0)


def attention_forward(
    levels,
    tokens,
    gain,
    offset,
    weight,
    bias,
    doc_row,
    past,
    book,
    past_book,
    past_age,
    mu_weight,
    sigma_weight,
    table,
):
    rows = tokens.shape[0]
    width = weight.shape[2]
    heads = width // DH
    vmem = pl.BlockSpec(memory_space=pltpu.VMEM)
    far = pl.BlockSpec(memory_space=pl.ANY) if levels > 8 else vmem
    dma = pltpu.SemaphoreType.DMA
    return pl.pallas_call(
        functools.partial(forward_kernel, levels),
        out_shape=(
            jax.ShapeDtypeStruct((rows, D), jnp.bfloat16),
            jax.ShapeDtypeStruct((2, rows, width), jnp.bfloat16),
            jax.ShapeDtypeStruct((levels, rows + 16, 2 * width), jnp.bfloat16),
            jax.ShapeDtypeStruct((rows, width), jnp.float32),
            jax.ShapeDtypeStruct((rows, 8), jnp.float32),
            jax.ShapeDtypeStruct((rows, width), jnp.bfloat16),
            jax.ShapeDtypeStruct((4, NB, width), jnp.bfloat16),
            jax.ShapeDtypeStruct((NB, 2 * width), jnp.bfloat16),
            jax.ShapeDtypeStruct((8, width), jnp.float32),
            jax.ShapeDtypeStruct((levels, rows // 2, 2 * width), jnp.bfloat16),
        ),
        in_specs=[vmem] * 12 + [pl.BlockSpec(memory_space=pl.ANY)],
        out_specs=(vmem,) * 9 + (far,),
        scratch_shapes=[
            pltpu.VMEM((2, heads, rows, 1), jnp.float32),
            pltpu.VMEM((2, heads, rows, 1), jnp.float32),
            pltpu.VMEM((2, rows, width), jnp.float32),
            pltpu.VMEM((rows, LANES_OUT), jnp.bfloat16),
            pltpu.VMEM((rows, LANES_OUT), jnp.bfloat16),
            dma((levels,)),
            dma((levels,)),
            dma((2,)),
            dma((2,)),
            pltpu.VMEM((levels, SEG // 2 + 16, 2 * width), jnp.bfloat16),
            pltpu.VMEM((levels, SEG // 2 + 16, 2 * width), jnp.bfloat16),
            pltpu.VMEM(table.shape[1:], jnp.bfloat16),
            dma((2, levels)),
            dma((2, levels)),
            dma((2, levels)),
            dma((2, 3)),
            dma(()),
            pltpu.VMEM((rows, 1), jnp.float32),
            pltpu.VMEM((rows, width), jnp.float32),
            pltpu.VMEM((rows // 2, 2 * width), jnp.bfloat16),
            dma((2, levels)),
        ],
        name="attention_forward",
        compiler_params=pltpu.CompilerParams(
            collective_id=1, has_side_effects=True, vmem_limit_bytes=VMEM_LIMIT
        ),
    )(
        tokens,
        gain,
        offset,
        weight,
        bias,
        doc_row,
        past,
        book,
        past_book,
        past_age,
        mu_weight,
        sigma_weight,
        table,
    )


def column_copy(block_ref, from_level, landing_ref, send_sem, recv_sem, to_level):
    seq, tp = lax.axis_index("seq"), lax.axis_index("tp")
    return pltpu.make_async_remote_copy(
        block_ref,
        landing_ref.at[from_level],
        send_sem.at[to_level],
        recv_sem.at[from_level],
        device_id=(2 * to_level + seq % 2, tp),
        device_id_type=MESH_ID,
    )


class Scatter:
    def __init__(self, levels, blocks, plane_in, plane_sum, column_in, sems):
        self.levels, self.blocks = levels, blocks
        self.plane_in, self.plane_sum, self.column_in = plane_in, plane_sum, column_in
        self.plane_send, self.plane_recv, self.column_send, self.column_recv = sems
        seq, tp = lax.axis_index("seq"), lax.axis_index("tp")
        self.level, self.side, self.tp = seq // 2, seq % 2, tp

    def plane_copy(self, to_level):
        return pltpu.make_async_remote_copy(
            self.blocks.at[2 * to_level + 1 - self.side],
            self.plane_in.at[to_level],
            self.plane_send.at[to_level],
            self.plane_recv.at[to_level],
            device_id=(2 * self.level + 1 - self.side, self.tp),
            device_id_type=MESH_ID,
        )

    def swap_copy(self, from_level, to_level):
        return column_copy(
            self.plane_sum.at[to_level], from_level, self.column_in, self.column_send, self.column_recv, to_level
        )

    def loop(self, first, body):
        def one(step, unused):
            body(lax.rem(self.level + step, self.levels))
            return unused

        lax.fori_loop(first, self.levels, one, 0)

    def start(self):
        self.loop(1, lambda other: self.plane_copy(other).start())
        self.plane_copy(self.level).start()

    def middle(self):
        def one(other):
            self.plane_copy(other).wait_recv()
            total = self.blocks[2 * other + self.side].astype(jnp.float32) + self.plane_in[other].astype(
                jnp.float32
            )
            self.plane_sum[other] = total.astype(jnp.bfloat16)
            self.swap_copy(self.level, other).start()

        self.loop(1, one)

    def finish(self, out_ref):
        self.plane_copy(self.level).wait_recv()
        out_ref[...] = self.blocks[2 * self.level + self.side].astype(jnp.float32) + self.plane_in[
            self.level
        ].astype(jnp.float32)

        def one(other):
            self.swap_copy(other, self.level).wait_recv()
            out_ref[...] += self.column_in[other].astype(jnp.float32)

        self.loop(1, one)
        self.loop(0, lambda other: self.plane_copy(other).wait_send())
        self.loop(1, lambda other: self.swap_copy(self.level, other).wait_send())

    @staticmethod
    def scratch(levels, rows, width):
        buffer = pltpu.VMEM((levels, rows, width), jnp.bfloat16)
        return [buffer] * 3 + [pltpu.SemaphoreType.DMA((levels,))] * 4


class SmallSum:
    def __init__(self, levels, small, plane_in, column_in, sems):
        self.levels, self.small, self.plane_in, self.column_in = levels, small, plane_in, column_in
        self.plane_sem, self.column_send, self.column_recv = sems
        seq, tp = lax.axis_index("seq"), lax.axis_index("tp")
        self.level, self.side, self.tp = seq // 2, seq % 2, tp

    def plane_copy(self):
        return pltpu.make_async_remote_copy(
            self.small,
            self.plane_in,
            self.plane_sem.at[0],
            self.plane_sem.at[1],
            device_id=(2 * self.level + 1 - self.side, self.tp),
            device_id_type=MESH_ID,
        )

    def swap_copy(self, from_level, to_level):
        return column_copy(
            self.column_in.at[from_level], from_level, self.column_in, self.column_send, self.column_recv, to_level
        )

    def loop(self, body):
        def one(step, unused):
            body(lax.rem(self.level + step, self.levels))
            return unused

        lax.fori_loop(1, self.levels, one, 0)

    def start(self):
        self.plane_copy().start()

    def middle(self):
        self.plane_copy().wait()
        self.column_in[self.level] = self.small[...] + self.plane_in[...]
        self.loop(lambda other: self.swap_copy(self.level, other).start())

    def finish(self, out_ref):
        self.loop(lambda other: self.swap_copy(other, self.level).wait_recv())
        self.loop(lambda other: self.swap_copy(self.level, other).wait_send())
        out_ref[...] = self.column_in[0]

        def one(other, unused):
            out_ref[...] += self.column_in[other]
            return unused

        lax.fori_loop(1, self.levels, one, 0)

    @staticmethod
    def scratch(levels, shape):
        dma = pltpu.SemaphoreType.DMA
        return [
            pltpu.VMEM(shape, jnp.float32),
            pltpu.VMEM((levels,) + shape, jnp.float32),
            dma((2,)),
            dma((levels,)),
            dma((levels,)),
        ]


def tp_partner(kind):
    seq, tp = lax.axis_index("seq"), lax.axis_index("tp")
    if kind == "core":
        return (seq, tp + 1 - 2 * (tp % 2))
    return (seq, lax.rem(tp + 2, 4))


def greet_tp():
    barrier = pltpu.get_barrier_semaphore()
    for kind in ("core", "chip"):
        pl.semaphore_signal(barrier, inc=1, device_id=tp_partner(kind), device_id_type=MESH_ID)
    return barrier, 2


def swap_with(kind, source, target, sems, index):
    send, recv = sems
    return pltpu.make_async_remote_copy(
        source, target, send.at[index], recv.at[index], device_id=tp_partner(kind), device_id_type=MESH_ID
    )


class TpSum:
    def __init__(self, core_out, core_in, chip_out, chip_in, sems):
        self.core_out, self.core_in, self.chip_out, self.chip_in = core_out, core_in, chip_out, chip_in
        self.core_sems, self.chip_sems = sems[:2], sems[2:]

    def core_copy(self, part):
        return swap_with("core", self.core_out.at[part], self.core_in.at[part], self.core_sems, part)

    def chip_copy(self, part):
        return swap_with("chip", self.chip_out.at[part], self.chip_in.at[part], self.chip_sems, part)

    def start(self, part, for_other_core):
        self.core_out[part] = for_other_core.astype(jnp.bfloat16)
        self.core_copy(part).start()

    def middle(self, part, own):
        self.core_copy(part).wait()
        self.chip_out[part] = (own + self.core_in[part].astype(jnp.float32)).astype(jnp.bfloat16)
        self.chip_copy(part).start()

    def result(self, part):
        self.chip_copy(part).wait()
        return self.chip_out[part].astype(jnp.float32) + self.chip_in[part].astype(jnp.float32)

    @staticmethod
    def scratch(parts, rows, width):
        buffer = pltpu.VMEM((parts, rows, width), jnp.bfloat16)
        return [buffer] * 4 + [pltpu.SemaphoreType.DMA((parts,))] * 4

    COUNT = 8


class RowShare:
    def __init__(self, whole, rows, sems):
        self.whole, self.rows, self.sems = whole, rows, sems

    def copy(self, part, start):
        here = self.whole.at[pl.ds(pl.multiple_of(start, self.rows), self.rows), :]
        return swap_with("core", here, here, self.sems, part)


def normalize(v):
    centred = v - jnp.mean(v, axis=1, keepdims=True)
    scale = lax.rsqrt(jnp.mean(centred * centred, axis=1, keepdims=True) + EPS)
    return centred * scale, scale


def norm_back(grad, nhat, scale, gain):
    inner = grad * gain
    return (
        inner
        - jnp.mean(inner, axis=1, keepdims=True)
        - nhat * jnp.mean(inner * nhat, axis=1, keepdims=True)
    ) * scale


def gelu_and_slope(f):
    root = (2.0 / np.pi) ** 0.5
    square = f * f
    bend = jnp.tanh(root * f * (1.0 + 0.044715 * square))
    half = 0.5 * (1.0 + bend)
    slope = half + 0.5 * f * (1.0 - bend * bend) * (root * (1.0 + 3.0 * 0.044715 * square))
    return f * half, slope


def dot_columns(left, right):
    return lax.dot_general(left, right, (((0,), (0,)), ((), ())), preferred_element_type=jnp.float32)


def column_sum(v):
    return jnp.sum(v, axis=0, keepdims=True)


class LateOutput:
    def __init__(self, base, own, other, whole, sems):
        self.base, self.own, self.other, self.whole = base, own, other, whole
        self.half = own.shape[0]
        self.core_in, self.chip_out, self.chip_in = sems[:3]
        self.core_sems, self.chip_sems, self.share_sems = sems[3:5], sems[5:7], sems[7:9]
        self.share = RowShare(whole, self.half, self.share_sems)
        self.core = lax.axis_index("tp") % 2

    COUNT = 9

    def core_copy(self):
        return swap_with("core", self.other, self.core_in, self.core_sems, 0)

    def chip_copy(self):
        return swap_with("chip", self.chip_out, self.chip_in, self.chip_sems, 0)

    def start(self):
        self.core_copy().start()

    def middle(self):
        self.core_copy().wait()
        self.chip_out[...] = (self.own[...] + self.core_in[...].astype(jnp.float32)).astype(jnp.bfloat16)
        self.chip_copy().start()

    def late(self):
        self.chip_copy().wait()
        total = self.chip_out[...].astype(jnp.float32) + self.chip_in[...].astype(jnp.float32)
        here = pl.ds(pl.multiple_of(self.core * self.half, self.half), self.half)
        self.whole[here, :] = (self.base[...] + total).astype(jnp.bfloat16)
        self.share.copy(0, self.core * self.half).start()

    def finish(self):
        self.share.copy(0, (1 - self.core) * self.half).wait_recv()
        self.share.copy(0, self.core * self.half).wait_send()

    @staticmethod
    def scratch(half, width):
        buffer = pltpu.VMEM((half, width), jnp.bfloat16)
        return [buffer] * 3 + [pltpu.SemaphoreType.DMA((1,))] * 6


PARTS = 2


def back_kernel(levels, names, *refs):
    r = SimpleNamespace(**dict(zip(names, refs)))
    seq, tp = lax.axis_index("seq"), lax.axis_index("tp")
    level, side, core = seq // 2, seq % 2, tp % 2
    rows, width = r.heads.shape
    heads = width // DH
    half = rows // 2
    size = half // PARTS
    partner = (2 * level + 1 - side, tp)
    lane_head = head_of_lane(width)
    head_mask = head_masks(width)
    chunk = rows
    staged = hasattr(r, "stage_query")

    first, second, third = (
        TpSum(*(getattr(r, f"{name}_{i}") for i in range(4)), [getattr(r, f"{name}_{i}") for i in range(4, 8)])
        for name in ("first", "second", "third")
    )
    scatters = [
        Scatter(
            levels,
            getattr(r, f"{name}_blocks"),
            *(getattr(r, f"{name}_{i}") for i in range(3)),
            [getattr(r, f"{name}_{i}") for i in range(3, 7)],
        )
        for name in ("proj", "fc", "mix", "kv")
    ]
    small = SmallSum(levels, r.small, r.small_0, r.small_1, (r.small_2, r.small_3, r.small_4))
    late = LateOutput(
        r.base, r.own_two, r.other_two, r.output, [getattr(r, f"late_{i}") for i in range(LateOutput.COUNT)]
    )
    c_share = RowShare(r.c, size, (r.share_0, r.share_1))
    e_share = RowShare(r.e1, size, (r.share_2, r.share_3))
    token_share = RowShare(r.tokens_out, size, (r.share_4, r.share_5))
    gain, offset, out_b, fc_b, proj_b, first_gain = (
        ref[...][None, :] for ref in (r.ln2_gain, r.ln2_bias, r.out_b, r.fc_b, r.proj_b, r.ln1_gain)
    )
    barrier, greetings = greet(levels, True)

    def span(start, count=size):
        return pl.ds(pl.multiple_of(start, size), count)

    def mine(part):
        return core * half + part * size

    def theirs(part):
        return (1 - core) * half + part * size

    def block_of(blocks_ref, from_level, place):
        if not staged:
            return blocks_ref.at[from_level]
        target = getattr(r, "stage_" + place)
        copy = pltpu.make_async_copy(blocks_ref.at[from_level], target, r.stage_sem)
        copy.start()
        copy.wait()
        return target

    def down_copy(source_ref, landing_ref, sems, from_level, to_level):
        send, recv = sems
        return pltpu.make_async_remote_copy(
            source_ref,
            landing_ref.at[from_level],
            send.at[to_level],
            recv.at[from_level],
            device_id=(2 * to_level + side, tp),
            device_id_type=MESH_ID,
        )

    def side_copy(source_ref, landing_ref, sems, from_level):
        send, recv = sems
        return pltpu.make_async_remote_copy(
            source_ref,
            landing_ref.at[from_level],
            send.at[from_level],
            recv.at[from_level],
            device_id=partner,
            device_id_type=MESH_ID,
        )

    def query_side(from_level):
        return side_copy(r.query_col.at[from_level], r.query_oth, (r.qs_send, r.qs_recv), from_level)

    def grad_down(from_level, to_level):
        return (
            down_copy(r.pack, r.grad_col, (r.gd_send, r.gd_recv), from_level, to_level),
            down_copy(r.far_rows, r.rows_col, (r.rd_send, r.rd_recv), from_level, to_level),
        )

    def grad_side(from_level):
        return (
            side_copy(r.grad_col.at[from_level], r.grad_oth, (r.gs_send, r.gs_recv), from_level),
            side_copy(r.rows_col.at[from_level], r.rows_oth, (r.rs_send, r.rs_recv), from_level),
        )

    def own_grad_side():
        return (
            side_copy(r.pack, r.grad_oth, (r.gs_send, r.gs_recv), level),
            side_copy(r.far_rows, r.rows_oth, (r.rs_send, r.rs_recv), level),
        )

    def start_all(copies):
        for copy in copies:
            copy.start()

    def wait_recv_all(copies):
        for copy in copies:
            copy.wait_recv()

    def wait_send_all(copies):
        for copy in copies:
            copy.wait_send()

    def opened(block_ref, target):
        target[:half, :] = block_ref[:, :width]
        target[half:, :] = block_ref[:, width:]
        return target

    def each_below(body):
        def one(step, unused):
            body(level - step)
            return unused

        lax.fori_loop(1, level + 1, one, 0)

    def each_above(body):
        def one(step, unused):
            body(level + step)
            return unused

        lax.fori_loop(1, levels - level, one, 0)

    pl.semaphore_wait(barrier, greetings)

    each_above(lambda other: query_side(other).start())

    for part in range(PARTS):
        first.start(part, dot_plain(r.heads[span(theirs(part)), :], r.out_w[...]))
        r.own[span(part * size), :] = dot_plain(r.heads[span(mine(part)), :], r.out_w[...])
    for part in range(PARTS):
        first.middle(part, r.own[span(part * size), :])

    def early(index, unused):
        here = span(index * size)
        r.pull[here, :] = dot_rows(r.cot[here, :], r.proj_w[...])
        return unused

    lax.fori_loop(0, rows // size, early, 0)
    r.small[...] = jnp.zeros(r.small.shape, jnp.float32)
    r.fold[...] = jnp.zeros(r.fold.shape, jnp.float32)
    r.small[6:7, :] = column_sum(r.cot[...].astype(jnp.float32))

    def feed(start):
        here = span(start)
        f = dot_plain(r.c[here, :], r.fc_w[...]) + fc_b
        u, slope = gelu_and_slope(f)
        r.u[here, :] = u.astype(jnp.bfloat16)
        ef = (r.pull[here, :] * slope).astype(jnp.bfloat16)
        r.ef[here, :] = ef
        return dot_rows(ef, r.fc_w[...])

    for part in range(PARTS):
        total = first.result(part) + out_b
        h1 = r.tok[span(mine(part)), :].astype(jnp.float32) + total
        r.h1[span(part * size), :] = h1
        nhat, scale = normalize(h1)
        r.c[span(mine(part)), :] = (nhat * gain + offset).astype(jnp.bfloat16)
        c_share.copy(part, mine(part)).start()
        r.own[span(part * size), :] = feed(mine(part))
        c_share.copy(part, theirs(part)).wait_recv()
        second.start(part, feed(theirs(part)))
        r.other_two[span(part * size), :] = dot_plain(r.u[span(theirs(part)), :], r.proj_w[...]).astype(
            jnp.bfloat16
        )
        r.own_two[span(part * size), :] = dot_plain(r.u[span(mine(part)), :], r.proj_w[...])
        second.middle(part, r.own[span(part * size), :])

    r.base[...] = r.h1[...] + proj_b
    bite = 384

    def weight_blocks(blocks_ref, left_ref, right, extra=None, place_of=0):
        slab, columns = blocks_ref.shape[1], right.shape[1]
        for index in range(D // bite):
            value = dot_columns(left_ref[:, index * bite : (index + 1) * bite], right)
            if extra is not None:
                start = index * bite + extra
                value = value + r.pull[:bite, start : start + columns]
            for place in range(bite // slab):
                blocks_ref[
                    index * (bite // slab) + place, :, place_of * columns : (place_of + 1) * columns
                ] = value[place * slab : (place + 1) * slab].astype(jnp.bfloat16)

    weight_blocks(r.proj_blocks, r.cot, r.u[...])
    scatters[0].start()
    weight_blocks(r.fc_blocks, r.c, r.ef[...])
    scatters[1].start()

    gain_sum = jnp.zeros((1, D), jnp.float32)
    offset_sum = jnp.zeros((1, D), jnp.float32)
    out_sum = jnp.zeros((1, D), jnp.float32)
    for part in range(PARTS):
        grad = second.result(part)
        nhat, scale = normalize(r.h1[span(part * size), :])
        gain_sum = gain_sum + column_sum(grad * nhat)
        offset_sum = offset_sum + column_sum(grad)
        mid = r.cot[span(mine(part)), :].astype(jnp.float32) + norm_back(grad, nhat, scale, gain)
        r.mid[span(part * size), :] = mid
        e1 = mid.astype(jnp.bfloat16)
        out_sum = out_sum + column_sum(e1.astype(jnp.float32))
        r.e1[span(mine(part)), :] = e1
        e_share.copy(part, mine(part)).start()
        r.grad[span(mine(part)), :] = dot_rows(e1, r.out_w[...]).astype(jnp.bfloat16)
    r.fold[2:3, :] = gain_sum
    r.fold[3:4, :] = offset_sum
    r.fold[4:5, :] = out_sum
    for part in range(PARTS):
        e_share.copy(part, theirs(part)).wait_recv()
        r.grad[span(theirs(part)), :] = dot_rows(r.e1[span(theirs(part)), :], r.out_w[...]).astype(jnp.bfloat16)

    r.pack[...] = packed(r.grad[...])
    own_grad_side()[0].start()
    each_below(lambda other: grad_down(level, other)[0].start())
    doc_row, doc_column = doc_vectors(r.doc)
    r.doc_col[...] = doc_column
    doc_first = doc_row[0:1, 0:1]
    last = (level == levels - 1) & (side == 1)

    def prepare(index, unused):
        here = pl.ds(pl.multiple_of(index * chunk, chunk), chunk)
        grad = r.grad[here, :]
        product = grad.astype(jnp.float32) * r.attended[here, :]
        far = jnp.where(last & (r.doc_col[here, :] != doc_first), -NEGATIVE, 0.0)
        lses = [r.lse[here, head : head + 1] for head in range(heads)]
        deltas = [
            jnp.sum(jnp.where(lane_head == head, product, 0.0), axis=1, keepdims=True)
            for head in range(heads)
        ]
        r.near_rows[:, here] = stats_as_rows(lses + deltas)
        r.far_rows[:, here] = stats_as_rows([lse + far for lse in lses] + deltas)
        for head in range(heads):
            r.near_lse[head, here, :] = lses[head]
            r.stat[0, head, here, :] = lses[head] + far
            r.stat[0, heads + head, here, :] = deltas[head]
        return unused

    lax.fori_loop(0, rows // chunk, prepare, 0)
    own_grad_side()[1].start()
    each_below(lambda other: grad_down(level, other)[1].start())
    late.start()
    r.small[5:6, :] = column_sum(r.ef[...].astype(jnp.float32))

    r.mem_acc[...] = jnp.zeros(r.mem_acc.shape, jnp.float32)
    r.pulls[...] = jnp.zeros(r.pulls.shape, jnp.float32)

    def memory_back(index, unused):
        here = pl.ds(pl.multiple_of(index * chunk, chunk), chunk)
        query = r.pair[0, here, :].astype(jnp.float32)
        grad = r.grad[here, :]
        val_parts, mu_pulls, sigma_pulls = [], [], []
        for head in range(heads):
            place = memory_place(query, r.spot_rows[0:2, :], lane_head == head)
            slope = place.gap / place.spread
            square = place.gap * slope
            density = place.height * jnp.exp(-0.5 * square)
            val_parts.append(dot_columns(density.astype(jnp.bfloat16), grad))
            weighed = dot_rows(grad * head_mask[head], r.mem[:, width:]) * density
            to_centre = -jnp.sum(weighed * slope, axis=1, keepdims=True)
            to_spread = 0.5 * jnp.sum(weighed * (square - 1.0), axis=1, keepdims=True) / place.spread
            mu_pulls.append(to_centre * place.centre * (1.0 - place.centre))
            sigma_pulls.append(to_spread * SPREAD / (1.0 + jnp.exp(-place.loose)))
        mu_pull, sigma_pull = pick_heads(mu_pulls, lane_head), pick_heads(sigma_pulls, lane_head)
        r.dq[0, here, :] = mu_pull * r.spot_rows[0:1, :] + sigma_pull * r.spot_rows[1:2, :]
        r.mem_acc[...] += pick_heads(val_parts, lane_head)
        r.pulls[0:1, :] += column_sum(mu_pull * query)
        r.pulls[1:2, :] += column_sum(sigma_pull * query)
        return unused

    lax.fori_loop(0, rows // chunk, memory_back, 0)
    by_head = lax.broadcasted_iota(jnp.int32, (8, 1), 0) == lane_head
    pulls = [jnp.where(by_head, r.pulls[i : i + 1, :], 0.0) for i in range(2)]
    for index in range(2):
        spot_grad = sum(dot_rows(part, r.mem[:, :width]) for part in thirds(pulls[index]))
        r.small[8 + heads * index : 8 + heads * (index + 1), :NB] = spot_grad[:heads, :]
    key_grad = dot_columns(
        jnp.concatenate(spot_rows_of(r.mu_w, r.sigma_w), axis=0).astype(jnp.bfloat16), jnp.concatenate(pulls, axis=0).astype(jnp.bfloat16)
    )
    r.mem_grad[...] = jnp.concatenate([key_grad, r.mem_acc[...]], axis=1).astype(jnp.bfloat16)
    for slot in range(4):
        r.pull[
            (slot % 2) * width : (slot % 2 + 1) * width,
            2 * width * (slot // 2) : 2 * width * (slot // 2 + 1),
        ] = dot_columns(r.coeff[slot], r.mem_grad[...])
    scatters[0].middle()

    r.dq[1] = jnp.zeros((rows, width), jnp.float32)
    r.dk[...] = jnp.zeros(r.dk.shape, jnp.float32)
    r.dv[...] = jnp.zeros(r.dv.shape, jnp.float32)

    def query_fold(slot, grad_ref, block_ref, own):
        if not own:
            mask_rows = block_ref[rows:, :].astype(jnp.float32)
            key_mask = jnp.concatenate([mask_rows[0:1, :half], mask_rows[1:2, :half]], axis=1)

        def part(index, unused):
            here = pl.ds(pl.multiple_of(index * chunk, chunk), chunk)
            query = r.pair[slot, here, :]
            grad = grad_ref[here, :]
            keys = block_ref[:rows, :width]
            vals = block_ref[:rows, width:]
            if own:
                q_pos = index * chunk + lax.broadcasted_iota(jnp.int32, (chunk, rows), 0)
                k_pos = lax.broadcasted_iota(jnp.int32, (chunk, rows), 1)
                visible = (q_pos >= k_pos) & (r.doc_col[here, :] == doc_row)
            products = []
            for head in range(heads):
                scores = dot_rows(query * head_mask[head], keys)
                if own:
                    scores = jnp.where(visible, scores, NEGATIVE)
                    lse = r.near_lse[head, here, :]
                else:
                    scores = scores + key_mask
                    lse = r.stat[slot, head, here, :]
                probs = jnp.exp(scores - lse)
                pull = dot_rows(grad * head_mask[head], vals) - r.stat[slot, heads + head, here, :]
                products.append(dot_plain((probs * pull).astype(jnp.bfloat16), keys))
            r.dq[slot, here, :] = r.dq[slot, here, :] + pick_heads(products, lane_head)
            return unused

        lax.fori_loop(0, rows // chunk, part, 0)

    query_fold(0, r.grad, block_of(r.kv_col, level, "keys"), True)

    def own_earlier(from_level, unused):
        query_fold(0, r.grad, block_of(r.kv_col, from_level, "keys"), False)
        return unused

    lax.fori_loop(0, level, own_earlier, 0)
    scatters[1].middle()
    wait_recv_all(own_grad_side())
    other_grad_ref = opened(block_of(r.grad_oth, level, "grad"), r.other_grad)
    other_columns = jnp.transpose(
        jnp.concatenate([r.rows_oth[level], jnp.zeros((120, rows), jnp.float32)], axis=0)
    )
    for row in range(2 * heads):
        r.stat[1, row] = other_columns[:, row : row + 1]

    def other_earlier(from_level, unused):
        query_fold(1, other_grad_ref, block_of(r.kv_col, from_level, "keys"), False)
        return unused

    lax.fori_loop(0, level + 1 - side, other_earlier, 0)
    r.dq_out[...] = r.dq[1].astype(jnp.bfloat16)
    dq_copy = pltpu.make_async_remote_copy(
        r.dq_out, r.dq_in, r.dq_sem.at[0], r.dq_sem.at[1], device_id=partner, device_id_type=MESH_ID
    )
    dq_copy.start()
    late.middle()

    own_block_ref = block_of(r.kv_col, level, "keys")

    def key_fold(query_ref, grad_ref, stats, own):
        def part(index, unused):
            here = pl.ds(pl.multiple_of(index * chunk, chunk), chunk)
            keys = own_block_ref[here, :width]
            vals = own_block_ref[here, width:]
            query = query_ref[...]
            grad = grad_ref[...]
            if own:
                k_pos = index * chunk + lax.broadcasted_iota(jnp.int32, (chunk, rows), 0)
                q_pos = lax.broadcasted_iota(jnp.int32, (chunk, rows), 1)
                visible = (q_pos >= k_pos) & (r.doc_col[here, :] == doc_row)
            key_parts, val_parts = [], []
            for head in range(heads):
                scores = dot_rows(keys * head_mask[head], query)
                if own:
                    scores = jnp.where(visible, scores, NEGATIVE)
                probs = jnp.exp(scores - stats[head : head + 1, :])
                val_parts.append(dot_plain(probs.astype(jnp.bfloat16), grad))
                pull = dot_rows(vals * head_mask[head], grad) - stats[heads + head : heads + head + 1, :]
                key_parts.append(dot_plain((probs * pull).astype(jnp.bfloat16), query))
            r.dk[here, :] = r.dk[here, :] + pick_heads(key_parts, lane_head)
            r.dv[here, :] = r.dv[here, :] + pick_heads(val_parts, lane_head)
            return unused

        lax.fori_loop(0, rows // chunk, part, 0)

    @pl.when(side == 0)
    def _():
        key_fold(r.pair.at[1], r.other_grad, r.rows_oth[level], False)

    def later(from_level):
        wait_recv_all(grad_down(from_level, level))
        start_all(grad_side(from_level))
        key_fold(
            opened(block_of(r.query_col, from_level, "query"), r.open_query),
            opened(block_of(r.grad_col, from_level, "grad"), r.open_grad),
            r.rows_col[from_level],
            False,
        )
        query_side(from_level).wait_recv()
        wait_recv_all(grad_side(from_level))
        key_fold(
            opened(block_of(r.query_oth, from_level, "query"), r.open_query),
            opened(block_of(r.grad_oth, from_level, "grad"), r.open_grad),
            r.rows_oth[from_level],
            False,
        )

    dq_copy.wait()
    r.grads[0] = ((r.dq[0] + r.dq_in[...].astype(jnp.float32)) * (DH**-0.5)).astype(jnp.bfloat16)
    weight_blocks(r.mix_blocks, r.normed, r.grads[0], None, 0)
    weight_blocks(r.mix_blocks, r.e1, r.heads[...], None, 1)
    scatters[2].start()
    each_above(later)
    scatters[2].middle()
    reaches = r.doc_col[...] >= ((seq + 1) * rows).astype(jnp.float32)
    r.dk[...] = jnp.where(reaches, r.dk[...], 0.0)
    r.dv[...] = jnp.where(reaches, r.dv[...], 0.0)
    key_fold(r.pair.at[0], r.grad, r.near_rows[...], True)
    r.grads[1] = r.dk[...].astype(jnp.bfloat16)
    r.grads[2] = r.dv[...].astype(jnp.bfloat16)

    def norm_grad(start):
        return sum(dot_rows(r.grads[index, span(start), :], r.qkv_w[index]) for index in range(3))

    for part in range(PARTS):
        third.start(part, norm_grad(theirs(part)))
        r.own[span(part * size), :] = norm_grad(mine(part))
    for index in range(2):
        weight_blocks(
            r.kv_blocks,
            r.normed,
            r.grads[1 + index],
            index * width,
            index,
        )
    scatters[3].start()
    for part in range(PARTS):
        third.middle(part, r.own[span(part * size), :])
    r.small[7:8, :] = jnp.concatenate(
        [column_sum(r.grads[index].astype(jnp.float32)) for index in (0, 2)]
        + [jnp.zeros((1, D - 2 * width), jnp.float32)],
        axis=1,
    )

    gain_sum = jnp.zeros((1, D), jnp.float32)
    offset_sum = jnp.zeros((1, D), jnp.float32)
    for part in range(PARTS):
        for start, grad in (
            (mine(part), r.own[span(part * size), :]),
            (theirs(part), third.core_out[part].astype(jnp.float32)),
        ):
            nhat, scale = normalize(r.tok[span(start), :].astype(jnp.float32))
            gain_sum = gain_sum + column_sum(grad * nhat)
            offset_sum = offset_sum + column_sum(grad)
    r.fold[0:1, :] = gain_sum
    r.fold[1:2, :] = offset_sum
    fold_copy = swap_with("core", r.fold, r.fold_in, (r.share_6, r.share_7), 0)
    fold_copy.start()
    late.late()
    fold_copy.wait()
    r.chip_fold[...] = r.fold[...] + r.fold_in[...]
    chip_copy = swap_with("chip", r.chip_fold, r.chip_fold_in, (r.share_8, r.share_9), 0)
    chip_copy.start()
    scatters[3].middle()

    def norm_part(part):
        grad = third.result(part)
        nhat, scale = normalize(r.tok[span(mine(part)), :].astype(jnp.float32))
        out = r.mid[span(part * size), :] + norm_back(grad, nhat, scale, first_gain)
        r.tokens_out[span(mine(part)), :] = out.astype(jnp.bfloat16)
        token_share.copy(part, mine(part)).start()

    chip_copy.wait()
    r.small[0:2, :] = r.chip_fold[0:2, :] + r.chip_fold_in[0:2, :]
    r.small[2:5, :] = r.chip_fold[2:5, :]
    small.start()
    norm_part(0)
    small.middle()
    for part in range(1, PARTS):
        norm_part(part)
    scatters[0].finish(r.proj_share)
    scatters[1].finish(r.fc_share)
    scatters[2].finish(r.mix_share)
    scatters[3].finish(r.kv_share)
    small.finish(r.small_out)
    late.finish()
    for part in range(PARTS):
        token_share.copy(part, theirs(part)).wait_recv()
        token_share.copy(part, mine(part)).wait_send()
        c_share.copy(part, mine(part)).wait_send()
        e_share.copy(part, mine(part)).wait_send()
    wait_send_all(own_grad_side())
    each_below(lambda other: wait_send_all(grad_down(level, other)))
    each_above(lambda other: wait_send_all(grad_side(other)))
    each_above(lambda other: query_side(other).wait_send())


def layer_back(levels, inputs):
    rows, width = inputs["heads"].shape
    heads = width // DH
    half = rows // 2
    size = half // PARTS
    hidden = inputs["fc_w"].shape[1]
    slab = D // (2 * levels)
    staged = levels > 8
    bf, fl = jnp.bfloat16, jnp.float32
    vmem = pl.BlockSpec(memory_space=pltpu.VMEM)
    far = pl.BlockSpec(memory_space=pl.ANY)
    dma = pltpu.SemaphoreType.DMA
    shape = jax.ShapeDtypeStruct
    outs = {
        "output": shape((rows, D), bf),
        "tokens_out": shape((rows, D), bf),
        "proj_share": shape((slab, hidden), fl),
        "fc_share": shape((slab, hidden), fl),
        "mix_share": shape((slab, 2 * width), fl),
        "kv_share": shape((slab, 2 * width), fl),
        "small_out": shape((16, D), fl),
    }
    gathered = {
        "query_oth": ((levels, half, 2 * width), bf),
        "grad_col": ((levels, half, 2 * width), bf),
        "grad_oth": ((levels, half, 2 * width), bf),
    }
    scratch = {}
    out_specs = [vmem] * len(outs)
    if staged:
        for name, (dims, kind) in gathered.items():
            outs[name] = shape(dims, kind)
            out_specs.append(far)
        scratch["stage_query"] = pltpu.VMEM((half, 2 * width), bf)
        scratch["stage_grad"] = pltpu.VMEM((half, 2 * width), bf)
        scratch["stage_keys"] = pltpu.VMEM(inputs["kv_col"].shape[1:], bf)
        scratch["stage_sem"] = dma(())
    else:
        for name, (dims, kind) in gathered.items():
            scratch[name] = pltpu.VMEM(dims, kind)
    for name, dims, kind in (
        ("c", (rows, D), bf),
        ("e1", (rows, D), bf),
        ("u", (rows, hidden), bf),
        ("ef", (rows, hidden), bf),
        ("pull", (rows, hidden), fl),
        ("h1", (half, D), fl),
        ("own", (half, D), fl),
        ("base", (half, D), fl),
        ("mid", (half, D), fl),
        ("own_two", (half, D), fl),
        ("other_two", (half, D), bf),
        ("fold", (8, D), fl),
        ("fold_in", (8, D), fl),
        ("chip_fold", (8, D), fl),
        ("chip_fold_in", (8, D), fl),
        ("small", (16, D), fl),
        ("grad", (rows, width), bf),
        ("pack", (half, 2 * width), bf),
        ("near_rows", (8, rows), fl),
        ("far_rows", (8, rows), fl),
        ("rows_col", (levels, 8, rows), fl),
        ("rows_oth", (levels, 8, rows), fl),
        ("other_grad", (rows, width), bf),
        ("open_query", (rows, width), bf),
        ("open_grad", (rows, width), bf),
        ("doc_col", (rows, 1), fl),
        ("near_lse", (heads, rows, 1), fl),
        ("stat", (2, 2 * heads, rows, 1), fl),
        ("mem_acc", (NB, width), fl),
        ("pulls", (8, width), fl),
        ("mem_grad", (NB, 2 * width), bf),
        ("dq", (2, rows, width), fl),
        ("dk", (rows, width), fl),
        ("dv", (rows, width), fl),
        ("dq_out", (rows, width), bf),
        ("dq_in", (rows, width), bf),
        ("grads", (3, rows, width), bf),
        ("proj_blocks", (2 * levels, slab, hidden), bf),
        ("fc_blocks", (2 * levels, slab, hidden), bf),
        ("mix_blocks", (2 * levels, slab, 2 * width), bf),
        ("kv_blocks", (2 * levels, slab, 2 * width), bf),
    ):
        scratch[name] = pltpu.VMEM(dims, kind)

    def several(prefix, items):
        scratch.update({f"{prefix}_{index}": item for index, item in enumerate(items)})

    for name in ("first", "second", "third"):
        several(name, TpSum.scratch(PARTS, size, D))
    for name, columns in (("proj", hidden), ("fc", hidden), ("mix", 2 * width), ("kv", 2 * width)):
        several(name, Scatter.scratch(levels, slab, columns))
    several("small", SmallSum.scratch(levels, (16, D)))
    several("late", LateOutput.scratch(half, D))
    several("share", [dma((PARTS,))] * 10)
    for name in ("qs", "gd", "gs", "rd", "rs"):
        scratch[name + "_send"] = dma((levels,))
        scratch[name + "_recv"] = dma((levels,))
    scratch["dq_sem"] = dma((2,))
    names = [*inputs, *outs, *scratch]
    results = pl.pallas_call(
        functools.partial(back_kernel, levels, names),
        out_shape=tuple(outs.values()),
        in_specs=[far if staged and name in ("kv_col", "query_col") else vmem for name in inputs],
        out_specs=tuple(out_specs),
        scratch_shapes=list(scratch.values()),
        name="layer_back",
        compiler_params=pltpu.CompilerParams(
            collective_id=2, has_side_effects=True, vmem_limit_bytes=VMEM_LIMIT
        ),
    )(*inputs.values())
    return SimpleNamespace(**dict(zip(outs, results)))


def unpack_kernel(output_ref, tokens_ref, proj_ref, fc_ref, mix_ref, kv_ref, small_ref, *outs):
    slab, width = kv_ref.shape[0], kv_ref.shape[1] // 2
    output_out, tokens_out, qkv_out, qv_out, out_out, out_b, fc_out, fc_b, proj_out, proj_b, *rest = outs
    output_out[...] = output_ref[...]
    tokens_out[...] = tokens_ref[...]
    qkv_out[0] = mix_ref[:, :width]
    for index in range(2):
        qkv_out[1 + index] = kv_ref[:, index * width : (index + 1) * width]
        qv_out[index : index + 1, :] = small_ref[7:8, index * width : (index + 1) * width]
    fill = jnp.zeros((128 - slab, width), jnp.float32)
    out_out[...] = jnp.transpose(jnp.concatenate([mix_ref[:, width:], fill], axis=0))[:, :slab]
    fc_out[...] = fc_ref[...]
    proj_out[...] = proj_ref[...]
    for row, ref in zip((4, 5, 6, 0, 1, 2, 3), (out_b, fc_b, proj_b, *rest[:4])):
        ref[...] = small_ref[row, :]
    heads = rest[4].shape[0]
    rest[4][...] = small_ref[8 : 8 + heads, :NB]
    rest[5][...] = small_ref[8 + heads : 8 + 2 * heads, :NB]


def unpack(done, heads):
    slab, width = done.kv_share.shape[0], done.kv_share.shape[1] // 2
    hidden = done.fc_share.shape[1]
    vmem = pl.BlockSpec(memory_space=pltpu.VMEM)

    def full(*dims):
        return jax.ShapeDtypeStruct(dims, jnp.float32)

    row = full(D)
    results = pl.pallas_call(
        unpack_kernel,
        out_shape=(
            jax.ShapeDtypeStruct(done.output.shape, jnp.bfloat16),
            jax.ShapeDtypeStruct(done.output.shape, jnp.bfloat16),
            full(3, slab, width),
            full(2, width),
            full(width, slab),
            row,
            full(slab, hidden),
            row,
            full(slab, hidden),
            row,
            row,
            row,
            row,
            row,
            full(heads, NB),
            full(heads, NB),
        ),
        in_specs=[vmem] * 7,
        out_specs=(vmem,) * 16,
        name="unpack",
        compiler_params=pltpu.CompilerParams(vmem_limit_bytes=VMEM_LIMIT),
    )(
        done.output,
        done.tokens_out,
        done.proj_share,
        done.fc_share,
        done.mix_share,
        done.kv_share,
        done.small_out,
    )
    results = list(results)
    results[2] = jnp.transpose(results[2], (1, 0, 2))
    results[8] = results[8].T
    return tuple(results)


def local(
    tokens,
    cotangent,
    past_states,
    doc_ids,
    cur_book,
    past_book,
    past_age,
    ln1_gain,
    ln1_bias,
    qkv_weight,
    qv_bias,
    out_weight,
    out_bias,
    ln2_gain,
    ln2_bias,
    fc_weight,
    fc_bias,
    proj_weight,
    proj_bias,
    mu_weight,
    sigma_weight,
):
    heads_here = mu_weight.shape[0]
    seq_count = lax.axis_size("seq")
    levels = seq_count // 2
    qkv_by_kind = jnp.transpose(qkv_weight, (1, 0, 2))
    doc_row = doc_ids[None, :]
    table = jnp.asarray(np.stack(coefficient_tables(seq_count // BOOKS, NB, SEG), axis=1))
    normed, pair, kv_col, attended, lse, heads_out, coeff, memory, spot_rows, query_col = (
        attention_forward(
        levels,
        tokens,
        ln1_gain,
        ln1_bias,
        qkv_by_kind,
        qv_bias,
        doc_row,
        past_states,
        cur_book[None],
        past_book[None],
        past_age[None],
        mu_weight,
        sigma_weight,
        table,
        )
    )
    done = layer_back(
        levels,
        {
            "heads": heads_out,
            "tok": tokens,
            "cot": cotangent,
            "out_w": out_weight,
            "fc_w": fc_weight,
            "proj_w": proj_weight,
            "ln1_gain": ln1_gain,
            "ln2_gain": ln2_gain,
            "ln2_bias": ln2_bias,
            "out_b": out_bias,
            "fc_b": fc_bias,
            "proj_b": proj_bias,
            "qkv_w": qkv_by_kind,
            "attended": attended,
            "lse": lse,
            "pair": pair,
            "kv_col": kv_col,
            "query_col": query_col,
            "doc": doc_row,
            "normed": normed,
            "coeff": coeff,
            "mem": memory,
            "spot_rows": spot_rows,
            "mu_w": mu_weight,
            "sigma_w": sigma_weight,
        },
    )
    return unpack(done, heads_here)


def solution(mesh):
    in_specs = (
        P("seq", None),
        P("seq", None),
        P("seq", None),
        P("seq"),
        P("seq"),
        P("seq"),
        P("seq"),
        P(),
        P(),
        P(None, None, "tp"),
        P(None, "tp"),
        P("tp", None),
        P(),
        P(),
        P(),
        P(None, "tp"),
        P("tp"),
        P("tp", None),
        P(),
        P("tp", None),
        P("tp", None),
    )
    out_specs = (
        P("seq", None),
        P("seq", None),
        P("seq", None, "tp"),
        P(None, "tp"),
        P("tp", "seq"),
        P(),
        P("seq", "tp"),
        P("tp"),
        P("tp", "seq"),
        P(),
        P(),
        P(),
        P(),
        P(),
        P("tp", None),
        P("tp", None),
    )
    return jax.shard_map(local, mesh=mesh, in_specs=in_specs, out_specs=out_specs, check_vma=False)
```
